32 devices in a mesh: groups: 2 (over y), mp: 4 (over z), section: 2 (over x), rows: 2 (over core).
Axes of the slice: x: 2, y: 2, z: 4, core: 2. Of those that a mesh axis runs over, the one named last changes fastest.
Arguments:
- thinker_act: bfloat16 [1536, 18944], P(('groups', 'section', 'rows'), 'mp'), parts along dimension 0, may hold values from -6 to 6
- w_think: bfloat16 [18944, 3584], P('mp', ('section', 'rows')), may hold values from -0.046875 to 0.046875
- w_proj: bfloat16 [3584, 896], P('mp'), may hold values from -0.09375 to 0.09375
- talker_gain: float32 [896], replicated, may hold values from 0.25 to 1.75
- w_query: bfloat16 [896, 1536], P(None, ('section', 'rows')), may hold values from -0.1875 to 0.1875
- w_key: bfloat16 [896, 512], P(None, ('section', 'rows')), may hold values from -0.1875 to 0.1875
- w_value: bfloat16 [896, 512], P(None, ('section', 'rows')), may hold values from -0.1875 to 0.1875
- talker_slot: int32 [8, 192], P(('groups', 'section', 'rows')), parts along dimension 0, may hold values from 0 to 191, each once within a row
- kv_len: int32 [1536], P(('groups', 'mp', 'section', 'rows')), parts along dimension 0, may hold values from 1 to 256, 98304 in all
- kv_cache: bfloat16 [1536, 256, 1024], P(('groups', 'mp', 'section', 'rows')), parts along dimension 0, may hold values from -6 to 6
Outputs:
- thinker_out: bfloat16 [1536, 3584], P(('groups', 'section', 'rows'), 'mp'), parts along dimension 0
- talker_kv: bfloat16 [1536, 1024], P(('groups', 'mp', 'section', 'rows')), parts along dimension 0
- talker_ctx: float32 [1536, 1536], P(('groups', 'mp', 'section', 'rows')), parts along dimension 0
The draws below stay inside these ranges and needn't reach their ends.
There are 2 independent parts, one for each index of `groups`. The reference program is written for one: setup_inputs(seed, part) draws one part's arguments, and reference() takes and returns one part's arrays. A program takes and returns all parts, laid end to end along the dimension named above; an argument that names none is the same for every part. Nothing has to cross between parts.
Inputs may be any that keep to these rules, and one draw needn't show every extreme that they name: Each row of talker_slot holds every number of 0 to 191 once.
All inputs are finite; a program needn't handle non-finite values. No bound on the sum of `kv_len` on one device may be relied on, other than what follows from the above.
Results may differ from the reference program's by a relative error of at most 0.008.
Values may be sent and summed in bfloat16 or wider, within the bound.
No kernel may reach another device: no remote copies, remote signals or barrier semaphores. Data moves between devices by JAX's collectives and lax.ppermute only.
A program may use at most 192 MiB of HBM per device.

```python
import math
import jax
import jax.numpy as jnp
import numpy as np
from jax import lax

D = 3584
FF = 18944
TD = 896
HEADS = 12
KV_HEADS = 4
HEAD_DIM = 128
ROW_DEV = 192
CACHE = 256
QW = 1536
BLOCKS = 4
ROWS_ALL = 768
OWNED = 48


def block_levels(key, dims, split, least, high):
    loudness = 1.0
    for dim, blocks in split:
        draws = jax.random.uniform(jax.random.fold_in(jax.random.fold_in(key, 6), dim), (blocks,), jnp.float32, least / len(split), high / len(split))
        loudness = loudness * jnp.repeat(jnp.exp(draws), dims[dim] // blocks).reshape((-1,) + (1,) * (len(dims) - 1 - dim))
    return loudness


def split_up(number_of, total, bound, lean):
    weights = [(1 << 20) // math.isqrt(standing ** lean) + 1 for standing in range(2, number_of + 1)]
    rest, given = total - bound - (number_of - 1), [1] * (number_of - 1)
    while rest > 0:
        movable = [i for i in range(number_of - 1) if given[i] < bound]
        whole, left = sum([weights[i] for i in movable]), rest
        for i in movable:
            more = min(bound - given[i], max(1, left * weights[i] // whole), rest)
            given[i] = given[i] + more
            rest = rest - more
    return np.array([bound] + given)


def ragged(stream_key, number_of, total, limit, skew):
    if number_of == 2:
        one = jax.random.randint(stream_key, (), max(1, total - limit), min(limit, total - 1) + 1)
        return jnp.stack([one, total - one])
    sizes = jnp.asarray(split_up(number_of, total, limit, skew), jnp.int32)
    twos = (number_of - 1) // 2
    donor, receiver = sizes[1:1 + 2 * twos:2], sizes[2:2 + 2 * twos:2]
    slack = jnp.minimum(donor - 1, limit - receiver)
    moved = jax.random.randint(jax.random.fold_in(stream_key, 1), (twos,), 0, 1 << 20) % (slack + 1)
    sizes = sizes.at[1:1 + 2 * twos:2].set(donor - moved).at[2:2 + 2 * twos:2].set(receiver + moved)
    return sizes[jax.random.permutation(jax.random.fold_in(stream_key, 2), number_of)]


def bell_draw(own_key, shape, spread, most, cuts=(), kind=jnp.bfloat16):
    result = jax.random.normal(own_key, shape, jnp.float32) * spread
    if len(cuts) > 0:
        result = block_levels(own_key, shape, cuts, -0.22, 0.18) * result
    return jnp.clip(result, min=-most, max=most).astype(kind)


def setup_inputs(seed: int = 0, part: int = 0) -> dict:
    seeds = jax.random.split(jax.random.key(seed), 11)
    part_keys = jax.random.split(jax.random.fold_in(seeds[10], part), 11)
    return {
        "thinker_act": bell_draw(part_keys[0], (ROWS_ALL, FF), 1.0, 6.0, ((0, 4), (1, 4))),
        "w_think": bell_draw(seeds[1], (FF, D), FF ** -0.5, 0.046875, ((0, 4), (1, 4))),
        "w_proj": bell_draw(seeds[2], (D, TD), D ** -0.5, 0.09375, ((0, 4),)),
        "talker_gain": jnp.clip(1.0 + 0.15 * jax.random.normal(seeds[3], (TD,), jnp.float32), 0.25, 1.75),
        "w_query": bell_draw(seeds[4], (TD, QW), TD ** -0.5, 0.1875, ((1, 4),)),
        "w_key": bell_draw(seeds[5], (TD, KV_HEADS * HEAD_DIM), TD ** -0.5, 0.1875, ((1, 4),)),
        "w_value": bell_draw(seeds[6], (TD, KV_HEADS * HEAD_DIM), TD ** -0.5, 0.1875, ((1, 4),)),
        "talker_slot": jax.vmap(lambda own: jax.random.permutation(own, ROW_DEV))(jax.random.split(part_keys[7], BLOCKS)).reshape((BLOCKS, ROW_DEV)).astype(jnp.int32),
        "kv_len": ragged(part_keys[8], ROWS_ALL, ROWS_ALL * CACHE // 2, CACHE, 2).astype(jnp.int32),
        "kv_cache": bell_draw(part_keys[9], (ROWS_ALL, CACHE, 2 * KV_HEADS * HEAD_DIM), 1.0, 6.0, ((0, 16),)),
    }


def reference(thinker_act, w_think, w_proj, talker_gain, w_query, w_key, w_value, talker_slot, kv_len, kv_cache):
    thinker_out = jnp.dot(thinker_act, w_think, preferred_element_type=jnp.float32).astype(jnp.bfloat16)
    projected = jnp.dot(thinker_out, w_proj, preferred_element_type=jnp.float32)
    block_ids = jnp.arange(BLOCKS, dtype=jnp.int32)[:, None]
    target = talker_slot // OWNED * (BLOCKS * OWNED) + block_ids * OWNED + talker_slot % OWNED
    target = target.reshape(-1).astype(jnp.int32)
    talker_in = jnp.zeros((ROWS_ALL, TD), jnp.float32).at[target].set(projected)
    scale = lax.rsqrt(lax.optimization_barrier(jnp.mean(talker_in * talker_in, axis=1, keepdims=True)) + 1e-06)
    normed = (talker_in * scale * talker_gain).astype(jnp.bfloat16)
    query = jnp.dot(normed, w_query, preferred_element_type=jnp.float32).astype(jnp.bfloat16)
    new_key = jnp.dot(normed, w_key, preferred_element_type=jnp.float32).astype(jnp.bfloat16)
    new_value = jnp.dot(normed, w_value, preferred_element_type=jnp.float32).astype(jnp.bfloat16)
    talker_kv = jnp.concatenate([new_key, new_value], axis=1)
    group = HEADS // KV_HEADS
    kvw = KV_HEADS * HEAD_DIM
    qf = query.astype(jnp.float32).reshape(ROWS_ALL, KV_HEADS, group, HEAD_DIM)
    keys = kv_cache[:, :, :kvw].astype(jnp.float32).reshape(ROWS_ALL, CACHE, KV_HEADS, HEAD_DIM)
    values = kv_cache[:, :, kvw:].astype(jnp.float32).reshape(ROWS_ALL, CACHE, KV_HEADS, HEAD_DIM)
    nk = new_key.astype(jnp.float32).reshape(ROWS_ALL, KV_HEADS, HEAD_DIM)
    nv = new_value.astype(jnp.float32).reshape(ROWS_ALL, KV_HEADS, HEAD_DIM)
    inv = 1.0 / HEAD_DIM ** 0.5
    scores = jnp.einsum('rgjd,rpgd->rgjp', qf, keys) * inv
    own = jnp.einsum('rgjd,rgd->rgj', qf, nk) * inv
    valid = (jnp.arange(CACHE, dtype=jnp.int32)[None, :] < kv_len[:, None])[:, None, None, :]
    scores = jnp.where(valid, scores, -jnp.inf)
    top = jnp.maximum(lax.optimization_barrier(jnp.max(scores, axis=3)), own)
    expo = jnp.where(valid, jnp.exp(scores - top[..., None]), 0.0)
    own_expo = jnp.exp(own - top)
    total = lax.optimization_barrier(jnp.sum(expo, axis=3)) + own_expo
    probs = (expo / total[..., None]).astype(jnp.bfloat16).astype(jnp.float32)
    own_prob = (own_expo / total).astype(jnp.bfloat16).astype(jnp.float32)
    ctx = jnp.einsum('rgjp,rpgd->rgjd', probs, values) + own_prob[..., None] * nv[:, :, None, :]
    talker_ctx = ctx.reshape(ROWS_ALL, QW)
    return (thinker_out, talker_kv, talker_ctx)
```

```python
import functools

import jax
import jax.numpy as jnp
from jax import lax
from jax.experimental import pallas as pl
from jax.experimental.pallas import tpu as pltpu
from jax.sharding import PartitionSpec as P

HEAD_DIM = 128
ROW_STEP = 8


def attention_kernel(first_row, kv_heads, group, len_ref, q_ref, nkv_ref, kv_ref, out_ref):
    rows, cached, _ = kv_ref.shape
    width = kv_heads * HEAD_DIM
    lanes = 16
    step = pl.program_id(0)
    inv = 1.0 / HEAD_DIM**0.5
    which = lax.broadcasted_iota(jnp.int32, (lanes, width), 0)
    head = lax.broadcasted_iota(jnp.int32, (lanes, width), 1) // HEAD_DIM
    picks = [(which == j * kv_heads + head).astype(jnp.float32) for j in range(group)]
    position = lax.broadcasted_iota(jnp.int32, (lanes, cached), 1)
    for r in range(rows):
        q = q_ref[r : r + 1, :].astype(jnp.float32)
        spread = jnp.zeros((lanes, width), jnp.float32)
        for j in range(group):
            part = jnp.concatenate(
                [
                    q[:, (g * group + j) * HEAD_DIM : (g * group + j + 1) * HEAD_DIM]
                    for g in range(kv_heads)
                ],
                axis=1,
            )
            spread = spread + picks[j] * part
        nk = nkv_ref[r : r + 1, :width].astype(jnp.float32)
        nv = nkv_ref[r : r + 1, width:].astype(jnp.float32)
        own = jnp.sum(spread * nk, axis=1, keepdims=True) * inv
        scores = (
            lax.dot_general(
                spread.astype(jnp.bfloat16),
                kv_ref[r, :, :width],
                (((1,), (1,)), ((), ())),
                preferred_element_type=jnp.float32,
            )
            * inv
        )
        valid = position < len_ref[first_row + step * rows + r]
        scores = jnp.where(valid, scores, -jnp.inf)
        top = jnp.maximum(jnp.max(scores, axis=1, keepdims=True), own)
        expo = jnp.where(valid, jnp.exp(scores - top), 0.0)
        own_expo = jnp.exp(own - top)
        total = jnp.sum(expo, axis=1, keepdims=True) + own_expo
        probs = (expo / total).astype(jnp.bfloat16)
        own_prob = (own_expo / total).astype(jnp.bfloat16).astype(jnp.float32)
        ctx = lax.dot_general(
            probs,
            kv_ref[r, :, width:],
            (((1,), (0,)), ((), ())),
            preferred_element_type=jnp.float32,
        )
        ctx = ctx + own_prob * nv
        for g in range(kv_heads):
            for j in range(group):
                h = g * group + j
                i = j * kv_heads + g
                out_ref[r : r + 1, h * HEAD_DIM : (h + 1) * HEAD_DIM] = ctx[
                    i : i + 1, g * HEAD_DIM : (g + 1) * HEAD_DIM
                ]


def attention(first_row, query, new_kv, kv_len, kv_cache):
    rows, q_width = query.shape
    _, cached, kv_width = kv_cache.shape
    kv_heads = kv_width // 2 // HEAD_DIM
    group = q_width // (kv_width // 2)
    step = ROW_STEP
    offset = first_row // step
    return pl.pallas_call(
        functools.partial(attention_kernel, first_row, kv_heads, group),
        out_shape=jax.ShapeDtypeStruct((rows, q_width), jnp.float32),
        grid_spec=pltpu.PrefetchScalarGridSpec(
            num_scalar_prefetch=1,
            grid=(rows // step,),
            in_specs=[
                pl.BlockSpec((step, q_width), lambda i, _: (i, 0)),
                pl.BlockSpec((step, kv_width), lambda i, _: (i, 0)),
                pl.BlockSpec((step, cached, kv_width), lambda i, _: (i + offset, 0, 0)),
            ],
            out_specs=pl.BlockSpec((step, q_width), lambda i, _: (i, 0)),
        ),
        cost_estimate=pl.CostEstimate(
            flops=4 * rows * cached * q_width,
            bytes_accessed=2 * rows * cached * kv_width,
            transcendentals=rows * cached * q_width // HEAD_DIM,
        ),
        compiler_params=pltpu.CompilerParams(vmem_limit_bytes=32 * 1024 * 1024),
    )(kv_len, query, new_kv, kv_cache)


def rms_norm(talker_in, talker_gain):
    scale = lax.rsqrt(jnp.mean(talker_in * talker_in, axis=1, keepdims=True) + 1e-06)
    return (talker_in * scale * talker_gain).astype(jnp.bfloat16)


def talker_step(talker_in, talker_gain, w_query, w_key, w_value, kv_len, kv_cache):
    owned = talker_in.shape[0]
    cached = kv_cache.shape[1]
    kv_width = w_key.shape[1]
    head_dim = HEAD_DIM
    kv_heads = kv_width // head_dim
    group = w_query.shape[1] // kv_width
    normed = rms_norm(talker_in, talker_gain)
    query = jnp.dot(normed, w_query, preferred_element_type=jnp.float32).astype(jnp.bfloat16)
    new_key = jnp.dot(normed, w_key, preferred_element_type=jnp.float32).astype(jnp.bfloat16)
    new_value = jnp.dot(normed, w_value, preferred_element_type=jnp.float32).astype(jnp.bfloat16)
    talker_kv = jnp.concatenate([new_key, new_value], axis=1)
    qb = query.reshape(owned, kv_heads, group, head_dim)
    keys = kv_cache[:, :, :kv_width].reshape(owned, cached, kv_heads, head_dim)
    values = kv_cache[:, :, kv_width:].reshape(owned, cached, kv_heads, head_dim)
    nk = new_key.reshape(owned, kv_heads, head_dim)
    nv = new_value.reshape(owned, kv_heads, head_dim)
    inv = 1.0 / head_dim**0.5
    scores = jnp.einsum("rgjd,rpgd->rgjp", qb, keys, preferred_element_type=jnp.float32) * inv
    own = jnp.einsum("rgjd,rgd->rgj", qb, nk, preferred_element_type=jnp.float32) * inv
    valid = (jnp.arange(cached, dtype=jnp.int32)[None, :] < kv_len[:, None])[:, None, None, :]
    scores = jnp.where(valid, scores, -jnp.inf)
    top = jnp.maximum(jnp.max(scores, axis=3), own)
    expo = jnp.where(valid, jnp.exp(scores - top[..., None]), 0.0)
    own_expo = jnp.exp(own - top)
    total = jnp.sum(expo, axis=3) + own_expo
    probs = (expo / total[..., None]).astype(jnp.bfloat16)
    own_prob = (own_expo / total).astype(jnp.bfloat16)
    ctx = jnp.einsum("rgjp,rpgd->rgjd", probs, values, preferred_element_type=jnp.float32)
    ctx = ctx + own_prob.astype(jnp.float32)[..., None] * nv.astype(jnp.float32)[:, :, None, :]
    return (talker_kv, ctx.reshape(owned, w_query.shape[1]))


def any_mesh(
    thinker_act,
    w_think,
    w_proj,
    talker_gain,
    w_query,
    w_key,
    w_value,
    talker_slot,
    kv_len,
    kv_cache,
):
    partial_sums = jnp.dot(
        thinker_act,
        lax.all_gather(w_think, ("section", "rows"), axis=1, tiled=True),
        preferred_element_type=jnp.float32,
    )
    full_query, full_key, full_value = (
        lax.all_gather(w_query, ("section", "rows"), axis=1, tiled=True),
        lax.all_gather(w_key, ("section", "rows"), axis=1, tiled=True),
        lax.all_gather(w_value, ("section", "rows"), axis=1, tiled=True),
    )
    mine = lax.psum_scatter(partial_sums, "mp", scatter_dimension=1, tiled=True)
    thinker_out = mine.astype(jnp.bfloat16)
    order = jnp.argsort(talker_slot[0], stable=True)
    sorted_out = thinker_out[order]
    talker_in = lax.psum_scatter(
        jnp.dot(sorted_out, w_proj, preferred_element_type=jnp.float32),
        "mp",
        scatter_dimension=0,
        tiled=True,
    )
    talker_kv, talker_ctx = talker_step(
        talker_in, talker_gain, full_query, full_key, full_value, kv_len, kv_cache
    )
    return (thinker_out, talker_kv, talker_ctx)


PLANE = ("section", "rows")
GROUP = ("mp", "section", "rows")


def over_core(x):
    return lax.ppermute(x, "rows", [(0, 1), (1, 0)])


def over_section(x):
    return lax.ppermute(x, "section", [(0, 1), (1, 0)])


def gathered_qkv(w_query, w_key, w_value, after):
    mine = jnp.concatenate([w_query, w_key, w_value], axis=1)
    half = mine.shape[0] // 2
    g = lax.axis_index("groups")
    piece = lax.dynamic_slice_in_dim(mine, g * half, half, axis=0)
    piece, _ = lax.optimization_barrier((piece, after))
    crossed = over_section(piece)
    other = lax.ppermute(crossed, "groups", [(0, 1), (1, 0)])
    pair = jnp.stack([crossed, other])
    across = pair[jnp.arange(2) ^ g].reshape(mine.shape)
    four = [mine, over_core(mine), across, over_core(across)]
    c = lax.axis_index(PLANE)
    return jnp.stack(four)[jnp.arange(4) ^ c]


def four_planes(
    thinker_act,
    w_think,
    w_proj,
    talker_gain,
    w_query,
    w_key,
    w_value,
    talker_slot,
    kv_len,
    kv_cache,
):
    planes = 4
    owned = kv_cache.shape[0]
    m = lax.axis_index("mp")
    c = lax.axis_index(PLANE)
    columns = w_think.shape[1]
    slots = talker_slot[0]
    chunks = [(0, 32), (32, 16)]

    sent = []
    for first, n in chunks:
        plane = (m + jnp.arange(planes, dtype=jnp.int32)) % planes
        want = (plane[:, None] * owned + first + jnp.arange(n, dtype=jnp.int32)[None, :]).reshape(-1)
        pick = (want[:, None] == slots[None, :]).astype(jnp.bfloat16)
        rows = jnp.dot(pick, thinker_act, preferred_element_type=jnp.float32).astype(jnp.bfloat16)
        sent.append(rows)

    crossed = []
    for rows in sent:
        if crossed:
            rows, _ = lax.optimization_barrier((rows, crossed[-1]))
        crossed.append(over_section(rows))
    w_qkv = gathered_qkv(w_query, w_key, w_value, crossed[-1])

    returned, kvs, ctxs = [], [], []
    for (first, n), own_rows, across in zip(chunks, sent, crossed):
        blocks = []
        for near, far in ((own_rows, over_core(own_rows)), (across, over_core(across))):
            sums = [
                jnp.dot(x, w_think, preferred_element_type=jnp.float32).reshape(planes, n, columns)
                for x in (near, far)
            ]
            total = jnp.stack([s[0] for s in sums])
            for d in range(1, planes):
                out = jnp.stack([s[d] for s in sums]).astype(jnp.bfloat16)
                got = lax.ppermute(out, "mp", [(i, (i + d) % planes) for i in range(planes)])
                total = total + got.astype(jnp.float32)
            blocks.append(total.astype(jnp.bfloat16))
        mine = jnp.concatenate(blocks, axis=0)
        home = []
        for k in range(planes):
            out = lax.dynamic_index_in_dim(mine, m ^ k, axis=0, keepdims=False)
            pairs = [
                (p * 4 + b, b * 4 + (b ^ p ^ k)) for p in range(planes) for b in range(4)
            ]
            home.append(lax.ppermute(out, GROUP, pairs))
        home = jnp.stack(home)
        returned.append(home)
        projected = jnp.dot(
            home.reshape(planes * n, columns), w_proj, preferred_element_type=jnp.float32
        ).astype(jnp.bfloat16)
        projected = projected.reshape(planes, n, -1)
        talker_in = 0.0
        for k in range(planes):
            pairs = [
                (p * 4 + b, (p ^ b ^ k) * 4 + b) for p in range(planes) for b in range(4)
            ]
            talker_in = talker_in + lax.ppermute(projected[k], GROUP, pairs).astype(jnp.float32)
        normed = rms_norm(talker_in, talker_gain)
        qkv = jnp.einsum("rk,bkn->brn", normed, w_qkv, preferred_element_type=jnp.float32)
        qkv = qkv.astype(jnp.bfloat16)
        q_cols, k_cols = w_query.shape[1], w_key.shape[1]

        def across_blocks(x):
            return jnp.moveaxis(x, 0, 1).reshape(n, -1)

        query = across_blocks(qkv[:, :, :q_cols])
        new_kv = jnp.concatenate(
            [
                across_blocks(qkv[:, :, q_cols : q_cols + k_cols]),
                across_blocks(qkv[:, :, q_cols + k_cols :]),
            ],
            axis=1,
        )
        kvs.append(new_kv)
        ctxs.append(attention(first, query, new_kv, kv_len, kv_cache))

    where_to = []
    for first, n in chunks:
        plane = m ^ c ^ jnp.arange(planes, dtype=jnp.int32)
        where_to.append(
            (plane[:, None] * owned + first + jnp.arange(n, dtype=jnp.int32)[None, :]).reshape(-1)
        )
    pick = (slots[:, None] == jnp.concatenate(where_to)[None, :]).astype(jnp.bfloat16)
    home = jnp.concatenate([h.reshape(-1, columns) for h in returned], axis=0)
    thinker_out = jnp.dot(pick, home, preferred_element_type=jnp.float32).astype(jnp.bfloat16)
    return (thinker_out, jnp.concatenate(kvs, axis=0), jnp.concatenate(ctxs, axis=0))


def solution(mesh):
    in_specs = (
        P(("groups", "section", "rows"), "mp"),
        P("mp", ("section", "rows")),
        P("mp", None),
        P(),
        P(None, ("section", "rows")),
        P(None, ("section", "rows")),
        P(None, ("section", "rows")),
        P(("groups", "section", "rows"), None),
        P(("groups", "mp", "section", "rows")),
        P(("groups", "mp", "section", "rows"), None, None),
    )
    out_specs = (
        P(("groups", "section", "rows"), "mp"),
        P(("groups", "mp", "section", "rows"), None),
        P(("groups", "mp", "section", "rows"), None),
    )
    sizes = tuple(mesh.shape[a] for a in ("groups", "section", "rows", "mp"))
    shards = four_planes if sizes == (2, 2, 2, 4) else any_mesh
    return jax.shard_map(shards, mesh=mesh, in_specs=in_specs, out_specs=out_specs, check_vma=False)
```

```python
import functools

import jax
import jax.numpy as jnp
from jax import lax
from jax.experimental import pallas as pl
from jax.experimental.pallas import tpu as pltpu
from jax.sharding import PartitionSpec as P

HEAD_DIM = 128
ROW_STEP = 8
LANES = 128


def talker_kernel(
    first_row, heads, len_ref, block_ref, sums_ref, gain_ref, w0, w1, w2, w3, kv_ref,
    new_kv_ref, out_ref, qkv, spread, gathered,
):
    step = pl.program_id(0)
    blocks = qkv.shape[0]
    group = heads // blocks
    slot = LANES // ROW_STEP
    cached = kv_ref.shape[1]
    width = blocks * HEAD_DIM
    inv = 1.0 / HEAD_DIM**0.5

    @pl.when(step == 0)
    def _():
        talker_in = sums_ref[0].astype(jnp.float32)
        for k in range(1, sums_ref.shape[0]):
            talker_in = talker_in + sums_ref[k].astype(jnp.float32)
        scale = lax.rsqrt(jnp.mean(talker_in * talker_in, axis=1, keepdims=True) + 1e-06)
        normed = (talker_in * scale * gain_ref[...]).astype(jnp.bfloat16)
        for e, w in enumerate((w0, w1, w2, w3)):
            made = jnp.dot(normed, w[...], preferred_element_type=jnp.float32)
            qkv[e ^ block_ref[0]] = made.astype(jnp.bfloat16).astype(jnp.float32)
        for g in range(blocks):
            key, value = group * HEAD_DIM, (group + 1) * HEAD_DIM
            new_kv_ref[:, g * HEAD_DIM : (g + 1) * HEAD_DIM] = qkv[g, :, key:value].astype(
                jnp.bfloat16
            )
            new_kv_ref[:, width + g * HEAD_DIM : width + (g + 1) * HEAD_DIM] = qkv[
                g, :, value:
            ].astype(jnp.bfloat16)
        spread[...] = jnp.zeros_like(spread)

    here = pl.ds(pl.multiple_of(step * ROW_STEP, ROW_STEP), ROW_STEP)
    for h in range(heads):
        g, j = h // group, h % group
        spread[pl.ds(h, ROW_STEP, stride=slot), :] = qkv[
            g, here, j * HEAD_DIM : (j + 1) * HEAD_DIM
        ]
    query = spread[...].T
    lane = lax.broadcasted_iota(jnp.int32, (HEAD_DIM, LANES), 1)
    lane_row, lane_block = lane // slot, lane % slot // group
    by_block = [
        jnp.where(lane_block == g, query, 0.0).astype(jnp.bfloat16) for g in range(blocks)
    ]

    scores = jnp.zeros((cached, LANES), jnp.float32)
    for r in range(ROW_STEP):
        mine = lane_row == r
        right = jnp.concatenate(
            [jnp.where(mine, q, jnp.zeros_like(q)) for q in by_block], axis=0
        )
        scores = scores + jnp.dot(
            kv_ref[r, :, :width], right, preferred_element_type=jnp.float32
        )
    own = jnp.zeros((ROW_STEP, LANES), jnp.float32)
    for g in range(blocks):
        key = qkv[g, here, group * HEAD_DIM : (group + 1) * HEAD_DIM].astype(jnp.bfloat16)
        own = own + jnp.dot(key, by_block[g], preferred_element_type=jnp.float32)
    own_row = lax.broadcasted_iota(jnp.int32, own.shape, 0)
    own = jnp.sum(jnp.where(own_row == lane_row[:ROW_STEP], own, 0.0), axis=0, keepdims=True)

    scores, own = scores * inv, own * inv
    lens = jnp.zeros((1, LANES), jnp.int32)
    for r in range(ROW_STEP):
        lens = jnp.where(lane_row[:1] == r, len_ref[first_row + step * ROW_STEP + r], lens)
    valid = lax.broadcasted_iota(jnp.int32, scores.shape, 0) < lens
    scores = jnp.where(valid, scores, -jnp.inf)
    top = jnp.maximum(jnp.max(scores, axis=0, keepdims=True), own)
    expo = jnp.where(valid, jnp.exp(scores - top), 0.0)
    own_expo = jnp.exp(own - top)
    total = jnp.sum(expo, axis=0, keepdims=True) + own_expo
    probs = (expo / total).T.astype(jnp.bfloat16)
    own_prob = (own_expo / total).astype(jnp.bfloat16).astype(jnp.float32)
    own_prob = jnp.broadcast_to(own_prob, (LANES, LANES)).T

    row_block = lax.broadcasted_iota(jnp.int32, (slot, HEAD_DIM), 0) // group
    for r in range(ROW_STEP):
        rows = slice(r * slot, (r + 1) * slot)
        made = jnp.dot(
            probs[rows], kv_ref[r, :, width:], preferred_element_type=jnp.float32
        )
        values = qkv.at[:, here]
        ctx = jnp.zeros((slot, HEAD_DIM), jnp.float32)
        value = jnp.zeros((slot, HEAD_DIM), jnp.float32)
        for g in range(blocks):
            new = values[g, r : r + 1, (group + 1) * HEAD_DIM :]
            ctx = jnp.where(row_block == g, made[:, g * HEAD_DIM : (g + 1) * HEAD_DIM], ctx)
            value = jnp.where(row_block == g, new, value)
        gathered[rows, :] = ctx + own_prob[rows] * value
    for h in range(heads):
        out_ref[:, h * HEAD_DIM : (h + 1) * HEAD_DIM] = gathered[
            pl.ds(h, ROW_STEP, stride=slot), :
        ]


def talker_rows(first_row, block, sums, talker_gain, weights, kv_len, kv_cache):
    terms, rows, wide = sums.shape
    _, cached, kv_width = kv_cache.shape
    columns = weights[0].shape[1]
    q_width = len(weights) * columns - kv_width
    heads = q_width // HEAD_DIM
    offset = first_row // ROW_STEP
    whole = lambda *shape: pl.BlockSpec(shape, lambda i, *_: (0,) * len(shape))
    return pl.pallas_call(
        functools.partial(talker_kernel, first_row, heads),
        out_shape=(
            jax.ShapeDtypeStruct((rows, kv_width), jnp.bfloat16),
            jax.ShapeDtypeStruct((rows, q_width), jnp.float32),
        ),
        grid_spec=pltpu.PrefetchScalarGridSpec(
            num_scalar_prefetch=2,
            grid=(rows // ROW_STEP,),
            in_specs=[
                whole(terms, rows, wide),
                whole(1, wide),
                *[whole(wide, columns) for _ in weights],
                pl.BlockSpec((ROW_STEP, cached, kv_width), lambda i, *_: (i + offset, 0, 0)),
            ],
            out_specs=(
                whole(rows, kv_width),
                pl.BlockSpec((ROW_STEP, q_width), lambda i, *_: (i, 0)),
            ),
            scratch_shapes=[
                pltpu.VMEM((len(weights), rows, columns), jnp.float32),
                pltpu.VMEM((LANES, HEAD_DIM), jnp.float32),
                pltpu.VMEM((LANES, HEAD_DIM), jnp.float32),
            ],
        ),
        cost_estimate=pl.CostEstimate(
            flops=4 * rows * cached * q_width,
            bytes_accessed=2 * rows * cached * kv_width,
            transcendentals=rows * cached * heads,
        ),
        compiler_params=pltpu.CompilerParams(vmem_limit_bytes=32 * 1024 * 1024),
    )(kv_len, block, sums, talker_gain.reshape(1, wide), *weights, kv_cache)


def rms_norm(talker_in, talker_gain):
    scale = lax.rsqrt(jnp.mean(talker_in * talker_in, axis=1, keepdims=True) + 1e-06)
    return (talker_in * scale * talker_gain).astype(jnp.bfloat16)


def talker_step(talker_in, talker_gain, w_query, w_key, w_value, kv_len, kv_cache):
    owned = talker_in.shape[0]
    cached = kv_cache.shape[1]
    kv_width = w_key.shape[1]
    head_dim = HEAD_DIM
    kv_heads = kv_width // head_dim
    group = w_query.shape[1] // kv_width
    normed = rms_norm(talker_in, talker_gain)
    query = jnp.dot(normed, w_query, preferred_element_type=jnp.float32).astype(jnp.bfloat16)
    new_key = jnp.dot(normed, w_key, preferred_element_type=jnp.float32).astype(jnp.bfloat16)
    new_value = jnp.dot(normed, w_value, preferred_element_type=jnp.float32).astype(jnp.bfloat16)
    talker_kv = jnp.concatenate([new_key, new_value], axis=1)
    qb = query.reshape(owned, kv_heads, group, head_dim)
    keys = kv_cache[:, :, :kv_width].reshape(owned, cached, kv_heads, head_dim)
    values = kv_cache[:, :, kv_width:].reshape(owned, cached, kv_heads, head_dim)
    nk = new_key.reshape(owned, kv_heads, head_dim)
    nv = new_value.reshape(owned, kv_heads, head_dim)
    inv = 1.0 / head_dim**0.5
    scores = jnp.einsum("rgjd,rpgd->rgjp", qb, keys, preferred_element_type=jnp.float32) * inv
    own = jnp.einsum("rgjd,rgd->rgj", qb, nk, preferred_element_type=jnp.float32) * inv
    valid = (jnp.arange(cached, dtype=jnp.int32)[None, :] < kv_len[:, None])[:, None, None, :]
    scores = jnp.where(valid, scores, -jnp.inf)
    top = jnp.maximum(jnp.max(scores, axis=3), own)
    expo = jnp.where(valid, jnp.exp(scores - top[..., None]), 0.0)
    own_expo = jnp.exp(own - top)
    total = jnp.sum(expo, axis=3) + own_expo
    probs = (expo / total[..., None]).astype(jnp.bfloat16)
    own_prob = (own_expo / total).astype(jnp.bfloat16)
    ctx = jnp.einsum("rgjp,rpgd->rgjd", probs, values, preferred_element_type=jnp.float32)
    ctx = ctx + own_prob.astype(jnp.float32)[..., None] * nv.astype(jnp.float32)[:, :, None, :]
    return (talker_kv, ctx.reshape(owned, w_query.shape[1]))


def any_mesh(
    thinker_act,
    w_think,
    w_proj,
    talker_gain,
    w_query,
    w_key,
    w_value,
    talker_slot,
    kv_len,
    kv_cache,
):
    partial_sums = jnp.dot(
        thinker_act,
        lax.all_gather(w_think, ("section", "rows"), axis=1, tiled=True),
        preferred_element_type=jnp.float32,
    )
    full_query, full_key, full_value = (
        lax.all_gather(w_query, ("section", "rows"), axis=1, tiled=True),
        lax.all_gather(w_key, ("section", "rows"), axis=1, tiled=True),
        lax.all_gather(w_value, ("section", "rows"), axis=1, tiled=True),
    )
    mine = lax.psum_scatter(partial_sums, "mp", scatter_dimension=1, tiled=True)
    thinker_out = mine.astype(jnp.bfloat16)
    order = jnp.argsort(talker_slot[0], stable=True)
    sorted_out = thinker_out[order]
    talker_in = lax.psum_scatter(
        jnp.dot(sorted_out, w_proj, preferred_element_type=jnp.float32),
        "mp",
        scatter_dimension=0,
        tiled=True,
    )
    talker_kv, talker_ctx = talker_step(
        talker_in, talker_gain, full_query, full_key, full_value, kv_len, kv_cache
    )
    return (thinker_out, talker_kv, talker_ctx)


PLANE = ("section", "rows")


def over_core(x):
    return lax.ppermute(x, "rows", [(0, 1), (1, 0)])


def over_section(x):
    return lax.ppermute(x, "section", [(0, 1), (1, 0)])


def after(x, *others):
    return lax.optimization_barrier((x, *others))[0]


def four_planes(
    thinker_act,
    w_think,
    w_proj,
    talker_gain,
    w_query,
    w_key,
    w_value,
    talker_slot,
    kv_len,
    kv_cache,
):
    planes = 4
    owned = kv_cache.shape[0]
    g, m, c = lax.axis_index("groups"), lax.axis_index("mp"), lax.axis_index(PLANE)
    columns = w_think.shape[1]
    slots = talker_slot[0]
    chunks = [(0, 32), (32, 16)]

    wanted, sent = [], []
    for first, n in chunks:
        plane = jnp.arange(planes, dtype=jnp.int32)[:, None] * owned
        want = (plane + first + jnp.arange(n, dtype=jnp.int32)[None, :]).reshape(-1)
        pick = (want[:, None] == slots[None, :]).astype(jnp.bfloat16)
        rows = jnp.dot(pick, thinker_act, preferred_element_type=jnp.float32)
        wanted.append(want)
        sent.append(rows.astype(jnp.bfloat16))

    mine = jnp.concatenate([w_query, w_key, w_value], axis=1)
    depth = mine.shape[0] // (2 * planes)
    piece = lax.dynamic_slice_in_dim(mine, (g * planes + m) * depth, depth, axis=0)
    piece = over_section(piece)
    crossed = [over_section(after(sent[0], piece))]
    other = lax.all_gather(piece, ("groups", "mp"), axis=0, tiled=True)
    crossed.append(over_section(after(sent[1], crossed[0])))
    weights = [mine, over_core(mine), other, over_core(other)]

    def times_w(x):
        return jnp.dot(x, w_think, preferred_element_type=jnp.float32).astype(jnp.bfloat16)

    near = [(times_w(rows), times_w(over_core(rows))) for rows in sent]
    returned, kvs, ctxs = [], [], []
    for (first, n), own, across in zip(chunks, near, crossed):
        four = [*own, times_w(across), times_w(over_core(across))]
        swapped = [jnp.where(c & 1, four[e ^ 1], four[e]) for e in range(4)]
        blocks = jnp.stack([jnp.where(c & 2, swapped[e ^ 2], swapped[e]) for e in range(4)])
        mixed = lax.all_to_all(blocks, PLANE, 0, 0)
        terms = lax.all_to_all(mixed, "mp", 0, 0)
        home = jnp.sum(terms.astype(jnp.float32), axis=0).astype(jnp.bfloat16)
        returned.append(home)
        projected = jnp.dot(home, w_proj, preferred_element_type=jnp.float32)
        projected = projected.astype(jnp.bfloat16).reshape(planes, n, -1)
        sums = lax.all_to_all(projected, "mp", 0, 0)
        new_kv, ctx = talker_rows(
            first, c.reshape(1), sums, talker_gain, weights, kv_len, kv_cache
        )
        kvs.append(new_kv)
        ctxs.append(ctx)

    pick = (slots[:, None] == jnp.concatenate(wanted)[None, :]).astype(jnp.bfloat16)
    home = jnp.concatenate(returned, axis=0)
    thinker_out = jnp.dot(pick, home, preferred_element_type=jnp.float32).astype(jnp.bfloat16)
    return (thinker_out, jnp.concatenate(kvs, axis=0), jnp.concatenate(ctxs, axis=0))


def solution(mesh):
    in_specs = (
        P(("groups", "section", "rows"), "mp"),
        P("mp", ("section", "rows")),
        P("mp", None),
        P(),
        P(None, ("section", "rows")),
        P(None, ("section", "rows")),
        P(None, ("section", "rows")),
        P(("groups", "section", "rows"), None),
        P(("groups", "mp", "section", "rows")),
        P(("groups", "mp", "section", "rows"), None, None),
    )
    out_specs = (
        P(("groups", "section", "rows"), "mp"),
        P(("groups", "mp", "section", "rows"), None),
        P(("groups", "mp", "section", "rows"), None),
    )
    sizes = tuple(mesh.shape[a] for a in ("groups", "section", "rows", "mp"))
    shards = four_planes if sizes == (2, 2, 2, 4) else any_mesh
    return jax.shard_map(shards, mesh=mesh, in_specs=in_specs, out_specs=out_specs, check_vma=False)
```

```python
import functools

import jax
import jax.numpy as jnp
from jax import lax
from jax.experimental import pallas as pl
from jax.experimental.pallas import tpu as pltpu
from jax.sharding import PartitionSpec as P

HEAD_DIM = 128
ROW_STEP = 8
LANES = 128


def down_kernel(counts, planes, cuts, *refs):
    groups = len(counts)
    xs, (w, out, x_all, w_all, acc, x_sem, w_sem) = refs[:groups], refs[groups:]
    first = [planes * sum(counts[:i]) for i in range(groups)]
    pulls = [
        pltpu.make_async_copy(
            xs[i], x_all.at[pl.ds(first[i], planes * counts[i])], x_sem.at[i]
        )
        for i in range(groups)
    ]
    loads = [
        pltpu.make_async_copy(w.at[pl.ds(lo, hi - lo)], w_all.at[pl.ds(lo, hi - lo)], w_sem.at[i])
        for i, (lo, hi) in enumerate(cuts)
    ]
    for copy in (*pulls, *loads):
        copy.start()
    for copy in pulls:
        copy.wait()
    for i, (lo, hi) in enumerate(cuts):
        loads[i].wait()
        part = jnp.dot(x_all[:, lo:hi], w_all[lo:hi, :], preferred_element_type=jnp.float32)
        acc[...] = part if i == 0 else acc[...] + part
    for i, n in enumerate(counts):
        row = sum(counts[:i])
        for p in range(planes):
            at = first[i] + p * n
            out[p, row : row + n, :] = acc[at : at + n, :].astype(out.dtype)


def down(xs, w, planes):
    depth, columns = w.shape
    counts = [x.shape[0] // planes for x in xs]
    rows = sum(counts)
    tiles, parts = depth // LANES, 4
    ends = [LANES * (tiles * i // parts) for i in range(parts)] + [depth]
    return pl.pallas_call(
        functools.partial(down_kernel, counts, planes, list(zip(ends[:-1], ends[1:]))),
        out_shape=jax.ShapeDtypeStruct((planes, rows, columns), jnp.bfloat16),
        in_specs=[pl.BlockSpec(memory_space=pl.ANY)] * (len(xs) + 1),
        out_specs=pl.BlockSpec(memory_space=pltpu.VMEM),
        scratch_shapes=[
            pltpu.VMEM((planes * rows, depth), jnp.bfloat16),
            pltpu.VMEM((depth, columns), jnp.bfloat16),
            pltpu.VMEM((planes * rows, columns), jnp.float32),
            pltpu.SemaphoreType.DMA((len(xs),)),
            pltpu.SemaphoreType.DMA((parts,)),
        ],
        cost_estimate=pl.CostEstimate(
            flops=2 * planes * rows * depth * columns,
            bytes_accessed=2 * depth * (columns + planes * rows),
            transcendentals=0,
        ),
        compiler_params=pltpu.CompilerParams(vmem_limit_bytes=28 * 1024 * 1024),
    )(*xs, w)


def finish_kernel(terms, w, near, far):
    total = terms[0].astype(jnp.float32)
    for k in range(1, terms.shape[0]):
        total = total + terms[k].astype(jnp.float32)
    features = total.astype(jnp.bfloat16)
    projected = jnp.dot(features, w[...], preferred_element_type=jnp.float32)
    projected = projected.astype(jnp.bfloat16)
    n = features.shape[0] // 2
    for out, at in ((near, 0), (far, n)):
        out[0] = features[at : at + n]
        out[1] = projected[at : at + n]


def finish(terms, w_proj):
    _, rows, columns = terms.shape
    half = jax.ShapeDtypeStruct((2, rows // 2, columns), jnp.bfloat16)
    vmem = pl.BlockSpec(memory_space=pltpu.VMEM)
    return pl.pallas_call(
        finish_kernel,
        out_shape=(half, half),
        in_specs=[vmem, vmem],
        out_specs=(vmem, vmem),
        cost_estimate=pl.CostEstimate(
            flops=2 * rows * columns * columns,
            bytes_accessed=2 * columns * (columns + 6 * rows),
            transcendentals=0,
        ),
        compiler_params=pltpu.CompilerParams(vmem_limit_bytes=16 * 1024 * 1024),
    )(terms, w_proj)


def prepare_kernel(group, spans, block_ref, gain, w0, w1, w2, w3, *refs):
    pieces, (home, new_kv, qkv) = refs[: sum(map(len, spans))], refs[sum(map(len, spans)) :]
    at = 0
    total = None
    for e, span in enumerate(spans):
        terms = []
        for first, n in span:
            home[e ^ block_ref[0], first : first + n, :] = pieces[at][0]
            terms.append(pieces[at][1].astype(jnp.float32))
            at += 1
        term = jnp.concatenate(terms, axis=0) if len(terms) > 1 else terms[0]
        total = term if total is None else total + term
    scale = lax.rsqrt(jnp.mean(total * total, axis=1, keepdims=True) + 1e-06)
    normed = (total * scale * gain[...]).astype(jnp.bfloat16)
    for e, w in enumerate((w0, w1, w2, w3)):
        made = jnp.dot(normed, w[...], preferred_element_type=jnp.float32)
        qkv[e ^ block_ref[0]] = made.astype(jnp.bfloat16).astype(jnp.float32)
    blocks = qkv.shape[0]
    key, value = group * HEAD_DIM, (group + 1) * HEAD_DIM
    for g in range(blocks):
        for place, start in ((g, key), (blocks + g, value)):
            new_kv[:, place * HEAD_DIM : (place + 1) * HEAD_DIM] = qkv[
                g, :, start : start + HEAD_DIM
            ].astype(jnp.bfloat16)


def prepare(block, pieces, spans, talker_gain, weights):
    flat = [p for piece in pieces for p in piece]
    rows = sum(n for _, n in spans[0])
    wide, columns = weights[0].shape
    group = columns // HEAD_DIM - 2
    vmem = pl.BlockSpec(memory_space=pltpu.VMEM)
    return pl.pallas_call(
        functools.partial(prepare_kernel, group, spans),
        out_shape=(
            jax.ShapeDtypeStruct((len(weights), rows, flat[0].shape[2]), jnp.bfloat16),
            jax.ShapeDtypeStruct((rows, 2 * len(weights) * HEAD_DIM), jnp.bfloat16),
            jax.ShapeDtypeStruct((len(weights), rows, columns), jnp.float32),
        ),
        in_specs=[pl.BlockSpec(memory_space=pltpu.SMEM)] + [vmem] * (5 + len(flat)),
        out_specs=(vmem, vmem, vmem),
        cost_estimate=pl.CostEstimate(
            flops=2 * rows * wide * columns * len(weights),
            bytes_accessed=2 * wide * columns * len(weights),
            transcendentals=rows,
        ),
        compiler_params=pltpu.CompilerParams(vmem_limit_bytes=24 * 1024 * 1024),
    )(block, talker_gain.reshape(1, wide), *weights, *flat)


def attention_kernel(heads, len_ref, qkv, kv_ref, out_ref, spread, gathered):
    step = pl.program_id(0)
    blocks = qkv.shape[0]
    group = heads // blocks
    slot = LANES // ROW_STEP
    cached = kv_ref.shape[1]
    width = blocks * HEAD_DIM
    inv = 1.0 / HEAD_DIM**0.5

    @pl.when(step == 0)
    def _():
        spread[...] = jnp.zeros_like(spread)

    for h in range(heads):
        g, j = h // group, h % group
        spread[pl.ds(h, ROW_STEP, stride=slot), :] = qkv[g, :, j * HEAD_DIM : (j + 1) * HEAD_DIM]
    query = spread[...].T
    lane = lax.broadcasted_iota(jnp.int32, (HEAD_DIM, LANES), 1)
    lane_row, lane_block = lane // slot, lane % slot // group
    by_block = [
        jnp.where(lane_block == g, query, 0.0).astype(jnp.bfloat16) for g in range(blocks)
    ]

    scores = jnp.zeros((cached, LANES), jnp.float32)
    for r in range(ROW_STEP):
        mine = lane_row == r
        right = jnp.concatenate(
            [jnp.where(mine, q, jnp.zeros_like(q)) for q in by_block], axis=0
        )
        scores = scores + jnp.dot(
            kv_ref[r, :, :width], right, preferred_element_type=jnp.float32
        )
    own = jnp.zeros((ROW_STEP, LANES), jnp.float32)
    for g in range(blocks):
        key = qkv[g, :, group * HEAD_DIM : (group + 1) * HEAD_DIM].astype(jnp.bfloat16)
        own = own + jnp.dot(key, by_block[g], preferred_element_type=jnp.float32)
    own_row = lax.broadcasted_iota(jnp.int32, own.shape, 0)
    own = jnp.sum(jnp.where(own_row == lane_row[:ROW_STEP], own, 0.0), axis=0, keepdims=True)

    scores, own = scores * inv, own * inv
    lens = jnp.zeros((1, LANES), jnp.int32)
    for r in range(ROW_STEP):
        lens = jnp.where(lane_row[:1] == r, len_ref[step * ROW_STEP + r], lens)
    valid = lax.broadcasted_iota(jnp.int32, scores.shape, 0) < lens
    scores = jnp.where(valid, scores, -jnp.inf)
    top = jnp.maximum(jnp.max(scores, axis=0, keepdims=True), own)
    expo = jnp.where(valid, jnp.exp(scores - top), 0.0)
    own_expo = jnp.exp(own - top)
    total = jnp.sum(expo, axis=0, keepdims=True) + own_expo
    probs = (expo / total).T.astype(jnp.bfloat16)
    own_prob = (own_expo / total).astype(jnp.bfloat16).astype(jnp.float32)
    own_prob = jnp.broadcast_to(own_prob, (LANES, LANES)).T

    row_block = lax.broadcasted_iota(jnp.int32, (slot, HEAD_DIM), 0) // group
    for r in range(ROW_STEP):
        rows = slice(r * slot, (r + 1) * slot)
        made = jnp.dot(
            probs[rows], kv_ref[r, :, width:], preferred_element_type=jnp.float32
        )
        ctx = jnp.zeros((slot, HEAD_DIM), jnp.float32)
        value = jnp.zeros((slot, HEAD_DIM), jnp.float32)
        for g in range(blocks):
            new = qkv[g, r : r + 1, (group + 1) * HEAD_DIM :]
            ctx = jnp.where(row_block == g, made[:, g * HEAD_DIM : (g + 1) * HEAD_DIM], ctx)
            value = jnp.where(row_block == g, new, value)
        gathered[rows, :] = ctx + own_prob[rows] * value
    for h in range(heads):
        out_ref[:, h * HEAD_DIM : (h + 1) * HEAD_DIM] = gathered[
            pl.ds(h, ROW_STEP, stride=slot), :
        ]


def attention(qkv, kv_len, kv_cache):
    blocks, rows, columns = qkv.shape
    _, cached, kv_width = kv_cache.shape
    q_width = blocks * columns - kv_width
    heads = q_width // HEAD_DIM
    return pl.pallas_call(
        functools.partial(attention_kernel, heads),
        out_shape=jax.ShapeDtypeStruct((rows, q_width), jnp.float32),
        grid_spec=pltpu.PrefetchScalarGridSpec(
            num_scalar_prefetch=1,
            grid=(rows // ROW_STEP,),
            in_specs=[
                pl.BlockSpec((blocks, ROW_STEP, columns), lambda i, *_: (0, i, 0)),
                pl.BlockSpec((ROW_STEP, cached, kv_width), lambda i, *_: (i, 0, 0)),
            ],
            out_specs=pl.BlockSpec((ROW_STEP, q_width), lambda i, *_: (i, 0)),
            scratch_shapes=[
                pltpu.VMEM((LANES, HEAD_DIM), jnp.float32),
                pltpu.VMEM((LANES, HEAD_DIM), jnp.float32),
            ],
        ),
        cost_estimate=pl.CostEstimate(
            flops=4 * rows * cached * q_width,
            bytes_accessed=2 * rows * cached * kv_width,
            transcendentals=rows * cached * heads,
        ),
        compiler_params=pltpu.CompilerParams(vmem_limit_bytes=32 * 1024 * 1024),
    )(kv_len, qkv, kv_cache)


def rms_norm(talker_in, talker_gain):
    scale = lax.rsqrt(jnp.mean(talker_in * talker_in, axis=1, keepdims=True) + 1e-06)
    return (talker_in * scale * talker_gain).astype(jnp.bfloat16)


def talker_step(talker_in, talker_gain, w_query, w_key, w_value, kv_len, kv_cache):
    owned = talker_in.shape[0]
    cached = kv_cache.shape[1]
    kv_width = w_key.shape[1]
    head_dim = HEAD_DIM
    kv_heads = kv_width // head_dim
    group = w_query.shape[1] // kv_width
    normed = rms_norm(talker_in, talker_gain)
    query = jnp.dot(normed, w_query, preferred_element_type=jnp.float32).astype(jnp.bfloat16)
    new_key = jnp.dot(normed, w_key, preferred_element_type=jnp.float32).astype(jnp.bfloat16)
    new_value = jnp.dot(normed, w_value, preferred_element_type=jnp.float32).astype(jnp.bfloat16)
    talker_kv = jnp.concatenate([new_key, new_value], axis=1)
    qb = query.reshape(owned, kv_heads, group, head_dim)
    keys = kv_cache[:, :, :kv_width].reshape(owned, cached, kv_heads, head_dim)
    values = kv_cache[:, :, kv_width:].reshape(owned, cached, kv_heads, head_dim)
    nk = new_key.reshape(owned, kv_heads, head_dim)
    nv = new_value.reshape(owned, kv_heads, head_dim)
    inv = 1.0 / head_dim**0.5
    scores = jnp.einsum("rgjd,rpgd->rgjp", qb, keys, preferred_element_type=jnp.float32) * inv
    own = jnp.einsum("rgjd,rgd->rgj", qb, nk, preferred_element_type=jnp.float32) * inv
    valid = (jnp.arange(cached, dtype=jnp.int32)[None, :] < kv_len[:, None])[:, None, None, :]
    scores = jnp.where(valid, scores, -jnp.inf)
    top = jnp.maximum(jnp.max(scores, axis=3), own)
    expo = jnp.where(valid, jnp.exp(scores - top[..., None]), 0.0)
    own_expo = jnp.exp(own - top)
    total = jnp.sum(expo, axis=3) + own_expo
    probs = (expo / total[..., None]).astype(jnp.bfloat16)
    own_prob = (own_expo / total).astype(jnp.bfloat16)
    ctx = jnp.einsum("rgjp,rpgd->rgjd", probs, values, preferred_element_type=jnp.float32)
    ctx = ctx + own_prob.astype(jnp.float32)[..., None] * nv.astype(jnp.float32)[:, :, None, :]
    return (talker_kv, ctx.reshape(owned, w_query.shape[1]))


def any_mesh(
    thinker_act,
    w_think,
    w_proj,
    talker_gain,
    w_query,
    w_key,
    w_value,
    talker_slot,
    kv_len,
    kv_cache,
):
    partial_sums = jnp.dot(
        thinker_act,
        lax.all_gather(w_think, ("section", "rows"), axis=1, tiled=True),
        preferred_element_type=jnp.float32,
    )
    full_query, full_key, full_value = (
        lax.all_gather(w_query, ("section", "rows"), axis=1, tiled=True),
        lax.all_gather(w_key, ("section", "rows"), axis=1, tiled=True),
        lax.all_gather(w_value, ("section", "rows"), axis=1, tiled=True),
    )
    mine = lax.psum_scatter(partial_sums, "mp", scatter_dimension=1, tiled=True)
    thinker_out = mine.astype(jnp.bfloat16)
    order = jnp.argsort(talker_slot[0], stable=True)
    sorted_out = thinker_out[order]
    talker_in = lax.psum_scatter(
        jnp.dot(sorted_out, w_proj, preferred_element_type=jnp.float32),
        "mp",
        scatter_dimension=0,
        tiled=True,
    )
    talker_kv, talker_ctx = talker_step(
        talker_in, talker_gain, full_query, full_key, full_value, kv_len, kv_cache
    )
    return (thinker_out, talker_kv, talker_ctx)


PLANE = ("section", "rows")
GROUP = ("mp", "section", "rows")


def over_core(x):
    return lax.ppermute(x, "rows", [(0, 1), (1, 0)])


def over_section(x):
    return lax.ppermute(x, "section", [(0, 1), (1, 0)])


def over_groups(x):
    return lax.ppermute(x, "groups", [(0, 1), (1, 0)])


def over_plane(x, e):
    return lax.ppermute(x, PLANE, [(b, b ^ e) for b in range(4)])


def after(x, *others):
    return lax.optimization_barrier((x, *others))[0]


def feature_block(w_proj, g, m, c):
    half = w_proj.shape[0] // 2
    piece = lax.dynamic_slice_in_dim(w_proj, g * half, half, axis=0)
    got = lax.ppermute(piece, GROUP, [(b * 4 + b, (b ^ 2) * 4 + b) for b in range(4)])
    piece = jnp.where(m == c, piece, got)
    pairs = [(b * 4 + b, (b ^ 1) * 4 + b) for b in range(4)]
    pairs += [((b ^ 2) * 4 + b, (b ^ 3) * 4 + b) for b in range(4)]
    got = lax.ppermute(piece, GROUP, pairs)
    piece = jnp.where((m == c) | (m == c ^ 2), piece, got)
    other = over_groups(piece)
    return jnp.concatenate(
        [jnp.where(g == 0, piece, other), jnp.where(g == 0, other, piece)], axis=0
    )


def four_planes(
    thinker_act,
    w_think,
    w_proj,
    talker_gain,
    w_query,
    w_key,
    w_value,
    talker_slot,
    kv_len,
    kv_cache,
):
    planes = 4
    owned = kv_cache.shape[0]
    g, m, c = lax.axis_index("groups"), lax.axis_index("mp"), lax.axis_index(PLANE)
    slots = talker_slot[0]
    chunks = [(0, 32), (32, 16)]

    depth = w_query.shape[0] // (2 * planes)
    piece = jnp.concatenate(
        [
            lax.dynamic_slice_in_dim(w, (g * planes + m) * depth, depth, axis=0)
            for w in (w_query, w_key, w_value)
        ],
        axis=1,
    )
    piece = over_section(piece)

    sent = []
    for first, n in chunks:
        plane = jnp.arange(planes, dtype=jnp.int32)[:, None] * owned
        want = (plane + first + jnp.arange(n, dtype=jnp.int32)[None, :]).reshape(-1)
        pick = (want[:, None] == slots[None, :]).astype(jnp.bfloat16)
        rows = jnp.dot(pick, thinker_act, preferred_element_type=jnp.float32)
        sent.append(rows.astype(jnp.bfloat16))
    crossed = [over_section(sent[0])]
    crossed.append(over_section(after(sent[1], crossed[0])))

    near = down([*sent, *[over_core(x) for x in sent]], w_think, planes)
    near = lax.all_to_all(near, "mp", 0, 0)
    block_w = feature_block(w_proj, g, m, c)
    mine = jnp.concatenate([w_query, w_key, w_value], axis=1)
    other = lax.all_gather(piece, ("groups", "mp"), axis=0, tiled=True)
    weights = [mine, over_core(mine), other, over_core(other)]
    own, next_core = finish(near, block_w)
    pieces = [[own], [over_core(next_core)], [], []]
    for x in crossed:
        far = lax.all_to_all(down([x, over_core(x)], w_think, planes), "mp", 0, 0)
        across = finish(far, block_w)
        pieces[2].append(over_plane(across[0], 2))
        pieces[3].append(over_plane(across[1], 3))
    spans = [[(0, owned)], [(0, owned)], chunks, chunks]
    home, new_kv, qkv = prepare(c.reshape(1), pieces, spans, talker_gain, weights)
    home = lax.all_to_all(home, "mp", 0, 0)
    ctx = attention(qkv, kv_len, kv_cache)
    pick = (slots[:, None] == jnp.arange(planes * owned)[None, :]).astype(jnp.bfloat16)
    thinker_out = jnp.dot(
        pick, home.reshape(planes * owned, -1), preferred_element_type=jnp.float32
    )
    return (thinker_out.astype(jnp.bfloat16), new_kv, ctx)


def solution(mesh):
    in_specs = (
        P(("groups", "section", "rows"), "mp"),
        P("mp", ("section", "rows")),
        P("mp", None),
        P(),
        P(None, ("section", "rows")),
        P(None, ("section", "rows")),
        P(None, ("section", "rows")),
        P(("groups", "section", "rows"), None),
        P(("groups", "mp", "section", "rows")),
        P(("groups", "mp", "section", "rows"), None, None),
    )
    out_specs = (
        P(("groups", "section", "rows"), "mp"),
        P(("groups", "mp", "section", "rows"), None),
        P(("groups", "mp", "section", "rows"), None),
    )
    sizes = tuple(mesh.shape[a] for a in ("groups", "section", "rows", "mp"))
    shards = four_planes if sizes == (2, 2, 2, 4) else any_mesh
    return jax.shard_map(shards, mesh=mesh, in_specs=in_specs, out_specs=out_specs, check_vma=False)
```

```python
import functools

import jax
import jax.numpy as jnp
from jax import lax
from jax.experimental import pallas as pl
from jax.experimental.pallas import tpu as pltpu
from jax.sharding import PartitionSpec as P

HEAD_DIM = 128
ROW_STEP = 8
LANES = 128


def down_kernel(counts, planes, cuts, *refs):
    groups = len(counts)
    xs, (w, out, x_all, w_all, acc, x_sem, w_sem) = refs[:groups], refs[groups:]
    first = [planes * sum(counts[:i]) for i in range(groups)]
    loads = []
    for s, (lo, hi) in enumerate(cuts):
        deep = pl.ds(lo, hi - lo)
        copies = [pltpu.make_async_copy(w.at[deep], w_all.at[deep], w_sem.at[s])]
        for i in range(groups):
            here = pl.ds(first[i], planes * counts[i])
            copies.append(
                pltpu.make_async_copy(
                    xs[i].at[:, deep], x_all.at[here, deep], x_sem.at[s, i]
                )
            )
        for copy in copies:
            copy.start()
        loads.append(copies)
    for s, (lo, hi) in enumerate(cuts):
        for copy in loads[s]:
            copy.wait()
        part = jnp.dot(x_all[:, lo:hi], w_all[lo:hi, :], preferred_element_type=jnp.float32)
        acc[...] = part if s == 0 else acc[...] + part
    for i, n in enumerate(counts):
        row = sum(counts[:i])
        for p in range(planes):
            at = first[i] + p * n
            out[p, row : row + n, :] = acc[at : at + n, :].astype(out.dtype)


def down(xs, w, planes):
    depth, columns = w.shape
    counts = [x.shape[0] // planes for x in xs]
    rows = sum(counts)
    tiles, parts = depth // LANES, 6
    ends = [LANES * (tiles * i // parts) for i in range(parts)] + [depth]
    return pl.pallas_call(
        functools.partial(down_kernel, counts, planes, list(zip(ends[:-1], ends[1:]))),
        out_shape=jax.ShapeDtypeStruct((planes, rows, columns), jnp.bfloat16),
        in_specs=[pl.BlockSpec(memory_space=pl.ANY)] * (len(xs) + 1),
        out_specs=pl.BlockSpec(memory_space=pltpu.VMEM),
        scratch_shapes=[
            pltpu.VMEM((planes * rows, depth), jnp.bfloat16),
            pltpu.VMEM((depth, columns), jnp.bfloat16),
            pltpu.VMEM((planes * rows, columns), jnp.float32),
            pltpu.SemaphoreType.DMA((parts, len(xs))),
            pltpu.SemaphoreType.DMA((parts,)),
        ],
        cost_estimate=pl.CostEstimate(
            flops=2 * planes * rows * depth * columns,
            bytes_accessed=2 * depth * (columns + planes * rows),
            transcendentals=0,
        ),
        compiler_params=pltpu.CompilerParams(vmem_limit_bytes=56 * 1024 * 1024),
    )(*xs, w)


def finish_kernel(terms, w, near, far):
    total = terms[0].astype(jnp.float32)
    for k in range(1, terms.shape[0]):
        total = total + terms[k].astype(jnp.float32)
    features = total.astype(jnp.bfloat16)
    projected = jnp.dot(features, w[...], preferred_element_type=jnp.float32)
    projected = projected.astype(jnp.bfloat16)
    n = features.shape[0] // 2
    for out, at in ((near, 0), (far, n)):
        out[0] = features[at : at + n]
        out[1] = projected[at : at + n]


def finish(terms, w_proj):
    _, rows, columns = terms.shape
    half = jax.ShapeDtypeStruct((2, rows // 2, columns), jnp.bfloat16)
    vmem = pl.BlockSpec(memory_space=pltpu.VMEM)
    return pl.pallas_call(
        finish_kernel,
        out_shape=(half, half),
        in_specs=[vmem, vmem],
        out_specs=(vmem, vmem),
        cost_estimate=pl.CostEstimate(
            flops=2 * rows * columns * columns,
            bytes_accessed=2 * columns * (columns + 6 * rows),
            transcendentals=0,
        ),
        compiler_params=pltpu.CompilerParams(vmem_limit_bytes=16 * 1024 * 1024),
    )(terms, w_proj)


def prepare_kernel(group, spans, block_ref, gain, w0, w1, w2, w3, *refs):
    pieces, (home, new_kv, qkv) = refs[: sum(map(len, spans))], refs[sum(map(len, spans)) :]
    at = 0
    total = None
    for e, span in enumerate(spans):
        terms = []
        for first, n in span:
            home[e ^ block_ref[0], first : first + n, :] = pieces[at][0]
            terms.append(pieces[at][1].astype(jnp.float32))
            at += 1
        term = jnp.concatenate(terms, axis=0) if len(terms) > 1 else terms[0]
        total = term if total is None else total + term
    scale = lax.rsqrt(jnp.mean(total * total, axis=1, keepdims=True) + 1e-06)
    normed = (total * scale * gain[...]).astype(jnp.bfloat16)
    for e, w in enumerate((w0, w1, w2, w3)):
        made = jnp.dot(normed, w[...], preferred_element_type=jnp.float32)
        qkv[e ^ block_ref[0]] = made.astype(jnp.bfloat16).astype(jnp.float32)
    blocks = qkv.shape[0]
    key, value = group * HEAD_DIM, (group + 1) * HEAD_DIM
    for g in range(blocks):
        for place, start in ((g, key), (blocks + g, value)):
            new_kv[:, place * HEAD_DIM : (place + 1) * HEAD_DIM] = qkv[
                g, :, start : start + HEAD_DIM
            ].astype(jnp.bfloat16)


def prepare(block, pieces, spans, talker_gain, weights):
    flat = [p for piece in pieces for p in piece]
    rows = sum(n for _, n in spans[0])
    wide, columns = weights[0].shape
    group = columns // HEAD_DIM - 2
    vmem = pl.BlockSpec(memory_space=pltpu.VMEM)
    return pl.pallas_call(
        functools.partial(prepare_kernel, group, spans),
        out_shape=(
            jax.ShapeDtypeStruct((len(weights), rows, flat[0].shape[2]), jnp.bfloat16),
            jax.ShapeDtypeStruct((rows, 2 * len(weights) * HEAD_DIM), jnp.bfloat16),
            jax.ShapeDtypeStruct((len(weights), rows, columns), jnp.float32),
        ),
        in_specs=[pl.BlockSpec(memory_space=pltpu.SMEM)] + [vmem] * (5 + len(flat)),
        out_specs=(vmem, vmem, vmem),
        cost_estimate=pl.CostEstimate(
            flops=2 * rows * wide * columns * len(weights),
            bytes_accessed=2 * wide * columns * len(weights),
            transcendentals=rows,
        ),
        compiler_params=pltpu.CompilerParams(vmem_limit_bytes=24 * 1024 * 1024),
    )(block, talker_gain.reshape(1, wide), *weights, *flat)


def attention_kernel(heads, len_ref, qkv, kv_ref, out_ref, spreads, gathereds):
    step = pl.program_id(0)
    blocks = qkv.shape[0]
    group = heads // blocks
    slot = LANES // ROW_STEP
    rows, cached, _ = kv_ref.shape
    width = blocks * HEAD_DIM
    inv = 1.0 / HEAD_DIM**0.5

    @pl.when(step == 0)
    def _():
        spreads[...] = jnp.zeros_like(spreads)

    lane = lax.broadcasted_iota(jnp.int32, (HEAD_DIM, LANES), 1)
    lane_row, lane_block = lane // slot, lane % slot // group
    row_block = lax.broadcasted_iota(jnp.int32, (slot, HEAD_DIM), 0) // group
    own_row = lax.broadcasted_iota(jnp.int32, (ROW_STEP, LANES), 0)
    for part in range(rows // ROW_STEP):
        at = part * ROW_STEP
        here = slice(at, at + ROW_STEP)
        spread, gathered = spreads.at[part], gathereds.at[part]
        for h in range(heads):
            g, j = h // group, h % group
            spread[pl.ds(h, ROW_STEP, stride=slot), :] = qkv[
                g, here, j * HEAD_DIM : (j + 1) * HEAD_DIM
            ]
        query = spread[...].T
        by_block = [
            jnp.where(lane_block == g, query, 0.0).astype(jnp.bfloat16) for g in range(blocks)
        ]

        scores = jnp.zeros((cached, LANES), jnp.float32)
        for r in range(ROW_STEP):
            mine = lane_row == r
            right = jnp.concatenate(
                [jnp.where(mine, q, jnp.zeros_like(q)) for q in by_block], axis=0
            )
            scores = scores + jnp.dot(
                kv_ref[at + r, :, :width], right, preferred_element_type=jnp.float32
            )
        own = jnp.zeros((ROW_STEP, LANES), jnp.float32)
        for g in range(blocks):
            key = qkv[g, here, group * HEAD_DIM : (group + 1) * HEAD_DIM].astype(jnp.bfloat16)
            own = own + jnp.dot(key, by_block[g], preferred_element_type=jnp.float32)
        own = jnp.where(own_row == lane_row[:ROW_STEP], own, 0.0)
        own = jnp.sum(own, axis=0, keepdims=True)

        scores, own = scores * inv, own * inv
        lens = jnp.zeros((1, LANES), jnp.int32)
        for r in range(ROW_STEP):
            lens = jnp.where(lane_row[:1] == r, len_ref[step * rows + at + r], lens)
        valid = lax.broadcasted_iota(jnp.int32, scores.shape, 0) < lens
        scores = jnp.where(valid, scores, -jnp.inf)
        top = jnp.maximum(jnp.max(scores, axis=0, keepdims=True), own)
        expo = jnp.where(valid, jnp.exp(scores - top), 0.0)
        own_expo = jnp.exp(own - top)
        total = jnp.sum(expo, axis=0, keepdims=True) + own_expo
        probs = (expo / total).T.astype(jnp.bfloat16)
        own_prob = (own_expo / total).astype(jnp.bfloat16).astype(jnp.float32)
        own_prob = jnp.broadcast_to(own_prob, (LANES, LANES)).T

        for r in range(ROW_STEP):
            lanes = slice(r * slot, (r + 1) * slot)
            made = jnp.dot(
                probs[lanes], kv_ref[at + r, :, width:], preferred_element_type=jnp.float32
            )
            ctx = jnp.zeros((slot, HEAD_DIM), jnp.float32)
            value = jnp.zeros((slot, HEAD_DIM), jnp.float32)
            for g in range(blocks):
                new = qkv[g, at + r : at + r + 1, (group + 1) * HEAD_DIM :]
                block = made[:, g * HEAD_DIM : (g + 1) * HEAD_DIM]
                ctx = jnp.where(row_block == g, block, ctx)
                value = jnp.where(row_block == g, new, value)
            gathered[lanes, :] = ctx + own_prob[lanes] * value
        for h in range(heads):
            out_ref[here, h * HEAD_DIM : (h + 1) * HEAD_DIM] = gathered[
                pl.ds(h, ROW_STEP, stride=slot), :
            ]


def attention(qkv, kv_len, kv_cache):
    blocks, rows, columns = qkv.shape
    _, cached, kv_width = kv_cache.shape
    q_width = blocks * columns - kv_width
    heads = q_width // HEAD_DIM
    step = 2 * ROW_STEP
    return pl.pallas_call(
        functools.partial(attention_kernel, heads),
        out_shape=jax.ShapeDtypeStruct((rows, q_width), jnp.float32),
        grid_spec=pltpu.PrefetchScalarGridSpec(
            num_scalar_prefetch=1,
            grid=(rows // step,),
            in_specs=[
                pl.BlockSpec((blocks, step, columns), lambda i, *_: (0, i, 0)),
                pl.BlockSpec((step, cached, kv_width), lambda i, *_: (i, 0, 0)),
            ],
            out_specs=pl.BlockSpec((step, q_width), lambda i, *_: (i, 0)),
            scratch_shapes=[
                pltpu.VMEM((step // ROW_STEP, LANES, HEAD_DIM), jnp.float32),
                pltpu.VMEM((step // ROW_STEP, LANES, HEAD_DIM), jnp.float32),
            ],
        ),
        cost_estimate=pl.CostEstimate(
            flops=4 * rows * cached * q_width,
            bytes_accessed=2 * rows * cached * kv_width,
            transcendentals=rows * cached * heads,
        ),
        compiler_params=pltpu.CompilerParams(vmem_limit_bytes=40 * 1024 * 1024),
    )(kv_len, qkv, kv_cache)


def rms_norm(talker_in, talker_gain):
    scale = lax.rsqrt(jnp.mean(talker_in * talker_in, axis=1, keepdims=True) + 1e-06)
    return (talker_in * scale * talker_gain).astype(jnp.bfloat16)


def talker_step(talker_in, talker_gain, w_query, w_key, w_value, kv_len, kv_cache):
    owned = talker_in.shape[0]
    cached = kv_cache.shape[1]
    kv_width = w_key.shape[1]
    head_dim = HEAD_DIM
    kv_heads = kv_width // head_dim
    group = w_query.shape[1] // kv_width
    normed = rms_norm(talker_in, talker_gain)
    query = jnp.dot(normed, w_query, preferred_element_type=jnp.float32).astype(jnp.bfloat16)
    new_key = jnp.dot(normed, w_key, preferred_element_type=jnp.float32).astype(jnp.bfloat16)
    new_value = jnp.dot(normed, w_value, preferred_element_type=jnp.float32).astype(jnp.bfloat16)
    talker_kv = jnp.concatenate([new_key, new_value], axis=1)
    qb = query.reshape(owned, kv_heads, group, head_dim)
    keys = kv_cache[:, :, :kv_width].reshape(owned, cached, kv_heads, head_dim)
    values = kv_cache[:, :, kv_width:].reshape(owned, cached, kv_heads, head_dim)
    nk = new_key.reshape(owned, kv_heads, head_dim)
    nv = new_value.reshape(owned, kv_heads, head_dim)
    inv = 1.0 / head_dim**0.5
    scores = jnp.einsum("rgjd,rpgd->rgjp", qb, keys, preferred_element_type=jnp.float32) * inv
    own = jnp.einsum("rgjd,rgd->rgj", qb, nk, preferred_element_type=jnp.float32) * inv
    valid = (jnp.arange(cached, dtype=jnp.int32)[None, :] < kv_len[:, None])[:, None, None, :]
    scores = jnp.where(valid, scores, -jnp.inf)
    top = jnp.maximum(jnp.max(scores, axis=3), own)
    expo = jnp.where(valid, jnp.exp(scores - top[..., None]), 0.0)
    own_expo = jnp.exp(own - top)
    total = jnp.sum(expo, axis=3) + own_expo
    probs = (expo / total[..., None]).astype(jnp.bfloat16)
    own_prob = (own_expo / total).astype(jnp.bfloat16)
    ctx = jnp.einsum("rgjp,rpgd->rgjd", probs, values, preferred_element_type=jnp.float32)
    ctx = ctx + own_prob.astype(jnp.float32)[..., None] * nv.astype(jnp.float32)[:, :, None, :]
    return (talker_kv, ctx.reshape(owned, w_query.shape[1]))


def any_mesh(
    thinker_act,
    w_think,
    w_proj,
    talker_gain,
    w_query,
    w_key,
    w_value,
    talker_slot,
    kv_len,
    kv_cache,
):
    partial_sums = jnp.dot(
        thinker_act,
        lax.all_gather(w_think, ("section", "rows"), axis=1, tiled=True),
        preferred_element_type=jnp.float32,
    )
    full_query, full_key, full_value = (
        lax.all_gather(w_query, ("section", "rows"), axis=1, tiled=True),
        lax.all_gather(w_key, ("section", "rows"), axis=1, tiled=True),
        lax.all_gather(w_value, ("section", "rows"), axis=1, tiled=True),
    )
    mine = lax.psum_scatter(partial_sums, "mp", scatter_dimension=1, tiled=True)
    thinker_out = mine.astype(jnp.bfloat16)
    order = jnp.argsort(talker_slot[0], stable=True)
    sorted_out = thinker_out[order]
    talker_in = lax.psum_scatter(
        jnp.dot(sorted_out, w_proj, preferred_element_type=jnp.float32),
        "mp",
        scatter_dimension=0,
        tiled=True,
    )
    talker_kv, talker_ctx = talker_step(
        talker_in, talker_gain, full_query, full_key, full_value, kv_len, kv_cache
    )
    return (thinker_out, talker_kv, talker_ctx)


PLANE = ("section", "rows")
GROUP = ("mp", "section", "rows")


def over_core(x):
    return lax.ppermute(x, "rows", [(0, 1), (1, 0)])


def over_section(x):
    return lax.ppermute(x, "section", [(0, 1), (1, 0)])


def over_groups(x):
    return lax.ppermute(x, "groups", [(0, 1), (1, 0)])


def over_plane(x, e):
    return lax.ppermute(x, PLANE, [(b, b ^ e) for b in range(4)])


def after(x, *others):
    return lax.optimization_barrier((x, *others))[0]


def feature_block(w_proj, g, m, c, first, second):
    half = w_proj.shape[0] // 2
    piece = lax.dynamic_slice_in_dim(w_proj, g * half, half, axis=0)
    got = lax.ppermute(piece, GROUP, [(b * 4 + b, (b ^ 2) * 4 + b) for b in range(4)])
    piece = jnp.where(m == c, piece, after(got, first))
    pairs = [(b * 4 + b, (b ^ 1) * 4 + b) for b in range(4)]
    pairs += [((b ^ 2) * 4 + b, (b ^ 3) * 4 + b) for b in range(4)]
    got = lax.ppermute(piece, GROUP, pairs)
    piece = jnp.where((m == c) | (m == c ^ 2), piece, after(got, second))
    other = over_groups(piece)
    return jnp.concatenate(
        [jnp.where(g == 0, piece, other), jnp.where(g == 0, other, piece)], axis=0
    )


def four_planes(
    thinker_act,
    w_think,
    w_proj,
    talker_gain,
    w_query,
    w_key,
    w_value,
    talker_slot,
    kv_len,
    kv_cache,
):
    planes = 4
    owned = kv_cache.shape[0]
    g, m, c = lax.axis_index("groups"), lax.axis_index("mp"), lax.axis_index(PLANE)
    slots = talker_slot[0]
    chunks = [(0, 32), (32, 16)]

    sent = []
    for first, n in chunks:
        plane = jnp.arange(planes, dtype=jnp.int32)[:, None] * owned
        want = (plane + first + jnp.arange(n, dtype=jnp.int32)[None, :]).reshape(-1)
        pick = (want[:, None] == slots[None, :]).astype(jnp.bfloat16)
        rows = jnp.dot(pick, thinker_act, preferred_element_type=jnp.float32)
        sent.append(rows.astype(jnp.bfloat16))

    crossed = [over_section(sent[0])]
    near = down([*sent, *[over_core(x) for x in sent]], w_think, planes)
    crossed.append(over_section(after(sent[1], near)))
    near_terms = lax.all_to_all(near, "mp", 0, 0)
    far = [down([crossed[0], over_core(crossed[0])], w_think, planes)]
    late = after(crossed[1], far[0])
    far.append(down([late, over_core(late)], w_think, planes))
    far_terms = [lax.all_to_all(x, "mp", 0, 0) for x in far]

    block_w = feature_block(w_proj, g, m, c, near, far[0])
    mine = jnp.concatenate([w_query, w_key, w_value], axis=1)
    other = over_section(after(mine, late))
    weights = [mine, over_core(mine), other, over_core(other)]

    own, next_core = finish(near_terms, block_w)
    pieces = [[own], [over_core(next_core)], [], []]
    for terms in far_terms:
        across = finish(terms, block_w)
        pieces[2].append(over_plane(across[0], 2))
        pieces[3].append(over_plane(across[1], 3))
    spans = [[(0, owned)], [(0, owned)], chunks, chunks]
    home, new_kv, qkv = prepare(c.reshape(1), pieces, spans, talker_gain, weights)
    home = lax.all_to_all(home, "mp", 0, 0)
    ctx = attention(qkv, kv_len, kv_cache)
    pick = (slots[:, None] == jnp.arange(planes * owned)[None, :]).astype(jnp.bfloat16)
    thinker_out = jnp.dot(
        pick, home.reshape(planes * owned, -1), preferred_element_type=jnp.float32
    )
    return (thinker_out.astype(jnp.bfloat16), new_kv, ctx)


def solution(mesh):
    in_specs = (
        P(("groups", "section", "rows"), "mp"),
        P("mp", ("section", "rows")),
        P("mp", None),
        P(),
        P(None, ("section", "rows")),
        P(None, ("section", "rows")),
        P(None, ("section", "rows")),
        P(("groups", "section", "rows"), None),
        P(("groups", "mp", "section", "rows")),
        P(("groups", "mp", "section", "rows"), None, None),
    )
    out_specs = (
        P(("groups", "section", "rows"), "mp"),
        P(("groups", "mp", "section", "rows"), None),
        P(("groups", "mp", "section", "rows"), None),
    )
    sizes = tuple(mesh.shape[a] for a in ("groups", "section", "rows", "mp"))
    shards = four_planes if sizes == (2, 2, 2, 4) else any_mesh
    return jax.shard_map(shards, mesh=mesh, in_specs=in_specs, out_specs=out_specs, check_vma=False)
```

```python
import functools

import jax
import jax.numpy as jnp
from jax import lax
from jax.experimental import pallas as pl
from jax.experimental.pallas import tpu as pltpu
from jax.sharding import PartitionSpec as P

HEAD_DIM = 128
ROW_STEP = 8
LANES = 128
DOWN_LIMIT = 28
PAGES = 2


def down_kernel(counts, planes, cuts, *refs):
    groups = len(counts)
    xs, (w, out, x_part, acc) = refs[:groups], refs[groups:]
    first = [planes * sum(counts[:i]) for i in range(groups)]
    for s, (lo, hi) in enumerate(cuts):
        for i in range(groups):
            x_part[first[i] : first[i] + planes * counts[i], : hi - lo] = xs[i][:, lo:hi]
        part = jnp.dot(
            x_part[:, : hi - lo], w[lo:hi, :], preferred_element_type=jnp.float32
        )
        acc[...] = part if s == 0 else acc[...] + part
    for i, n in enumerate(counts):
        row = sum(counts[:i])
        for p in range(planes):
            at = first[i] + p * n
            out[p, row : row + n, :] = acc[at : at + n, :].astype(out.dtype)


def down(xs, w, planes):
    depth, columns = w.shape
    counts = [x.shape[0] // planes for x in xs]
    rows = sum(counts)
    tiles, parts = depth // LANES, 4
    ends = [LANES * (tiles * i // parts) for i in range(parts)] + [depth]
    most = max(hi - lo for lo, hi in zip(ends[:-1], ends[1:]))
    vmem = pl.BlockSpec(memory_space=pltpu.VMEM)
    return pl.pallas_call(
        functools.partial(down_kernel, counts, planes, list(zip(ends[:-1], ends[1:]))),
        out_shape=jax.ShapeDtypeStruct((planes, rows, columns), jnp.bfloat16),
        in_specs=[vmem] * (len(xs) + 1),
        out_specs=vmem,
        scratch_shapes=[
            pltpu.VMEM((planes * rows, most), jnp.bfloat16),
            pltpu.VMEM((planes * rows, columns), jnp.float32),
        ],
        cost_estimate=pl.CostEstimate(
            flops=2 * planes * rows * depth * columns,
            bytes_accessed=2 * depth * (columns + planes * rows),
            transcendentals=0,
        ),
        compiler_params=pltpu.CompilerParams(vmem_limit_bytes=DOWN_LIMIT * 1024 * 1024),
    )(*xs, w)


def finish_kernel(terms, w, near, far):
    total = terms[0].astype(jnp.float32)
    for k in range(1, terms.shape[0]):
        total = total + terms[k].astype(jnp.float32)
    features = total.astype(jnp.bfloat16)
    projected = jnp.dot(features, w[...], preferred_element_type=jnp.float32)
    projected = projected.astype(jnp.bfloat16)
    n = features.shape[0] // 2
    for out, at in ((near, 0), (far, n)):
        out[0] = features[at : at + n]
        out[1] = projected[at : at + n]


def finish(terms, w_proj):
    _, rows, columns = terms.shape
    half = jax.ShapeDtypeStruct((2, rows // 2, columns), jnp.bfloat16)
    vmem = pl.BlockSpec(memory_space=pltpu.VMEM)
    return pl.pallas_call(
        finish_kernel,
        out_shape=(half, half),
        in_specs=[vmem, vmem],
        out_specs=(vmem, vmem),
        cost_estimate=pl.CostEstimate(
            flops=2 * rows * columns * columns,
            bytes_accessed=2 * columns * (columns + 6 * rows),
            transcendentals=0,
        ),
        compiler_params=pltpu.CompilerParams(vmem_limit_bytes=16 * 1024 * 1024),
    )(terms, w_proj)


def collect_kernel(spans, block_ref, *refs):
    pieces, home = refs[:-1], refs[-1]
    at = 0
    for e, span in enumerate(spans):
        for first, n in span:
            home[e ^ block_ref[0], first : first + n, :] = pieces[at][0]
            at += 1


def collect(block, pieces, spans):
    flat = [p for piece in pieces for p in piece]
    rows = sum(n for _, n in spans[0])
    vmem = pl.BlockSpec(memory_space=pltpu.VMEM)
    return pl.pallas_call(
        functools.partial(collect_kernel, spans),
        out_shape=jax.ShapeDtypeStruct((len(spans), rows, flat[0].shape[2]), jnp.bfloat16),
        in_specs=[pl.BlockSpec(memory_space=pltpu.SMEM)] + [vmem] * len(flat),
        out_specs=vmem,
        compiler_params=pltpu.CompilerParams(vmem_limit_bytes=16 * 1024 * 1024),
    )(block, *flat)


def page_copies(len_ref, kv_hbm, kv_ref, sem, r):
    page = kv_ref.shape[1] // PAGES
    out = []
    for p in range(PAGES):
        at = pl.ds(p * page, page)
        copy = pltpu.make_async_copy(kv_hbm.at[r, at], kv_ref.at[r, at], sem.at[r, p])
        out.append((copy, len_ref[r] > p * page))
    return out


def talker_kernel(spans, block_ref, len_ref, gain, w0, w1, w2, w3, *refs):
    count = sum(map(len, spans))
    pieces, (kv_hbm, new_kv, out_ref, kv_ref, sem, qkv, spreads, gathereds) = (
        refs[:count],
        refs[count:],
    )
    blocks = qkv.shape[0]
    rows, cached, kv_width = kv_ref.shape
    width = kv_width // 2
    page = cached // PAGES
    heads = out_ref.shape[1] // HEAD_DIM
    group = heads // blocks
    slot = LANES // ROW_STEP
    sets = spreads.shape[0]
    key, value = group * HEAD_DIM, (group + 1) * HEAD_DIM
    inv = 1.0 / HEAD_DIM**0.5

    @pl.loop(0, rows)
    def _(r):
        for p, (copy, needed) in enumerate(page_copies(len_ref, kv_hbm, kv_ref, sem, r)):
            if p == 0:
                copy.start()
            else:
                pl.when(needed)(copy.start)

    at = 0
    total = None
    for span in spans:
        terms = [pieces[at + i][1].astype(jnp.float32) for i in range(len(span))]
        at += len(span)
        term = jnp.concatenate(terms, axis=0) if len(terms) > 1 else terms[0]
        total = term if total is None else total + term
    scale = lax.rsqrt(jnp.mean(total * total, axis=1, keepdims=True) + 1e-06)
    normed = (total * scale * gain[...]).astype(jnp.bfloat16)
    for e, w in enumerate((w0, w1, w2, w3)):
        made = jnp.dot(normed, w[...], preferred_element_type=jnp.float32)
        qkv[e ^ block_ref[0]] = made.astype(jnp.bfloat16).astype(jnp.float32)
    for g in range(blocks):
        for place, start in ((g, key), (blocks + g, value)):
            new_kv[:, place * HEAD_DIM : (place + 1) * HEAD_DIM] = qkv[
                g, :, start : start + HEAD_DIM
            ].astype(jnp.bfloat16)

    spreads[...] = jnp.zeros_like(spreads)
    lane = lax.broadcasted_iota(jnp.int32, (HEAD_DIM, LANES), 1)
    lane_row, lane_block = lane // slot, lane % slot // group
    row_block = lax.broadcasted_iota(jnp.int32, (slot, HEAD_DIM), 0) // group
    own_row = lax.broadcasted_iota(jnp.int32, (ROW_STEP, LANES), 0)

    def one_set(at, spread, gathered):
        here = pl.ds(at, ROW_STEP)
        for h in range(heads):
            g, j = h // group, h % group
            spread[pl.ds(h, ROW_STEP, stride=slot), :] = qkv[
                g, here, j * HEAD_DIM : (j + 1) * HEAD_DIM
            ]
        query = spread[...].T
        by_block = [
            jnp.where(lane_block == g, query, 0.0).astype(jnp.bfloat16) for g in range(blocks)
        ]

        scores = jnp.zeros((cached, LANES), jnp.float32)
        for r in range(ROW_STEP):
            mine = lane_row == r
            right = jnp.concatenate(
                [jnp.where(mine, q, jnp.zeros_like(q)) for q in by_block], axis=0
            )
            scores = scores + jnp.dot(
                kv_ref[at + r, :, :width], right, preferred_element_type=jnp.float32
            )
        own = jnp.zeros((ROW_STEP, LANES), jnp.float32)
        for g in range(blocks):
            new_key = qkv[g, here, key:value].astype(jnp.bfloat16)
            own = own + jnp.dot(new_key, by_block[g], preferred_element_type=jnp.float32)
        own = jnp.where(own_row == lane_row[:ROW_STEP], own, 0.0)
        own = jnp.sum(own, axis=0, keepdims=True)

        scores, own = scores * inv, own * inv
        lens = jnp.zeros((1, LANES), jnp.int32)
        for r in range(ROW_STEP):
            lens = jnp.where(lane_row[:1] == r, len_ref[at + r], lens)
        valid = lax.broadcasted_iota(jnp.int32, scores.shape, 0) < lens
        scores = jnp.where(valid, scores, -jnp.inf)
        top = jnp.maximum(jnp.max(scores, axis=0, keepdims=True), own)
        expo = jnp.where(valid, jnp.exp(scores - top), 0.0)
        own_expo = jnp.exp(own - top)
        total = jnp.sum(expo, axis=0, keepdims=True) + own_expo
        probs = (expo / total).T.astype(jnp.bfloat16)
        own_prob = (own_expo / total).astype(jnp.bfloat16).astype(jnp.float32)
        own_prob = jnp.broadcast_to(own_prob, (LANES, LANES)).T
        value_rows = qkv.at[:, here, value:]

        for r in range(ROW_STEP):
            lanes = slice(r * slot, (r + 1) * slot)
            made = jnp.dot(
                probs[lanes], kv_ref[at + r, :, width:], preferred_element_type=jnp.float32
            )
            ctx = jnp.zeros((slot, HEAD_DIM), jnp.float32)
            new = jnp.zeros((slot, HEAD_DIM), jnp.float32)
            for g in range(blocks):
                block = made[:, g * HEAD_DIM : (g + 1) * HEAD_DIM]
                ctx = jnp.where(row_block == g, block, ctx)
                new = jnp.where(row_block == g, value_rows[g, r : r + 1, :], new)
            gathered[lanes, :] = ctx + own_prob[lanes] * new
        for h in range(heads):
            out_ref[here, h * HEAD_DIM : (h + 1) * HEAD_DIM] = gathered[
                pl.ds(h, ROW_STEP, stride=slot), :
            ]

    @pl.loop(0, rows // (sets * ROW_STEP))
    def _(i):
        first = pl.multiple_of(i * sets * ROW_STEP, sets * ROW_STEP)
        for k in range(sets * ROW_STEP):
            r = first + k
            for p, (copy, needed) in enumerate(page_copies(len_ref, kv_hbm, kv_ref, sem, r)):
                if p == 0:
                    copy.wait()
                    continue
                pl.when(needed)(copy.wait)

                @pl.when(jnp.logical_not(needed))
                def _(p=p, r=r):
                    kv_ref[r, p * page : (p + 1) * page, :] = jnp.zeros(
                        (page, kv_width), kv_ref.dtype
                    )

        for k in range(sets):
            at = pl.multiple_of(first + k * ROW_STEP, ROW_STEP)
            one_set(at, spreads.at[k], gathereds.at[k])


def talker(block, pieces, spans, talker_gain, weights, kv_len, kv_cache):
    flat = [p for piece in pieces for p in piece]
    rows, cached, kv_width = kv_cache.shape
    wide, columns = weights[0].shape
    blocks = len(weights)
    q_width = blocks * columns - kv_width
    sets = 2
    vmem = pl.BlockSpec(memory_space=pltpu.VMEM)
    smem = pl.BlockSpec(memory_space=pltpu.SMEM)
    return pl.pallas_call(
        functools.partial(talker_kernel, spans),
        out_shape=(
            jax.ShapeDtypeStruct((rows, kv_width), jnp.bfloat16),
            jax.ShapeDtypeStruct((rows, q_width), jnp.float32),
        ),
        in_specs=[smem, smem]
        + [vmem] * (1 + blocks + len(flat))
        + [pl.BlockSpec(memory_space=pltpu.HBM)],
        out_specs=(vmem, vmem),
        scratch_shapes=[
            pltpu.VMEM((rows, cached, kv_width), jnp.bfloat16),
            pltpu.SemaphoreType.DMA((rows, PAGES)),
            pltpu.VMEM((blocks, rows, columns), jnp.float32),
            pltpu.VMEM((sets, LANES, HEAD_DIM), jnp.float32),
            pltpu.VMEM((sets, LANES, HEAD_DIM), jnp.float32),
        ],
        cost_estimate=pl.CostEstimate(
            flops=4 * rows * cached * q_width,
            bytes_accessed=2 * rows * cached * kv_width,
            transcendentals=rows * cached * q_width // HEAD_DIM,
        ),
        compiler_params=pltpu.CompilerParams(vmem_limit_bytes=46 * 1024 * 1024),
    )(block, kv_len, talker_gain.reshape(1, wide), *weights, *flat, kv_cache)


def rms_norm(talker_in, talker_gain):
    scale = lax.rsqrt(jnp.mean(talker_in * talker_in, axis=1, keepdims=True) + 1e-06)
    return (talker_in * scale * talker_gain).astype(jnp.bfloat16)


def talker_step(talker_in, talker_gain, w_query, w_key, w_value, kv_len, kv_cache):
    owned = talker_in.shape[0]
    cached = kv_cache.shape[1]
    kv_width = w_key.shape[1]
    head_dim = HEAD_DIM
    kv_heads = kv_width // head_dim
    group = w_query.shape[1] // kv_width
    normed = rms_norm(talker_in, talker_gain)
    query = jnp.dot(normed, w_query, preferred_element_type=jnp.float32).astype(jnp.bfloat16)
    new_key = jnp.dot(normed, w_key, preferred_element_type=jnp.float32).astype(jnp.bfloat16)
    new_value = jnp.dot(normed, w_value, preferred_element_type=jnp.float32).astype(jnp.bfloat16)
    talker_kv = jnp.concatenate([new_key, new_value], axis=1)
    qb = query.reshape(owned, kv_heads, group, head_dim)
    keys = kv_cache[:, :, :kv_width].reshape(owned, cached, kv_heads, head_dim)
    values = kv_cache[:, :, kv_width:].reshape(owned, cached, kv_heads, head_dim)
    nk = new_key.reshape(owned, kv_heads, head_dim)
    nv = new_value.reshape(owned, kv_heads, head_dim)
    inv = 1.0 / head_dim**0.5
    scores = jnp.einsum("rgjd,rpgd->rgjp", qb, keys, preferred_element_type=jnp.float32) * inv
    own = jnp.einsum("rgjd,rgd->rgj", qb, nk, preferred_element_type=jnp.float32) * inv
    valid = (jnp.arange(cached, dtype=jnp.int32)[None, :] < kv_len[:, None])[:, None, None, :]
    scores = jnp.where(valid, scores, -jnp.inf)
    top = jnp.maximum(jnp.max(scores, axis=3), own)
    expo = jnp.where(valid, jnp.exp(scores - top[..., None]), 0.0)
    own_expo = jnp.exp(own - top)
    total = jnp.sum(expo, axis=3) + own_expo
    probs = (expo / total[..., None]).astype(jnp.bfloat16)
    own_prob = (own_expo / total).astype(jnp.bfloat16)
    ctx = jnp.einsum("rgjp,rpgd->rgjd", probs, values, preferred_element_type=jnp.float32)
    ctx = ctx + own_prob.astype(jnp.float32)[..., None] * nv.astype(jnp.float32)[:, :, None, :]
    return (talker_kv, ctx.reshape(owned, w_query.shape[1]))


def any_mesh(
    thinker_act,
    w_think,
    w_proj,
    talker_gain,
    w_query,
    w_key,
    w_value,
    talker_slot,
    kv_len,
    kv_cache,
):
    partial_sums = jnp.dot(
        thinker_act,
        lax.all_gather(w_think, ("section", "rows"), axis=1, tiled=True),
        preferred_element_type=jnp.float32,
    )
    full_query, full_key, full_value = (
        lax.all_gather(w_query, ("section", "rows"), axis=1, tiled=True),
        lax.all_gather(w_key, ("section", "rows"), axis=1, tiled=True),
        lax.all_gather(w_value, ("section", "rows"), axis=1, tiled=True),
    )
    mine = lax.psum_scatter(partial_sums, "mp", scatter_dimension=1, tiled=True)
    thinker_out = mine.astype(jnp.bfloat16)
    order = jnp.argsort(talker_slot[0], stable=True)
    sorted_out = thinker_out[order]
    talker_in = lax.psum_scatter(
        jnp.dot(sorted_out, w_proj, preferred_element_type=jnp.float32),
        "mp",
        scatter_dimension=0,
        tiled=True,
    )
    talker_kv, talker_ctx = talker_step(
        talker_in, talker_gain, full_query, full_key, full_value, kv_len, kv_cache
    )
    return (thinker_out, talker_kv, talker_ctx)


PLANE = ("section", "rows")
GROUP = ("mp", "section", "rows")


def over_core(x):
    return lax.ppermute(x, "rows", [(0, 1), (1, 0)])


def over_section(x):
    return lax.ppermute(x, "section", [(0, 1), (1, 0)])


def over_groups(x):
    return lax.ppermute(x, "groups", [(0, 1), (1, 0)])


def over_plane(x, e):
    return lax.ppermute(x, PLANE, [(b, b ^ e) for b in range(4)])


def after(x, *others):
    return lax.optimization_barrier((x, *others))[0]


def feature_block(w_proj, g, m, c, first, second):
    half = w_proj.shape[0] // 2
    piece = lax.dynamic_slice_in_dim(w_proj, g * half, half, axis=0)
    got = lax.ppermute(piece, GROUP, [(b * 4 + b, (b ^ 2) * 4 + b) for b in range(4)])
    piece = jnp.where(m == c, piece, after(got, first))
    pairs = [(b * 4 + b, (b ^ 1) * 4 + b) for b in range(4)]
    pairs += [((b ^ 2) * 4 + b, (b ^ 3) * 4 + b) for b in range(4)]
    got = lax.ppermute(piece, GROUP, pairs)
    piece = jnp.where((m == c) | (m == c ^ 2), piece, after(got, second))
    other = over_groups(piece)
    return jnp.concatenate(
        [jnp.where(g == 0, piece, other), jnp.where(g == 0, other, piece)], axis=0
    )


def four_planes(
    thinker_act,
    w_think,
    w_proj,
    talker_gain,
    w_query,
    w_key,
    w_value,
    talker_slot,
    kv_len,
    kv_cache,
):
    planes = 4
    owned = kv_cache.shape[0]
    g, m, c = lax.axis_index("groups"), lax.axis_index("mp"), lax.axis_index(PLANE)
    slots = talker_slot[0]
    chunks = [(0, 32), (32, 16)]

    sent = []
    for first, n in chunks:
        plane = jnp.arange(planes, dtype=jnp.int32)[:, None] * owned
        want = (plane + first + jnp.arange(n, dtype=jnp.int32)[None, :]).reshape(-1)
        pick = (want[:, None] == slots[None, :]).astype(jnp.bfloat16)
        rows = jnp.dot(pick, thinker_act, preferred_element_type=jnp.float32)
        sent.append(rows.astype(jnp.bfloat16))

    crossed = [over_section(sent[0])]
    near = down([*sent, *[over_core(x) for x in sent]], w_think, planes)
    near_terms = lax.all_to_all(near, "mp", 0, 0)
    crossed[0] = after(crossed[0], near)
    crossed.append(over_section(after(sent[1], near)))
    far = [down([crossed[0], over_core(crossed[0])], w_think, planes)]
    late = after(crossed[1], far[0])
    far.append(down([late, over_core(late)], w_think, planes))
    far_terms = [lax.all_to_all(x, "mp", 0, 0) for x in far]

    block_w = feature_block(w_proj, g, m, c, near, far[0])
    mine = jnp.concatenate([w_query, w_key, w_value], axis=1)
    other = over_section(after(mine, late))

    own, next_core = finish(near_terms, block_w)
    pieces = [[own], [over_core(next_core)], [], []]
    for terms in far_terms:
        across = finish(terms, block_w)
        pieces[2].append(over_plane(across[0], 2))
        pieces[3].append(over_plane(across[1], 3))
    other = after(other, across[0])
    weights = [mine, over_core(mine), other, over_core(other)]
    spans = [[(0, owned)], [(0, owned)], chunks, chunks]
    home = lax.all_to_all(collect(c.reshape(1), pieces, spans), "mp", 0, 0)
    new_kv, ctx = talker(c.reshape(1), pieces, spans, talker_gain, weights, kv_len, kv_cache)
    pick = (slots[:, None] == jnp.arange(planes * owned)[None, :]).astype(jnp.bfloat16)
    thinker_out = jnp.dot(
        pick, home.reshape(planes * owned, -1), preferred_element_type=jnp.float32
    )
    return (thinker_out.astype(jnp.bfloat16), new_kv, ctx)


def solution(mesh):
    in_specs = (
        P(("groups", "section", "rows"), "mp"),
        P("mp", ("section", "rows")),
        P("mp", None),
        P(),
        P(None, ("section", "rows")),
        P(None, ("section", "rows")),
        P(None, ("section", "rows")),
        P(("groups", "section", "rows"), None),
        P(("groups", "mp", "section", "rows")),
        P(("groups", "mp", "section", "rows"), None, None),
    )
    out_specs = (
        P(("groups", "section", "rows"), "mp"),
        P(("groups", "mp", "section", "rows"), None),
        P(("groups", "mp", "section", "rows"), None),
    )
    sizes = tuple(mesh.shape[a] for a in ("groups", "section", "rows", "mp"))
    shards = four_planes if sizes == (2, 2, 2, 4) else any_mesh
    return jax.shard_map(shards, mesh=mesh, in_specs=in_specs, out_specs=out_specs, check_vma=False)
```

```python
import functools

import jax
import jax.numpy as jnp
from jax import lax
from jax.experimental import pallas as pl
from jax.experimental.pallas import tpu as pltpu
from jax.sharding import PartitionSpec as P

HEAD_DIM = 128
ROW_STEP = 8
LANES = 128
DOWN_LIMIT = 20
PAGES = 2
SHORT = pl.CostEstimate(flops=1, bytes_accessed=1, transcendentals=0)


def down_kernel(counts, planes, cuts, *refs):
    groups = len(counts)
    xs, (w, out, x_part, acc) = refs[:groups], refs[groups:]
    first = [planes * sum(counts[:i]) for i in range(groups)]
    for s, (lo, hi) in enumerate(cuts):
        for i in range(groups):
            x_part[first[i] : first[i] + planes * counts[i], : hi - lo] = xs[i][:, lo:hi]
        part = jnp.dot(
            x_part[:, : hi - lo], w[lo:hi, :], preferred_element_type=jnp.float32
        )
        acc[...] = part if s == 0 else acc[...] + part
    for i, n in enumerate(counts):
        row = sum(counts[:i])
        for p in range(planes):
            at = first[i] + p * n
            out[p, row : row + n, :] = acc[at : at + n, :].astype(out.dtype)


def down(xs, w, planes):
    depth, columns = w.shape
    counts = [x.shape[0] // planes for x in xs]
    rows = sum(counts)
    tiles, parts = depth // LANES, 4
    ends = [LANES * (tiles * i // parts) for i in range(parts)] + [depth]
    most = max(hi - lo for lo, hi in zip(ends[:-1], ends[1:]))
    vmem = pl.BlockSpec(memory_space=pltpu.VMEM)
    return pl.pallas_call(
        functools.partial(down_kernel, counts, planes, list(zip(ends[:-1], ends[1:]))),
        out_shape=jax.ShapeDtypeStruct((planes, rows, columns), jnp.bfloat16),
        in_specs=[vmem] * (len(xs) + 1),
        out_specs=vmem,
        scratch_shapes=[
            pltpu.VMEM((planes * rows, most), jnp.bfloat16),
            pltpu.VMEM((planes * rows, columns), jnp.float32),
        ],
        cost_estimate=SHORT,
        compiler_params=pltpu.CompilerParams(vmem_limit_bytes=DOWN_LIMIT * 1024 * 1024),
    )(*xs, w)


def finish_kernel(turn_ref, terms, w_mine, w_other, *refs):
    outs, w = refs[:-1], refs[-1]
    half = w_mine.shape[0]
    g = turn_ref[0]
    w[pl.ds(pl.multiple_of(g * half, half), half), :] = w_mine[...]
    w[pl.ds(pl.multiple_of((1 - g) * half, half), half), :] = w_other[...]
    total = terms[0].astype(jnp.float32)
    for k in range(1, terms.shape[0]):
        total = total + terms[k].astype(jnp.float32)
    features = total.astype(jnp.bfloat16)
    projected = jnp.dot(features, w[...], preferred_element_type=jnp.float32)
    projected = projected.astype(jnp.bfloat16)
    n = features.shape[0] // len(outs)
    for i, out in enumerate(outs):
        out[0] = features[i * n : (i + 1) * n]
        out[1] = projected[i * n : (i + 1) * n]


def finish(turn, terms, w_halves, parts):
    _, rows, columns = terms.shape
    wide = w_halves[0].shape[1]
    part = jax.ShapeDtypeStruct((2, rows // parts, columns), jnp.bfloat16)
    vmem = pl.BlockSpec(memory_space=pltpu.VMEM)
    return pl.pallas_call(
        finish_kernel,
        out_shape=(part,) * parts,
        in_specs=[pl.BlockSpec(memory_space=pltpu.SMEM), vmem, vmem, vmem],
        out_specs=(vmem,) * parts,
        scratch_shapes=[pltpu.VMEM((columns, wide), jnp.bfloat16)],
        cost_estimate=SHORT,
        compiler_params=pltpu.CompilerParams(vmem_limit_bytes=16 * 1024 * 1024),
    )(turn, terms, *w_halves)


def collect_kernel(spans, block_ref, *refs):
    pieces, home = refs[:-1], refs[-1]
    at = 0
    for e, span in enumerate(spans):
        for first, n in span:
            home[e ^ block_ref[0], first : first + n, :] = pieces[at][0]
            at += 1


def collect(block, pieces, spans):
    flat = [p for piece in pieces for p in piece]
    rows = sum(n for _, n in spans[0])
    vmem = pl.BlockSpec(memory_space=pltpu.VMEM)
    return pl.pallas_call(
        functools.partial(collect_kernel, spans),
        out_shape=jax.ShapeDtypeStruct((len(spans), rows, flat[0].shape[2]), jnp.bfloat16),
        in_specs=[pl.BlockSpec(memory_space=pltpu.SMEM)] + [vmem] * len(flat),
        out_specs=vmem,
        cost_estimate=SHORT,
        compiler_params=pltpu.CompilerParams(vmem_limit_bytes=16 * 1024 * 1024),
    )(block, *flat)


def page_copies(len_ref, kv_hbm, kv_ref, sem, r):
    page = kv_ref.shape[1] // PAGES
    out = []
    for p in range(PAGES):
        at = pl.ds(p * page, page)
        copy = pltpu.make_async_copy(kv_hbm.at[r, at], kv_ref.at[r, at], sem.at[r, p])
        out.append((copy, len_ref[r] > p * page))
    return out


def talker_kernel(spans, block_ref, len_ref, gain, w0, w1, w2, w3, *refs):
    count = sum(map(len, spans))
    pieces, (kv_hbm, new_kv, out_ref, kv_ref, sem, qkv, spreads, gathereds) = (
        refs[:count],
        refs[count:],
    )
    blocks = qkv.shape[0]
    rows, cached, kv_width = kv_ref.shape
    width = kv_width // 2
    page = cached // PAGES
    heads = out_ref.shape[1] // HEAD_DIM
    group = heads // blocks
    slot = LANES // ROW_STEP
    sets = spreads.shape[0]
    key, value = group * HEAD_DIM, (group + 1) * HEAD_DIM
    inv = 1.0 / HEAD_DIM**0.5

    @pl.loop(0, rows)
    def _(r):
        for p, (copy, needed) in enumerate(page_copies(len_ref, kv_hbm, kv_ref, sem, r)):
            if p == 0:
                copy.start()
            else:
                pl.when(needed)(copy.start)

    at = 0
    total = None
    for span in spans:
        terms = [pieces[at + i][1].astype(jnp.float32) for i in range(len(span))]
        at += len(span)
        term = jnp.concatenate(terms, axis=0) if len(terms) > 1 else terms[0]
        total = term if total is None else total + term
    scale = lax.rsqrt(jnp.mean(total * total, axis=1, keepdims=True) + 1e-06)
    normed = (total * scale * gain[...]).astype(jnp.bfloat16)
    for e, w in enumerate((w0, w1, w2, w3)):
        made = jnp.dot(normed, w[...], preferred_element_type=jnp.float32)
        qkv[e ^ block_ref[0]] = made.astype(jnp.bfloat16).astype(jnp.float32)
    for g in range(blocks):
        for place, start in ((g, key), (blocks + g, value)):
            new_kv[:, place * HEAD_DIM : (place + 1) * HEAD_DIM] = qkv[
                g, :, start : start + HEAD_DIM
            ].astype(jnp.bfloat16)

    spreads[...] = jnp.zeros_like(spreads)
    lane = lax.broadcasted_iota(jnp.int32, (HEAD_DIM, LANES), 1)
    lane_row, lane_block = lane // slot, lane % slot // group
    row_block = lax.broadcasted_iota(jnp.int32, (slot, HEAD_DIM), 0) // group
    own_row = lax.broadcasted_iota(jnp.int32, (ROW_STEP, LANES), 0)

    def scores_of(at, spread):
        here = pl.ds(at, ROW_STEP)
        for h in range(heads):
            g, j = h // group, h % group
            spread[pl.ds(h, ROW_STEP, stride=slot), :] = qkv[
                g, here, j * HEAD_DIM : (j + 1) * HEAD_DIM
            ]
        query = spread[...].T
        by_block = [
            jnp.where(lane_block == g, query, 0.0).astype(jnp.bfloat16) for g in range(blocks)
        ]
        scores = jnp.zeros((cached, LANES), jnp.float32)
        for r in range(ROW_STEP):
            mine = lane_row == r
            right = jnp.concatenate(
                [jnp.where(mine, q, jnp.zeros_like(q)) for q in by_block], axis=0
            )
            scores = scores + jnp.dot(
                kv_ref[at + r, :, :width], right, preferred_element_type=jnp.float32
            )
        own = jnp.zeros((ROW_STEP, LANES), jnp.float32)
        for g in range(blocks):
            new_key = qkv[g, here, key:value].astype(jnp.bfloat16)
            own = own + jnp.dot(new_key, by_block[g], preferred_element_type=jnp.float32)
        own = jnp.where(own_row == lane_row[:ROW_STEP], own, 0.0)
        return scores * inv, jnp.sum(own, axis=0, keepdims=True) * inv

    def softmax(at, scores, own):
        lens = jnp.zeros((1, LANES), jnp.int32)
        for r in range(ROW_STEP):
            lens = jnp.where(lane_row[:1] == r, len_ref[at + r], lens)
        valid = lax.broadcasted_iota(jnp.int32, scores.shape, 0) < lens
        scores = jnp.where(valid, scores, -jnp.inf)
        top = jnp.maximum(jnp.max(scores, axis=0, keepdims=True), own)
        expo = jnp.where(valid, jnp.exp(scores - top), 0.0)
        own_expo = jnp.exp(own - top)
        total = jnp.sum(expo, axis=0, keepdims=True) + own_expo
        probs = (expo / total).T.astype(jnp.bfloat16)
        own_prob = (own_expo / total).astype(jnp.bfloat16).astype(jnp.float32)
        return probs, jnp.broadcast_to(own_prob, (LANES, LANES)).T

    def context(at, probs, own_prob, gathered):
        here = pl.ds(at, ROW_STEP)
        value_rows = qkv.at[:, here, value:]
        for r in range(ROW_STEP):
            lanes = slice(r * slot, (r + 1) * slot)
            made = jnp.dot(
                probs[lanes], kv_ref[at + r, :, width:], preferred_element_type=jnp.float32
            )
            ctx = jnp.zeros((slot, HEAD_DIM), jnp.float32)
            new = jnp.zeros((slot, HEAD_DIM), jnp.float32)
            for g in range(blocks):
                block = made[:, g * HEAD_DIM : (g + 1) * HEAD_DIM]
                ctx = jnp.where(row_block == g, block, ctx)
                new = jnp.where(row_block == g, value_rows[g, r : r + 1, :], new)
            gathered[lanes, :] = ctx + own_prob[lanes] * new
        for h in range(heads):
            out_ref[here, h * HEAD_DIM : (h + 1) * HEAD_DIM] = gathered[
                pl.ds(h, ROW_STEP, stride=slot), :
            ]

    @pl.loop(0, rows // (sets * ROW_STEP))
    def _(i):
        first = pl.multiple_of(i * sets * ROW_STEP, sets * ROW_STEP)
        for k in range(sets * ROW_STEP):
            r = first + k
            for p, (copy, needed) in enumerate(page_copies(len_ref, kv_hbm, kv_ref, sem, r)):
                if p == 0:
                    copy.wait()
                    continue
                pl.when(needed)(copy.wait)

                @pl.when(jnp.logical_not(needed))
                def _(p=p, r=r):
                    kv_ref[r, p * page : (p + 1) * page, :] = jnp.zeros(
                        (page, kv_width), kv_ref.dtype
                    )

        ats = [pl.multiple_of(first + k * ROW_STEP, ROW_STEP) for k in range(sets)]
        scored = [scores_of(at, spreads.at[k]) for k, at in enumerate(ats)]
        weighed = [softmax(at, *s) for at, s in zip(ats, scored)]
        for k, at in enumerate(ats):
            context(at, *weighed[k], gathereds.at[k])


def talker(block, pieces, spans, talker_gain, weights, kv_len, kv_cache):
    flat = [p for piece in pieces for p in piece]
    rows, cached, kv_width = kv_cache.shape
    wide, columns = weights[0].shape
    blocks = len(weights)
    q_width = blocks * columns - kv_width
    sets = 2
    vmem = pl.BlockSpec(memory_space=pltpu.VMEM)
    smem = pl.BlockSpec(memory_space=pltpu.SMEM)
    return pl.pallas_call(
        functools.partial(talker_kernel, spans),
        out_shape=(
            jax.ShapeDtypeStruct((rows, kv_width), jnp.bfloat16),
            jax.ShapeDtypeStruct((rows, q_width), jnp.float32),
        ),
        in_specs=[smem, smem]
        + [vmem] * (1 + blocks + len(flat))
        + [pl.BlockSpec(memory_space=pltpu.HBM)],
        out_specs=(vmem, vmem),
        scratch_shapes=[
            pltpu.VMEM((rows, cached, kv_width), jnp.bfloat16),
            pltpu.SemaphoreType.DMA((rows, PAGES)),
            pltpu.VMEM((blocks, rows, columns), jnp.float32),
            pltpu.VMEM((sets, LANES, HEAD_DIM), jnp.float32),
            pltpu.VMEM((sets, LANES, HEAD_DIM), jnp.float32),
        ],
        cost_estimate=SHORT,
        compiler_params=pltpu.CompilerParams(vmem_limit_bytes=46 * 1024 * 1024),
    )(block, kv_len, talker_gain.reshape(1, wide), *weights, *flat, kv_cache)


def rms_norm(talker_in, talker_gain):
    scale = lax.rsqrt(jnp.mean(talker_in * talker_in, axis=1, keepdims=True) + 1e-06)
    return (talker_in * scale * talker_gain).astype(jnp.bfloat16)


def talker_step(talker_in, talker_gain, w_query, w_key, w_value, kv_len, kv_cache):
    owned = talker_in.shape[0]
    cached = kv_cache.shape[1]
    kv_width = w_key.shape[1]
    head_dim = HEAD_DIM
    kv_heads = kv_width // head_dim
    group = w_query.shape[1] // kv_width
    normed = rms_norm(talker_in, talker_gain)
    query = jnp.dot(normed, w_query, preferred_element_type=jnp.float32).astype(jnp.bfloat16)
    new_key = jnp.dot(normed, w_key, preferred_element_type=jnp.float32).astype(jnp.bfloat16)
    new_value = jnp.dot(normed, w_value, preferred_element_type=jnp.float32).astype(jnp.bfloat16)
    talker_kv = jnp.concatenate([new_key, new_value], axis=1)
    qb = query.reshape(owned, kv_heads, group, head_dim)
    keys = kv_cache[:, :, :kv_width].reshape(owned, cached, kv_heads, head_dim)
    values = kv_cache[:, :, kv_width:].reshape(owned, cached, kv_heads, head_dim)
    nk = new_key.reshape(owned, kv_heads, head_dim)
    nv = new_value.reshape(owned, kv_heads, head_dim)
    inv = 1.0 / head_dim**0.5
    scores = jnp.einsum("rgjd,rpgd->rgjp", qb, keys, preferred_element_type=jnp.float32) * inv
    own = jnp.einsum("rgjd,rgd->rgj", qb, nk, preferred_element_type=jnp.float32) * inv
    valid = (jnp.arange(cached, dtype=jnp.int32)[None, :] < kv_len[:, None])[:, None, None, :]
    scores = jnp.where(valid, scores, -jnp.inf)
    top = jnp.maximum(jnp.max(scores, axis=3), own)
    expo = jnp.where(valid, jnp.exp(scores - top[..., None]), 0.0)
    own_expo = jnp.exp(own - top)
    total = jnp.sum(expo, axis=3) + own_expo
    probs = (expo / total[..., None]).astype(jnp.bfloat16)
    own_prob = (own_expo / total).astype(jnp.bfloat16)
    ctx = jnp.einsum("rgjp,rpgd->rgjd", probs, values, preferred_element_type=jnp.float32)
    ctx = ctx + own_prob.astype(jnp.float32)[..., None] * nv.astype(jnp.float32)[:, :, None, :]
    return (talker_kv, ctx.reshape(owned, w_query.shape[1]))


def any_mesh(
    thinker_act,
    w_think,
    w_proj,
    talker_gain,
    w_query,
    w_key,
    w_value,
    talker_slot,
    kv_len,
    kv_cache,
):
    partial_sums = jnp.dot(
        thinker_act,
        lax.all_gather(w_think, ("section", "rows"), axis=1, tiled=True),
        preferred_element_type=jnp.float32,
    )
    full_query, full_key, full_value = (
        lax.all_gather(w_query, ("section", "rows"), axis=1, tiled=True),
        lax.all_gather(w_key, ("section", "rows"), axis=1, tiled=True),
        lax.all_gather(w_value, ("section", "rows"), axis=1, tiled=True),
    )
    mine = lax.psum_scatter(partial_sums, "mp", scatter_dimension=1, tiled=True)
    thinker_out = mine.astype(jnp.bfloat16)
    order = jnp.argsort(talker_slot[0], stable=True)
    sorted_out = thinker_out[order]
    talker_in = lax.psum_scatter(
        jnp.dot(sorted_out, w_proj, preferred_element_type=jnp.float32),
        "mp",
        scatter_dimension=0,
        tiled=True,
    )
    talker_kv, talker_ctx = talker_step(
        talker_in, talker_gain, full_query, full_key, full_value, kv_len, kv_cache
    )
    return (thinker_out, talker_kv, talker_ctx)


PLANE = ("section", "rows")
GROUP = ("mp", "section", "rows")


def over_core(x):
    return lax.ppermute(x, "rows", [(0, 1), (1, 0)])


def over_section(x):
    return lax.ppermute(x, "section", [(0, 1), (1, 0)])


def over_groups(x):
    return lax.ppermute(x, "groups", [(0, 1), (1, 0)])


def over_plane(x, e):
    return lax.ppermute(x, PLANE, [(b, b ^ e) for b in range(4)])


def after(x, *others):
    return lax.optimization_barrier((x, *others))[0]


def feature_block(w_proj, g, m, c, later):
    half = w_proj.shape[0] // 2
    piece = lax.dynamic_slice_in_dim(w_proj, g * half, half, axis=0)
    two = lax.ppermute(piece, GROUP, [(b * 4 + b, (b ^ 2) * 4 + b) for b in range(4)])
    one = lax.ppermute(piece, GROUP, [(b * 4 + b, (b ^ 1) * 4 + b) for b in range(4)])
    two, one, _ = lax.optimization_barrier((two, one, later))
    three = lax.ppermute(two, GROUP, [((b ^ 2) * 4 + b, (b ^ 3) * 4 + b) for b in range(4)])
    piece = jnp.where(m == c, piece, jnp.where(m == c ^ 2, two, jnp.where(m == c ^ 1, one, three)))
    return piece, over_groups(piece)


def four_planes(
    thinker_act,
    w_think,
    w_proj,
    talker_gain,
    w_query,
    w_key,
    w_value,
    talker_slot,
    kv_len,
    kv_cache,
):
    planes = 4
    owned = kv_cache.shape[0]
    g, m, c = lax.axis_index("groups"), lax.axis_index("mp"), lax.axis_index(PLANE)
    slots = talker_slot[0]

    pick = (jnp.arange(planes * owned)[:, None] == slots[None, :]).astype(jnp.bfloat16)
    rows = jnp.dot(pick, thinker_act, preferred_element_type=jnp.float32).astype(jnp.bfloat16)

    across = over_section(rows)
    peer = over_core(rows)
    near = down([rows, peer], w_think, planes)
    near_terms = lax.all_to_all(near, "mp", 0, 0)
    block_w = feature_block(after(w_proj, peer), g, m, c, near)
    across = after(across, near)
    far = [down([x], w_think, planes) for x in (across, over_core(across))]
    far_terms = [lax.all_to_all(x, "mp", 0, 0) for x in far]

    mine = jnp.concatenate([w_query, w_key, w_value], axis=1)
    other = over_section(after(mine, across))

    turn = g.reshape(1)
    own, next_core = finish(turn, near_terms, block_w, 2)
    pieces = [[own], [over_core(next_core)], [], []]
    for e, terms in zip((2, 3), far_terms):
        (made,) = finish(turn, terms, block_w, 1)
        pieces[e].append(over_plane(made, e))
    other = after(other, made)
    weights = [mine, over_core(mine), other, over_core(other)]
    spans = [[(0, owned)]] * 4
    home = lax.all_to_all(collect(c.reshape(1), pieces, spans), "mp", 0, 0)
    new_kv, ctx = talker(c.reshape(1), pieces, spans, talker_gain, weights, kv_len, kv_cache)
    home = after(home, ctx)
    pick = (slots[:, None] == jnp.arange(planes * owned)[None, :]).astype(jnp.bfloat16)
    thinker_out = jnp.dot(
        pick, home.reshape(planes * owned, -1), preferred_element_type=jnp.float32
    )
    return (thinker_out.astype(jnp.bfloat16), new_kv, ctx)


def solution(mesh):
    in_specs = (
        P(("groups", "section", "rows"), "mp"),
        P("mp", ("section", "rows")),
        P("mp", None),
        P(),
        P(None, ("section", "rows")),
        P(None, ("section", "rows")),
        P(None, ("section", "rows")),
        P(("groups", "section", "rows"), None),
        P(("groups", "mp", "section", "rows")),
        P(("groups", "mp", "section", "rows"), None, None),
    )
    out_specs = (
        P(("groups", "section", "rows"), "mp"),
        P(("groups", "mp", "section", "rows"), None),
        P(("groups", "mp", "section", "rows"), None),
    )
    sizes = tuple(mesh.shape[a] for a in ("groups", "section", "rows", "mp"))
    shards = four_planes if sizes == (2, 2, 2, 4) else any_mesh
    return jax.shard_map(shards, mesh=mesh, in_specs=in_specs, out_specs=out_specs, check_vma=False)
```

```python
import functools

import jax
import jax.numpy as jnp
from jax import lax
from jax.experimental import pallas as pl
from jax.experimental.pallas import tpu as pltpu
from jax.sharding import PartitionSpec as P

HEAD_DIM = 128
ROW_STEP = 8
LANES = 128
PAGES = 2
SHORT = pl.CostEstimate(flops=1, bytes_accessed=1, transcendentals=0)
LONG = pl.CostEstimate(flops=1 << 36, bytes_accessed=1 << 27, transcendentals=0)


def down_kernel(counts, planes, cuts, fresh, *refs):
    groups = len(counts)
    xs, w, rest = refs[:groups], refs[groups], refs[groups + 1 :]
    if fresh:
        out, w_kept, x_all, acc, x_sem, w_sem = rest
    else:
        out, x_all, acc, x_sem = rest
        w_kept = w
    first = [planes * sum(counts[:i]) for i in range(groups)]
    loads = []
    for s, (lo, hi) in enumerate(cuts):
        deep = pl.ds(lo, hi - lo)
        copies = []
        if fresh:
            copies.append(pltpu.make_async_copy(w.at[deep], w_kept.at[deep], w_sem.at[s]))
        for i in range(groups):
            here = pl.ds(first[i], planes * counts[i])
            copies.append(
                pltpu.make_async_copy(
                    xs[i].at[:, deep], x_all.at[here, deep], x_sem.at[s, i]
                )
            )
        for copy in copies:
            copy.start()
        loads.append(copies)
    for s, (lo, hi) in enumerate(cuts):
        for copy in loads[s]:
            copy.wait()
        part = jnp.dot(x_all[:, lo:hi], w_kept[lo:hi, :], preferred_element_type=jnp.float32)
        acc[...] = part if s == 0 else acc[...] + part
    for i, n in enumerate(counts):
        row = sum(counts[:i])
        for p in range(planes):
            at = first[i] + p * n
            out[p, row : row + n, :] = acc[at : at + n, :].astype(out.dtype)


def down(xs, w, planes, fresh, cost):
    depth, columns = w.shape
    counts = [x.shape[0] // planes for x in xs]
    rows = sum(counts)
    tiles, parts = depth // LANES, 6
    ends = [LANES * (tiles * i // parts) for i in range(parts)] + [depth]
    vmem = pl.BlockSpec(memory_space=pltpu.VMEM)
    anywhere = pl.BlockSpec(memory_space=pl.ANY)
    sums = jax.ShapeDtypeStruct((planes, rows, columns), jnp.bfloat16)
    return pl.pallas_call(
        functools.partial(down_kernel, counts, planes, list(zip(ends[:-1], ends[1:])), fresh),
        out_shape=(sums, pltpu.VMEM(w.shape, w.dtype)) if fresh else sums,
        in_specs=[anywhere] * len(xs) + [pl.BlockSpec(memory_space=pltpu.HBM) if fresh else vmem],
        out_specs=(vmem, vmem) if fresh else vmem,
        scratch_shapes=[
            pltpu.VMEM((planes * rows, depth), jnp.bfloat16),
            pltpu.VMEM((planes * rows, columns), jnp.float32),
            pltpu.SemaphoreType.DMA((parts, len(xs))),
            *([pltpu.SemaphoreType.DMA((parts,))] if fresh else []),
        ],
        cost_estimate=cost,
        compiler_params=pltpu.CompilerParams(vmem_limit_bytes=(48 if fresh else 14) * 1024 * 1024),
    )(*xs, w)


def finish_kernel(turn_ref, terms, w_mine, w_other, *refs):
    outs, w = refs[:-1], refs[-1]
    half = w_mine.shape[0]
    g = turn_ref[0]
    w[pl.ds(pl.multiple_of(g * half, half), half), :] = w_mine[...]
    w[pl.ds(pl.multiple_of((1 - g) * half, half), half), :] = w_other[...]
    total = terms[0].astype(jnp.float32)
    for k in range(1, terms.shape[0]):
        total = total + terms[k].astype(jnp.float32)
    features = total.astype(jnp.bfloat16)
    projected = jnp.dot(features, w[...], preferred_element_type=jnp.float32)
    projected = projected.astype(jnp.bfloat16)
    n = features.shape[0] // len(outs)
    for i, out in enumerate(outs):
        out[0] = features[i * n : (i + 1) * n]
        out[1] = projected[i * n : (i + 1) * n]


def finish(turn, terms, w_halves, parts):
    _, rows, columns = terms.shape
    wide = w_halves[0].shape[1]
    part = jax.ShapeDtypeStruct((2, rows // parts, columns), jnp.bfloat16)
    vmem = pl.BlockSpec(memory_space=pltpu.VMEM)
    return pl.pallas_call(
        finish_kernel,
        out_shape=(part,) * parts,
        in_specs=[pl.BlockSpec(memory_space=pltpu.SMEM), vmem, vmem, vmem],
        out_specs=(vmem,) * parts,
        scratch_shapes=[pltpu.VMEM((columns, wide), jnp.bfloat16)],
        cost_estimate=SHORT,
        compiler_params=pltpu.CompilerParams(vmem_limit_bytes=16 * 1024 * 1024),
    )(turn, terms, *w_halves)


def collect_kernel(spans, block_ref, *refs):
    pieces, home = refs[:-1], refs[-1]
    at = 0
    for e, span in enumerate(spans):
        for first, n in span:
            home[e ^ block_ref[0], first : first + n, :] = pieces[at][0]
            at += 1


def collect(block, pieces, spans):
    flat = [p for piece in pieces for p in piece]
    rows = sum(n for _, n in spans[0])
    vmem = pl.BlockSpec(memory_space=pltpu.VMEM)
    return pl.pallas_call(
        functools.partial(collect_kernel, spans),
        out_shape=jax.ShapeDtypeStruct((len(spans), rows, flat[0].shape[2]), jnp.bfloat16),
        in_specs=[pl.BlockSpec(memory_space=pltpu.SMEM)] + [vmem] * len(flat),
        out_specs=vmem,
        cost_estimate=SHORT,
        compiler_params=pltpu.CompilerParams(vmem_limit_bytes=16 * 1024 * 1024),
    )(block, *flat)


def page_copies(len_ref, kv_hbm, kv_ref, sem, r):
    page = kv_ref.shape[1] // PAGES
    out = []
    for p in range(PAGES):
        at = pl.ds(p * page, page)
        copy = pltpu.make_async_copy(kv_hbm.at[r, at], kv_ref.at[r, at], sem.at[r, p])
        out.append((copy, len_ref[r] > p * page))
    return out


def talker_kernel(spans, block_ref, len_ref, gain, w0, w1, w2, w3, *refs):
    count = sum(map(len, spans))
    pieces, (kv_hbm, new_kv, out_ref, kv_ref, sem, qkv, spreads, gathereds) = (
        refs[:count],
        refs[count:],
    )
    blocks = qkv.shape[0]
    rows, cached, kv_width = kv_ref.shape
    width = kv_width // 2
    page = cached // PAGES
    heads = out_ref.shape[1] // HEAD_DIM
    group = heads // blocks
    slot = LANES // ROW_STEP
    sets = spreads.shape[0]
    key, value = group * HEAD_DIM, (group + 1) * HEAD_DIM
    inv = 1.0 / HEAD_DIM**0.5

    @pl.loop(0, rows)
    def _(r):
        for p, (copy, needed) in enumerate(page_copies(len_ref, kv_hbm, kv_ref, sem, r)):
            if p == 0:
                copy.start()
            else:
                pl.when(needed)(copy.start)

    at = 0
    total = None
    for span in spans:
        terms = [pieces[at + i][1].astype(jnp.float32) for i in range(len(span))]
        at += len(span)
        term = jnp.concatenate(terms, axis=0) if len(terms) > 1 else terms[0]
        total = term if total is None else total + term
    scale = lax.rsqrt(jnp.mean(total * total, axis=1, keepdims=True) + 1e-06)
    normed = (total * scale * gain[...]).astype(jnp.bfloat16)
    for e, w in enumerate((w0, w1, w2, w3)):
        made = jnp.dot(normed, w[...], preferred_element_type=jnp.float32)
        qkv[e ^ block_ref[0]] = made.astype(jnp.bfloat16).astype(jnp.float32)
    for g in range(blocks):
        for place, start in ((g, key), (blocks + g, value)):
            new_kv[:, place * HEAD_DIM : (place + 1) * HEAD_DIM] = qkv[
                g, :, start : start + HEAD_DIM
            ].astype(jnp.bfloat16)

    spreads[...] = jnp.zeros_like(spreads)
    lane = lax.broadcasted_iota(jnp.int32, (HEAD_DIM, LANES), 1)
    lane_row, lane_block = lane // slot, lane % slot // group
    row_block = lax.broadcasted_iota(jnp.int32, (slot, HEAD_DIM), 0) // group
    own_row = lax.broadcasted_iota(jnp.int32, (ROW_STEP, LANES), 0)

    def scores_of(at, spread):
        here = pl.ds(at, ROW_STEP)
        for h in range(heads):
            g, j = h // group, h % group
            spread[pl.ds(h, ROW_STEP, stride=slot), :] = qkv[
                g, here, j * HEAD_DIM : (j + 1) * HEAD_DIM
            ]
        query = spread[...].T
        by_block = [
            jnp.where(lane_block == g, query, 0.0).astype(jnp.bfloat16) for g in range(blocks)
        ]
        scores = jnp.zeros((cached, LANES), jnp.float32)
        for r in range(ROW_STEP):
            mine = lane_row == r
            right = jnp.concatenate(
                [jnp.where(mine, q, jnp.zeros_like(q)) for q in by_block], axis=0
            )
            scores = scores + jnp.dot(
                kv_ref[at + r, :, :width], right, preferred_element_type=jnp.float32
            )
        own = jnp.zeros((ROW_STEP, LANES), jnp.float32)
        for g in range(blocks):
            new_key = qkv[g, here, key:value].astype(jnp.bfloat16)
            own = own + jnp.dot(new_key, by_block[g], preferred_element_type=jnp.float32)
        own = jnp.where(own_row == lane_row[:ROW_STEP], own, 0.0)
        return scores * inv, jnp.sum(own, axis=0, keepdims=True) * inv

    def softmax(at, scores, own):
        lens = jnp.zeros((1, LANES), jnp.int32)
        for r in range(ROW_STEP):
            lens = jnp.where(lane_row[:1] == r, len_ref[at + r], lens)
        valid = lax.broadcasted_iota(jnp.int32, scores.shape, 0) < lens
        scores = jnp.where(valid, scores, -jnp.inf)
        top = jnp.maximum(jnp.max(scores, axis=0, keepdims=True), own)
        expo = jnp.where(valid, jnp.exp(scores - top), 0.0)
        own_expo = jnp.exp(own - top)
        total = jnp.sum(expo, axis=0, keepdims=True) + own_expo
        probs = (expo / total).T.astype(jnp.bfloat16)
        own_prob = (own_expo / total).astype(jnp.bfloat16).astype(jnp.float32)
        return probs, jnp.broadcast_to(own_prob, (LANES, LANES)).T

    def context(at, probs, own_prob, gathered):
        here = pl.ds(at, ROW_STEP)
        value_rows = qkv.at[:, here, value:]
        for r in range(ROW_STEP):
            lanes = slice(r * slot, (r + 1) * slot)
            made = jnp.dot(
                probs[lanes], kv_ref[at + r, :, width:], preferred_element_type=jnp.float32
            )
            ctx = jnp.zeros((slot, HEAD_DIM), jnp.float32)
            new = jnp.zeros((slot, HEAD_DIM), jnp.float32)
            for g in range(blocks):
                block = made[:, g * HEAD_DIM : (g + 1) * HEAD_DIM]
                ctx = jnp.where(row_block == g, block, ctx)
                new = jnp.where(row_block == g, value_rows[g, r : r + 1, :], new)
            gathered[lanes, :] = ctx + own_prob[lanes] * new
        for h in range(heads):
            out_ref[here, h * HEAD_DIM : (h + 1) * HEAD_DIM] = gathered[
                pl.ds(h, ROW_STEP, stride=slot), :
            ]

    @pl.loop(0, rows // (sets * ROW_STEP))
    def _(i):
        first = pl.multiple_of(i * sets * ROW_STEP, sets * ROW_STEP)
        for k in range(sets * ROW_STEP):
            r = first + k
            for p, (copy, needed) in enumerate(page_copies(len_ref, kv_hbm, kv_ref, sem, r)):
                if p == 0:
                    copy.wait()
                    continue
                pl.when(needed)(copy.wait)

                @pl.when(jnp.logical_not(needed))
                def _(p=p, r=r):
                    kv_ref[r, p * page : (p + 1) * page, :] = jnp.zeros(
                        (page, kv_width), kv_ref.dtype
                    )

        ats = [pl.multiple_of(first + k * ROW_STEP, ROW_STEP) for k in range(sets)]
        scored = [scores_of(at, spreads.at[k]) for k, at in enumerate(ats)]
        weighed = [softmax(at, *s) for at, s in zip(ats, scored)]
        for k, at in enumerate(ats):
            context(at, *weighed[k], gathereds.at[k])


def talker(block, pieces, spans, talker_gain, weights, kv_len, kv_cache):
    flat = [p for piece in pieces for p in piece]
    rows, cached, kv_width = kv_cache.shape
    wide, columns = weights[0].shape
    blocks = len(weights)
    q_width = blocks * columns - kv_width
    sets = 2
    vmem = pl.BlockSpec(memory_space=pltpu.VMEM)
    smem = pl.BlockSpec(memory_space=pltpu.SMEM)
    return pl.pallas_call(
        functools.partial(talker_kernel, spans),
        out_shape=(
            jax.ShapeDtypeStruct((rows, kv_width), jnp.bfloat16),
            jax.ShapeDtypeStruct((rows, q_width), jnp.float32),
        ),
        in_specs=[smem, smem]
        + [vmem] * (1 + blocks + len(flat))
        + [pl.BlockSpec(memory_space=pltpu.HBM)],
        out_specs=(vmem, vmem),
        scratch_shapes=[
            pltpu.VMEM((rows, cached, kv_width), jnp.bfloat16),
            pltpu.SemaphoreType.DMA((rows, PAGES)),
            pltpu.VMEM((blocks, rows, columns), jnp.float32),
            pltpu.VMEM((sets, LANES, HEAD_DIM), jnp.float32),
            pltpu.VMEM((sets, LANES, HEAD_DIM), jnp.float32),
        ],
        cost_estimate=SHORT,
        compiler_params=pltpu.CompilerParams(vmem_limit_bytes=46 * 1024 * 1024),
    )(block, kv_len, talker_gain.reshape(1, wide), *weights, *flat, kv_cache)


def rms_norm(talker_in, talker_gain):
    scale = lax.rsqrt(jnp.mean(talker_in * talker_in, axis=1, keepdims=True) + 1e-06)
    return (talker_in * scale * talker_gain).astype(jnp.bfloat16)


def talker_step(talker_in, talker_gain, w_query, w_key, w_value, kv_len, kv_cache):
    owned = talker_in.shape[0]
    cached = kv_cache.shape[1]
    kv_width = w_key.shape[1]
    head_dim = HEAD_DIM
    kv_heads = kv_width // head_dim
    group = w_query.shape[1] // kv_width
    normed = rms_norm(talker_in, talker_gain)
    query = jnp.dot(normed, w_query, preferred_element_type=jnp.float32).astype(jnp.bfloat16)
    new_key = jnp.dot(normed, w_key, preferred_element_type=jnp.float32).astype(jnp.bfloat16)
    new_value = jnp.dot(normed, w_value, preferred_element_type=jnp.float32).astype(jnp.bfloat16)
    talker_kv = jnp.concatenate([new_key, new_value], axis=1)
    qb = query.reshape(owned, kv_heads, group, head_dim)
    keys = kv_cache[:, :, :kv_width].reshape(owned, cached, kv_heads, head_dim)
    values = kv_cache[:, :, kv_width:].reshape(owned, cached, kv_heads, head_dim)
    nk = new_key.reshape(owned, kv_heads, head_dim)
    nv = new_value.reshape(owned, kv_heads, head_dim)
    inv = 1.0 / head_dim**0.5
    scores = jnp.einsum("rgjd,rpgd->rgjp", qb, keys, preferred_element_type=jnp.float32) * inv
    own = jnp.einsum("rgjd,rgd->rgj", qb, nk, preferred_element_type=jnp.float32) * inv
    valid = (jnp.arange(cached, dtype=jnp.int32)[None, :] < kv_len[:, None])[:, None, None, :]
    scores = jnp.where(valid, scores, -jnp.inf)
    top = jnp.maximum(jnp.max(scores, axis=3), own)
    expo = jnp.where(valid, jnp.exp(scores - top[..., None]), 0.0)
    own_expo = jnp.exp(own - top)
    total = jnp.sum(expo, axis=3) + own_expo
    probs = (expo / total[..., None]).astype(jnp.bfloat16)
    own_prob = (own_expo / total).astype(jnp.bfloat16)
    ctx = jnp.einsum("rgjp,rpgd->rgjd", probs, values, preferred_element_type=jnp.float32)
    ctx = ctx + own_prob.astype(jnp.float32)[..., None] * nv.astype(jnp.float32)[:, :, None, :]
    return (talker_kv, ctx.reshape(owned, w_query.shape[1]))


def any_mesh(
    thinker_act,
    w_think,
    w_proj,
    talker_gain,
    w_query,
    w_key,
    w_value,
    talker_slot,
    kv_len,
    kv_cache,
):
    partial_sums = jnp.dot(
        thinker_act,
        lax.all_gather(w_think, ("section", "rows"), axis=1, tiled=True),
        preferred_element_type=jnp.float32,
    )
    full_query, full_key, full_value = (
        lax.all_gather(w_query, ("section", "rows"), axis=1, tiled=True),
        lax.all_gather(w_key, ("section", "rows"), axis=1, tiled=True),
        lax.all_gather(w_value, ("section", "rows"), axis=1, tiled=True),
    )
    mine = lax.psum_scatter(partial_sums, "mp", scatter_dimension=1, tiled=True)
    thinker_out = mine.astype(jnp.bfloat16)
    order = jnp.argsort(talker_slot[0], stable=True)
    sorted_out = thinker_out[order]
    talker_in = lax.psum_scatter(
        jnp.dot(sorted_out, w_proj, preferred_element_type=jnp.float32),
        "mp",
        scatter_dimension=0,
        tiled=True,
    )
    talker_kv, talker_ctx = talker_step(
        talker_in, talker_gain, full_query, full_key, full_value, kv_len, kv_cache
    )
    return (thinker_out, talker_kv, talker_ctx)


PLANE = ("section", "rows")
GROUP = ("mp", "section", "rows")


def over_core(x):
    return lax.ppermute(x, "rows", [(0, 1), (1, 0)])


def over_section(x):
    return lax.ppermute(x, "section", [(0, 1), (1, 0)])


def over_groups(x):
    return lax.ppermute(x, "groups", [(0, 1), (1, 0)])


def over_plane(x, e):
    return lax.ppermute(x, PLANE, [(b, b ^ e) for b in range(4)])


def after(x, *others):
    return lax.optimization_barrier((x, *others))[0]


def feature_block(w_proj, g, m, c, later):
    half = w_proj.shape[0] // 2
    piece = lax.dynamic_slice_in_dim(w_proj, g * half, half, axis=0)
    two = lax.ppermute(piece, GROUP, [(b * 4 + b, (b ^ 2) * 4 + b) for b in range(4)])
    one = lax.ppermute(piece, GROUP, [(b * 4 + b, (b ^ 1) * 4 + b) for b in range(4)])
    two, one, _ = lax.optimization_barrier((two, one, later))
    three = lax.ppermute(two, GROUP, [((b ^ 2) * 4 + b, (b ^ 3) * 4 + b) for b in range(4)])
    piece = jnp.where(m == c, piece, jnp.where(m == c ^ 2, two, jnp.where(m == c ^ 1, one, three)))
    return piece, over_groups(piece)


def four_planes(
    thinker_act,
    w_think,
    w_proj,
    talker_gain,
    w_query,
    w_key,
    w_value,
    talker_slot,
    kv_len,
    kv_cache,
):
    planes = 4
    owned = kv_cache.shape[0]
    g, m, c = lax.axis_index("groups"), lax.axis_index("mp"), lax.axis_index(PLANE)
    slots = talker_slot[0]

    chunks = [(0, 32), (32, 16)]

    sent = []
    for first, n in chunks:
        plane = jnp.arange(planes, dtype=jnp.int32)[:, None] * owned
        want = (plane + first + jnp.arange(n, dtype=jnp.int32)[None, :]).reshape(-1)
        pick = (want[:, None] == slots[None, :]).astype(jnp.bfloat16)
        rows = jnp.dot(pick, thinker_act, preferred_element_type=jnp.float32)
        sent.append(rows.astype(jnp.bfloat16))

    crossed = [over_section(x) for x in sent]
    peers = [over_core(x) for x in sent]
    near, w_kept = down([*sent, *peers], w_think, planes, True, LONG)
    near_terms = lax.all_to_all(near, "mp", 0, 0)
    far = []
    made = near_terms
    for x in crossed:
        x = after(x, made)
        made = down([x, over_core(x)], w_kept, planes, False, SHORT)
        far.append(made)
    far_terms = [lax.all_to_all(x, "mp", 0, 0) for x in far]
    block_w = feature_block(after(w_proj, near), g, m, c, far[0])

    mine = jnp.concatenate([w_query, w_key, w_value], axis=1)
    other = over_section(after(mine, x))

    turn = g.reshape(1)
    own, next_core = finish(turn, after(near_terms, made), block_w, 2)
    pieces = [[own], [over_core(next_core)], [], []]
    halves = [own]
    for terms in far_terms:
        halves = finish(turn, after(terms, halves[0]), block_w, 2)
        for e in (2, 3):
            pieces[e].append(over_plane(halves[e - 2], e))
    other = after(other, halves[0])
    weights = [mine, over_core(mine), other, over_core(other)]
    spans = [[(0, owned)], [(0, owned)], chunks, chunks]
    home = lax.all_to_all(collect(c.reshape(1), pieces, spans), "mp", 0, 0)
    new_kv, ctx = talker(c.reshape(1), pieces, spans, talker_gain, weights, kv_len, kv_cache)
    home = after(home, ctx)
    pick = (slots[:, None] == jnp.arange(planes * owned)[None, :]).astype(jnp.bfloat16)
    thinker_out = jnp.dot(
        pick, home.reshape(planes * owned, -1), preferred_element_type=jnp.float32
    )
    return (thinker_out.astype(jnp.bfloat16), new_kv, ctx)


def solution(mesh):
    in_specs = (
        P(("groups", "section", "rows"), "mp"),
        P("mp", ("section", "rows")),
        P("mp", None),
        P(),
        P(None, ("section", "rows")),
        P(None, ("section", "rows")),
        P(None, ("section", "rows")),
        P(("groups", "section", "rows"), None),
        P(("groups", "mp", "section", "rows")),
        P(("groups", "mp", "section", "rows"), None, None),
    )
    out_specs = (
        P(("groups", "section", "rows"), "mp"),
        P(("groups", "mp", "section", "rows"), None),
        P(("groups", "mp", "section", "rows"), None),
    )
    sizes = tuple(mesh.shape[a] for a in ("groups", "section", "rows", "mp"))
    shards = four_planes if sizes == (2, 2, 2, 4) else any_mesh
    return jax.shard_map(shards, mesh=mesh, in_specs=in_specs, out_specs=out_specs, check_vma=False)
```

```python
import functools

import jax
import jax.numpy as jnp
from jax import lax
from jax.experimental import pallas as pl
from jax.experimental.pallas import tpu as pltpu
from jax.sharding import PartitionSpec as P

HEAD_DIM = 128
ROW_STEP = 8
LANES = 128
PAGES = 2
SHORT = pl.CostEstimate(flops=1, bytes_accessed=1, transcendentals=0)
MOST_VMEM = 56 * 1024 * 1024


def down_kernel(counts, planes, cuts, *refs):
    groups = len(counts)
    xs, (w, out, x_all, w_all, acc, x_sem, w_sem) = refs[:groups], refs[groups:]
    first = [planes * sum(counts[:i]) for i in range(groups)]
    loads = []
    for s, (lo, hi) in enumerate(cuts):
        deep = pl.ds(lo, hi - lo)
        copies = [pltpu.make_async_copy(w.at[deep], w_all.at[deep], w_sem.at[s])]
        for i in range(groups):
            here = pl.ds(first[i], planes * counts[i])
            copies.append(
                pltpu.make_async_copy(
                    xs[i].at[:, deep], x_all.at[here, deep], x_sem.at[s, i]
                )
            )
        for copy in copies:
            copy.start()
        loads.append(copies)
    for s, (lo, hi) in enumerate(cuts):
        for copy in loads[s]:
            copy.wait()
        part = jnp.dot(x_all[:, lo:hi], w_all[lo:hi, :], preferred_element_type=jnp.float32)
        acc[...] = part if s == 0 else acc[...] + part
    for i, n in enumerate(counts):
        row = sum(counts[:i])
        for p in range(planes):
            at = first[i] + p * n
            out[p, row : row + n, :] = acc[at : at + n, :].astype(out.dtype)


def down(xs, w, planes):
    depth, columns = w.shape
    counts = [x.shape[0] // planes for x in xs]
    rows = sum(counts)
    tiles, parts = depth // LANES, 6
    ends = [LANES * (tiles * i // parts) for i in range(parts)] + [depth]
    anywhere = pl.BlockSpec(memory_space=pl.ANY)
    return pl.pallas_call(
        functools.partial(down_kernel, counts, planes, list(zip(ends[:-1], ends[1:]))),
        out_shape=jax.ShapeDtypeStruct((planes, rows, columns), jnp.bfloat16),
        in_specs=[anywhere] * (len(xs) + 1),
        out_specs=pl.BlockSpec(memory_space=pltpu.VMEM),
        scratch_shapes=[
            pltpu.VMEM((planes * rows, depth), jnp.bfloat16),
            pltpu.VMEM((depth, columns), jnp.bfloat16),
            pltpu.VMEM((planes * rows, columns), jnp.float32),
            pltpu.SemaphoreType.DMA((parts, len(xs))),
            pltpu.SemaphoreType.DMA((parts,)),
        ],
        cost_estimate=SHORT,
        compiler_params=pltpu.CompilerParams(vmem_limit_bytes=MOST_VMEM),
    )(*xs, w)


def finish_kernel(turn_ref, terms, w_mine, w_other, *refs):
    outs, w = refs[:-1], refs[-1]
    half = w_mine.shape[0]
    g = turn_ref[0]
    w[pl.ds(pl.multiple_of(g * half, half), half), :] = w_mine[...]
    w[pl.ds(pl.multiple_of((1 - g) * half, half), half), :] = w_other[...]
    total = terms[0].astype(jnp.float32)
    for k in range(1, terms.shape[0]):
        total = total + terms[k].astype(jnp.float32)
    features = total.astype(jnp.bfloat16)
    projected = jnp.dot(features, w[...], preferred_element_type=jnp.float32)
    projected = projected.astype(jnp.bfloat16)
    n = features.shape[0] // len(outs)
    for i, out in enumerate(outs):
        out[0] = features[i * n : (i + 1) * n]
        out[1] = projected[i * n : (i + 1) * n]


def finish(turn, terms, w_halves, parts):
    _, rows, columns = terms.shape
    wide = w_halves[0].shape[1]
    part = jax.ShapeDtypeStruct((2, rows // parts, columns), jnp.bfloat16)
    vmem = pl.BlockSpec(memory_space=pltpu.VMEM)
    return pl.pallas_call(
        finish_kernel,
        out_shape=(part,) * parts,
        in_specs=[pl.BlockSpec(memory_space=pltpu.SMEM), vmem, vmem, vmem],
        out_specs=(vmem,) * parts,
        scratch_shapes=[pltpu.VMEM((columns, wide), jnp.bfloat16)],
        cost_estimate=SHORT,
        compiler_params=pltpu.CompilerParams(vmem_limit_bytes=16 * 1024 * 1024),
    )(turn, terms, *w_halves)


def collect_kernel(spans, block_ref, *refs):
    pieces, home = refs[:-1], refs[-1]
    at = 0
    for e, span in enumerate(spans):
        for first, n in span:
            home[e ^ block_ref[0], first : first + n, :] = pieces[at][0]
            at += 1


def collect(block, pieces, spans):
    flat = [p for piece in pieces for p in piece]
    rows = sum(n for _, n in spans[0])
    vmem = pl.BlockSpec(memory_space=pltpu.VMEM)
    return pl.pallas_call(
        functools.partial(collect_kernel, spans),
        out_shape=jax.ShapeDtypeStruct((len(spans), rows, flat[0].shape[2]), jnp.bfloat16),
        in_specs=[pl.BlockSpec(memory_space=pltpu.SMEM)] + [vmem] * len(flat),
        out_specs=vmem,
        cost_estimate=SHORT,
        compiler_params=pltpu.CompilerParams(vmem_limit_bytes=16 * 1024 * 1024),
    )(block, *flat)


def page_copies(len_ref, kv_hbm, kv_ref, sem, r):
    page = kv_ref.shape[1] // PAGES
    out = []
    for p in range(PAGES):
        at = pl.ds(p * page, page)
        copy = pltpu.make_async_copy(kv_hbm.at[r, at], kv_ref.at[r, at], sem.at[r, p])
        out.append((copy, len_ref[r] > p * page))
    return out


def talker_kernel(spans, blocks, block_ref, len_ref, gain, *refs):
    count = sum(map(len, spans))
    w_hbm, pieces = refs[:blocks], refs[blocks : blocks + count]
    kv_hbm, new_kv, out_ref, kv_ref, sem, w_ref, w_sem, qkv, spreads, gathereds = refs[
        blocks + count :
    ]
    rows, cached, kv_width = kv_ref.shape
    width = kv_width // 2
    page = cached // PAGES
    heads = out_ref.shape[1] // HEAD_DIM
    group = heads // blocks
    slot = LANES // ROW_STEP
    sets = spreads.shape[0]
    key, value = group * HEAD_DIM, (group + 1) * HEAD_DIM
    inv = 1.0 / HEAD_DIM**0.5

    w_copies = [
        pltpu.make_async_copy(w_hbm[e], w_ref.at[e], w_sem.at[e]) for e in range(blocks)
    ]
    for copy in w_copies:
        copy.start()

    @pl.loop(0, rows)
    def _(r):
        for p, (copy, needed) in enumerate(page_copies(len_ref, kv_hbm, kv_ref, sem, r)):
            if p == 0:
                copy.start()
            else:
                pl.when(needed)(copy.start)

    at = 0
    total = None
    for span in spans:
        terms = [pieces[at + i][1].astype(jnp.float32) for i in range(len(span))]
        at += len(span)
        term = jnp.concatenate(terms, axis=0) if len(terms) > 1 else terms[0]
        total = term if total is None else total + term
    scale = lax.rsqrt(jnp.mean(total * total, axis=1, keepdims=True) + 1e-06)
    normed = (total * scale * gain[...]).astype(jnp.bfloat16)
    for e in range(blocks):
        w_copies[e].wait()
        made = jnp.dot(normed, w_ref[e], preferred_element_type=jnp.float32)
        qkv[e ^ block_ref[0]] = made.astype(jnp.bfloat16).astype(jnp.float32)
    for g in range(blocks):
        for place, start in ((g, key), (blocks + g, value)):
            new_kv[:, place * HEAD_DIM : (place + 1) * HEAD_DIM] = qkv[
                g, :, start : start + HEAD_DIM
            ].astype(jnp.bfloat16)

    spreads[...] = jnp.zeros_like(spreads)
    lane = lax.broadcasted_iota(jnp.int32, (HEAD_DIM, LANES), 1)
    lane_row, lane_block = lane // slot, lane % slot // group
    row_block = lax.broadcasted_iota(jnp.int32, (slot, HEAD_DIM), 0) // group
    own_row = lax.broadcasted_iota(jnp.int32, (ROW_STEP, LANES), 0)

    def scores_of(at, spread):
        here = pl.ds(at, ROW_STEP)
        for h in range(heads):
            g, j = h // group, h % group
            spread[pl.ds(h, ROW_STEP, stride=slot), :] = qkv[
                g, here, j * HEAD_DIM : (j + 1) * HEAD_DIM
            ]
        query = spread[...].T
        by_block = [
            jnp.where(lane_block == g, query, 0.0).astype(jnp.bfloat16) for g in range(blocks)
        ]
        scores = jnp.zeros((cached, LANES), jnp.float32)
        for r in range(ROW_STEP):
            mine = lane_row == r
            right = jnp.concatenate(
                [jnp.where(mine, q, jnp.zeros_like(q)) for q in by_block], axis=0
            )
            scores = scores + jnp.dot(
                kv_ref[at + r, :, :width], right, preferred_element_type=jnp.float32
            )
        own = jnp.zeros((ROW_STEP, LANES), jnp.float32)
        for g in range(blocks):
            new_key = qkv[g, here, key:value].astype(jnp.bfloat16)
            own = own + jnp.dot(new_key, by_block[g], preferred_element_type=jnp.float32)
        own = jnp.where(own_row == lane_row[:ROW_STEP], own, 0.0)
        return scores * inv, jnp.sum(own, axis=0, keepdims=True) * inv

    def softmax(at, scores, own):
        lens = jnp.zeros((1, LANES), jnp.int32)
        for r in range(ROW_STEP):
            lens = jnp.where(lane_row[:1] == r, len_ref[at + r], lens)
        valid = lax.broadcasted_iota(jnp.int32, scores.shape, 0) < lens
        scores = jnp.where(valid, scores, -jnp.inf)
        top = jnp.maximum(jnp.max(scores, axis=0, keepdims=True), own)
        expo = jnp.where(valid, jnp.exp(scores - top), 0.0)
        own_expo = jnp.exp(own - top)
        total = jnp.sum(expo, axis=0, keepdims=True) + own_expo
        probs = (expo / total).T.astype(jnp.bfloat16)
        own_prob = (own_expo / total).astype(jnp.bfloat16).astype(jnp.float32)
        return probs, jnp.broadcast_to(own_prob, (LANES, LANES)).T

    def context(at, probs, own_prob, gathered):
        here = pl.ds(at, ROW_STEP)
        value_rows = qkv.at[:, here, value:]
        for r in range(ROW_STEP):
            lanes = slice(r * slot, (r + 1) * slot)
            made = jnp.dot(
                probs[lanes], kv_ref[at + r, :, width:], preferred_element_type=jnp.float32
            )
            ctx = jnp.zeros((slot, HEAD_DIM), jnp.float32)
            new = jnp.zeros((slot, HEAD_DIM), jnp.float32)
            for g in range(blocks):
                block = made[:, g * HEAD_DIM : (g + 1) * HEAD_DIM]
                ctx = jnp.where(row_block == g, block, ctx)
                new = jnp.where(row_block == g, value_rows[g, r : r + 1, :], new)
            gathered[lanes, :] = ctx + own_prob[lanes] * new
        for h in range(heads):
            out_ref[here, h * HEAD_DIM : (h + 1) * HEAD_DIM] = gathered[
                pl.ds(h, ROW_STEP, stride=slot), :
            ]

    @pl.loop(0, rows // (sets * ROW_STEP))
    def _(i):
        first = pl.multiple_of(i * sets * ROW_STEP, sets * ROW_STEP)
        for k in range(sets * ROW_STEP):
            r = first + k
            for p, (copy, needed) in enumerate(page_copies(len_ref, kv_hbm, kv_ref, sem, r)):
                if p == 0:
                    copy.wait()
                    continue
                pl.when(needed)(copy.wait)

                @pl.when(jnp.logical_not(needed))
                def _(p=p, r=r):
                    kv_ref[r, p * page : (p + 1) * page, :] = jnp.zeros(
                        (page, kv_width), kv_ref.dtype
                    )

        ats = [pl.multiple_of(first + k * ROW_STEP, ROW_STEP) for k in range(sets)]
        scored = [scores_of(at, spreads.at[k]) for k, at in enumerate(ats)]
        weighed = [softmax(at, *s) for at, s in zip(ats, scored)]
        for k, at in enumerate(ats):
            context(at, *weighed[k], gathereds.at[k])


def talker(block, pieces, spans, talker_gain, weights, kv_len, kv_cache):
    flat = [p for piece in pieces for p in piece]
    rows, cached, kv_width = kv_cache.shape
    wide, columns = weights[0].shape
    blocks = len(weights)
    q_width = blocks * columns - kv_width
    sets = 2
    vmem = pl.BlockSpec(memory_space=pltpu.VMEM)
    smem = pl.BlockSpec(memory_space=pltpu.SMEM)
    return pl.pallas_call(
        functools.partial(talker_kernel, spans, blocks),
        out_shape=(
            jax.ShapeDtypeStruct((rows, kv_width), jnp.bfloat16),
            jax.ShapeDtypeStruct((rows, q_width), jnp.float32),
        ),
        in_specs=[smem, smem, vmem]
        + [pl.BlockSpec(memory_space=pl.ANY)] * blocks
        + [vmem] * len(flat)
        + [pl.BlockSpec(memory_space=pl.ANY)],
        out_specs=(vmem, vmem),
        scratch_shapes=[
            pltpu.VMEM((rows, cached, kv_width), jnp.bfloat16),
            pltpu.SemaphoreType.DMA((rows, PAGES)),
            pltpu.VMEM((blocks, wide, columns), jnp.bfloat16),
            pltpu.SemaphoreType.DMA((blocks,)),
            pltpu.VMEM((blocks, rows, columns), jnp.float32),
            pltpu.VMEM((sets, LANES, HEAD_DIM), jnp.float32),
            pltpu.VMEM((sets, LANES, HEAD_DIM), jnp.float32),
        ],
        cost_estimate=SHORT,
        compiler_params=pltpu.CompilerParams(vmem_limit_bytes=48 * 1024 * 1024),
    )(block, kv_len, talker_gain.reshape(1, wide), *weights, *flat, kv_cache)


def rms_norm(talker_in, talker_gain):
    scale = lax.rsqrt(jnp.mean(talker_in * talker_in, axis=1, keepdims=True) + 1e-06)
    return (talker_in * scale * talker_gain).astype(jnp.bfloat16)


def talker_step(talker_in, talker_gain, w_query, w_key, w_value, kv_len, kv_cache):
    owned = talker_in.shape[0]
    cached = kv_cache.shape[1]
    kv_width = w_key.shape[1]
    head_dim = HEAD_DIM
    kv_heads = kv_width // head_dim
    group = w_query.shape[1] // kv_width
    normed = rms_norm(talker_in, talker_gain)
    query = jnp.dot(normed, w_query, preferred_element_type=jnp.float32).astype(jnp.bfloat16)
    new_key = jnp.dot(normed, w_key, preferred_element_type=jnp.float32).astype(jnp.bfloat16)
    new_value = jnp.dot(normed, w_value, preferred_element_type=jnp.float32).astype(jnp.bfloat16)
    talker_kv = jnp.concatenate([new_key, new_value], axis=1)
    qb = query.reshape(owned, kv_heads, group, head_dim)
    keys = kv_cache[:, :, :kv_width].reshape(owned, cached, kv_heads, head_dim)
    values = kv_cache[:, :, kv_width:].reshape(owned, cached, kv_heads, head_dim)
    nk = new_key.reshape(owned, kv_heads, head_dim)
    nv = new_value.reshape(owned, kv_heads, head_dim)
    inv = 1.0 / head_dim**0.5
    scores = jnp.einsum("rgjd,rpgd->rgjp", qb, keys, preferred_element_type=jnp.float32) * inv
    own = jnp.einsum("rgjd,rgd->rgj", qb, nk, preferred_element_type=jnp.float32) * inv
    valid = (jnp.arange(cached, dtype=jnp.int32)[None, :] < kv_len[:, None])[:, None, None, :]
    scores = jnp.where(valid, scores, -jnp.inf)
    top = jnp.maximum(jnp.max(scores, axis=3), own)
    expo = jnp.where(valid, jnp.exp(scores - top[..., None]), 0.0)
    own_expo = jnp.exp(own - top)
    total = jnp.sum(expo, axis=3) + own_expo
    probs = (expo / total[..., None]).astype(jnp.bfloat16)
    own_prob = (own_expo / total).astype(jnp.bfloat16)
    ctx = jnp.einsum("rgjp,rpgd->rgjd", probs, values, preferred_element_type=jnp.float32)
    ctx = ctx + own_prob.astype(jnp.float32)[..., None] * nv.astype(jnp.float32)[:, :, None, :]
    return (talker_kv, ctx.reshape(owned, w_query.shape[1]))


def any_mesh(
    thinker_act,
    w_think,
    w_proj,
    talker_gain,
    w_query,
    w_key,
    w_value,
    talker_slot,
    kv_len,
    kv_cache,
):
    partial_sums = jnp.dot(
        thinker_act,
        lax.all_gather(w_think, ("section", "rows"), axis=1, tiled=True),
        preferred_element_type=jnp.float32,
    )
    full_query, full_key, full_value = (
        lax.all_gather(w_query, ("section", "rows"), axis=1, tiled=True),
        lax.all_gather(w_key, ("section", "rows"), axis=1, tiled=True),
        lax.all_gather(w_value, ("section", "rows"), axis=1, tiled=True),
    )
    mine = lax.psum_scatter(partial_sums, "mp", scatter_dimension=1, tiled=True)
    thinker_out = mine.astype(jnp.bfloat16)
    order = jnp.argsort(talker_slot[0], stable=True)
    sorted_out = thinker_out[order]
    talker_in = lax.psum_scatter(
        jnp.dot(sorted_out, w_proj, preferred_element_type=jnp.float32),
        "mp",
        scatter_dimension=0,
        tiled=True,
    )
    talker_kv, talker_ctx = talker_step(
        talker_in, talker_gain, full_query, full_key, full_value, kv_len, kv_cache
    )
    return (thinker_out, talker_kv, talker_ctx)


PLANE = ("section", "rows")
GROUP = ("mp", "section", "rows")


def over_core(x):
    return lax.ppermute(x, "rows", [(0, 1), (1, 0)])


def over_section(x):
    return lax.ppermute(x, "section", [(0, 1), (1, 0)])


def over_groups(x):
    return lax.ppermute(x, "groups", [(0, 1), (1, 0)])


def over_plane(x, e):
    return lax.ppermute(x, PLANE, [(b, b ^ e) for b in range(4)])


def after(x, *others):
    return lax.optimization_barrier((x, *others))[0]


def feature_block_first(w_proj, g):
    half = w_proj.shape[0] // 2
    piece = lax.dynamic_slice_in_dim(w_proj, g * half, half, axis=0)
    two = lax.ppermute(piece, GROUP, [(b * 4 + b, (b ^ 2) * 4 + b) for b in range(4)])
    one = lax.ppermute(piece, GROUP, [(b * 4 + b, (b ^ 1) * 4 + b) for b in range(4)])
    return piece, one, two


def feature_block(piece, one, two, m, c, later):
    three = lax.ppermute(two, GROUP, [((b ^ 2) * 4 + b, (b ^ 3) * 4 + b) for b in range(4)])
    three = after(three, later)
    piece = jnp.where(m == c, piece, jnp.where(m == c ^ 2, two, jnp.where(m == c ^ 1, one, three)))
    return piece, over_groups(piece)


def four_planes(
    thinker_act,
    w_think,
    w_proj,
    talker_gain,
    w_query,
    w_key,
    w_value,
    talker_slot,
    kv_len,
    kv_cache,
):
    planes = 4
    owned = kv_cache.shape[0]
    g, m, c = lax.axis_index("groups"), lax.axis_index("mp"), lax.axis_index(PLANE)
    slots = talker_slot[0]

    pick = (jnp.arange(planes * owned)[:, None] == slots[None, :]).astype(jnp.bfloat16)
    rows = jnp.dot(pick, thinker_act, preferred_element_type=jnp.float32).astype(jnp.bfloat16)

    across = over_section(rows)
    peer = over_core(rows)
    near = down([rows, peer], w_think, planes)
    near_terms = lax.all_to_all(near, "mp", 0, 0)
    early_w = feature_block_first(after(w_proj, peer), g)
    mine = jnp.concatenate([w_query, w_key, w_value], axis=1)

    across, near_terms, mine, *early_w = lax.optimization_barrier(
        (across, near_terms, mine, *early_w)
    )
    far = [down([across], w_think, planes)]
    far.append(down([after(over_core(across), far[0])], w_think, planes))
    far_terms = [lax.all_to_all(x, "mp", 0, 0) for x in far]
    other = over_section(after(mine, across))
    block_w = feature_block(*early_w, m, c, far[1])

    turn = g.reshape(1)
    own, next_core = finish(turn, after(near_terms, far[1]), block_w, 2)
    pieces = [[own], [over_core(next_core)], [], []]
    made = own
    for e, terms in zip((2, 3), far_terms):
        (made,) = finish(turn, after(terms, made), block_w, 1)
        pieces[e].append(over_plane(made, e))
    other = after(other, made)
    weights = [mine, over_core(mine), other, over_core(other)]
    spans = [[(0, owned)]] * 4
    home = lax.all_to_all(collect(c.reshape(1), pieces, spans), "mp", 0, 0)
    new_kv, ctx = talker(c.reshape(1), pieces, spans, talker_gain, weights, kv_len, kv_cache)
    home = after(home, ctx)
    pick = (slots[:, None] == jnp.arange(planes * owned)[None, :]).astype(jnp.bfloat16)
    thinker_out = jnp.dot(
        pick, home.reshape(planes * owned, -1), preferred_element_type=jnp.float32
    )
    return (thinker_out.astype(jnp.bfloat16), new_kv, ctx)


def solution(mesh):
    in_specs = (
        P(("groups", "section", "rows"), "mp"),
        P("mp", ("section", "rows")),
        P("mp", None),
        P(),
        P(None, ("section", "rows")),
        P(None, ("section", "rows")),
        P(None, ("section", "rows")),
        P(("groups", "section", "rows"), None),
        P(("groups", "mp", "section", "rows")),
        P(("groups", "mp", "section", "rows"), None, None),
    )
    out_specs = (
        P(("groups", "section", "rows"), "mp"),
        P(("groups", "mp", "section", "rows"), None),
        P(("groups", "mp", "section", "rows"), None),
    )
    sizes = tuple(mesh.shape[a] for a in ("groups", "section", "rows", "mp"))
    shards = four_planes if sizes == (2, 2, 2, 4) else any_mesh
    return jax.shard_map(shards, mesh=mesh, in_specs=in_specs, out_specs=out_specs, check_vma=False)
```

```python
import functools

import jax
import jax.numpy as jnp
from jax import lax
from jax.experimental import pallas as pl
from jax.experimental.pallas import tpu as pltpu
from jax.sharding import PartitionSpec as P

HEAD_DIM = 128
ROW_STEP = 8
LANES = 128
PAGES = 2
SHORT = pl.CostEstimate(flops=1, bytes_accessed=1, transcendentals=0)
MOST_VMEM = 56 * 1024 * 1024


def down_kernel(counts, planes, cuts, *refs):
    groups = len(counts)
    xs, (w, out, x_all, w_all, acc, x_sem, w_sem) = refs[:groups], refs[groups:]
    first = [planes * sum(counts[:i]) for i in range(groups)]
    loads = []
    for s, (lo, hi) in enumerate(cuts):
        deep = pl.ds(lo, hi - lo)
        copies = [pltpu.make_async_copy(w.at[deep], w_all.at[deep], w_sem.at[s])]
        for i in range(groups):
            here = pl.ds(first[i], planes * counts[i])
            copies.append(
                pltpu.make_async_copy(
                    xs[i].at[:, deep], x_all.at[here, deep], x_sem.at[s, i]
                )
            )
        for copy in copies:
            copy.start()
        loads.append(copies)
    for s, (lo, hi) in enumerate(cuts):
        for copy in loads[s]:
            copy.wait()
        part = jnp.dot(x_all[:, lo:hi], w_all[lo:hi, :], preferred_element_type=jnp.float32)
        acc[...] = part if s == 0 else acc[...] + part
    for i, n in enumerate(counts):
        row = sum(counts[:i])
        for p in range(planes):
            at = first[i] + p * n
            out[p, row : row + n, :] = acc[at : at + n, :].astype(out.dtype)


def down(xs, w, planes):
    depth, columns = w.shape
    counts = [x.shape[0] // planes for x in xs]
    rows = sum(counts)
    tiles, parts = depth // LANES, 6
    ends = [LANES * (tiles * i // parts) for i in range(parts)] + [depth]
    anywhere = pl.BlockSpec(memory_space=pl.ANY)
    return pl.pallas_call(
        functools.partial(down_kernel, counts, planes, list(zip(ends[:-1], ends[1:]))),
        out_shape=jax.ShapeDtypeStruct((planes, rows, columns), jnp.bfloat16),
        in_specs=[anywhere] * (len(xs) + 1),
        out_specs=pl.BlockSpec(memory_space=pltpu.VMEM),
        scratch_shapes=[
            pltpu.VMEM((planes * rows, depth), jnp.bfloat16),
            pltpu.VMEM((depth, columns), jnp.bfloat16),
            pltpu.VMEM((planes * rows, columns), jnp.float32),
            pltpu.SemaphoreType.DMA((parts, len(xs))),
            pltpu.SemaphoreType.DMA((parts,)),
        ],
        cost_estimate=SHORT,
        compiler_params=pltpu.CompilerParams(vmem_limit_bytes=MOST_VMEM),
    )(*xs, w)


def add_kernel(terms, *outs):
    total = terms[0].astype(jnp.float32)
    for k in range(1, terms.shape[0]):
        total = total + terms[k].astype(jnp.float32)
    n = outs[0].shape[0]
    for i, out in enumerate(outs):
        out[...] = total[i * n : (i + 1) * n].astype(out.dtype)


def add(terms, parts):
    _, rows, columns = terms.shape
    part = jax.ShapeDtypeStruct((rows // parts, columns), jnp.bfloat16)
    vmem = pl.BlockSpec(memory_space=pltpu.VMEM)
    return pl.pallas_call(
        add_kernel,
        out_shape=(part,) * parts,
        in_specs=[vmem],
        out_specs=(vmem,) * parts,
        cost_estimate=SHORT,
        compiler_params=pltpu.CompilerParams(vmem_limit_bytes=16 * 1024 * 1024),
    )(terms)


def collect_kernel(block_ref, *refs):
    for e, piece in enumerate(refs[:-1]):
        refs[-1][e ^ block_ref[0]] = piece[...]


def collect(block, pieces):
    vmem = pl.BlockSpec(memory_space=pltpu.VMEM)
    return pl.pallas_call(
        collect_kernel,
        out_shape=jax.ShapeDtypeStruct((len(pieces), *pieces[0].shape), jnp.bfloat16),
        in_specs=[pl.BlockSpec(memory_space=pltpu.SMEM)] + [vmem] * len(pieces),
        out_specs=vmem,
        cost_estimate=SHORT,
        compiler_params=pltpu.CompilerParams(vmem_limit_bytes=16 * 1024 * 1024),
    )(block, *pieces)


def page_copies(len_ref, kv_hbm, kv_ref, sem, r):
    page = kv_ref.shape[1] // PAGES
    out = []
    for p in range(PAGES):
        at = pl.ds(p * page, page)
        copy = pltpu.make_async_copy(kv_hbm.at[r, at], kv_ref.at[r, at], sem.at[r, p])
        out.append((copy, len_ref[r] > p * page))
    return out


def talker_kernel(blocks, block_ref, len_ref, gain, *refs):
    w_hbm, refs = refs[:blocks], refs[blocks:]
    terms, kv_hbm, new_kv, out_ref, kv_ref, sem, w_ref, w_sem, qkv, spreads, gathereds = refs
    rows, cached, kv_width = kv_ref.shape
    width = kv_width // 2
    page = cached // PAGES
    heads = out_ref.shape[1] // HEAD_DIM
    group = heads // blocks
    slot = LANES // ROW_STEP
    sets = spreads.shape[0]
    key, value = group * HEAD_DIM, (group + 1) * HEAD_DIM
    inv = 1.0 / HEAD_DIM**0.5

    w_copies = [
        pltpu.make_async_copy(w_hbm[e], w_ref.at[e], w_sem.at[e]) for e in range(blocks)
    ]
    for copy in w_copies:
        copy.start()

    @pl.loop(0, rows)
    def _(r):
        for p, (copy, needed) in enumerate(page_copies(len_ref, kv_hbm, kv_ref, sem, r)):
            if p == 0:
                copy.start()
            else:
                pl.when(needed)(copy.start)

    total = terms[0].astype(jnp.float32)
    for k in range(1, terms.shape[0]):
        total = total + terms[k].astype(jnp.float32)
    scale = lax.rsqrt(jnp.mean(total * total, axis=1, keepdims=True) + 1e-06)
    normed = (total * scale * gain[...]).astype(jnp.bfloat16)
    for e in range(blocks):
        w_copies[e].wait()
        made = jnp.dot(normed, w_ref[e], preferred_element_type=jnp.float32)
        qkv[e ^ block_ref[0]] = made.astype(jnp.bfloat16).astype(jnp.float32)
    for g in range(blocks):
        for place, start in ((g, key), (blocks + g, value)):
            new_kv[:, place * HEAD_DIM : (place + 1) * HEAD_DIM] = qkv[
                g, :, start : start + HEAD_DIM
            ].astype(jnp.bfloat16)

    spreads[...] = jnp.zeros_like(spreads)
    lane = lax.broadcasted_iota(jnp.int32, (HEAD_DIM, LANES), 1)
    lane_row, lane_block = lane // slot, lane % slot // group
    row_block = lax.broadcasted_iota(jnp.int32, (slot, HEAD_DIM), 0) // group
    own_row = lax.broadcasted_iota(jnp.int32, (ROW_STEP, LANES), 0)

    def scores_of(at, spread):
        here = pl.ds(at, ROW_STEP)
        for h in range(heads):
            g, j = h // group, h % group
            spread[pl.ds(h, ROW_STEP, stride=slot), :] = qkv[
                g, here, j * HEAD_DIM : (j + 1) * HEAD_DIM
            ]
        query = spread[...].T
        by_block = [
            jnp.where(lane_block == g, query, 0.0).astype(jnp.bfloat16) for g in range(blocks)
        ]
        scores = jnp.zeros((cached, LANES), jnp.float32)
        for r in range(ROW_STEP):
            mine = lane_row == r
            right = jnp.concatenate(
                [jnp.where(mine, q, jnp.zeros_like(q)) for q in by_block], axis=0
            )
            scores = scores + jnp.dot(
                kv_ref[at + r, :, :width], right, preferred_element_type=jnp.float32
            )
        own = jnp.zeros((ROW_STEP, LANES), jnp.float32)
        for g in range(blocks):
            new_key = qkv[g, here, key:value].astype(jnp.bfloat16)
            own = own + jnp.dot(new_key, by_block[g], preferred_element_type=jnp.float32)
        own = jnp.where(own_row == lane_row[:ROW_STEP], own, 0.0)
        return scores * inv, jnp.sum(own, axis=0, keepdims=True) * inv

    def softmax(at, scores, own):
        lens = jnp.zeros((1, LANES), jnp.int32)
        for r in range(ROW_STEP):
            lens = jnp.where(lane_row[:1] == r, len_ref[at + r], lens)
        valid = lax.broadcasted_iota(jnp.int32, scores.shape, 0) < lens
        scores = jnp.where(valid, scores, -jnp.inf)
        top = jnp.maximum(jnp.max(scores, axis=0, keepdims=True), own)
        expo = jnp.where(valid, jnp.exp(scores - top), 0.0)
        own_expo = jnp.exp(own - top)
        total = jnp.sum(expo, axis=0, keepdims=True) + own_expo
        probs = (expo / total).T.astype(jnp.bfloat16)
        own_prob = (own_expo / total).astype(jnp.bfloat16).astype(jnp.float32)
        return probs, jnp.broadcast_to(own_prob, (LANES, LANES)).T

    def context(at, probs, own_prob, gathered):
        here = pl.ds(at, ROW_STEP)
        value_rows = qkv.at[:, here, value:]
        for r in range(ROW_STEP):
            lanes = slice(r * slot, (r + 1) * slot)
            made = jnp.dot(
                probs[lanes], kv_ref[at + r, :, width:], preferred_element_type=jnp.float32
            )
            ctx = jnp.zeros((slot, HEAD_DIM), jnp.float32)
            new = jnp.zeros((slot, HEAD_DIM), jnp.float32)
            for g in range(blocks):
                block = made[:, g * HEAD_DIM : (g + 1) * HEAD_DIM]
                ctx = jnp.where(row_block == g, block, ctx)
                new = jnp.where(row_block == g, value_rows[g, r : r + 1, :], new)
            gathered[lanes, :] = ctx + own_prob[lanes] * new
        for h in range(heads):
            out_ref[here, h * HEAD_DIM : (h + 1) * HEAD_DIM] = gathered[
                pl.ds(h, ROW_STEP, stride=slot), :
            ]

    @pl.loop(0, rows // (sets * ROW_STEP))
    def _(i):
        first = pl.multiple_of(i * sets * ROW_STEP, sets * ROW_STEP)
        for k in range(sets * ROW_STEP):
            r = first + k
            for p, (copy, needed) in enumerate(page_copies(len_ref, kv_hbm, kv_ref, sem, r)):
                if p == 0:
                    copy.wait()
                    continue
                pl.when(needed)(copy.wait)

                @pl.when(jnp.logical_not(needed))
                def _(p=p, r=r):
                    kv_ref[r, p * page : (p + 1) * page, :] = jnp.zeros(
                        (page, kv_width), kv_ref.dtype
                    )

        ats = [pl.multiple_of(first + k * ROW_STEP, ROW_STEP) for k in range(sets)]
        scored = [scores_of(at, spreads.at[k]) for k, at in enumerate(ats)]
        weighed = [softmax(at, *s) for at, s in zip(ats, scored)]
        for k, at in enumerate(ats):
            context(at, *weighed[k], gathereds.at[k])


def talker(block, terms, talker_gain, weights, kv_len, kv_cache):
    rows, cached, kv_width = kv_cache.shape
    wide, columns = weights[0].shape
    blocks = len(weights)
    q_width = blocks * columns - kv_width
    sets = 2
    vmem = pl.BlockSpec(memory_space=pltpu.VMEM)
    smem = pl.BlockSpec(memory_space=pltpu.SMEM)
    return pl.pallas_call(
        functools.partial(talker_kernel, blocks),
        out_shape=(
            jax.ShapeDtypeStruct((rows, kv_width), jnp.bfloat16),
            jax.ShapeDtypeStruct((rows, q_width), jnp.float32),
        ),
        in_specs=[smem, smem, vmem]
        + [pl.BlockSpec(memory_space=pl.ANY)] * blocks
        + [vmem, pl.BlockSpec(memory_space=pl.ANY)],
        out_specs=(vmem, vmem),
        scratch_shapes=[
            pltpu.VMEM((rows, cached, kv_width), jnp.bfloat16),
            pltpu.SemaphoreType.DMA((rows, PAGES)),
            pltpu.VMEM((blocks, wide, columns), jnp.bfloat16),
            pltpu.SemaphoreType.DMA((blocks,)),
            pltpu.VMEM((blocks, rows, columns), jnp.float32),
            pltpu.VMEM((sets, LANES, HEAD_DIM), jnp.float32),
            pltpu.VMEM((sets, LANES, HEAD_DIM), jnp.float32),
        ],
        cost_estimate=SHORT,
        compiler_params=pltpu.CompilerParams(vmem_limit_bytes=48 * 1024 * 1024),
    )(block, kv_len, talker_gain.reshape(1, wide), *weights, terms, kv_cache)


def rms_norm(talker_in, talker_gain):
    scale = lax.rsqrt(jnp.mean(talker_in * talker_in, axis=1, keepdims=True) + 1e-06)
    return (talker_in * scale * talker_gain).astype(jnp.bfloat16)


def talker_step(talker_in, talker_gain, w_query, w_key, w_value, kv_len, kv_cache):
    owned = talker_in.shape[0]
    cached = kv_cache.shape[1]
    kv_width = w_key.shape[1]
    head_dim = HEAD_DIM
    kv_heads = kv_width // head_dim
    group = w_query.shape[1] // kv_width
    normed = rms_norm(talker_in, talker_gain)
    query = jnp.dot(normed, w_query, preferred_element_type=jnp.float32).astype(jnp.bfloat16)
    new_key = jnp.dot(normed, w_key, preferred_element_type=jnp.float32).astype(jnp.bfloat16)
    new_value = jnp.dot(normed, w_value, preferred_element_type=jnp.float32).astype(jnp.bfloat16)
    talker_kv = jnp.concatenate([new_key, new_value], axis=1)
    qb = query.reshape(owned, kv_heads, group, head_dim)
    keys = kv_cache[:, :, :kv_width].reshape(owned, cached, kv_heads, head_dim)
    values = kv_cache[:, :, kv_width:].reshape(owned, cached, kv_heads, head_dim)
    nk = new_key.reshape(owned, kv_heads, head_dim)
    nv = new_value.reshape(owned, kv_heads, head_dim)
    inv = 1.0 / head_dim**0.5
    scores = jnp.einsum("rgjd,rpgd->rgjp", qb, keys, preferred_element_type=jnp.float32) * inv
    own = jnp.einsum("rgjd,rgd->rgj", qb, nk, preferred_element_type=jnp.float32) * inv
    valid = (jnp.arange(cached, dtype=jnp.int32)[None, :] < kv_len[:, None])[:, None, None, :]
    scores = jnp.where(valid, scores, -jnp.inf)
    top = jnp.maximum(jnp.max(scores, axis=3), own)
    expo = jnp.where(valid, jnp.exp(scores - top[..., None]), 0.0)
    own_expo = jnp.exp(own - top)
    total = jnp.sum(expo, axis=3) + own_expo
    probs = (expo / total[..., None]).astype(jnp.bfloat16)
    own_prob = (own_expo / total).astype(jnp.bfloat16)
    ctx = jnp.einsum("rgjp,rpgd->rgjd", probs, values, preferred_element_type=jnp.float32)
    ctx = ctx + own_prob.astype(jnp.float32)[..., None] * nv.astype(jnp.float32)[:, :, None, :]
    return (talker_kv, ctx.reshape(owned, w_query.shape[1]))


def any_mesh(
    thinker_act,
    w_think,
    w_proj,
    talker_gain,
    w_query,
    w_key,
    w_value,
    talker_slot,
    kv_len,
    kv_cache,
):
    partial_sums = jnp.dot(
        thinker_act,
        lax.all_gather(w_think, ("section", "rows"), axis=1, tiled=True),
        preferred_element_type=jnp.float32,
    )
    full_query, full_key, full_value = (
        lax.all_gather(w_query, ("section", "rows"), axis=1, tiled=True),
        lax.all_gather(w_key, ("section", "rows"), axis=1, tiled=True),
        lax.all_gather(w_value, ("section", "rows"), axis=1, tiled=True),
    )
    mine = lax.psum_scatter(partial_sums, "mp", scatter_dimension=1, tiled=True)
    thinker_out = mine.astype(jnp.bfloat16)
    order = jnp.argsort(talker_slot[0], stable=True)
    sorted_out = thinker_out[order]
    talker_in = lax.psum_scatter(
        jnp.dot(sorted_out, w_proj, preferred_element_type=jnp.float32),
        "mp",
        scatter_dimension=0,
        tiled=True,
    )
    talker_kv, talker_ctx = talker_step(
        talker_in, talker_gain, full_query, full_key, full_value, kv_len, kv_cache
    )
    return (thinker_out, talker_kv, talker_ctx)


PLANE = ("section", "rows")
GROUP = ("mp", "section", "rows")


def over_core(x):
    return lax.ppermute(x, "rows", [(0, 1), (1, 0)])


def over_section(x):
    return lax.ppermute(x, "section", [(0, 1), (1, 0)])


def over_plane(x, e):
    return lax.ppermute(x, PLANE, [(b, b ^ e) for b in range(4)])


def after(x, *others):
    return lax.optimization_barrier((x, *others))[0]


def four_planes(
    thinker_act,
    w_think,
    w_proj,
    talker_gain,
    w_query,
    w_key,
    w_value,
    talker_slot,
    kv_len,
    kv_cache,
):
    planes = 4
    owned = kv_cache.shape[0]
    block = lax.axis_index(PLANE).reshape(1)
    slots = talker_slot[0]

    pick = (jnp.arange(planes * owned)[:, None] == slots[None, :]).astype(jnp.bfloat16)
    rows = jnp.dot(pick, thinker_act, preferred_element_type=jnp.float32).astype(jnp.bfloat16)

    across = over_section(rows)
    peer = over_core(rows)
    near = down([rows, peer], w_think, planes)
    near_terms = lax.all_to_all(near, "mp", 0, 0)
    mine = jnp.concatenate([w_query, w_key, w_value], axis=1)

    own, next_core = add(near_terms, 2)
    across, own, next_core, mine = lax.optimization_barrier((across, own, next_core, mine))
    far = [down([across], w_think, planes)]
    far.append(down([after(over_core(across), far[0])], w_think, planes))
    pieces = [own, over_core(next_core)]
    made = own
    for e, x in zip((2, 3), far):
        (made,) = add(after(lax.all_to_all(x, "mp", 0, 0), made, far[1]), 1)
        pieces.append(over_plane(made, e))
    other = over_section(after(mine, far[0]))

    home = lax.all_to_all(collect(block, pieces), "mp", 0, 0)
    projected = jnp.dot(
        home.reshape(planes * owned, -1), w_proj, preferred_element_type=jnp.float32
    )
    projected = projected.astype(jnp.bfloat16).reshape(planes, owned, -1)
    terms = lax.all_to_all(projected, "mp", 0, 0)
    other = after(other, made)
    weights = [mine, over_core(mine), other, over_core(other)]
    new_kv, ctx = talker(block, terms, talker_gain, weights, kv_len, kv_cache)
    home = after(home, projected)
    pick = (slots[:, None] == jnp.arange(planes * owned)[None, :]).astype(jnp.bfloat16)
    thinker_out = jnp.dot(
        pick, home.reshape(planes * owned, -1), preferred_element_type=jnp.float32
    )
    return (thinker_out.astype(jnp.bfloat16), new_kv, ctx)


def solution(mesh):
    in_specs = (
        P(("groups", "section", "rows"), "mp"),
        P("mp", ("section", "rows")),
        P("mp", None),
        P(),
        P(None, ("section", "rows")),
        P(None, ("section", "rows")),
        P(None, ("section", "rows")),
        P(("groups", "section", "rows"), None),
        P(("groups", "mp", "section", "rows")),
        P(("groups", "mp", "section", "rows"), None, None),
    )
    out_specs = (
        P(("groups", "section", "rows"), "mp"),
        P(("groups", "mp", "section", "rows"), None),
        P(("groups", "mp", "section", "rows"), None),
    )
    sizes = tuple(mesh.shape[a] for a in ("groups", "section", "rows", "mp"))
    shards = four_planes if sizes == (2, 2, 2, 4) else any_mesh
    return jax.shard_map(shards, mesh=mesh, in_specs=in_specs, out_specs=out_specs, check_vma=False)
```

```python
import functools

import jax
import jax.numpy as jnp
from jax import lax
from jax.experimental import pallas as pl
from jax.experimental.pallas import tpu as pltpu
from jax.sharding import PartitionSpec as P

HEAD_DIM = 128
ROW_STEP = 8
LANES = 128
PAGES = 2
SHORT = pl.CostEstimate(flops=1, bytes_accessed=1, transcendentals=0)
MOST_VMEM = 56 * 1024 * 1024


def down_kernel(owned, cuts, groups, *refs):
    slots, xs, refs = refs[:groups], refs[groups : 2 * groups], refs[2 * groups :]
    w, out, x_all, w_all, acc, x_sem, w_sem = refs
    n = xs[0].shape[0]
    loads = []
    for s, (lo, hi) in enumerate(cuts):
        deep = pl.ds(lo, hi - lo)
        copies = [pltpu.make_async_copy(w.at[deep], w_all.at[deep], w_sem.at[s])]
        for i in range(groups):
            copies.append(
                pltpu.make_async_copy(
                    xs[i].at[:, deep], x_all.at[pl.ds(i * n, n), deep], x_sem.at[s, i]
                )
            )
        for copy in copies:
            copy.start()
        loads.append(copies)
    for s, (lo, hi) in enumerate(cuts):
        for copy in loads[s]:
            copy.wait()
        part = jnp.dot(x_all[:, lo:hi], w_all[lo:hi, :], preferred_element_type=jnp.float32)
        acc[...] = part if s == 0 else acc[...] + part
    place = lax.broadcasted_iota(jnp.int32, (n, n), 0)
    for i in range(groups):
        pick = (place == slots[i][...]).astype(jnp.float32).astype(jnp.bfloat16)
        sums = acc[i * n : (i + 1) * n, :].astype(jnp.bfloat16)
        ordered = jnp.dot(pick, sums, preferred_element_type=jnp.float32).astype(out.dtype)
        for p in range(n // owned):
            out[p, i * owned : (i + 1) * owned, :] = ordered[p * owned : (p + 1) * owned, :]


def down(xs, slots, w, owned):
    depth, columns = w.shape
    groups, n = len(xs), xs[0].shape[0]
    tiles, parts = depth // LANES, 6
    ends = [LANES * (tiles * i // parts) for i in range(parts)] + [depth]
    anywhere = pl.BlockSpec(memory_space=pl.ANY)
    vmem = pl.BlockSpec(memory_space=pltpu.VMEM)
    return pl.pallas_call(
        functools.partial(down_kernel, owned, list(zip(ends[:-1], ends[1:])), groups),
        out_shape=jax.ShapeDtypeStruct((n // owned, groups * owned, columns), jnp.bfloat16),
        in_specs=[vmem] * groups + [anywhere] * (groups + 1),
        out_specs=vmem,
        scratch_shapes=[
            pltpu.VMEM((groups * n, depth), jnp.bfloat16),
            pltpu.VMEM((depth, columns), jnp.bfloat16),
            pltpu.VMEM((groups * n, columns), jnp.float32),
            pltpu.SemaphoreType.DMA((parts, groups)),
            pltpu.SemaphoreType.DMA((parts,)),
        ],
        cost_estimate=SHORT,
        compiler_params=pltpu.CompilerParams(vmem_limit_bytes=MOST_VMEM),
    )(*slots, *xs, w)


def finish_kernel(turn_ref, terms, w_mine, w_other, *refs):
    outs, w = refs[:-1], refs[-1]
    half = w_mine.shape[0]
    g = turn_ref[0]
    w[pl.ds(pl.multiple_of(g * half, half), half), :] = w_mine[...]
    w[pl.ds(pl.multiple_of((1 - g) * half, half), half), :] = w_other[...]
    total = terms[0].astype(jnp.float32)
    for k in range(1, terms.shape[0]):
        total = total + terms[k].astype(jnp.float32)
    features = total.astype(jnp.bfloat16)
    projected = jnp.dot(features, w[...], preferred_element_type=jnp.float32)
    projected = projected.astype(jnp.bfloat16)
    n = features.shape[0] // len(outs)
    for i, out in enumerate(outs):
        out[0] = features[i * n : (i + 1) * n]
        out[1] = projected[i * n : (i + 1) * n]


def finish(turn, terms, w_halves, parts):
    _, rows, columns = terms.shape
    wide = w_halves[0].shape[1]
    part = jax.ShapeDtypeStruct((2, rows // parts, columns), jnp.bfloat16)
    vmem = pl.BlockSpec(memory_space=pltpu.VMEM)
    return pl.pallas_call(
        finish_kernel,
        out_shape=(part,) * parts,
        in_specs=[pl.BlockSpec(memory_space=pltpu.SMEM), vmem, vmem, vmem],
        out_specs=(vmem,) * parts,
        scratch_shapes=[pltpu.VMEM((columns, wide), jnp.bfloat16)],
        cost_estimate=SHORT,
        compiler_params=pltpu.CompilerParams(vmem_limit_bytes=16 * 1024 * 1024),
    )(turn, terms, *w_halves)


def collect_kernel(block_ref, *refs):
    for e, piece in enumerate(refs[:-1]):
        refs[-1][e ^ block_ref[0]] = piece[0]


def collect(block, pieces):
    vmem = pl.BlockSpec(memory_space=pltpu.VMEM)
    return pl.pallas_call(
        collect_kernel,
        out_shape=jax.ShapeDtypeStruct((len(pieces), *pieces[0].shape[1:]), jnp.bfloat16),
        in_specs=[pl.BlockSpec(memory_space=pltpu.SMEM)] + [vmem] * len(pieces),
        out_specs=vmem,
        cost_estimate=SHORT,
        compiler_params=pltpu.CompilerParams(vmem_limit_bytes=16 * 1024 * 1024),
    )(block, *pieces)


def page_copies(len_ref, kv_hbm, kv_ref, sem, r):
    page = kv_ref.shape[1] // PAGES
    out = []
    for p in range(PAGES):
        at = pl.ds(p * page, page)
        copy = pltpu.make_async_copy(kv_hbm.at[r, at], kv_ref.at[r, at], sem.at[r, p])
        out.append((copy, len_ref[r] > p * page))
    return out


def talker_kernel(blocks, block_ref, len_ref, gain, *refs):
    w_hbm, refs = refs[:blocks], refs[blocks:]
    terms, refs = refs[:blocks], refs[blocks:]
    kv_hbm, new_kv, out_ref, kv_ref, sem, w_ref, w_sem, qkv, spreads, gathereds = refs
    rows, cached, kv_width = kv_ref.shape
    width = kv_width // 2
    page = cached // PAGES
    heads = out_ref.shape[1] // HEAD_DIM
    group = heads // blocks
    slot = LANES // ROW_STEP
    sets = spreads.shape[0]
    key, value = group * HEAD_DIM, (group + 1) * HEAD_DIM
    inv = 1.0 / HEAD_DIM**0.5

    w_copies = [
        pltpu.make_async_copy(w_hbm[e], w_ref.at[e], w_sem.at[e]) for e in range(blocks)
    ]
    for copy in w_copies:
        copy.start()

    @pl.loop(0, rows)
    def _(r):
        for p, (copy, needed) in enumerate(page_copies(len_ref, kv_hbm, kv_ref, sem, r)):
            if p == 0:
                copy.start()
            else:
                pl.when(needed)(copy.start)

    total = terms[0][1].astype(jnp.float32)
    for term in terms[1:]:
        total = total + term[1].astype(jnp.float32)
    scale = lax.rsqrt(jnp.mean(total * total, axis=1, keepdims=True) + 1e-06)
    normed = (total * scale * gain[...]).astype(jnp.bfloat16)
    for e in range(blocks):
        w_copies[e].wait()
        made = jnp.dot(normed, w_ref[e], preferred_element_type=jnp.float32)
        qkv[e ^ block_ref[0]] = made.astype(jnp.bfloat16).astype(jnp.float32)
    for g in range(blocks):
        for place, start in ((g, key), (blocks + g, value)):
            new_kv[:, place * HEAD_DIM : (place + 1) * HEAD_DIM] = qkv[
                g, :, start : start + HEAD_DIM
            ].astype(jnp.bfloat16)

    spreads[...] = jnp.zeros_like(spreads)
    lane = lax.broadcasted_iota(jnp.int32, (HEAD_DIM, LANES), 1)
    lane_row, lane_block = lane // slot, lane % slot // group
    row_block = lax.broadcasted_iota(jnp.int32, (slot, HEAD_DIM), 0) // group
    own_row = lax.broadcasted_iota(jnp.int32, (ROW_STEP, LANES), 0)

    def scores_of(at, spread):
        here = pl.ds(at, ROW_STEP)
        for h in range(heads):
            g, j = h // group, h % group
            spread[pl.ds(h, ROW_STEP, stride=slot), :] = qkv[
                g, here, j * HEAD_DIM : (j + 1) * HEAD_DIM
            ]
        query = spread[...].T
        by_block = [
            jnp.where(lane_block == g, query, 0.0).astype(jnp.bfloat16) for g in range(blocks)
        ]
        scores = jnp.zeros((cached, LANES), jnp.float32)
        for r in range(ROW_STEP):
            mine = lane_row == r
            right = jnp.concatenate(
                [jnp.where(mine, q, jnp.zeros_like(q)) for q in by_block], axis=0
            )
            scores = scores + jnp.dot(
                kv_ref[at + r, :, :width], right, preferred_element_type=jnp.float32
            )
        own = jnp.zeros((ROW_STEP, LANES), jnp.float32)
        for g in range(blocks):
            new_key = qkv[g, here, key:value].astype(jnp.bfloat16)
            own = own + jnp.dot(new_key, by_block[g], preferred_element_type=jnp.float32)
        own = jnp.where(own_row == lane_row[:ROW_STEP], own, 0.0)
        return scores * inv, jnp.sum(own, axis=0, keepdims=True) * inv

    def softmax(at, scores, own):
        lens = jnp.zeros((1, LANES), jnp.int32)
        for r in range(ROW_STEP):
            lens = jnp.where(lane_row[:1] == r, len_ref[at + r], lens)
        valid = lax.broadcasted_iota(jnp.int32, scores.shape, 0) < lens
        scores = jnp.where(valid, scores, -jnp.inf)
        top = jnp.maximum(jnp.max(scores, axis=0, keepdims=True), own)
        expo = jnp.where(valid, jnp.exp(scores - top), 0.0)
        own_expo = jnp.exp(own - top)
        total = jnp.sum(expo, axis=0, keepdims=True) + own_expo
        probs = (expo / total).T.astype(jnp.bfloat16)
        own_prob = (own_expo / total).astype(jnp.bfloat16).astype(jnp.float32)
        return probs, jnp.broadcast_to(own_prob, (LANES, LANES)).T

    def context(at, probs, own_prob, gathered):
        here = pl.ds(at, ROW_STEP)
        value_rows = qkv.at[:, here, value:]
        for r in range(ROW_STEP):
            lanes = slice(r * slot, (r + 1) * slot)
            made = jnp.dot(
                probs[lanes], kv_ref[at + r, :, width:], preferred_element_type=jnp.float32
            )
            ctx = jnp.zeros((slot, HEAD_DIM), jnp.float32)
            new = jnp.zeros((slot, HEAD_DIM), jnp.float32)
            for g in range(blocks):
                block = made[:, g * HEAD_DIM : (g + 1) * HEAD_DIM]
                ctx = jnp.where(row_block == g, block, ctx)
                new = jnp.where(row_block == g, value_rows[g, r : r + 1, :], new)
            gathered[lanes, :] = ctx + own_prob[lanes] * new
        for h in range(heads):
            out_ref[here, h * HEAD_DIM : (h + 1) * HEAD_DIM] = gathered[
                pl.ds(h, ROW_STEP, stride=slot), :
            ]

    @pl.loop(0, rows // (sets * ROW_STEP))
    def _(i):
        first = pl.multiple_of(i * sets * ROW_STEP, sets * ROW_STEP)
        for k in range(sets * ROW_STEP):
            r = first + k
            for p, (copy, needed) in enumerate(page_copies(len_ref, kv_hbm, kv_ref, sem, r)):
                if p == 0:
                    copy.wait()
                    continue
                pl.when(needed)(copy.wait)

                @pl.when(jnp.logical_not(needed))
                def _(p=p, r=r):
                    kv_ref[r, p * page : (p + 1) * page, :] = jnp.zeros(
                        (page, kv_width), kv_ref.dtype
                    )

        ats = [pl.multiple_of(first + k * ROW_STEP, ROW_STEP) for k in range(sets)]
        scored = [scores_of(at, spreads.at[k]) for k, at in enumerate(ats)]
        weighed = [softmax(at, *s) for at, s in zip(ats, scored)]
        for k, at in enumerate(ats):
            context(at, *weighed[k], gathereds.at[k])


def talker(block, pieces, talker_gain, weights, kv_len, kv_cache):
    rows, cached, kv_width = kv_cache.shape
    wide, columns = weights[0].shape
    blocks = len(weights)
    q_width = blocks * columns - kv_width
    sets = 2
    vmem = pl.BlockSpec(memory_space=pltpu.VMEM)
    smem = pl.BlockSpec(memory_space=pltpu.SMEM)
    return pl.pallas_call(
        functools.partial(talker_kernel, blocks),
        out_shape=(
            jax.ShapeDtypeStruct((rows, kv_width), jnp.bfloat16),
            jax.ShapeDtypeStruct((rows, q_width), jnp.float32),
        ),
        in_specs=[smem, smem, vmem]
        + [pl.BlockSpec(memory_space=pl.ANY)] * blocks
        + [vmem] * len(pieces)
        + [pl.BlockSpec(memory_space=pl.ANY)],
        out_specs=(vmem, vmem),
        scratch_shapes=[
            pltpu.VMEM((rows, cached, kv_width), jnp.bfloat16),
            pltpu.SemaphoreType.DMA((rows, PAGES)),
            pltpu.VMEM((blocks, wide, columns), jnp.bfloat16),
            pltpu.SemaphoreType.DMA((blocks,)),
            pltpu.VMEM((blocks, rows, columns), jnp.float32),
            pltpu.VMEM((sets, LANES, HEAD_DIM), jnp.float32),
            pltpu.VMEM((sets, LANES, HEAD_DIM), jnp.float32),
        ],
        cost_estimate=SHORT,
        compiler_params=pltpu.CompilerParams(vmem_limit_bytes=48 * 1024 * 1024),
    )(block, kv_len, talker_gain.reshape(1, wide), *weights, *pieces, kv_cache)


def rms_norm(talker_in, talker_gain):
    scale = lax.rsqrt(jnp.mean(talker_in * talker_in, axis=1, keepdims=True) + 1e-06)
    return (talker_in * scale * talker_gain).astype(jnp.bfloat16)


def talker_step(talker_in, talker_gain, w_query, w_key, w_value, kv_len, kv_cache):
    owned = talker_in.shape[0]
    cached = kv_cache.shape[1]
    kv_width = w_key.shape[1]
    head_dim = HEAD_DIM
    kv_heads = kv_width // head_dim
    group = w_query.shape[1] // kv_width
    normed = rms_norm(talker_in, talker_gain)
    query = jnp.dot(normed, w_query, preferred_element_type=jnp.float32).astype(jnp.bfloat16)
    new_key = jnp.dot(normed, w_key, preferred_element_type=jnp.float32).astype(jnp.bfloat16)
    new_value = jnp.dot(normed, w_value, preferred_element_type=jnp.float32).astype(jnp.bfloat16)
    talker_kv = jnp.concatenate([new_key, new_value], axis=1)
    qb = query.reshape(owned, kv_heads, group, head_dim)
    keys = kv_cache[:, :, :kv_width].reshape(owned, cached, kv_heads, head_dim)
    values = kv_cache[:, :, kv_width:].reshape(owned, cached, kv_heads, head_dim)
    nk = new_key.reshape(owned, kv_heads, head_dim)
    nv = new_value.reshape(owned, kv_heads, head_dim)
    inv = 1.0 / head_dim**0.5
    scores = jnp.einsum("rgjd,rpgd->rgjp", qb, keys, preferred_element_type=jnp.float32) * inv
    own = jnp.einsum("rgjd,rgd->rgj", qb, nk, preferred_element_type=jnp.float32) * inv
    valid = (jnp.arange(cached, dtype=jnp.int32)[None, :] < kv_len[:, None])[:, None, None, :]
    scores = jnp.where(valid, scores, -jnp.inf)
    top = jnp.maximum(jnp.max(scores, axis=3), own)
    expo = jnp.where(valid, jnp.exp(scores - top[..., None]), 0.0)
    own_expo = jnp.exp(own - top)
    total = jnp.sum(expo, axis=3) + own_expo
    probs = (expo / total[..., None]).astype(jnp.bfloat16)
    own_prob = (own_expo / total).astype(jnp.bfloat16)
    ctx = jnp.einsum("rgjp,rpgd->rgjd", probs, values, preferred_element_type=jnp.float32)
    ctx = ctx + own_prob.astype(jnp.float32)[..., None] * nv.astype(jnp.float32)[:, :, None, :]
    return (talker_kv, ctx.reshape(owned, w_query.shape[1]))


def any_mesh(
    thinker_act,
    w_think,
    w_proj,
    talker_gain,
    w_query,
    w_key,
    w_value,
    talker_slot,
    kv_len,
    kv_cache,
):
    partial_sums = jnp.dot(
        thinker_act,
        lax.all_gather(w_think, ("section", "rows"), axis=1, tiled=True),
        preferred_element_type=jnp.float32,
    )
    full_query, full_key, full_value = (
        lax.all_gather(w_query, ("section", "rows"), axis=1, tiled=True),
        lax.all_gather(w_key, ("section", "rows"), axis=1, tiled=True),
        lax.all_gather(w_value, ("section", "rows"), axis=1, tiled=True),
    )
    mine = lax.psum_scatter(partial_sums, "mp", scatter_dimension=1, tiled=True)
    thinker_out = mine.astype(jnp.bfloat16)
    order = jnp.argsort(talker_slot[0], stable=True)
    sorted_out = thinker_out[order]
    talker_in = lax.psum_scatter(
        jnp.dot(sorted_out, w_proj, preferred_element_type=jnp.float32),
        "mp",
        scatter_dimension=0,
        tiled=True,
    )
    talker_kv, talker_ctx = talker_step(
        talker_in, talker_gain, full_query, full_key, full_value, kv_len, kv_cache
    )
    return (thinker_out, talker_kv, talker_ctx)


PLANE = ("section", "rows")
GROUP = ("mp", "section", "rows")


def over_core(x):
    return lax.ppermute(x, "rows", [(0, 1), (1, 0)])


def over_section(x):
    return lax.ppermute(x, "section", [(0, 1), (1, 0)])


def over_plane(x, e):
    return lax.ppermute(x, PLANE, [(b, b ^ e) for b in range(4)])


def over_groups(x):
    return lax.ppermute(x, "groups", [(0, 1), (1, 0)])


def after(x, *others):
    return lax.optimization_barrier((x, *others))[0]


def four_planes(
    thinker_act,
    w_think,
    w_proj,
    talker_gain,
    w_query,
    w_key,
    w_value,
    talker_slot,
    kv_len,
    kv_cache,
):
    planes = 4
    owned = kv_cache.shape[0]
    g, m, c = lax.axis_index("groups"), lax.axis_index("mp"), lax.axis_index(PLANE)
    block, turn = c.reshape(1), g.reshape(1)
    slots = talker_slot[0]

    across, peer = over_section(thinker_act), over_core(thinker_act)
    peer_slots, across_slots = over_core(talker_slot), over_section(talker_slot)
    far_slots = over_core(across_slots)
    near = down([thinker_act, peer], [talker_slot, peer_slots], w_think, owned)
    near_terms = lax.all_to_all(near, "mp", 0, 0)
    mine = jnp.concatenate([w_query, w_key, w_value], axis=1)

    half = w_proj.shape[0] // 2
    half_w = lax.dynamic_slice_in_dim(w_proj, g * half, half, axis=0)
    half_w = lax.psum(jnp.where(m == c, half_w, jnp.zeros_like(half_w)), "mp")

    across, near_terms, mine, far_slots, half_w = lax.optimization_barrier(
        (across, near_terms, mine, far_slots, half_w)
    )
    far = [down([across], [across_slots], w_think, owned)]
    far.append(down([after(over_core(across), far[0])], [far_slots], w_think, owned))
    block_w = (half_w, over_groups(half_w))
    other = over_section(after(mine, far[0]))

    own, next_core = finish(turn, after(near_terms, far[1]), block_w, 2)
    pieces = [own, over_core(next_core)]
    made = own
    for e, x in zip((2, 3), far):
        (made,) = finish(turn, after(lax.all_to_all(x, "mp", 0, 0), made), block_w, 1)
        pieces.append(over_plane(made, e))
    other = after(other, made)
    weights = [mine, over_core(mine), other, over_core(other)]

    home = lax.all_to_all(collect(block, pieces), "mp", 0, 0)
    new_kv, ctx = talker(block, pieces, talker_gain, weights, kv_len, kv_cache)
    home = after(home, ctx)
    pick = (slots[:, None] == jnp.arange(planes * owned)[None, :]).astype(jnp.bfloat16)
    thinker_out = jnp.dot(
        pick, home.reshape(planes * owned, -1), preferred_element_type=jnp.float32
    )
    return (thinker_out.astype(jnp.bfloat16), new_kv, ctx)


def solution(mesh):
    in_specs = (
        P(("groups", "section", "rows"), "mp"),
        P("mp", ("section", "rows")),
        P("mp", None),
        P(),
        P(None, ("section", "rows")),
        P(None, ("section", "rows")),
        P(None, ("section", "rows")),
        P(("groups", "section", "rows"), None),
        P(("groups", "mp", "section", "rows")),
        P(("groups", "mp", "section", "rows"), None, None),
    )
    out_specs = (
        P(("groups", "section", "rows"), "mp"),
        P(("groups", "mp", "section", "rows"), None),
        P(("groups", "mp", "section", "rows"), None),
    )
    sizes = tuple(mesh.shape[a] for a in ("groups", "section", "rows", "mp"))
    shards = four_planes if sizes == (2, 2, 2, 4) else any_mesh
    return jax.shard_map(shards, mesh=mesh, in_specs=in_specs, out_specs=out_specs, check_vma=False)
```

```python
import functools

import jax
import jax.numpy as jnp
from jax import lax
from jax.experimental import pallas as pl
from jax.experimental.pallas import tpu as pltpu
from jax.sharding import PartitionSpec as P

HEAD_DIM = 128
ROW_STEP = 8
LANES = 128
PAGES = 2
SHORT = pl.CostEstimate(flops=1, bytes_accessed=1, transcendentals=0)
MOST_VMEM = 56 * 1024 * 1024


def down_kernel(owned, cuts, groups, *refs):
    slots, xs, refs = refs[:groups], refs[groups : 2 * groups], refs[2 * groups :]
    w, out, x_all, w_all, acc, x_sem, w_sem = refs
    n = xs[0].shape[0]
    loads = []
    for s, (lo, hi) in enumerate(cuts):
        deep = pl.ds(lo, hi - lo)
        copies = [pltpu.make_async_copy(w.at[deep], w_all.at[deep], w_sem.at[s])]
        for i in range(groups):
            copies.append(
                pltpu.make_async_copy(
                    xs[i].at[:, deep], x_all.at[pl.ds(i * n, n), deep], x_sem.at[s, i]
                )
            )
        for copy in copies:
            copy.start()
        loads.append(copies)
    for s, (lo, hi) in enumerate(cuts):
        for copy in loads[s]:
            copy.wait()
        part = jnp.dot(x_all[:, lo:hi], w_all[lo:hi, :], preferred_element_type=jnp.float32)
        acc[...] = part if s == 0 else acc[...] + part
    place = lax.broadcasted_iota(jnp.int32, (n, n), 0)
    for i in range(groups):
        pick = (place == slots[i][...]).astype(jnp.float32).astype(jnp.bfloat16)
        sums = acc[i * n : (i + 1) * n, :].astype(jnp.bfloat16)
        ordered = jnp.dot(pick, sums, preferred_element_type=jnp.float32).astype(out.dtype)
        for p in range(n // owned):
            out[p, i * owned : (i + 1) * owned, :] = ordered[p * owned : (p + 1) * owned, :]


def down(xs, slots, w, owned):
    depth, columns = w.shape
    groups, n = len(xs), xs[0].shape[0]
    tiles, parts = depth // LANES, 6
    ends = [LANES * (tiles * i // parts) for i in range(parts)] + [depth]
    anywhere = pl.BlockSpec(memory_space=pl.ANY)
    vmem = pl.BlockSpec(memory_space=pltpu.VMEM)
    return pl.pallas_call(
        functools.partial(down_kernel, owned, list(zip(ends[:-1], ends[1:])), groups),
        out_shape=jax.ShapeDtypeStruct((n // owned, groups * owned, columns), jnp.bfloat16),
        in_specs=[vmem] * groups + [anywhere] * (groups + 1),
        out_specs=vmem,
        scratch_shapes=[
            pltpu.VMEM((groups * n, depth), jnp.bfloat16),
            pltpu.VMEM((depth, columns), jnp.bfloat16),
            pltpu.VMEM((groups * n, columns), jnp.float32),
            pltpu.SemaphoreType.DMA((parts, groups)),
            pltpu.SemaphoreType.DMA((parts,)),
        ],
        cost_estimate=SHORT,
        compiler_params=pltpu.CompilerParams(vmem_limit_bytes=MOST_VMEM),
    )(*slots, *xs, w)


def finish_kernel(turn_ref, terms, w_mine, w_other, *refs):
    outs, w = refs[:-1], refs[-1]
    half = w_mine.shape[0]
    g = turn_ref[0]
    w[pl.ds(pl.multiple_of(g * half, half), half), :] = w_mine[...]
    w[pl.ds(pl.multiple_of((1 - g) * half, half), half), :] = w_other[...]
    total = terms[0].astype(jnp.float32)
    for k in range(1, terms.shape[0]):
        total = total + terms[k].astype(jnp.float32)
    features = total.astype(jnp.bfloat16)
    projected = jnp.dot(features, w[...], preferred_element_type=jnp.float32)
    projected = projected.astype(jnp.bfloat16)
    n = features.shape[0] // len(outs)
    for i, out in enumerate(outs):
        out[0] = features[i * n : (i + 1) * n]
        out[1] = projected[i * n : (i + 1) * n]


def finish(turn, terms, w_halves, parts):
    _, rows, columns = terms.shape
    wide = w_halves[0].shape[1]
    part = jax.ShapeDtypeStruct((2, rows // parts, columns), jnp.bfloat16)
    vmem = pl.BlockSpec(memory_space=pltpu.VMEM)
    return pl.pallas_call(
        finish_kernel,
        out_shape=(part,) * parts,
        in_specs=[pl.BlockSpec(memory_space=pltpu.SMEM), vmem, vmem, vmem],
        out_specs=(vmem,) * parts,
        scratch_shapes=[pltpu.VMEM((columns, wide), jnp.bfloat16)],
        cost_estimate=SHORT,
        compiler_params=pltpu.CompilerParams(vmem_limit_bytes=16 * 1024 * 1024),
    )(turn, terms, *w_halves)


def collect_kernel(block_ref, *refs):
    for e, piece in enumerate(refs[:-1]):
        refs[-1][e ^ block_ref[0]] = piece[0]


def collect(block, pieces):
    vmem = pl.BlockSpec(memory_space=pltpu.VMEM)
    return pl.pallas_call(
        collect_kernel,
        out_shape=jax.ShapeDtypeStruct((len(pieces), *pieces[0].shape[1:]), jnp.bfloat16),
        in_specs=[pl.BlockSpec(memory_space=pltpu.SMEM)] + [vmem] * len(pieces),
        out_specs=vmem,
        cost_estimate=SHORT,
        compiler_params=pltpu.CompilerParams(vmem_limit_bytes=16 * 1024 * 1024),
    )(block, *pieces)


def page_copies(len_ref, kv_hbm, kv_ref, sem, r):
    page = kv_ref.shape[1] // PAGES
    out = []
    for p in range(PAGES):
        at = pl.ds(p * page, page)
        copy = pltpu.make_async_copy(kv_hbm.at[r, at], kv_ref.at[r, at], sem.at[r, p])
        out.append((copy, len_ref[r] > p * page))
    return out


def talker_kernel(blocks, block_ref, len_ref, gain, *refs):
    w_hbm, refs = refs[:blocks], refs[blocks:]
    terms, refs = refs[:blocks], refs[blocks:]
    kv_hbm, new_kv, out_ref, kv_ref, sem, w_ref, w_sem, qkv, spreads, gathereds = refs
    rows, cached, kv_width = kv_ref.shape
    width = kv_width // 2
    page = cached // PAGES
    heads = out_ref.shape[1] // HEAD_DIM
    group = heads // blocks
    slot = LANES // ROW_STEP
    sets = spreads.shape[0]
    key, value = group * HEAD_DIM, (group + 1) * HEAD_DIM
    inv = 1.0 / HEAD_DIM**0.5

    w_copies = [
        pltpu.make_async_copy(w_hbm[e], w_ref.at[e], w_sem.at[e]) for e in range(blocks)
    ]
    for copy in w_copies:
        copy.start()

    @pl.loop(0, rows)
    def _(r):
        for p, (copy, needed) in enumerate(page_copies(len_ref, kv_hbm, kv_ref, sem, r)):
            if p == 0:
                copy.start()
            else:
                pl.when(needed)(copy.start)

    total = terms[0][1].astype(jnp.float32)
    for term in terms[1:]:
        total = total + term[1].astype(jnp.float32)
    scale = lax.rsqrt(jnp.mean(total * total, axis=1, keepdims=True) + 1e-06)
    normed = (total * scale * gain[...]).astype(jnp.bfloat16)
    for e in range(blocks):
        w_copies[e].wait()
        made = jnp.dot(normed, w_ref[e], preferred_element_type=jnp.float32)
        qkv[e ^ block_ref[0]] = made.astype(jnp.bfloat16).astype(jnp.float32)
    for g in range(blocks):
        for place, start in ((g, key), (blocks + g, value)):
            new_kv[:, place * HEAD_DIM : (place + 1) * HEAD_DIM] = qkv[
                g, :, start : start + HEAD_DIM
            ].astype(jnp.bfloat16)

    spreads[...] = jnp.zeros_like(spreads)
    lane = lax.broadcasted_iota(jnp.int32, (HEAD_DIM, LANES), 1)
    lane_row, lane_block = lane // slot, lane % slot // group
    row_block = lax.broadcasted_iota(jnp.int32, (slot, HEAD_DIM), 0) // group
    own_row = lax.broadcasted_iota(jnp.int32, (ROW_STEP, LANES), 0)

    def scores_of(at, spread):
        here = pl.ds(at, ROW_STEP)
        for h in range(heads):
            g, j = h // group, h % group
            spread[pl.ds(h, ROW_STEP, stride=slot), :] = qkv[
                g, here, j * HEAD_DIM : (j + 1) * HEAD_DIM
            ]
        query = spread[...].T
        by_block = [
            jnp.where(lane_block == g, query, 0.0).astype(jnp.bfloat16) for g in range(blocks)
        ]
        scores = jnp.zeros((cached, LANES), jnp.float32)
        for r in range(ROW_STEP):
            mine = lane_row == r
            right = jnp.concatenate(
                [jnp.where(mine, q, jnp.zeros_like(q)) for q in by_block], axis=0
            )
            scores = scores + jnp.dot(
                kv_ref[at + r, :, :width], right, preferred_element_type=jnp.float32
            )
        own = jnp.zeros((ROW_STEP, LANES), jnp.float32)
        for g in range(blocks):
            new_key = qkv[g, here, key:value].astype(jnp.bfloat16)
            own = own + jnp.dot(new_key, by_block[g], preferred_element_type=jnp.float32)
        own = jnp.where(own_row == lane_row[:ROW_STEP], own, 0.0)
        return scores * inv, jnp.sum(own, axis=0, keepdims=True) * inv

    def softmax(at, scores, own):
        lens = jnp.zeros((1, LANES), jnp.int32)
        for r in range(ROW_STEP):
            lens = jnp.where(lane_row[:1] == r, len_ref[at + r], lens)
        valid = lax.broadcasted_iota(jnp.int32, scores.shape, 0) < lens
        scores = jnp.where(valid, scores, -jnp.inf)
        top = jnp.maximum(jnp.max(scores, axis=0, keepdims=True), own)
        expo = jnp.where(valid, jnp.exp(scores - top), 0.0)
        own_expo = jnp.exp(own - top)
        total = jnp.sum(expo, axis=0, keepdims=True) + own_expo
        probs = (expo / total).T.astype(jnp.bfloat16)
        own_prob = (own_expo / total).astype(jnp.bfloat16).astype(jnp.float32)
        return probs, jnp.broadcast_to(own_prob, (LANES, LANES)).T

    def context(at, probs, own_prob, gathered):
        here = pl.ds(at, ROW_STEP)
        value_rows = qkv.at[:, here, value:]
        for r in range(ROW_STEP):
            lanes = slice(r * slot, (r + 1) * slot)
            made = jnp.dot(
                probs[lanes], kv_ref[at + r, :, width:], preferred_element_type=jnp.float32
            )
            ctx = jnp.zeros((slot, HEAD_DIM), jnp.float32)
            new = jnp.zeros((slot, HEAD_DIM), jnp.float32)
            for g in range(blocks):
                block = made[:, g * HEAD_DIM : (g + 1) * HEAD_DIM]
                ctx = jnp.where(row_block == g, block, ctx)
                new = jnp.where(row_block == g, value_rows[g, r : r + 1, :], new)
            gathered[lanes, :] = ctx + own_prob[lanes] * new
        for h in range(heads):
            out_ref[here, h * HEAD_DIM : (h + 1) * HEAD_DIM] = gathered[
                pl.ds(h, ROW_STEP, stride=slot), :
            ]

    @pl.loop(0, rows // (sets * ROW_STEP))
    def _(i):
        first = pl.multiple_of(i * sets * ROW_STEP, sets * ROW_STEP)
        for k in range(sets * ROW_STEP):
            r = first + k
            for p, (copy, needed) in enumerate(page_copies(len_ref, kv_hbm, kv_ref, sem, r)):
                if p == 0:
                    copy.wait()
                    continue
                pl.when(needed)(copy.wait)

                @pl.when(jnp.logical_not(needed))
                def _(p=p, r=r):
                    kv_ref[r, p * page : (p + 1) * page, :] = jnp.zeros(
                        (page, kv_width), kv_ref.dtype
                    )

        ats = [pl.multiple_of(first + k * ROW_STEP, ROW_STEP) for k in range(sets)]
        scored = [scores_of(at, spreads.at[k]) for k, at in enumerate(ats)]
        weighed = [softmax(at, *s) for at, s in zip(ats, scored)]
        for k, at in enumerate(ats):
            context(at, *weighed[k], gathereds.at[k])


def talker(block, pieces, talker_gain, weights, kv_len, kv_cache):
    rows, cached, kv_width = kv_cache.shape
    wide, columns = weights[0].shape
    blocks = len(weights)
    q_width = blocks * columns - kv_width
    sets = 2
    vmem = pl.BlockSpec(memory_space=pltpu.VMEM)
    smem = pl.BlockSpec(memory_space=pltpu.SMEM)
    return pl.pallas_call(
        functools.partial(talker_kernel, blocks),
        out_shape=(
            jax.ShapeDtypeStruct((rows, kv_width), jnp.bfloat16),
            jax.ShapeDtypeStruct((rows, q_width), jnp.float32),
        ),
        in_specs=[smem, smem, vmem]
        + [pl.BlockSpec(memory_space=pl.ANY)] * blocks
        + [vmem] * len(pieces)
        + [pl.BlockSpec(memory_space=pl.ANY)],
        out_specs=(vmem, vmem),
        scratch_shapes=[
            pltpu.VMEM((rows, cached, kv_width), jnp.bfloat16),
            pltpu.SemaphoreType.DMA((rows, PAGES)),
            pltpu.VMEM((blocks, wide, columns), jnp.bfloat16),
            pltpu.SemaphoreType.DMA((blocks,)),
            pltpu.VMEM((blocks, rows, columns), jnp.float32),
            pltpu.VMEM((sets, LANES, HEAD_DIM), jnp.float32),
            pltpu.VMEM((sets, LANES, HEAD_DIM), jnp.float32),
        ],
        cost_estimate=SHORT,
        compiler_params=pltpu.CompilerParams(vmem_limit_bytes=48 * 1024 * 1024),
    )(block, kv_len, talker_gain.reshape(1, wide), *weights, *pieces, kv_cache)


def rms_norm(talker_in, talker_gain):
    scale = lax.rsqrt(jnp.mean(talker_in * talker_in, axis=1, keepdims=True) + 1e-06)
    return (talker_in * scale * talker_gain).astype(jnp.bfloat16)


def talker_step(talker_in, talker_gain, w_query, w_key, w_value, kv_len, kv_cache):
    owned = talker_in.shape[0]
    cached = kv_cache.shape[1]
    kv_width = w_key.shape[1]
    head_dim = HEAD_DIM
    kv_heads = kv_width // head_dim
    group = w_query.shape[1] // kv_width
    normed = rms_norm(talker_in, talker_gain)
    query = jnp.dot(normed, w_query, preferred_element_type=jnp.float32).astype(jnp.bfloat16)
    new_key = jnp.dot(normed, w_key, preferred_element_type=jnp.float32).astype(jnp.bfloat16)
    new_value = jnp.dot(normed, w_value, preferred_element_type=jnp.float32).astype(jnp.bfloat16)
    talker_kv = jnp.concatenate([new_key, new_value], axis=1)
    qb = query.reshape(owned, kv_heads, group, head_dim)
    keys = kv_cache[:, :, :kv_width].reshape(owned, cached, kv_heads, head_dim)
    values = kv_cache[:, :, kv_width:].reshape(owned, cached, kv_heads, head_dim)
    nk = new_key.reshape(owned, kv_heads, head_dim)
    nv = new_value.reshape(owned, kv_heads, head_dim)
    inv = 1.0 / head_dim**0.5
    scores = jnp.einsum("rgjd,rpgd->rgjp", qb, keys, preferred_element_type=jnp.float32) * inv
    own = jnp.einsum("rgjd,rgd->rgj", qb, nk, preferred_element_type=jnp.float32) * inv
    valid = (jnp.arange(cached, dtype=jnp.int32)[None, :] < kv_len[:, None])[:, None, None, :]
    scores = jnp.where(valid, scores, -jnp.inf)
    top = jnp.maximum(jnp.max(scores, axis=3), own)
    expo = jnp.where(valid, jnp.exp(scores - top[..., None]), 0.0)
    own_expo = jnp.exp(own - top)
    total = jnp.sum(expo, axis=3) + own_expo
    probs = (expo / total[..., None]).astype(jnp.bfloat16)
    own_prob = (own_expo / total).astype(jnp.bfloat16)
    ctx = jnp.einsum("rgjp,rpgd->rgjd", probs, values, preferred_element_type=jnp.float32)
    ctx = ctx + own_prob.astype(jnp.float32)[..., None] * nv.astype(jnp.float32)[:, :, None, :]
    return (talker_kv, ctx.reshape(owned, w_query.shape[1]))


def any_mesh(
    thinker_act,
    w_think,
    w_proj,
    talker_gain,
    w_query,
    w_key,
    w_value,
    talker_slot,
    kv_len,
    kv_cache,
):
    partial_sums = jnp.dot(
        thinker_act,
        lax.all_gather(w_think, ("section", "rows"), axis=1, tiled=True),
        preferred_element_type=jnp.float32,
    )
    full_query, full_key, full_value = (
        lax.all_gather(w_query, ("section", "rows"), axis=1, tiled=True),
        lax.all_gather(w_key, ("section", "rows"), axis=1, tiled=True),
        lax.all_gather(w_value, ("section", "rows"), axis=1, tiled=True),
    )
    mine = lax.psum_scatter(partial_sums, "mp", scatter_dimension=1, tiled=True)
    thinker_out = mine.astype(jnp.bfloat16)
    order = jnp.argsort(talker_slot[0], stable=True)
    sorted_out = thinker_out[order]
    talker_in = lax.psum_scatter(
        jnp.dot(sorted_out, w_proj, preferred_element_type=jnp.float32),
        "mp",
        scatter_dimension=0,
        tiled=True,
    )
    talker_kv, talker_ctx = talker_step(
        talker_in, talker_gain, full_query, full_key, full_value, kv_len, kv_cache
    )
    return (thinker_out, talker_kv, talker_ctx)


PLANE = ("section", "rows")
GROUP = ("mp", "section", "rows")


def over_core(x):
    return lax.ppermute(x, "rows", [(0, 1), (1, 0)])


def over_section(x):
    return lax.ppermute(x, "section", [(0, 1), (1, 0)])


def over_plane(x, e):
    return lax.ppermute(x, PLANE, [(b, b ^ e) for b in range(4)])


def over_groups(x):
    return lax.ppermute(x, "groups", [(0, 1), (1, 0)])


def after(x, *others):
    return lax.optimization_barrier((x, *others))[0]


def four_planes(
    thinker_act,
    w_think,
    w_proj,
    talker_gain,
    w_query,
    w_key,
    w_value,
    talker_slot,
    kv_len,
    kv_cache,
):
    planes = 4
    owned = kv_cache.shape[0]
    g, m, c = lax.axis_index("groups"), lax.axis_index("mp"), lax.axis_index(PLANE)
    block, turn = c.reshape(1), g.reshape(1)
    slots = talker_slot[0]

    across, peer = over_section(thinker_act), over_core(thinker_act)
    peer_slots = over_core(talker_slot)
    near = down([thinker_act, peer], [talker_slot, peer_slots], w_think, owned)
    near_terms = lax.all_to_all(near, "mp", 0, 0)
    mine = jnp.concatenate([w_query, w_key, w_value], axis=1)

    half = w_proj.shape[0] // 2
    plane_w = lax.dynamic_slice_in_dim(after(w_proj, peer), g * half, half, axis=0)
    two = lax.ppermute(plane_w, GROUP, [(b * 4 + b, (b ^ 2) * 4 + b) for b in range(4)])
    one = lax.ppermute(plane_w, GROUP, [(b * 4 + b, (b ^ 1) * 4 + b) for b in range(4)])

    across, near_terms, mine, plane_w, one, two = lax.optimization_barrier(
        (across, near_terms, mine, plane_w, one, two)
    )
    far_slots = [over_plane(talker_slot, e) for e in (2, 3)]
    far = down([across, over_core(across)], far_slots, w_think, owned)
    far_terms = lax.all_to_all(far, "mp", 0, 0)
    three = lax.ppermute(two, GROUP, [((b ^ 2) * 4 + b, (b ^ 3) * 4 + b) for b in range(4)])
    three = after(three, far)
    mine_w = jnp.where(m == c ^ 1, one, jnp.where(m == c ^ 3, three, two))
    mine_w = jnp.where(m == c, plane_w, mine_w)
    block_w = (mine_w, over_groups(mine_w))
    other = over_section(after(mine, far))

    own, next_core = finish(turn, after(near_terms, far), block_w, 2)
    made, last = finish(turn, after(far_terms, own), block_w, 2)
    pieces = [own, over_core(next_core), over_plane(made, 2), over_plane(last, 3)]
    other = after(other, made)
    weights = [mine, over_core(mine), other, over_core(other)]

    home = lax.all_to_all(collect(block, pieces), "mp", 0, 0)
    new_kv, ctx = talker(block, pieces, talker_gain, weights, kv_len, kv_cache)
    home = after(home, ctx)
    pick = (slots[:, None] == jnp.arange(planes * owned)[None, :]).astype(jnp.bfloat16)
    thinker_out = jnp.dot(
        pick, home.reshape(planes * owned, -1), preferred_element_type=jnp.float32
    )
    return (thinker_out.astype(jnp.bfloat16), new_kv, ctx)


def solution(mesh):
    in_specs = (
        P(("groups", "section", "rows"), "mp"),
        P("mp", ("section", "rows")),
        P("mp", None),
        P(),
        P(None, ("section", "rows")),
        P(None, ("section", "rows")),
        P(None, ("section", "rows")),
        P(("groups", "section", "rows"), None),
        P(("groups", "mp", "section", "rows")),
        P(("groups", "mp", "section", "rows"), None, None),
    )
    out_specs = (
        P(("groups", "section", "rows"), "mp"),
        P(("groups", "mp", "section", "rows"), None),
        P(("groups", "mp", "section", "rows"), None),
    )
    sizes = tuple(mesh.shape[a] for a in ("groups", "section", "rows", "mp"))
    shards = four_planes if sizes == (2, 2, 2, 4) else any_mesh
    return jax.shard_map(shards, mesh=mesh, in_specs=in_specs, out_specs=out_specs, check_vma=False)
```

```python
import functools

import jax
import jax.numpy as jnp
from jax import lax
from jax.experimental import pallas as pl
from jax.experimental.pallas import tpu as pltpu
from jax.sharding import PartitionSpec as P

HEAD_DIM = 128
ROW_STEP = 8
LANES = 128
PAGES = 2
SHORT = pl.CostEstimate(flops=1, bytes_accessed=1, transcendentals=0)
MOST_VMEM = 56 * 1024 * 1024


def down_kernel(owned, cuts, groups, *refs):
    slots, xs, refs = refs[:groups], refs[groups : 2 * groups], refs[2 * groups :]
    w, out, x_all, w_all, acc, x_sem, w_sem = refs
    n = xs[0].shape[0]
    loads = []
    for s, (lo, hi) in enumerate(cuts):
        deep = pl.ds(lo, hi - lo)
        copies = [pltpu.make_async_copy(w.at[deep], w_all.at[deep], w_sem.at[s])]
        for i in range(groups):
            copies.append(
                pltpu.make_async_copy(
                    xs[i].at[:, deep], x_all.at[pl.ds(i * n, n), deep], x_sem.at[s, i]
                )
            )
        for copy in copies:
            copy.start()
        loads.append(copies)
    for s, (lo, hi) in enumerate(cuts):
        for copy in loads[s]:
            copy.wait()
        part = jnp.dot(x_all[:, lo:hi], w_all[lo:hi, :], preferred_element_type=jnp.float32)
        acc[...] = part if s == 0 else acc[...] + part
    place = lax.broadcasted_iota(jnp.int32, (n, n), 0)
    for i in range(groups):
        pick = (place == slots[i][...]).astype(jnp.float32).astype(jnp.bfloat16)
        sums = acc[i * n : (i + 1) * n, :].astype(jnp.bfloat16)
        ordered = jnp.dot(pick, sums, preferred_element_type=jnp.float32).astype(out.dtype)
        for p in range(n // owned):
            out[p, i * owned : (i + 1) * owned, :] = ordered[p * owned : (p + 1) * owned, :]


def down(xs, slots, w, owned):
    depth, columns = w.shape
    groups, n = len(xs), xs[0].shape[0]
    tiles, parts = depth // LANES, 6
    ends = [LANES * (tiles * i // parts) for i in range(parts)] + [depth]
    anywhere = pl.BlockSpec(memory_space=pl.ANY)
    vmem = pl.BlockSpec(memory_space=pltpu.VMEM)
    return pl.pallas_call(
        functools.partial(down_kernel, owned, list(zip(ends[:-1], ends[1:])), groups),
        out_shape=jax.ShapeDtypeStruct((n // owned, groups * owned, columns), jnp.bfloat16),
        in_specs=[vmem] * groups + [anywhere] * (groups + 1),
        out_specs=vmem,
        scratch_shapes=[
            pltpu.VMEM((groups * n, depth), jnp.bfloat16),
            pltpu.VMEM((depth, columns), jnp.bfloat16),
            pltpu.VMEM((groups * n, columns), jnp.float32),
            pltpu.SemaphoreType.DMA((parts, groups)),
            pltpu.SemaphoreType.DMA((parts,)),
        ],
        cost_estimate=SHORT,
        compiler_params=pltpu.CompilerParams(vmem_limit_bytes=MOST_VMEM),
    )(*slots, *xs, w)


def add_kernel(odd_ref, terms, even_out, odd_out):
    total = terms[0].astype(jnp.float32)
    for k in range(1, terms.shape[0]):
        total = total + terms[k].astype(jnp.float32)
    n = even_out.shape[0]
    first, second = total[:n].astype(jnp.bfloat16), total[n:].astype(jnp.bfloat16)
    odd = odd_ref[0] != 0
    even_out[...] = jnp.where(odd, second, first)
    odd_out[...] = jnp.where(odd, first, second)


def add(odd, terms):
    _, rows, columns = terms.shape
    part = jax.ShapeDtypeStruct((rows // 2, columns), jnp.bfloat16)
    vmem = pl.BlockSpec(memory_space=pltpu.VMEM)
    return pl.pallas_call(
        add_kernel,
        out_shape=(part, part),
        in_specs=[pl.BlockSpec(memory_space=pltpu.SMEM), vmem],
        out_specs=(vmem, vmem),
        cost_estimate=SHORT,
        compiler_params=pltpu.CompilerParams(vmem_limit_bytes=16 * 1024 * 1024),
    )(odd, terms)


def project_kernel(block_ref, w, *refs):
    planes = (len(refs) - 1) // 3
    near, far, home, outs = refs[:planes], refs[planes : 2 * planes], refs[2 * planes], refs[-planes:]
    for k in range(planes):
        home[k ^ block_ref[0]] = near[k][...] + far[k][...]
    for d in range(planes):
        made = jnp.dot(home[d], w[...], preferred_element_type=jnp.float32)
        outs[d][...] = made.astype(jnp.bfloat16)


def project(block, w_proj, near, far):
    planes = len(near)
    rows, columns = near[0].shape
    vmem = pl.BlockSpec(memory_space=pltpu.VMEM)
    made = jax.ShapeDtypeStruct((rows, w_proj.shape[1]), jnp.bfloat16)
    return pl.pallas_call(
        project_kernel,
        out_shape=(jax.ShapeDtypeStruct((planes, rows, columns), jnp.bfloat16), *[made] * planes),
        in_specs=[pl.BlockSpec(memory_space=pltpu.SMEM)] + [vmem] * (1 + 2 * planes),
        out_specs=(vmem,) * (1 + planes),
        cost_estimate=SHORT,
        compiler_params=pltpu.CompilerParams(vmem_limit_bytes=16 * 1024 * 1024),
    )(block, w_proj, *near, *far)


def page_copies(len_ref, kv_hbm, kv_ref, sem, r):
    page = kv_ref.shape[1] // PAGES
    out = []
    for p in range(PAGES):
        at = pl.ds(p * page, page)
        copy = pltpu.make_async_copy(kv_hbm.at[r, at], kv_ref.at[r, at], sem.at[r, p])
        out.append((copy, len_ref[r] > p * page))
    return out


def talker_kernel(blocks, block_ref, len_ref, gain, *refs):
    w_hbm, refs = refs[:blocks], refs[blocks:]
    terms, refs = refs[:-10], refs[-10:]
    kv_hbm, new_kv, out_ref, kv_ref, sem, w_ref, w_sem, qkv, spreads, gathereds = refs
    rows, cached, kv_width = kv_ref.shape
    width = kv_width // 2
    page = cached // PAGES
    heads = out_ref.shape[1] // HEAD_DIM
    group = heads // blocks
    slot = LANES // ROW_STEP
    sets = spreads.shape[0]
    key, value = group * HEAD_DIM, (group + 1) * HEAD_DIM
    inv = 1.0 / HEAD_DIM**0.5

    w_copies = [
        pltpu.make_async_copy(w_hbm[e], w_ref.at[e], w_sem.at[e]) for e in range(blocks)
    ]
    for copy in w_copies:
        copy.start()

    @pl.loop(0, rows)
    def _(r):
        for p, (copy, needed) in enumerate(page_copies(len_ref, kv_hbm, kv_ref, sem, r)):
            if p == 0:
                copy.start()
            else:
                pl.when(needed)(copy.start)

    total = terms[0][...].astype(jnp.float32)
    for term in terms[1:]:
        total = total + term[...].astype(jnp.float32)
    scale = lax.rsqrt(jnp.mean(total * total, axis=1, keepdims=True) + 1e-06)
    normed = (total * scale * gain[...]).astype(jnp.bfloat16)
    for e in range(blocks):
        w_copies[e].wait()
        made = jnp.dot(normed, w_ref[e], preferred_element_type=jnp.float32)
        qkv[e ^ block_ref[0]] = made.astype(jnp.bfloat16).astype(jnp.float32)
    for g in range(blocks):
        for place, start in ((g, key), (blocks + g, value)):
            new_kv[:, place * HEAD_DIM : (place + 1) * HEAD_DIM] = qkv[
                g, :, start : start + HEAD_DIM
            ].astype(jnp.bfloat16)

    spreads[...] = jnp.zeros_like(spreads)
    lane = lax.broadcasted_iota(jnp.int32, (HEAD_DIM, LANES), 1)
    lane_row, lane_block = lane // slot, lane % slot // group
    row_block = lax.broadcasted_iota(jnp.int32, (slot, HEAD_DIM), 0) // group
    own_row = lax.broadcasted_iota(jnp.int32, (ROW_STEP, LANES), 0)

    def scores_of(at, spread):
        here = pl.ds(at, ROW_STEP)
        for h in range(heads):
            g, j = h // group, h % group
            spread[pl.ds(h, ROW_STEP, stride=slot), :] = qkv[
                g, here, j * HEAD_DIM : (j + 1) * HEAD_DIM
            ]
        query = spread[...].T
        by_block = [
            jnp.where(lane_block == g, query, 0.0).astype(jnp.bfloat16) for g in range(blocks)
        ]
        scores = jnp.zeros((cached, LANES), jnp.float32)
        for r in range(ROW_STEP):
            mine = lane_row == r
            right = jnp.concatenate(
                [jnp.where(mine, q, jnp.zeros_like(q)) for q in by_block], axis=0
            )
            scores = scores + jnp.dot(
                kv_ref[at + r, :, :width], right, preferred_element_type=jnp.float32
            )
        own = jnp.zeros((ROW_STEP, LANES), jnp.float32)
        for g in range(blocks):
            new_key = qkv[g, here, key:value].astype(jnp.bfloat16)
            own = own + jnp.dot(new_key, by_block[g], preferred_element_type=jnp.float32)
        own = jnp.where(own_row == lane_row[:ROW_STEP], own, 0.0)
        return scores * inv, jnp.sum(own, axis=0, keepdims=True) * inv

    def softmax(at, scores, own):
        lens = jnp.zeros((1, LANES), jnp.int32)
        for r in range(ROW_STEP):
            lens = jnp.where(lane_row[:1] == r, len_ref[at + r], lens)
        valid = lax.broadcasted_iota(jnp.int32, scores.shape, 0) < lens
        scores = jnp.where(valid, scores, -jnp.inf)
        top = jnp.maximum(jnp.max(scores, axis=0, keepdims=True), own)
        expo = jnp.where(valid, jnp.exp(scores - top), 0.0)
        own_expo = jnp.exp(own - top)
        total = jnp.sum(expo, axis=0, keepdims=True) + own_expo
        probs = (expo / total).T.astype(jnp.bfloat16)
        own_prob = (own_expo / total).astype(jnp.bfloat16).astype(jnp.float32)
        return probs, jnp.broadcast_to(own_prob, (LANES, LANES)).T

    def context(at, probs, own_prob, gathered):
        here = pl.ds(at, ROW_STEP)
        value_rows = qkv.at[:, here, value:]
        for r in range(ROW_STEP):
            lanes = slice(r * slot, (r + 1) * slot)
            made = jnp.dot(
                probs[lanes], kv_ref[at + r, :, width:], preferred_element_type=jnp.float32
            )
            ctx = jnp.zeros((slot, HEAD_DIM), jnp.float32)
            new = jnp.zeros((slot, HEAD_DIM), jnp.float32)
            for g in range(blocks):
                block = made[:, g * HEAD_DIM : (g + 1) * HEAD_DIM]
                ctx = jnp.where(row_block == g, block, ctx)
                new = jnp.where(row_block == g, value_rows[g, r : r + 1, :], new)
            gathered[lanes, :] = ctx + own_prob[lanes] * new
        for h in range(heads):
            out_ref[here, h * HEAD_DIM : (h + 1) * HEAD_DIM] = gathered[
                pl.ds(h, ROW_STEP, stride=slot), :
            ]

    @pl.loop(0, rows // (sets * ROW_STEP))
    def _(i):
        first = pl.multiple_of(i * sets * ROW_STEP, sets * ROW_STEP)
        for k in range(sets * ROW_STEP):
            r = first + k
            for p, (copy, needed) in enumerate(page_copies(len_ref, kv_hbm, kv_ref, sem, r)):
                if p == 0:
                    copy.wait()
                    continue
                pl.when(needed)(copy.wait)

                @pl.when(jnp.logical_not(needed))
                def _(p=p, r=r):
                    kv_ref[r, p * page : (p + 1) * page, :] = jnp.zeros(
                        (page, kv_width), kv_ref.dtype
                    )

        ats = [pl.multiple_of(first + k * ROW_STEP, ROW_STEP) for k in range(sets)]
        scored = [scores_of(at, spreads.at[k]) for k, at in enumerate(ats)]
        weighed = [softmax(at, *s) for at, s in zip(ats, scored)]
        for k, at in enumerate(ats):
            context(at, *weighed[k], gathereds.at[k])


def talker(block, terms, talker_gain, weights, kv_len, kv_cache):
    rows, cached, kv_width = kv_cache.shape
    wide, columns = weights[0].shape
    blocks = len(weights)
    q_width = blocks * columns - kv_width
    sets = 2
    vmem = pl.BlockSpec(memory_space=pltpu.VMEM)
    smem = pl.BlockSpec(memory_space=pltpu.SMEM)
    return pl.pallas_call(
        functools.partial(talker_kernel, blocks),
        out_shape=(
            jax.ShapeDtypeStruct((rows, kv_width), jnp.bfloat16),
            jax.ShapeDtypeStruct((rows, q_width), jnp.float32),
        ),
        in_specs=[smem, smem, vmem]
        + [pl.BlockSpec(memory_space=pl.ANY)] * blocks
        + [vmem] * len(terms)
        + [pl.BlockSpec(memory_space=pl.ANY)],
        out_specs=(vmem, vmem),
        scratch_shapes=[
            pltpu.VMEM((rows, cached, kv_width), jnp.bfloat16),
            pltpu.SemaphoreType.DMA((rows, PAGES)),
            pltpu.VMEM((blocks, wide, columns), jnp.bfloat16),
            pltpu.SemaphoreType.DMA((blocks,)),
            pltpu.VMEM((blocks, rows, columns), jnp.float32),
            pltpu.VMEM((sets, LANES, HEAD_DIM), jnp.float32),
            pltpu.VMEM((sets, LANES, HEAD_DIM), jnp.float32),
        ],
        cost_estimate=SHORT,
        compiler_params=pltpu.CompilerParams(vmem_limit_bytes=48 * 1024 * 1024),
    )(block, kv_len, talker_gain.reshape(1, wide), *weights, *terms, kv_cache)


def rms_norm(talker_in, talker_gain):
    scale = lax.rsqrt(jnp.mean(talker_in * talker_in, axis=1, keepdims=True) + 1e-06)
    return (talker_in * scale * talker_gain).astype(jnp.bfloat16)


def talker_step(talker_in, talker_gain, w_query, w_key, w_value, kv_len, kv_cache):
    owned = talker_in.shape[0]
    cached = kv_cache.shape[1]
    kv_width = w_key.shape[1]
    head_dim = HEAD_DIM
    kv_heads = kv_width // head_dim
    group = w_query.shape[1] // kv_width
    normed = rms_norm(talker_in, talker_gain)
    query = jnp.dot(normed, w_query, preferred_element_type=jnp.float32).astype(jnp.bfloat16)
    new_key = jnp.dot(normed, w_key, preferred_element_type=jnp.float32).astype(jnp.bfloat16)
    new_value = jnp.dot(normed, w_value, preferred_element_type=jnp.float32).astype(jnp.bfloat16)
    talker_kv = jnp.concatenate([new_key, new_value], axis=1)
    qb = query.reshape(owned, kv_heads, group, head_dim)
    keys = kv_cache[:, :, :kv_width].reshape(owned, cached, kv_heads, head_dim)
    values = kv_cache[:, :, kv_width:].reshape(owned, cached, kv_heads, head_dim)
    nk = new_key.reshape(owned, kv_heads, head_dim)
    nv = new_value.reshape(owned, kv_heads, head_dim)
    inv = 1.0 / head_dim**0.5
    scores = jnp.einsum("rgjd,rpgd->rgjp", qb, keys, preferred_element_type=jnp.float32) * inv
    own = jnp.einsum("rgjd,rgd->rgj", qb, nk, preferred_element_type=jnp.float32) * inv
    valid = (jnp.arange(cached, dtype=jnp.int32)[None, :] < kv_len[:, None])[:, None, None, :]
    scores = jnp.where(valid, scores, -jnp.inf)
    top = jnp.maximum(jnp.max(scores, axis=3), own)
    expo = jnp.where(valid, jnp.exp(scores - top[..., None]), 0.0)
    own_expo = jnp.exp(own - top)
    total = jnp.sum(expo, axis=3) + own_expo
    probs = (expo / total[..., None]).astype(jnp.bfloat16)
    own_prob = (own_expo / total).astype(jnp.bfloat16)
    ctx = jnp.einsum("rgjp,rpgd->rgjd", probs, values, preferred_element_type=jnp.float32)
    ctx = ctx + own_prob.astype(jnp.float32)[..., None] * nv.astype(jnp.float32)[:, :, None, :]
    return (talker_kv, ctx.reshape(owned, w_query.shape[1]))


def any_mesh(
    thinker_act,
    w_think,
    w_proj,
    talker_gain,
    w_query,
    w_key,
    w_value,
    talker_slot,
    kv_len,
    kv_cache,
):
    partial_sums = jnp.dot(
        thinker_act,
        lax.all_gather(w_think, ("section", "rows"), axis=1, tiled=True),
        preferred_element_type=jnp.float32,
    )
    full_query, full_key, full_value = (
        lax.all_gather(w_query, ("section", "rows"), axis=1, tiled=True),
        lax.all_gather(w_key, ("section", "rows"), axis=1, tiled=True),
        lax.all_gather(w_value, ("section", "rows"), axis=1, tiled=True),
    )
    mine = lax.psum_scatter(partial_sums, "mp", scatter_dimension=1, tiled=True)
    thinker_out = mine.astype(jnp.bfloat16)
    order = jnp.argsort(talker_slot[0], stable=True)
    sorted_out = thinker_out[order]
    talker_in = lax.psum_scatter(
        jnp.dot(sorted_out, w_proj, preferred_element_type=jnp.float32),
        "mp",
        scatter_dimension=0,
        tiled=True,
    )
    talker_kv, talker_ctx = talker_step(
        talker_in, talker_gain, full_query, full_key, full_value, kv_len, kv_cache
    )
    return (thinker_out, talker_kv, talker_ctx)


PLANE = ("section", "rows")
GROUP = ("mp", "section", "rows")


def over_core(x):
    return lax.ppermute(x, "rows", [(0, 1), (1, 0)])


def over_section(x):
    return lax.ppermute(x, "section", [(0, 1), (1, 0)])


def over_plane(x, e):
    return lax.ppermute(x, PLANE, [(b, b ^ e) for b in range(4)])


def sent_home(even, odd, upper):
    out = []
    for k in range(4):
        pairs = [
            (p * 4 + c, c * 4 + (c ^ p ^ k))
            for p in range(4)
            for c in range(4)
            if (p ^ k) // 2 == upper
        ]
        out.append(lax.ppermute(odd if k % 2 else even, GROUP, pairs))
    return out


def after(x, *others):
    return lax.optimization_barrier((x, *others))[0]


def four_planes(
    thinker_act,
    w_think,
    w_proj,
    talker_gain,
    w_query,
    w_key,
    w_value,
    talker_slot,
    kv_len,
    kv_cache,
):
    planes = 4
    owned = kv_cache.shape[0]
    m, c = lax.axis_index("mp"), lax.axis_index(PLANE)
    block, odd = c.reshape(1), (m & 1).reshape(1)
    slots = talker_slot[0]

    across, peer = over_section(thinker_act), over_core(thinker_act)
    near = down([thinker_act, peer], [talker_slot, over_core(talker_slot)], w_think, owned)
    near_terms = lax.all_to_all(near, "mp", 0, 0)
    mine = jnp.concatenate([w_query, w_key, w_value], axis=1)

    across, near_terms, mine = lax.optimization_barrier((across, near_terms, mine))
    far_slots = [over_plane(talker_slot, e) for e in (2, 3)]
    far = down([across, over_core(across)], far_slots, w_think, owned)
    far_terms = lax.all_to_all(far, "mp", 0, 0)
    other = over_section(after(mine, far))

    near_home = sent_home(*add(odd, after(near_terms, far)), 0)
    far_home = sent_home(*add(odd, after(far_terms, *near_home)), 1)
    home, *projected = project(block, w_proj, near_home, far_home)
    terms = projected[:1]
    for d in range(1, planes):
        terms.append(lax.ppermute(projected[d], "mp", [(p, p ^ d) for p in range(planes)]))
    other = after(other, *far_home)
    weights = [mine, over_core(mine), other, over_core(other)]
    new_kv, ctx = talker(block, terms, talker_gain, weights, kv_len, kv_cache)

    place = (jnp.arange(planes)[:, None] ^ m) * owned + jnp.arange(owned)[None, :]
    pick = (slots[:, None] == place.reshape(-1)[None, :]).astype(jnp.bfloat16)
    thinker_out = jnp.dot(
        pick, home.reshape(planes * owned, -1), preferred_element_type=jnp.float32
    )
    return (thinker_out.astype(jnp.bfloat16), new_kv, ctx)


def solution(mesh):
    in_specs = (
        P(("groups", "section", "rows"), "mp"),
        P("mp", ("section", "rows")),
        P("mp", None),
        P(),
        P(None, ("section", "rows")),
        P(None, ("section", "rows")),
        P(None, ("section", "rows")),
        P(("groups", "section", "rows"), None),
        P(("groups", "mp", "section", "rows")),
        P(("groups", "mp", "section", "rows"), None, None),
    )
    out_specs = (
        P(("groups", "section", "rows"), "mp"),
        P(("groups", "mp", "section", "rows"), None),
        P(("groups", "mp", "section", "rows"), None),
    )
    sizes = tuple(mesh.shape[a] for a in ("groups", "section", "rows", "mp"))
    shards = four_planes if sizes == (2, 2, 2, 4) else any_mesh
    return jax.shard_map(shards, mesh=mesh, in_specs=in_specs, out_specs=out_specs, check_vma=False)
```

```python
import functools

import jax
import jax.numpy as jnp
from jax import lax
from jax.experimental import pallas as pl
from jax.experimental.pallas import tpu as pltpu
from jax.sharding import PartitionSpec as P

HEAD_DIM = 128
ROW_STEP = 8
LANES = 128
PAGES = 2
SHORT = pl.CostEstimate(flops=1, bytes_accessed=1, transcendentals=0)
MOST_VMEM = 56 * 1024 * 1024


def down_kernel(owned, cuts, groups, *refs):
    slots, xs, refs = refs[:groups], refs[groups : 2 * groups], refs[2 * groups :]
    w, out, x_all, w_all, acc, x_sem, w_sem = refs
    n = xs[0].shape[0]
    loads = []
    for s, (lo, hi) in enumerate(cuts):
        deep = pl.ds(lo, hi - lo)
        copies = [pltpu.make_async_copy(w.at[deep], w_all.at[deep], w_sem.at[s])]
        for i in range(groups):
            copies.append(
                pltpu.make_async_copy(
                    xs[i].at[:, deep], x_all.at[pl.ds(i * n, n), deep], x_sem.at[s, i]
                )
            )
        for copy in copies:
            copy.start()
        loads.append(copies)
    for s, (lo, hi) in enumerate(cuts):
        for copy in loads[s]:
            copy.wait()
        part = jnp.dot(x_all[:, lo:hi], w_all[lo:hi, :], preferred_element_type=jnp.float32)
        acc[...] = part if s == 0 else acc[...] + part
    place = lax.broadcasted_iota(jnp.int32, (n, n), 0)
    for i in range(groups):
        pick = (place == slots[i][...]).astype(jnp.float32).astype(jnp.bfloat16)
        sums = acc[i * n : (i + 1) * n, :].astype(jnp.bfloat16)
        ordered = jnp.dot(pick, sums, preferred_element_type=jnp.float32).astype(out.dtype)
        for p in range(n // owned):
            out[p, i * owned : (i + 1) * owned, :] = ordered[p * owned : (p + 1) * owned, :]


def down(xs, slots, w, owned):
    depth, columns = w.shape
    groups, n = len(xs), xs[0].shape[0]
    tiles, parts = depth // LANES, 6
    ends = [LANES * (tiles * i // parts) for i in range(parts)] + [depth]
    anywhere = pl.BlockSpec(memory_space=pl.ANY)
    vmem = pl.BlockSpec(memory_space=pltpu.VMEM)
    return pl.pallas_call(
        functools.partial(down_kernel, owned, list(zip(ends[:-1], ends[1:])), groups),
        out_shape=jax.ShapeDtypeStruct((n // owned, groups * owned, columns), jnp.bfloat16),
        in_specs=[vmem] * groups + [anywhere] * (groups - 1) + [vmem, anywhere],
        out_specs=vmem,
        scratch_shapes=[
            pltpu.VMEM((groups * n, depth), jnp.bfloat16),
            pltpu.VMEM((depth, columns), jnp.bfloat16),
            pltpu.VMEM((groups * n, columns), jnp.float32),
            pltpu.SemaphoreType.DMA((parts, groups)),
            pltpu.SemaphoreType.DMA((parts,)),
        ],
        cost_estimate=SHORT,
        compiler_params=pltpu.CompilerParams(vmem_limit_bytes=MOST_VMEM),
    )(*slots, *xs, w)


def add_kernel(terms, out):
    total = terms[0].astype(jnp.float32)
    for k in range(1, terms.shape[0]):
        total = total + terms[k].astype(jnp.float32)
    out[...] = total.astype(jnp.bfloat16)


def add(terms):
    vmem = pl.BlockSpec(memory_space=pltpu.VMEM)
    return pl.pallas_call(
        add_kernel,
        out_shape=jax.ShapeDtypeStruct(terms.shape[1:], jnp.bfloat16),
        in_specs=[vmem],
        out_specs=vmem,
        cost_estimate=SHORT,
        compiler_params=pltpu.CompilerParams(vmem_limit_bytes=16 * 1024 * 1024),
    )(terms)


def add_and_deal_kernel(plane_ref, near, terms, *refs):
    outs, sums = refs[:-1], refs[-1]
    total = terms[0].astype(jnp.float32)
    for k in range(1, terms.shape[0]):
        total = total + terms[k].astype(jnp.float32)
    rows = sums.shape[1]
    half = len(outs) // 2
    for e in range(half):
        sums[e] = near[e * rows : (e + 1) * rows, :]
        sums[half + e] = total[e * rows : (e + 1) * rows].astype(jnp.bfloat16)
    for k, out in enumerate(outs):
        out[...] = sums[plane_ref[0] ^ k]


def add_and_deal(plane, near, terms):
    rows, columns = near.shape
    blocks = 4
    part = jax.ShapeDtypeStruct((2 * rows // blocks, columns), jnp.bfloat16)
    vmem = pl.BlockSpec(memory_space=pltpu.VMEM)
    return pl.pallas_call(
        add_and_deal_kernel,
        out_shape=(part,) * blocks,
        in_specs=[pl.BlockSpec(memory_space=pltpu.SMEM), vmem, vmem],
        out_specs=(vmem,) * blocks,
        scratch_shapes=[pltpu.VMEM((blocks, *part.shape), jnp.bfloat16)],
        cost_estimate=SHORT,
        compiler_params=pltpu.CompilerParams(vmem_limit_bytes=16 * 1024 * 1024),
    )(plane, near, terms)


def project_kernel(block_ref, w_hbm, *refs):
    planes = (len(refs) - 4) // 2
    came, home, outs = refs[:planes], refs[planes], refs[planes + 1 : 2 * planes + 1]
    w, sem, w_sem = refs[-3:]
    copies = [
        pltpu.make_async_copy(came[k], home.at[k ^ block_ref[0]], sem.at[k])
        for k in range(planes)
    ]
    copies.append(pltpu.make_async_copy(w_hbm, w, w_sem))
    for copy in copies:
        copy.start()
    for copy in copies:
        copy.wait()
    for d in range(planes):
        made = jnp.dot(home[d], w[...], preferred_element_type=jnp.float32)
        outs[d][...] = made.astype(jnp.bfloat16)


def project(block, w_proj, came):
    planes = len(came)
    rows, columns = came[0].shape
    vmem = pl.BlockSpec(memory_space=pltpu.VMEM)
    made = jax.ShapeDtypeStruct((rows, w_proj.shape[1]), jnp.bfloat16)
    return pl.pallas_call(
        project_kernel,
        out_shape=(jax.ShapeDtypeStruct((planes, rows, columns), jnp.bfloat16), *[made] * planes),
        in_specs=[pl.BlockSpec(memory_space=pltpu.SMEM)]
        + [pl.BlockSpec(memory_space=pl.ANY)] * (1 + planes),
        out_specs=(vmem,) * (1 + planes),
        scratch_shapes=[
            pltpu.VMEM(w_proj.shape, w_proj.dtype),
            pltpu.SemaphoreType.DMA((planes,)),
            pltpu.SemaphoreType.DMA,
        ],
        cost_estimate=SHORT,
        compiler_params=pltpu.CompilerParams(vmem_limit_bytes=16 * 1024 * 1024),
    )(block, w_proj, *came)


def page_copies(len_ref, kv_hbm, kv_ref, sem, r):
    page = kv_ref.shape[1] // PAGES
    out = []
    for p in range(PAGES):
        at = pl.ds(p * page, page)
        copy = pltpu.make_async_copy(kv_hbm.at[r, at], kv_ref.at[r, at], sem.at[r, p])
        out.append((copy, len_ref[r] > p * page))
    return out


def talker_kernel(blocks, block_ref, len_ref, gain, *refs):
    w_hbm, refs = refs[:blocks], refs[blocks:]
    terms, refs = refs[:-10], refs[-10:]
    kv_hbm, new_kv, out_ref, kv_ref, sem, w_ref, w_sem, qkv, spreads, gathereds = refs
    rows, cached, kv_width = kv_ref.shape
    width = kv_width // 2
    page = cached // PAGES
    heads = out_ref.shape[1] // HEAD_DIM
    group = heads // blocks
    slot = LANES // ROW_STEP
    sets = spreads.shape[0]
    key, value = group * HEAD_DIM, (group + 1) * HEAD_DIM
    inv = 1.0 / HEAD_DIM**0.5

    w_copies = [
        pltpu.make_async_copy(w_hbm[e], w_ref.at[e], w_sem.at[e]) for e in range(blocks)
    ]
    for copy in w_copies:
        copy.start()

    @pl.loop(0, rows)
    def _(r):
        for p, (copy, needed) in enumerate(page_copies(len_ref, kv_hbm, kv_ref, sem, r)):
            if p == 0:
                copy.start()
            else:
                pl.when(needed)(copy.start)

    total = terms[0][...].astype(jnp.float32)
    for term in terms[1:]:
        total = total + term[...].astype(jnp.float32)
    scale = lax.rsqrt(jnp.mean(total * total, axis=1, keepdims=True) + 1e-06)
    normed = (total * scale * gain[...]).astype(jnp.bfloat16)
    for e in range(blocks):
        w_copies[e].wait()
        made = jnp.dot(normed, w_ref[e], preferred_element_type=jnp.float32)
        qkv[e ^ block_ref[0]] = made.astype(jnp.bfloat16).astype(jnp.float32)
    for g in range(blocks):
        for place, start in ((g, key), (blocks + g, value)):
            new_kv[:, place * HEAD_DIM : (place + 1) * HEAD_DIM] = qkv[
                g, :, start : start + HEAD_DIM
            ].astype(jnp.bfloat16)

    spreads[...] = jnp.zeros_like(spreads)
    lane = lax.broadcasted_iota(jnp.int32, (HEAD_DIM, LANES), 1)
    lane_row, lane_block = lane // slot, lane % slot // group
    row_block = lax.broadcasted_iota(jnp.int32, (slot, HEAD_DIM), 0) // group
    own_row = lax.broadcasted_iota(jnp.int32, (ROW_STEP, LANES), 0)

    def scores_of(at, spread):
        here = pl.ds(at, ROW_STEP)
        for h in range(heads):
            g, j = h // group, h % group
            spread[pl.ds(h, ROW_STEP, stride=slot), :] = qkv[
                g, here, j * HEAD_DIM : (j + 1) * HEAD_DIM
            ]
        query = spread[...].T
        by_block = [
            jnp.where(lane_block == g, query, 0.0).astype(jnp.bfloat16) for g in range(blocks)
        ]
        scores = jnp.zeros((cached, LANES), jnp.float32)
        for r in range(ROW_STEP):
            mine = lane_row == r
            right = jnp.concatenate(
                [jnp.where(mine, q, jnp.zeros_like(q)) for q in by_block], axis=0
            )
            scores = scores + jnp.dot(
                kv_ref[at + r, :, :width], right, preferred_element_type=jnp.float32
            )
        own = jnp.zeros((ROW_STEP, LANES), jnp.float32)
        for g in range(blocks):
            new_key = qkv[g, here, key:value].astype(jnp.bfloat16)
            own = own + jnp.dot(new_key, by_block[g], preferred_element_type=jnp.float32)
        own = jnp.where(own_row == lane_row[:ROW_STEP], own, 0.0)
        return scores * inv, jnp.sum(own, axis=0, keepdims=True) * inv

    def softmax(at, scores, own):
        lens = jnp.zeros((1, LANES), jnp.int32)
        for r in range(ROW_STEP):
            lens = jnp.where(lane_row[:1] == r, len_ref[at + r], lens)
        valid = lax.broadcasted_iota(jnp.int32, scores.shape, 0) < lens
        scores = jnp.where(valid, scores, -jnp.inf)
        top = jnp.maximum(jnp.max(scores, axis=0, keepdims=True), own)
        expo = jnp.where(valid, jnp.exp(scores - top), 0.0)
        own_expo = jnp.exp(own - top)
        total = jnp.sum(expo, axis=0, keepdims=True) + own_expo
        probs = (expo / total).T.astype(jnp.bfloat16)
        own_prob = (own_expo / total).astype(jnp.bfloat16).astype(jnp.float32)
        return probs, jnp.broadcast_to(own_prob, (LANES, LANES)).T

    def context(at, probs, own_prob, gathered):
        here = pl.ds(at, ROW_STEP)
        value_rows = qkv.at[:, here, value:]
        for r in range(ROW_STEP):
            lanes = slice(r * slot, (r + 1) * slot)
            made = jnp.dot(
                probs[lanes], kv_ref[at + r, :, width:], preferred_element_type=jnp.float32
            )
            ctx = jnp.zeros((slot, HEAD_DIM), jnp.float32)
            new = jnp.zeros((slot, HEAD_DIM), jnp.float32)
            for g in range(blocks):
                block = made[:, g * HEAD_DIM : (g + 1) * HEAD_DIM]
                ctx = jnp.where(row_block == g, block, ctx)
                new = jnp.where(row_block == g, value_rows[g, r : r + 1, :], new)
            gathered[lanes, :] = ctx + own_prob[lanes] * new
        for h in range(heads):
            out_ref[here, h * HEAD_DIM : (h + 1) * HEAD_DIM] = gathered[
                pl.ds(h, ROW_STEP, stride=slot), :
            ]

    @pl.loop(0, rows // (sets * ROW_STEP))
    def _(i):
        first = pl.multiple_of(i * sets * ROW_STEP, sets * ROW_STEP)
        for k in range(sets * ROW_STEP):
            r = first + k
            for p, (copy, needed) in enumerate(page_copies(len_ref, kv_hbm, kv_ref, sem, r)):
                if p == 0:
                    copy.wait()
                    continue
                pl.when(needed)(copy.wait)

                @pl.when(jnp.logical_not(needed))
                def _(p=p, r=r):
                    kv_ref[r, p * page : (p + 1) * page, :] = jnp.zeros(
                        (page, kv_width), kv_ref.dtype
                    )

        ats = [pl.multiple_of(first + k * ROW_STEP, ROW_STEP) for k in range(sets)]
        scored = [scores_of(at, spreads.at[k]) for k, at in enumerate(ats)]
        weighed = [softmax(at, *s) for at, s in zip(ats, scored)]
        for k, at in enumerate(ats):
            context(at, *weighed[k], gathereds.at[k])


def talker(block, terms, talker_gain, weights, kv_len, kv_cache):
    rows, cached, kv_width = kv_cache.shape
    wide, columns = weights[0].shape
    blocks = len(weights)
    q_width = blocks * columns - kv_width
    sets = 2
    vmem = pl.BlockSpec(memory_space=pltpu.VMEM)
    smem = pl.BlockSpec(memory_space=pltpu.SMEM)
    return pl.pallas_call(
        functools.partial(talker_kernel, blocks),
        out_shape=(
            jax.ShapeDtypeStruct((rows, kv_width), jnp.bfloat16),
            jax.ShapeDtypeStruct((rows, q_width), jnp.float32),
        ),
        in_specs=[smem, smem, vmem]
        + [pl.BlockSpec(memory_space=pl.ANY)] * blocks
        + [vmem] * len(terms)
        + [pl.BlockSpec(memory_space=pl.ANY)],
        out_specs=(vmem, vmem),
        scratch_shapes=[
            pltpu.VMEM((rows, cached, kv_width), jnp.bfloat16),
            pltpu.SemaphoreType.DMA((rows, PAGES)),
            pltpu.VMEM((blocks, wide, columns), jnp.bfloat16),
            pltpu.SemaphoreType.DMA((blocks,)),
            pltpu.VMEM((blocks, rows, columns), jnp.float32),
            pltpu.VMEM((sets, LANES, HEAD_DIM), jnp.float32),
            pltpu.VMEM((sets, LANES, HEAD_DIM), jnp.float32),
        ],
        cost_estimate=SHORT,
        compiler_params=pltpu.CompilerParams(vmem_limit_bytes=48 * 1024 * 1024),
    )(block, kv_len, talker_gain.reshape(1, wide), *weights, *terms, kv_cache)


def rms_norm(talker_in, talker_gain):
    scale = lax.rsqrt(jnp.mean(talker_in * talker_in, axis=1, keepdims=True) + 1e-06)
    return (talker_in * scale * talker_gain).astype(jnp.bfloat16)


def talker_step(talker_in, talker_gain, w_query, w_key, w_value, kv_len, kv_cache):
    owned = talker_in.shape[0]
    cached = kv_cache.shape[1]
    kv_width = w_key.shape[1]
    head_dim = HEAD_DIM
    kv_heads = kv_width // head_dim
    group = w_query.shape[1] // kv_width
    normed = rms_norm(talker_in, talker_gain)
    query = jnp.dot(normed, w_query, preferred_element_type=jnp.float32).astype(jnp.bfloat16)
    new_key = jnp.dot(normed, w_key, preferred_element_type=jnp.float32).astype(jnp.bfloat16)
    new_value = jnp.dot(normed, w_value, preferred_element_type=jnp.float32).astype(jnp.bfloat16)
    talker_kv = jnp.concatenate([new_key, new_value], axis=1)
    qb = query.reshape(owned, kv_heads, group, head_dim)
    keys = kv_cache[:, :, :kv_width].reshape(owned, cached, kv_heads, head_dim)
    values = kv_cache[:, :, kv_width:].reshape(owned, cached, kv_heads, head_dim)
    nk = new_key.reshape(owned, kv_heads, head_dim)
    nv = new_value.reshape(owned, kv_heads, head_dim)
    inv = 1.0 / head_dim**0.5
    scores = jnp.einsum("rgjd,rpgd->rgjp", qb, keys, preferred_element_type=jnp.float32) * inv
    own = jnp.einsum("rgjd,rgd->rgj", qb, nk, preferred_element_type=jnp.float32) * inv
    valid = (jnp.arange(cached, dtype=jnp.int32)[None, :] < kv_len[:, None])[:, None, None, :]
    scores = jnp.where(valid, scores, -jnp.inf)
    top = jnp.maximum(jnp.max(scores, axis=3), own)
    expo = jnp.where(valid, jnp.exp(scores - top[..., None]), 0.0)
    own_expo = jnp.exp(own - top)
    total = jnp.sum(expo, axis=3) + own_expo
    probs = (expo / total[..., None]).astype(jnp.bfloat16)
    own_prob = (own_expo / total).astype(jnp.bfloat16)
    ctx = jnp.einsum("rgjp,rpgd->rgjd", probs, values, preferred_element_type=jnp.float32)
    ctx = ctx + own_prob.astype(jnp.float32)[..., None] * nv.astype(jnp.float32)[:, :, None, :]
    return (talker_kv, ctx.reshape(owned, w_query.shape[1]))


def any_mesh(
    thinker_act,
    w_think,
    w_proj,
    talker_gain,
    w_query,
    w_key,
    w_value,
    talker_slot,
    kv_len,
    kv_cache,
):
    partial_sums = jnp.dot(
        thinker_act,
        lax.all_gather(w_think, ("section", "rows"), axis=1, tiled=True),
        preferred_element_type=jnp.float32,
    )
    full_query, full_key, full_value = (
        lax.all_gather(w_query, ("section", "rows"), axis=1, tiled=True),
        lax.all_gather(w_key, ("section", "rows"), axis=1, tiled=True),
        lax.all_gather(w_value, ("section", "rows"), axis=1, tiled=True),
    )
    mine = lax.psum_scatter(partial_sums, "mp", scatter_dimension=1, tiled=True)
    thinker_out = mine.astype(jnp.bfloat16)
    order = jnp.argsort(talker_slot[0], stable=True)
    sorted_out = thinker_out[order]
    talker_in = lax.psum_scatter(
        jnp.dot(sorted_out, w_proj, preferred_element_type=jnp.float32),
        "mp",
        scatter_dimension=0,
        tiled=True,
    )
    talker_kv, talker_ctx = talker_step(
        talker_in, talker_gain, full_query, full_key, full_value, kv_len, kv_cache
    )
    return (thinker_out, talker_kv, talker_ctx)


PLANE = ("section", "rows")
GROUP = ("mp", "section", "rows")


def over_core(x):
    return lax.ppermute(x, "rows", [(0, 1), (1, 0)])


def over_section(x):
    return lax.ppermute(x, "section", [(0, 1), (1, 0)])


def over_plane(x, e):
    return lax.ppermute(x, PLANE, [(b, b ^ e) for b in range(4)])


def over_groups(x):
    return lax.ppermute(x, "groups", [(0, 1), (1, 0)])


def after(x, *others):
    return lax.optimization_barrier((x, *others))[0]


def four_planes(
    thinker_act,
    w_think,
    w_proj,
    talker_gain,
    w_query,
    w_key,
    w_value,
    talker_slot,
    kv_len,
    kv_cache,
):
    planes = 4
    owned = kv_cache.shape[0]
    g, m, c = lax.axis_index("groups"), lax.axis_index("mp"), lax.axis_index(PLANE)
    block, plane = c.reshape(1), m.reshape(1)
    slots = talker_slot[0]

    across, peer = over_section(thinker_act), over_core(thinker_act)
    peer_slots = over_core(talker_slot)
    far_slots = over_section(jnp.concatenate([talker_slot, peer_slots], axis=0))
    near = down([thinker_act, peer], [talker_slot, peer_slots], w_think, owned)
    near_terms = lax.all_to_all(near, "mp", 0, 0)
    mine = jnp.concatenate([w_query, w_key, w_value], axis=1)
    half = mine.shape[0] // 2
    my_half = lax.dynamic_slice_in_dim(mine, g * half, half, axis=0)

    across, near_terms, far_slots, mine, my_half = lax.optimization_barrier(
        (across, near_terms, far_slots, mine, my_half)
    )
    far = down([across, over_core(across)], [far_slots[:1], far_slots[1:]], w_think, owned)
    far_terms = lax.all_to_all(far, "mp", 0, 0)

    my_half = over_section(after(my_half, far))
    near_sums = add(after(near_terms, far))

    dealt = add_and_deal(plane, near_sums, far_terms)
    came = [
        lax.ppermute(x, GROUP, [(p * 4 + b, b * 4 + (b ^ p ^ k)) for p in range(4) for b in range(4)])
        for k, x in enumerate(dealt)
    ]
    my_half = after(my_half, near_sums)
    came[0], other_half = lax.optimization_barrier((came[0], over_groups(my_half)))
    home, *projected = project(block, w_proj, came)
    terms = projected[:1]
    for d in range(1, planes):
        terms.append(lax.ppermute(projected[d], "mp", [(p, p ^ d) for p in range(planes)]))
    halves = [my_half, after(other_half, projected[0])]
    other = jnp.concatenate(
        [jnp.where(g == 0, *halves), jnp.where(g == 0, *halves[::-1])], axis=0
    )
    weights = [mine, over_core(mine), other, over_core(other)]
    new_kv, ctx = talker(block, terms, talker_gain, weights, kv_len, kv_cache)

    place = (jnp.arange(planes)[:, None] ^ m) * owned + jnp.arange(owned)[None, :]
    pick = (slots[:, None] == place.reshape(-1)[None, :]).astype(jnp.bfloat16)
    thinker_out = jnp.dot(
        pick, home.reshape(planes * owned, -1), preferred_element_type=jnp.float32
    )
    return (thinker_out.astype(jnp.bfloat16), new_kv, ctx)


def solution(mesh):
    in_specs = (
        P(("groups", "section", "rows"), "mp"),
        P("mp", ("section", "rows")),
        P("mp", None),
        P(),
        P(None, ("section", "rows")),
        P(None, ("section", "rows")),
        P(None, ("section", "rows")),
        P(("groups", "section", "rows"), None),
        P(("groups", "mp", "section", "rows")),
        P(("groups", "mp", "section", "rows"), None, None),
    )
    out_specs = (
        P(("groups", "section", "rows"), "mp"),
        P(("groups", "mp", "section", "rows"), None),
        P(("groups", "mp", "section", "rows"), None),
    )
    sizes = tuple(mesh.shape[a] for a in ("groups", "section", "rows", "mp"))
    shards = four_planes if sizes == (2, 2, 2, 4) else any_mesh
    return jax.shard_map(shards, mesh=mesh, in_specs=in_specs, out_specs=out_specs, check_vma=False)
```

```python
import functools

import jax
import jax.numpy as jnp
from jax import lax
from jax.experimental import pallas as pl
from jax.experimental.pallas import tpu as pltpu
from jax.sharding import PartitionSpec as P

HEAD_DIM = 128
ROW_STEP = 8
LANES = 128
PAGES = 2
SHORT = pl.CostEstimate(flops=1, bytes_accessed=1, transcendentals=0)
MOST_VMEM = 56 * 1024 * 1024


def down_kernel(planes, cuts, groups, *refs):
    xs, (w, out, x_all, w_all, acc, x_sem, w_sem) = refs[:groups], refs[groups:]
    n = xs[0].shape[0]
    loads = []
    for s, (lo, hi) in enumerate(cuts):
        deep = pl.ds(lo, hi - lo)
        copies = [pltpu.make_async_copy(w.at[deep], w_all.at[deep], w_sem.at[s])]
        for i in range(groups):
            copies.append(
                pltpu.make_async_copy(
                    xs[i].at[:, deep], x_all.at[pl.ds(i * n, n), deep], x_sem.at[s, i]
                )
            )
        for copy in copies:
            copy.start()
        loads.append(copies)
    for s, (lo, hi) in enumerate(cuts):
        for copy in loads[s]:
            copy.wait()
        part = jnp.dot(x_all[:, lo:hi], w_all[lo:hi, :], preferred_element_type=jnp.float32)
        acc[...] = part if s == 0 else acc[...] + part
    part = n // planes
    for i in range(groups):
        for p in range(planes):
            at = i * n + p * part
            out[p, i * part : (i + 1) * part, :] = acc[at : at + part, :].astype(out.dtype)


def down(xs, w, planes):
    depth, columns = w.shape
    groups, n = len(xs), xs[0].shape[0]
    tiles, parts = depth // LANES, 6
    ends = [LANES * (tiles * i // parts) for i in range(parts)] + [depth]
    return pl.pallas_call(
        functools.partial(down_kernel, planes, list(zip(ends[:-1], ends[1:])), groups),
        out_shape=jax.ShapeDtypeStruct((planes, groups * n // planes, columns), jnp.bfloat16),
        in_specs=[pl.BlockSpec(memory_space=pl.ANY)] * (groups + 1),
        out_specs=pl.BlockSpec(memory_space=pltpu.VMEM),
        scratch_shapes=[
            pltpu.VMEM((groups * n, depth), jnp.bfloat16),
            pltpu.VMEM((depth, columns), jnp.bfloat16),
            pltpu.VMEM((groups * n, columns), jnp.float32),
            pltpu.SemaphoreType.DMA((parts, groups)),
            pltpu.SemaphoreType.DMA((parts,)),
        ],
        cost_estimate=SHORT,
        compiler_params=pltpu.CompilerParams(vmem_limit_bytes=MOST_VMEM),
    )(*xs, w)


def add_kernel(odd_ref, terms, even_out, odd_out):
    total = terms[0].astype(jnp.float32)
    for k in range(1, terms.shape[0]):
        total = total + terms[k].astype(jnp.float32)
    n = even_out.shape[0]
    first, second = total[:n].astype(jnp.bfloat16), total[n:].astype(jnp.bfloat16)
    odd = odd_ref[0] != 0
    even_out[...] = jnp.where(odd, second, first)
    odd_out[...] = jnp.where(odd, first, second)


def add(odd, terms):
    _, rows, columns = terms.shape
    part = jax.ShapeDtypeStruct((rows // 2, columns), jnp.bfloat16)
    vmem = pl.BlockSpec(memory_space=pltpu.VMEM)
    return pl.pallas_call(
        add_kernel,
        out_shape=(part, part),
        in_specs=[pl.BlockSpec(memory_space=pltpu.SMEM), vmem],
        out_specs=(vmem, vmem),
        cost_estimate=SHORT,
        compiler_params=pltpu.CompilerParams(vmem_limit_bytes=16 * 1024 * 1024),
    )(odd, terms)


def project_kernel(planes, here_ref, slots, w_hbm, *refs):
    came, refs = refs[: 2 * planes], refs[2 * planes :]
    home, outs, (two, w, sem, w_sem) = refs[0], refs[1 : planes + 1], refs[planes + 1 :]
    plane, block = here_ref[0], here_ref[1]
    copies = [pltpu.make_async_copy(w_hbm, w, w_sem)]
    for i in range(2 * planes):
        to = two.at[i // planes, plane ^ block ^ (i % planes)]
        copies.append(pltpu.make_async_copy(came[i], to, sem.at[i]))
    for copy in copies:
        copy.start()
    for copy in copies:
        copy.wait()
    rows = two.shape[2]
    home[...] = (two[0] + two[1]).reshape(home.shape)
    n = home.shape[0]
    place = lax.broadcasted_iota(jnp.int32, (n, n), 0)
    place = ((place // rows) ^ plane) * rows + place % rows
    pick = (place == slots[...]).astype(jnp.float32).astype(jnp.bfloat16)
    ordered = jnp.dot(pick, home[...], preferred_element_type=jnp.float32).astype(jnp.bfloat16)
    made = jnp.dot(ordered, w[...], preferred_element_type=jnp.float32).astype(jnp.bfloat16)
    for d in range(planes):
        outs[d][...] = made[d * rows : (d + 1) * rows]


def project(here, slots, w_proj, near, far):
    planes = len(near)
    rows, columns = near[0].shape
    vmem = pl.BlockSpec(memory_space=pltpu.VMEM)
    made = jax.ShapeDtypeStruct((rows, w_proj.shape[1]), jnp.bfloat16)
    return pl.pallas_call(
        functools.partial(project_kernel, planes),
        out_shape=(jax.ShapeDtypeStruct((planes * rows, columns), jnp.bfloat16), *[made] * planes),
        in_specs=[pl.BlockSpec(memory_space=pltpu.SMEM), vmem]
        + [pl.BlockSpec(memory_space=pl.ANY)] * (1 + 2 * planes),
        out_specs=(vmem,) * (1 + planes),
        scratch_shapes=[
            pltpu.VMEM((2, planes, rows, columns), jnp.bfloat16),
            pltpu.VMEM(w_proj.shape, w_proj.dtype),
            pltpu.SemaphoreType.DMA((2 * planes,)),
            pltpu.SemaphoreType.DMA,
        ],
        cost_estimate=SHORT,
        compiler_params=pltpu.CompilerParams(vmem_limit_bytes=16 * 1024 * 1024),
    )(here, slots, w_proj, *near, *far)


def page_copies(len_ref, kv_hbm, kv_ref, sem, r):
    page = kv_ref.shape[1] // PAGES
    out = []
    for p in range(PAGES):
        at = pl.ds(p * page, page)
        copy = pltpu.make_async_copy(kv_hbm.at[r, at], kv_ref.at[r, at], sem.at[r, p])
        out.append((copy, len_ref[r] > p * page))
    return out


def talker_kernel(here_ref, len_ref, gain, *refs):
    w_hbm, terms, refs = refs[:6], refs[6:-10], refs[-10:]
    kv_hbm, new_kv, out_ref, kv_ref, sem, w_ref, w_sem, qkv, spreads, gathereds = refs
    block, turn = here_ref[1], here_ref[2]
    blocks = qkv.shape[0]
    rows, cached, kv_width = kv_ref.shape
    width = kv_width // 2
    page = cached // PAGES
    heads = out_ref.shape[1] // HEAD_DIM
    group = heads // blocks
    slot = LANES // ROW_STEP
    sets = spreads.shape[0]
    key, value = group * HEAD_DIM, (group + 1) * HEAD_DIM
    inv = 1.0 / HEAD_DIM**0.5

    half = w_ref.shape[1] // 2
    w_parts = [(w_ref.at[0],), (w_ref.at[1],)]
    for e in (2, 3):
        w_parts.append(
            [
                w_ref.at[e, pl.ds(pl.multiple_of(which * half, half), half)]
                for which in (turn, 1 - turn)
            ]
        )
    w_copies, at = [], 0
    for parts in w_parts:
        w_copies.append([])
        for part in parts:
            w_copies[-1].append(pltpu.make_async_copy(w_hbm[at], part, w_sem.at[at]))
            w_copies[-1][-1].start()
            at += 1

    @pl.loop(0, rows)
    def _(r):
        for p, (copy, needed) in enumerate(page_copies(len_ref, kv_hbm, kv_ref, sem, r)):
            if p == 0:
                copy.start()
            else:
                pl.when(needed)(copy.start)

    total = terms[0][...].astype(jnp.float32)
    for term in terms[1:]:
        total = total + term[...].astype(jnp.float32)
    scale = lax.rsqrt(jnp.mean(total * total, axis=1, keepdims=True) + 1e-06)
    normed = (total * scale * gain[...]).astype(jnp.bfloat16)
    for e in range(blocks):
        for copy in w_copies[e]:
            copy.wait()
        made = jnp.dot(normed, w_ref[e], preferred_element_type=jnp.float32)
        qkv[e ^ block] = made.astype(jnp.bfloat16).astype(jnp.float32)
    for g in range(blocks):
        for place, start in ((g, key), (blocks + g, value)):
            new_kv[:, place * HEAD_DIM : (place + 1) * HEAD_DIM] = qkv[
                g, :, start : start + HEAD_DIM
            ].astype(jnp.bfloat16)

    spreads[...] = jnp.zeros_like(spreads)
    lane = lax.broadcasted_iota(jnp.int32, (HEAD_DIM, LANES), 1)
    lane_row, lane_block = lane // slot, lane % slot // group
    row_block = lax.broadcasted_iota(jnp.int32, (slot, HEAD_DIM), 0) // group
    own_row = lax.broadcasted_iota(jnp.int32, (ROW_STEP, LANES), 0)

    def scores_of(at, spread):
        here = pl.ds(at, ROW_STEP)
        for h in range(heads):
            g, j = h // group, h % group
            spread[pl.ds(h, ROW_STEP, stride=slot), :] = qkv[
                g, here, j * HEAD_DIM : (j + 1) * HEAD_DIM
            ]
        query = spread[...].T
        by_block = [
            jnp.where(lane_block == g, query, 0.0).astype(jnp.bfloat16) for g in range(blocks)
        ]
        scores = jnp.zeros((cached, LANES), jnp.float32)
        for r in range(ROW_STEP):
            mine = lane_row == r
            right = jnp.concatenate(
                [jnp.where(mine, q, jnp.zeros_like(q)) for q in by_block], axis=0
            )
            scores = scores + jnp.dot(
                kv_ref[at + r, :, :width], right, preferred_element_type=jnp.float32
            )
        own = jnp.zeros((ROW_STEP, LANES), jnp.float32)
        for g in range(blocks):
            new_key = qkv[g, here, key:value].astype(jnp.bfloat16)
            own = own + jnp.dot(new_key, by_block[g], preferred_element_type=jnp.float32)
        own = jnp.where(own_row == lane_row[:ROW_STEP], own, 0.0)
        return scores * inv, jnp.sum(own, axis=0, keepdims=True) * inv

    def softmax(at, scores, own):
        lens = jnp.zeros((1, LANES), jnp.int32)
        for r in range(ROW_STEP):
            lens = jnp.where(lane_row[:1] == r, len_ref[at + r], lens)
        valid = lax.broadcasted_iota(jnp.int32, scores.shape, 0) < lens
        scores = jnp.where(valid, scores, -jnp.inf)
        top = jnp.maximum(jnp.max(scores, axis=0, keepdims=True), own)
        expo = jnp.where(valid, jnp.exp(scores - top), 0.0)
        own_expo = jnp.exp(own - top)
        total = jnp.sum(expo, axis=0, keepdims=True) + own_expo
        probs = (expo / total).T.astype(jnp.bfloat16)
        own_prob = (own_expo / total).astype(jnp.bfloat16).astype(jnp.float32)
        return probs, jnp.broadcast_to(own_prob, (LANES, LANES)).T

    def context(at, probs, own_prob, gathered):
        here = pl.ds(at, ROW_STEP)
        value_rows = qkv.at[:, here, value:]
        for r in range(ROW_STEP):
            lanes = slice(r * slot, (r + 1) * slot)
            made = jnp.dot(
                probs[lanes], kv_ref[at + r, :, width:], preferred_element_type=jnp.float32
            )
            ctx = jnp.zeros((slot, HEAD_DIM), jnp.float32)
            new = jnp.zeros((slot, HEAD_DIM), jnp.float32)
            for g in range(blocks):
                block = made[:, g * HEAD_DIM : (g + 1) * HEAD_DIM]
                ctx = jnp.where(row_block == g, block, ctx)
                new = jnp.where(row_block == g, value_rows[g, r : r + 1, :], new)
            gathered[lanes, :] = ctx + own_prob[lanes] * new
        for h in range(heads):
            out_ref[here, h * HEAD_DIM : (h + 1) * HEAD_DIM] = gathered[
                pl.ds(h, ROW_STEP, stride=slot), :
            ]

    @pl.loop(0, rows // (sets * ROW_STEP))
    def _(i):
        first = pl.multiple_of(i * sets * ROW_STEP, sets * ROW_STEP)
        for k in range(sets * ROW_STEP):
            r = first + k
            for p, (copy, needed) in enumerate(page_copies(len_ref, kv_hbm, kv_ref, sem, r)):
                if p == 0:
                    copy.wait()
                    continue
                pl.when(needed)(copy.wait)

                @pl.when(jnp.logical_not(needed))
                def _(p=p, r=r):
                    kv_ref[r, p * page : (p + 1) * page, :] = jnp.zeros(
                        (page, kv_width), kv_ref.dtype
                    )

        ats = [pl.multiple_of(first + k * ROW_STEP, ROW_STEP) for k in range(sets)]
        scored = [scores_of(at, spreads.at[k]) for k, at in enumerate(ats)]
        weighed = [softmax(at, *s) for at, s in zip(ats, scored)]
        for k, at in enumerate(ats):
            context(at, *weighed[k], gathereds.at[k])


def talker(here, terms, talker_gain, weights, kv_len, kv_cache):
    rows, cached, kv_width = kv_cache.shape
    wide, columns = weights[0].shape
    blocks = 4
    q_width = blocks * columns - kv_width
    sets = 2
    vmem = pl.BlockSpec(memory_space=pltpu.VMEM)
    smem = pl.BlockSpec(memory_space=pltpu.SMEM)
    return pl.pallas_call(
        talker_kernel,
        out_shape=(
            jax.ShapeDtypeStruct((rows, kv_width), jnp.bfloat16),
            jax.ShapeDtypeStruct((rows, q_width), jnp.float32),
        ),
        in_specs=[smem, smem, vmem]
        + [pl.BlockSpec(memory_space=pl.ANY)] * len(weights)
        + [vmem] * len(terms)
        + [pl.BlockSpec(memory_space=pl.ANY)],
        out_specs=(vmem, vmem),
        scratch_shapes=[
            pltpu.VMEM((rows, cached, kv_width), jnp.bfloat16),
            pltpu.SemaphoreType.DMA((rows, PAGES)),
            pltpu.VMEM((blocks, wide, columns), jnp.bfloat16),
            pltpu.SemaphoreType.DMA((len(weights),)),
            pltpu.VMEM((blocks, rows, columns), jnp.float32),
            pltpu.VMEM((sets, LANES, HEAD_DIM), jnp.float32),
            pltpu.VMEM((sets, LANES, HEAD_DIM), jnp.float32),
        ],
        cost_estimate=SHORT,
        compiler_params=pltpu.CompilerParams(vmem_limit_bytes=48 * 1024 * 1024),
    )(here, kv_len, talker_gain.reshape(1, wide), *weights, *terms, kv_cache)


def rms_norm(talker_in, talker_gain):
    scale = lax.rsqrt(jnp.mean(talker_in * talker_in, axis=1, keepdims=True) + 1e-06)
    return (talker_in * scale * talker_gain).astype(jnp.bfloat16)


def talker_step(talker_in, talker_gain, w_query, w_key, w_value, kv_len, kv_cache):
    owned = talker_in.shape[0]
    cached = kv_cache.shape[1]
    kv_width = w_key.shape[1]
    head_dim = HEAD_DIM
    kv_heads = kv_width // head_dim
    group = w_query.shape[1] // kv_width
    normed = rms_norm(talker_in, talker_gain)
    query = jnp.dot(normed, w_query, preferred_element_type=jnp.float32).astype(jnp.bfloat16)
    new_key = jnp.dot(normed, w_key, preferred_element_type=jnp.float32).astype(jnp.bfloat16)
    new_value = jnp.dot(normed, w_value, preferred_element_type=jnp.float32).astype(jnp.bfloat16)
    talker_kv = jnp.concatenate([new_key, new_value], axis=1)
    qb = query.reshape(owned, kv_heads, group, head_dim)
    keys = kv_cache[:, :, :kv_width].reshape(owned, cached, kv_heads, head_dim)
    values = kv_cache[:, :, kv_width:].reshape(owned, cached, kv_heads, head_dim)
    nk = new_key.reshape(owned, kv_heads, head_dim)
    nv = new_value.reshape(owned, kv_heads, head_dim)
    inv = 1.0 / head_dim**0.5
    scores = jnp.einsum("rgjd,rpgd->rgjp", qb, keys, preferred_element_type=jnp.float32) * inv
    own = jnp.einsum("rgjd,rgd->rgj", qb, nk, preferred_element_type=jnp.float32) * inv
    valid = (jnp.arange(cached, dtype=jnp.int32)[None, :] < kv_len[:, None])[:, None, None, :]
    scores = jnp.where(valid, scores, -jnp.inf)
    top = jnp.maximum(jnp.max(scores, axis=3), own)
    expo = jnp.where(valid, jnp.exp(scores - top[..., None]), 0.0)
    own_expo = jnp.exp(own - top)
    total = jnp.sum(expo, axis=3) + own_expo
    probs = (expo / total[..., None]).astype(jnp.bfloat16)
    own_prob = (own_expo / total).astype(jnp.bfloat16)
    ctx = jnp.einsum("rgjp,rpgd->rgjd", probs, values, preferred_element_type=jnp.float32)
    ctx = ctx + own_prob.astype(jnp.float32)[..., None] * nv.astype(jnp.float32)[:, :, None, :]
    return (talker_kv, ctx.reshape(owned, w_query.shape[1]))


def any_mesh(
    thinker_act,
    w_think,
    w_proj,
    talker_gain,
    w_query,
    w_key,
    w_value,
    talker_slot,
    kv_len,
    kv_cache,
):
    partial_sums = jnp.dot(
        thinker_act,
        lax.all_gather(w_think, ("section", "rows"), axis=1, tiled=True),
        preferred_element_type=jnp.float32,
    )
    full_query, full_key, full_value = (
        lax.all_gather(w_query, ("section", "rows"), axis=1, tiled=True),
        lax.all_gather(w_key, ("section", "rows"), axis=1, tiled=True),
        lax.all_gather(w_value, ("section", "rows"), axis=1, tiled=True),
    )
    mine = lax.psum_scatter(partial_sums, "mp", scatter_dimension=1, tiled=True)
    thinker_out = mine.astype(jnp.bfloat16)
    order = jnp.argsort(talker_slot[0], stable=True)
    sorted_out = thinker_out[order]
    talker_in = lax.psum_scatter(
        jnp.dot(sorted_out, w_proj, preferred_element_type=jnp.float32),
        "mp",
        scatter_dimension=0,
        tiled=True,
    )
    talker_kv, talker_ctx = talker_step(
        talker_in, talker_gain, full_query, full_key, full_value, kv_len, kv_cache
    )
    return (thinker_out, talker_kv, talker_ctx)


PLANE = ("section", "rows")
GROUP = ("mp", "section", "rows")


def over_core(x):
    return lax.ppermute(x, "rows", [(0, 1), (1, 0)])


def over_section(x):
    return lax.ppermute(x, "section", [(0, 1), (1, 0)])


def over_plane(x, e):
    return lax.ppermute(x, PLANE, [(b, b ^ e) for b in range(4)])


def over_groups(x):
    return lax.ppermute(x, "groups", [(0, 1), (1, 0)])


def sent_home(even, odd, upper):
    out = []
    for k in range(4):
        pairs = [
            (p * 4 + c, c * 4 + (c ^ p ^ k))
            for p in range(4)
            for c in range(4)
            if (p ^ k) // 2 == upper
        ]
        out.append(lax.ppermute(odd if k % 2 else even, GROUP, pairs))
    return out


def after(x, *others):
    return lax.optimization_barrier((x, *others))[0]


def four_planes(
    thinker_act,
    w_think,
    w_proj,
    talker_gain,
    w_query,
    w_key,
    w_value,
    talker_slot,
    kv_len,
    kv_cache,
):
    planes = 4
    g, m, c = lax.axis_index("groups"), lax.axis_index("mp"), lax.axis_index(PLANE)
    here, odd = jnp.stack([m, c, g]), (m & 1).reshape(1)

    across, peer = over_section(thinker_act), over_core(thinker_act)
    near = down([thinker_act, peer], w_think, planes)
    near_even, near_odd = add(odd, lax.all_to_all(near, "mp", 0, 0))
    mine = jnp.concatenate([w_query, w_key, w_value], axis=1)
    half = mine.shape[0] // 2
    my_half = lax.dynamic_slice_in_dim(mine, g * half, half, axis=0)

    across, near_even, near_odd, mine, my_half = lax.optimization_barrier(
        (across, near_even, near_odd, mine, my_half)
    )
    near_home = sent_home(near_even, near_odd, 0)
    across, other, *near_home = lax.optimization_barrier((across, over_core(across), *near_home))
    far = down([across, other], w_think, planes)
    far_even, far_odd = add(odd, lax.all_to_all(far, "mp", 0, 0))

    my_half = over_section(after(my_half, far))
    other_half = over_groups(my_half)

    far_home = sent_home(far_even, far_odd, 1)
    slots, other_half = lax.optimization_barrier((talker_slot, other_half))
    thinker_out, *projected = project(here, slots, w_proj, near_home, far_home)
    terms = projected[:1]
    for d in range(1, planes):
        terms.append(lax.ppermute(projected[d], "mp", [(p, p ^ d) for p in range(planes)]))
    weights = [mine, over_core(mine), my_half, other_half, over_core(my_half), over_core(other_half)]
    new_kv, ctx = talker(here, terms, talker_gain, weights, kv_len, kv_cache)
    return (thinker_out, new_kv, ctx)


def solution(mesh):
    in_specs = (
        P(("groups", "section", "rows"), "mp"),
        P("mp", ("section", "rows")),
        P("mp", None),
        P(),
        P(None, ("section", "rows")),
        P(None, ("section", "rows")),
        P(None, ("section", "rows")),
        P(("groups", "section", "rows"), None),
        P(("groups", "mp", "section", "rows")),
        P(("groups", "mp", "section", "rows"), None, None),
    )
    out_specs = (
        P(("groups", "section", "rows"), "mp"),
        P(("groups", "mp", "section", "rows"), None),
        P(("groups", "mp", "section", "rows"), None),
    )
    sizes = tuple(mesh.shape[a] for a in ("groups", "section", "rows", "mp"))
    shards = four_planes if sizes == (2, 2, 2, 4) else any_mesh
    return jax.shard_map(shards, mesh=mesh, in_specs=in_specs, out_specs=out_specs, check_vma=False)
```

```python
import functools

import jax
import jax.numpy as jnp
from jax import lax
from jax.experimental import pallas as pl
from jax.experimental.pallas import tpu as pltpu
from jax.sharding import PartitionSpec as P

HEAD_DIM = 128
ROW_STEP = 8
LANES = 128
PAGES = 2
SHORT = pl.CostEstimate(flops=1, bytes_accessed=1, transcendentals=0)


def in_hbm(x):
    return pltpu.with_memory_space_constraint(x, pltpu.HBM)


def down_kernel(planes, cuts, groups, *refs):
    xs, (w, out, x_all, w_all, acc, x_sem, w_sem) = refs[:groups], refs[groups:]
    n = xs[0].shape[0]
    loads = []
    for s, (lo, hi) in enumerate(cuts):
        deep = pl.ds(lo, hi - lo)
        copies = [pltpu.make_async_copy(w.at[deep], w_all.at[deep], w_sem.at[s])]
        for i in range(groups):
            copies.append(
                pltpu.make_async_copy(
                    xs[i].at[:, deep], x_all.at[pl.ds(i * n, n), deep], x_sem.at[s, i]
                )
            )
        for copy in copies:
            copy.start()
        loads.append(copies)
    for s, (lo, hi) in enumerate(cuts):
        for copy in loads[s]:
            copy.wait()
        part = jnp.dot(x_all[:, lo:hi], w_all[lo:hi, :], preferred_element_type=jnp.float32)
        acc[...] = part if s == 0 else acc[...] + part
    part = n // planes
    for i in range(groups):
        for p in range(planes):
            at = i * n + p * part
            out[p, i * part : (i + 1) * part, :] = acc[at : at + part, :].astype(out.dtype)


def down(xs, w, planes):
    depth, columns = w.shape
    groups, n = len(xs), xs[0].shape[0]
    tiles, parts = depth // LANES, 6
    ends = [LANES * (tiles * i // parts) for i in range(parts)] + [depth]
    return pl.pallas_call(
        functools.partial(down_kernel, planes, list(zip(ends[:-1], ends[1:])), groups),
        out_shape=jax.ShapeDtypeStruct((planes, groups * n // planes, columns), jnp.bfloat16),
        in_specs=[pl.BlockSpec(memory_space=pl.ANY)] * (groups + 1),
        out_specs=pl.BlockSpec(memory_space=pltpu.VMEM),
        scratch_shapes=[
            pltpu.VMEM((groups * n, depth), jnp.bfloat16),
            pltpu.VMEM((depth, columns), jnp.bfloat16),
            pltpu.VMEM((groups * n, columns), jnp.float32),
            pltpu.SemaphoreType.DMA((parts, groups)),
            pltpu.SemaphoreType.DMA((parts,)),
        ],
        cost_estimate=SHORT,
        compiler_params=pltpu.CompilerParams(vmem_limit_bytes=24 * 1024 * 1024),
    )(*xs, in_hbm(w))


def add_kernel(terms, out):
    total = terms[0].astype(jnp.float32)
    for k in range(1, terms.shape[0]):
        total = total + terms[k].astype(jnp.float32)
    out[...] = total.astype(jnp.bfloat16)


def add(terms):
    vmem = pl.BlockSpec(memory_space=pltpu.VMEM)
    return pl.pallas_call(
        add_kernel,
        out_shape=jax.ShapeDtypeStruct(terms.shape[1:], jnp.bfloat16),
        in_specs=[vmem],
        out_specs=vmem,
        cost_estimate=SHORT,
        compiler_params=pltpu.CompilerParams(vmem_limit_bytes=16 * 1024 * 1024),
    )(terms)


def add_and_deal_kernel(plane_ref, near, terms, *refs):
    outs, sums = refs[:-1], refs[-1]
    total = terms[0].astype(jnp.float32)
    for k in range(1, terms.shape[0]):
        total = total + terms[k].astype(jnp.float32)
    rows = sums.shape[1]
    half = len(outs) // 2
    for e in range(half):
        sums[e] = near[e * rows : (e + 1) * rows, :]
        sums[half + e] = total[e * rows : (e + 1) * rows].astype(jnp.bfloat16)
    for k, out in enumerate(outs):
        out[...] = sums[plane_ref[0] ^ k]


def add_and_deal(plane, near, terms):
    rows, columns = near.shape
    blocks = 4
    part = jax.ShapeDtypeStruct((2 * rows // blocks, columns), jnp.bfloat16)
    vmem = pl.BlockSpec(memory_space=pltpu.VMEM)
    return pl.pallas_call(
        add_and_deal_kernel,
        out_shape=(part,) * blocks,
        in_specs=[pl.BlockSpec(memory_space=pltpu.SMEM), vmem, vmem],
        out_specs=(vmem,) * blocks,
        scratch_shapes=[pltpu.VMEM((blocks, *part.shape), jnp.bfloat16)],
        cost_estimate=SHORT,
        compiler_params=pltpu.CompilerParams(vmem_limit_bytes=16 * 1024 * 1024),
    )(plane, near, terms)


def project_kernel(planes, here_ref, slots, w_hbm, *refs):
    came, refs = refs[:planes], refs[planes:]
    home, outs, (parts, w, sem, w_sem) = refs[0], refs[1 : planes + 1], refs[planes + 1 :]
    plane, block = here_ref[0], here_ref[1]
    copies = [pltpu.make_async_copy(w_hbm, w, w_sem)]
    for k in range(planes):
        copies.append(pltpu.make_async_copy(came[k], parts.at[plane ^ block ^ k], sem.at[k]))
    for copy in copies:
        copy.start()
    for copy in copies:
        copy.wait()
    rows = parts.shape[1]
    for p in range(planes):
        home[p * rows : (p + 1) * rows, :] = parts[p]
    n = home.shape[0]
    place = lax.broadcasted_iota(jnp.int32, (n, n), 0)
    place = ((place // rows) ^ plane) * rows + place % rows
    pick = (place == slots[...]).astype(jnp.float32).astype(jnp.bfloat16)
    ordered = jnp.dot(pick, home[...], preferred_element_type=jnp.float32).astype(jnp.bfloat16)
    made = jnp.dot(ordered, w[...], preferred_element_type=jnp.float32).astype(jnp.bfloat16)
    for d in range(planes):
        outs[d][...] = made[d * rows : (d + 1) * rows]


def project(here, slots, w_proj, came):
    planes = len(came)
    rows, columns = came[0].shape
    vmem = pl.BlockSpec(memory_space=pltpu.VMEM)
    made = jax.ShapeDtypeStruct((rows, w_proj.shape[1]), jnp.bfloat16)
    return pl.pallas_call(
        functools.partial(project_kernel, planes),
        out_shape=(jax.ShapeDtypeStruct((planes * rows, columns), jnp.bfloat16), *[made] * planes),
        in_specs=[pl.BlockSpec(memory_space=pltpu.SMEM), vmem]
        + [pl.BlockSpec(memory_space=pl.ANY)] * (1 + planes),
        out_specs=(vmem,) * (1 + planes),
        scratch_shapes=[
            pltpu.VMEM((planes, rows, columns), jnp.bfloat16),
            pltpu.VMEM(w_proj.shape, w_proj.dtype),
            pltpu.SemaphoreType.DMA((planes,)),
            pltpu.SemaphoreType.DMA,
        ],
        cost_estimate=SHORT,
        compiler_params=pltpu.CompilerParams(vmem_limit_bytes=16 * 1024 * 1024),
    )(here, slots, in_hbm(w_proj), *came)


def page_copies(len_ref, kv_hbm, kv_ref, sem, r):
    page = kv_ref.shape[1] // PAGES
    out = []
    for p in range(PAGES):
        at = pl.ds(p * page, page)
        copy = pltpu.make_async_copy(kv_hbm.at[r, at], kv_ref.at[r, at], sem.at[r, p])
        out.append((copy, len_ref[r] > p * page))
    return out


def talker_kernel(here_ref, len_ref, gain, *refs):
    w_hbm, terms, refs = refs[:6], refs[6:-10], refs[-10:]
    kv_hbm, new_kv, out_ref, kv_ref, sem, w_ref, w_sem, qkv, spreads, gathereds = refs
    block, turn = here_ref[1], here_ref[2]
    blocks = qkv.shape[0]
    rows, cached, kv_width = kv_ref.shape
    width = kv_width // 2
    page = cached // PAGES
    heads = out_ref.shape[1] // HEAD_DIM
    group = heads // blocks
    slot = LANES // ROW_STEP
    sets = spreads.shape[0]
    key, value = group * HEAD_DIM, (group + 1) * HEAD_DIM
    inv = 1.0 / HEAD_DIM**0.5

    half = w_ref.shape[1] // 2
    w_parts = [(w_ref.at[0],), (w_ref.at[1],)]
    for e in (2, 3):
        w_parts.append(
            [
                w_ref.at[e, pl.ds(pl.multiple_of(which * half, half), half)]
                for which in (turn, 1 - turn)
            ]
        )
    w_copies, at = [], 0
    for parts in w_parts:
        w_copies.append([])
        for part in parts:
            w_copies[-1].append(pltpu.make_async_copy(w_hbm[at], part, w_sem.at[at]))
            w_copies[-1][-1].start()
            at += 1

    @pl.loop(0, rows)
    def _(r):
        for p, (copy, needed) in enumerate(page_copies(len_ref, kv_hbm, kv_ref, sem, r)):
            if p == 0:
                copy.start()
            else:
                pl.when(needed)(copy.start)

    total = terms[0][...].astype(jnp.float32)
    for term in terms[1:]:
        total = total + term[...].astype(jnp.float32)
    scale = lax.rsqrt(jnp.mean(total * total, axis=1, keepdims=True) + 1e-06)
    normed = (total * scale * gain[...]).astype(jnp.bfloat16)
    for e in range(blocks):
        for copy in w_copies[e]:
            copy.wait()
        made = jnp.dot(normed, w_ref[e], preferred_element_type=jnp.float32)
        qkv[e ^ block] = made.astype(jnp.bfloat16).astype(jnp.float32)
    for g in range(blocks):
        for place, start in ((g, key), (blocks + g, value)):
            new_kv[:, place * HEAD_DIM : (place + 1) * HEAD_DIM] = qkv[
                g, :, start : start + HEAD_DIM
            ].astype(jnp.bfloat16)

    spreads[...] = jnp.zeros_like(spreads)
    lane = lax.broadcasted_iota(jnp.int32, (HEAD_DIM, LANES), 1)
    lane_row, lane_block = lane // slot, lane % slot // group
    row_block = lax.broadcasted_iota(jnp.int32, (slot, HEAD_DIM), 0) // group
    own_row = lax.broadcasted_iota(jnp.int32, (ROW_STEP, LANES), 0)

    def scores_of(at, spread):
        here = pl.ds(at, ROW_STEP)
        for h in range(heads):
            g, j = h // group, h % group
            spread[pl.ds(h, ROW_STEP, stride=slot), :] = qkv[
                g, here, j * HEAD_DIM : (j + 1) * HEAD_DIM
            ]
        query = spread[...].T
        by_block = [
            jnp.where(lane_block == g, query, 0.0).astype(jnp.bfloat16) for g in range(blocks)
        ]
        scores = jnp.zeros((cached, LANES), jnp.float32)
        for r in range(ROW_STEP):
            mine = lane_row == r
            right = jnp.concatenate(
                [jnp.where(mine, q, jnp.zeros_like(q)) for q in by_block], axis=0
            )
            scores = scores + jnp.dot(
                kv_ref[at + r, :, :width], right, preferred_element_type=jnp.float32
            )
        own = jnp.zeros((ROW_STEP, LANES), jnp.float32)
        for g in range(blocks):
            new_key = qkv[g, here, key:value].astype(jnp.bfloat16)
            own = own + jnp.dot(new_key, by_block[g], preferred_element_type=jnp.float32)
        own = jnp.where(own_row == lane_row[:ROW_STEP], own, 0.0)
        return scores * inv, jnp.sum(own, axis=0, keepdims=True) * inv

    def softmax(at, scores, own):
        lens = jnp.zeros((1, LANES), jnp.int32)
        for r in range(ROW_STEP):
            lens = jnp.where(lane_row[:1] == r, len_ref[at + r], lens)
        valid = lax.broadcasted_iota(jnp.int32, scores.shape, 0) < lens
        scores = jnp.where(valid, scores, -jnp.inf)
        top = jnp.maximum(jnp.max(scores, axis=0, keepdims=True), own)
        expo = jnp.where(valid, jnp.exp(scores - top), 0.0)
        own_expo = jnp.exp(own - top)
        total = jnp.sum(expo, axis=0, keepdims=True) + own_expo
        probs = (expo / total).T.astype(jnp.bfloat16)
        own_prob = (own_expo / total).astype(jnp.bfloat16).astype(jnp.float32)
        return probs, jnp.broadcast_to(own_prob, (LANES, LANES)).T

    def context(at, probs, own_prob, gathered):
        here = pl.ds(at, ROW_STEP)
        value_rows = qkv.at[:, here, value:]
        for r in range(ROW_STEP):
            lanes = slice(r * slot, (r + 1) * slot)
            made = jnp.dot(
                probs[lanes], kv_ref[at + r, :, width:], preferred_element_type=jnp.float32
            )
            ctx = jnp.zeros((slot, HEAD_DIM), jnp.float32)
            new = jnp.zeros((slot, HEAD_DIM), jnp.float32)
            for g in range(blocks):
                block = made[:, g * HEAD_DIM : (g + 1) * HEAD_DIM]
                ctx = jnp.where(row_block == g, block, ctx)
                new = jnp.where(row_block == g, value_rows[g, r : r + 1, :], new)
            gathered[lanes, :] = ctx + own_prob[lanes] * new
        for h in range(heads):
            out_ref[here, h * HEAD_DIM : (h + 1) * HEAD_DIM] = gathered[
                pl.ds(h, ROW_STEP, stride=slot), :
            ]

    @pl.loop(0, rows // (sets * ROW_STEP))
    def _(i):
        first = pl.multiple_of(i * sets * ROW_STEP, sets * ROW_STEP)
        for k in range(sets * ROW_STEP):
            r = first + k
            for p, (copy, needed) in enumerate(page_copies(len_ref, kv_hbm, kv_ref, sem, r)):
                if p == 0:
                    copy.wait()
                    continue
                pl.when(needed)(copy.wait)

                @pl.when(jnp.logical_not(needed))
                def _(p=p, r=r):
                    kv_ref[r, p * page : (p + 1) * page, :] = jnp.zeros(
                        (page, kv_width), kv_ref.dtype
                    )

        ats = [pl.multiple_of(first + k * ROW_STEP, ROW_STEP) for k in range(sets)]
        scored = [scores_of(at, spreads.at[k]) for k, at in enumerate(ats)]
        weighed = [softmax(at, *s) for at, s in zip(ats, scored)]
        for k, at in enumerate(ats):
            context(at, *weighed[k], gathereds.at[k])


def talker(here, terms, talker_gain, weights, kv_len, kv_cache):
    rows, cached, kv_width = kv_cache.shape
    wide, columns = weights[0].shape
    blocks = 4
    q_width = blocks * columns - kv_width
    sets = 2
    vmem = pl.BlockSpec(memory_space=pltpu.VMEM)
    smem = pl.BlockSpec(memory_space=pltpu.SMEM)
    return pl.pallas_call(
        talker_kernel,
        out_shape=(
            jax.ShapeDtypeStruct((rows, kv_width), jnp.bfloat16),
            jax.ShapeDtypeStruct((rows, q_width), jnp.float32),
        ),
        in_specs=[smem, smem, vmem]
        + [pl.BlockSpec(memory_space=pl.ANY)] * len(weights)
        + [vmem] * len(terms)
        + [pl.BlockSpec(memory_space=pl.ANY)],
        out_specs=(vmem, vmem),
        scratch_shapes=[
            pltpu.VMEM((rows, cached, kv_width), jnp.bfloat16),
            pltpu.SemaphoreType.DMA((rows, PAGES)),
            pltpu.VMEM((blocks, wide, columns), jnp.bfloat16),
            pltpu.SemaphoreType.DMA((len(weights),)),
            pltpu.VMEM((blocks, rows, columns), jnp.float32),
            pltpu.VMEM((sets, LANES, HEAD_DIM), jnp.float32),
            pltpu.VMEM((sets, LANES, HEAD_DIM), jnp.float32),
        ],
        cost_estimate=SHORT,
        compiler_params=pltpu.CompilerParams(vmem_limit_bytes=40 * 1024 * 1024),
    )(here, kv_len, talker_gain.reshape(1, wide), *weights, *terms, in_hbm(kv_cache))


def rms_norm(talker_in, talker_gain):
    scale = lax.rsqrt(jnp.mean(talker_in * talker_in, axis=1, keepdims=True) + 1e-06)
    return (talker_in * scale * talker_gain).astype(jnp.bfloat16)


def talker_step(talker_in, talker_gain, w_query, w_key, w_value, kv_len, kv_cache):
    owned = talker_in.shape[0]
    cached = kv_cache.shape[1]
    kv_width = w_key.shape[1]
    head_dim = HEAD_DIM
    kv_heads = kv_width // head_dim
    group = w_query.shape[1] // kv_width
    normed = rms_norm(talker_in, talker_gain)
    query = jnp.dot(normed, w_query, preferred_element_type=jnp.float32).astype(jnp.bfloat16)
    new_key = jnp.dot(normed, w_key, preferred_element_type=jnp.float32).astype(jnp.bfloat16)
    new_value = jnp.dot(normed, w_value, preferred_element_type=jnp.float32).astype(jnp.bfloat16)
    talker_kv = jnp.concatenate([new_key, new_value], axis=1)
    qb = query.reshape(owned, kv_heads, group, head_dim)
    keys = kv_cache[:, :, :kv_width].reshape(owned, cached, kv_heads, head_dim)
    values = kv_cache[:, :, kv_width:].reshape(owned, cached, kv_heads, head_dim)
    nk = new_key.reshape(owned, kv_heads, head_dim)
    nv = new_value.reshape(owned, kv_heads, head_dim)
    inv = 1.0 / head_dim**0.5
    scores = jnp.einsum("rgjd,rpgd->rgjp", qb, keys, preferred_element_type=jnp.float32) * inv
    own = jnp.einsum("rgjd,rgd->rgj", qb, nk, preferred_element_type=jnp.float32) * inv
    valid = (jnp.arange(cached, dtype=jnp.int32)[None, :] < kv_len[:, None])[:, None, None, :]
    scores = jnp.where(valid, scores, -jnp.inf)
    top = jnp.maximum(jnp.max(scores, axis=3), own)
    expo = jnp.where(valid, jnp.exp(scores - top[..., None]), 0.0)
    own_expo = jnp.exp(own - top)
    total = jnp.sum(expo, axis=3) + own_expo
    probs = (expo / total[..., None]).astype(jnp.bfloat16)
    own_prob = (own_expo / total).astype(jnp.bfloat16)
    ctx = jnp.einsum("rgjp,rpgd->rgjd", probs, values, preferred_element_type=jnp.float32)
    ctx = ctx + own_prob.astype(jnp.float32)[..., None] * nv.astype(jnp.float32)[:, :, None, :]
    return (talker_kv, ctx.reshape(owned, w_query.shape[1]))


def any_mesh(
    thinker_act,
    w_think,
    w_proj,
    talker_gain,
    w_query,
    w_key,
    w_value,
    talker_slot,
    kv_len,
    kv_cache,
):
    partial_sums = jnp.dot(
        thinker_act,
        lax.all_gather(w_think, ("section", "rows"), axis=1, tiled=True),
        preferred_element_type=jnp.float32,
    )
    full_query, full_key, full_value = (
        lax.all_gather(w_query, ("section", "rows"), axis=1, tiled=True),
        lax.all_gather(w_key, ("section", "rows"), axis=1, tiled=True),
        lax.all_gather(w_value, ("section", "rows"), axis=1, tiled=True),
    )
    mine = lax.psum_scatter(partial_sums, "mp", scatter_dimension=1, tiled=True)
    thinker_out = mine.astype(jnp.bfloat16)
    order = jnp.argsort(talker_slot[0], stable=True)
    sorted_out = thinker_out[order]
    talker_in = lax.psum_scatter(
        jnp.dot(sorted_out, w_proj, preferred_element_type=jnp.float32),
        "mp",
        scatter_dimension=0,
        tiled=True,
    )
    talker_kv, talker_ctx = talker_step(
        talker_in, talker_gain, full_query, full_key, full_value, kv_len, kv_cache
    )
    return (thinker_out, talker_kv, talker_ctx)


PLANE = ("section", "rows")
GROUP = ("mp", "section", "rows")


def over_core(x):
    return lax.ppermute(x, "rows", [(0, 1), (1, 0)])


def over_section(x):
    return lax.ppermute(x, "section", [(0, 1), (1, 0)])


def over_plane(x, e):
    return lax.ppermute(x, PLANE, [(b, b ^ e) for b in range(4)])


def over_groups(x):
    return lax.ppermute(x, "groups", [(0, 1), (1, 0)])


def after(x, *others):
    return lax.optimization_barrier((x, *others))[0]


def four_planes(
    thinker_act,
    w_think,
    w_proj,
    talker_gain,
    w_query,
    w_key,
    w_value,
    talker_slot,
    kv_len,
    kv_cache,
):
    planes = 4
    g, m, c = lax.axis_index("groups"), lax.axis_index("mp"), lax.axis_index(PLANE)
    here, plane = jnp.stack([m, c, g]), m.reshape(1)

    across, peer = over_section(thinker_act), over_core(thinker_act)
    near = down([in_hbm(thinker_act), peer], w_think, planes)
    near_terms = lax.all_to_all(near, "mp", 0, 0)
    mine = jnp.concatenate([w_query, w_key, w_value], axis=1)
    half = mine.shape[0] // 2
    my_half = lax.dynamic_slice_in_dim(mine, g * half, half, axis=0)

    across, near_terms, mine, my_half = lax.optimization_barrier(
        (across, near_terms, mine, my_half)
    )
    far = down([across, over_core(across)], w_think, planes)
    far_terms = lax.all_to_all(far, "mp", 0, 0)

    my_half = over_section(after(my_half, far))
    near_sums = add(after(near_terms, far))

    came = [
        lax.ppermute(x, GROUP, [(p * 4 + b, b * 4 + (b ^ p ^ k)) for p in range(4) for b in range(4)])
        for k, x in enumerate(add_and_deal(plane, near_sums, far_terms))
    ]
    my_half = after(my_half, near_sums)
    came[0], other_half = lax.optimization_barrier((came[0], over_groups(my_half)))
    thinker_out, *projected = project(here, talker_slot, w_proj, came)
    terms = projected[:1]
    for d in range(1, planes):
        terms.append(lax.ppermute(projected[d], "mp", [(p, p ^ d) for p in range(planes)]))
    other_half = after(other_half, projected[0])
    halves = [my_half, other_half, over_core(my_half), over_core(other_half)]
    weights = [mine, over_core(mine), *halves]
    new_kv, ctx = talker(here, terms, talker_gain, weights, kv_len, kv_cache)
    return (thinker_out, new_kv, ctx)


def solution(mesh):
    in_specs = (
        P(("groups", "section", "rows"), "mp"),
        P("mp", ("section", "rows")),
        P("mp", None),
        P(),
        P(None, ("section", "rows")),
        P(None, ("section", "rows")),
        P(None, ("section", "rows")),
        P(("groups", "section", "rows"), None),
        P(("groups", "mp", "section", "rows")),
        P(("groups", "mp", "section", "rows"), None, None),
    )
    out_specs = (
        P(("groups", "section", "rows"), "mp"),
        P(("groups", "mp", "section", "rows"), None),
        P(("groups", "mp", "section", "rows"), None),
    )
    sizes = tuple(mesh.shape[a] for a in ("groups", "section", "rows", "mp"))
    shards = four_planes if sizes == (2, 2, 2, 4) else any_mesh
    return jax.shard_map(shards, mesh=mesh, in_specs=in_specs, out_specs=out_specs, check_vma=False)
```

```python
import functools

import jax
import jax.numpy as jnp
from jax import lax
from jax.experimental import pallas as pl
from jax.experimental.pallas import tpu as pltpu
from jax.sharding import PartitionSpec as P

HEAD_DIM = 128
ROW_STEP = 8
LANES = 128
PAGES = 2
SHORT = pl.CostEstimate(flops=1, bytes_accessed=1, transcendentals=0)


def in_hbm(x):
    return pltpu.with_memory_space_constraint(x, pltpu.HBM)


def down_kernel(planes, cuts, groups, spans, *refs):
    xs, (w, out, x_all, w_all, acc, x_sem, w_sem) = refs[:groups], refs[groups:]
    n = xs[0].shape[0]
    loads = []
    for s, (lo, hi) in enumerate(cuts):
        deep = pl.ds(lo, hi - lo)
        copies = [pltpu.make_async_copy(w.at[deep], w_all.at[deep], w_sem.at[s])]
        for i in range(groups):
            copies.append(
                pltpu.make_async_copy(
                    xs[i].at[:, deep], x_all.at[pl.ds(i * n, n), deep], x_sem.at[s, i]
                )
            )
        for copy in copies:
            copy.start()
        loads.append(copies)
    for s, (lo, hi) in enumerate(cuts):
        for copy in loads[s]:
            copy.wait()
        part = jnp.dot(x_all[:, lo:hi], w_all[lo:hi, :], preferred_element_type=jnp.float32)
        acc[...] = part if s == 0 else acc[...] + part
    row = 0
    for i in range(groups):
        for start, length in spans:
            part = length // planes
            for p in range(planes):
                at = i * n + start + p * part
                out[p, row : row + part, :] = acc[at : at + part, :].astype(out.dtype)
            row += part


def down(xs, w, planes, spans):
    depth, columns = w.shape
    groups, n = len(xs), xs[0].shape[0]
    tiles, parts = depth // LANES, 6
    ends = [LANES * (tiles * i // parts) for i in range(parts)] + [depth]
    return pl.pallas_call(
        functools.partial(down_kernel, planes, list(zip(ends[:-1], ends[1:])), groups, spans),
        out_shape=jax.ShapeDtypeStruct((planes, groups * n // planes, columns), jnp.bfloat16),
        in_specs=[pl.BlockSpec(memory_space=pl.ANY)] * (groups + 1),
        out_specs=pl.BlockSpec(memory_space=pltpu.VMEM),
        scratch_shapes=[
            pltpu.VMEM((groups * n, depth), jnp.bfloat16),
            pltpu.VMEM((depth, columns), jnp.bfloat16),
            pltpu.VMEM((groups * n, columns), jnp.float32),
            pltpu.SemaphoreType.DMA((parts, groups)),
            pltpu.SemaphoreType.DMA((parts,)),
        ],
        cost_estimate=SHORT,
        compiler_params=pltpu.CompilerParams(vmem_limit_bytes=24 * 1024 * 1024),
    )(*xs, in_hbm(w))


def add_kernel(terms, out):
    total = terms[0].astype(jnp.float32)
    for k in range(1, terms.shape[0]):
        total = total + terms[k].astype(jnp.float32)
    out[...] = total.astype(jnp.bfloat16)


def add(terms):
    vmem = pl.BlockSpec(memory_space=pltpu.VMEM)
    return pl.pallas_call(
        add_kernel,
        out_shape=jax.ShapeDtypeStruct(terms.shape[1:], jnp.bfloat16),
        in_specs=[vmem],
        out_specs=vmem,
        cost_estimate=SHORT,
        compiler_params=pltpu.CompilerParams(vmem_limit_bytes=16 * 1024 * 1024),
    )(terms)


def add_and_deal_kernel(plane_ref, near, *refs):
    chunks, outs, sums = refs[:-5], refs[-5:-1], refs[-1]
    rows = sums.shape[1]
    half = len(outs) // 2
    for e in range(half):
        sums[e] = near[e * rows : (e + 1) * rows, :]
    row = 0
    for terms in chunks:
        total = terms[0].astype(jnp.float32)
        for k in range(1, terms.shape[0]):
            total = total + terms[k].astype(jnp.float32)
        part = total.shape[0] // half
        for e in range(half):
            sums[half + e, row : row + part, :] = total[e * part : (e + 1) * part].astype(
                jnp.bfloat16
            )
        row += part
    for k, out in enumerate(outs):
        out[...] = sums[plane_ref[0] ^ k]


def add_and_deal(plane, near, chunks):
    rows, columns = near.shape
    blocks = 4
    part = jax.ShapeDtypeStruct((2 * rows // blocks, columns), jnp.bfloat16)
    vmem = pl.BlockSpec(memory_space=pltpu.VMEM)
    return pl.pallas_call(
        add_and_deal_kernel,
        out_shape=(part,) * blocks,
        in_specs=[pl.BlockSpec(memory_space=pltpu.SMEM), vmem] + [vmem] * len(chunks),
        out_specs=(vmem,) * blocks,
        scratch_shapes=[pltpu.VMEM((blocks, *part.shape), jnp.bfloat16)],
        cost_estimate=SHORT,
        compiler_params=pltpu.CompilerParams(vmem_limit_bytes=16 * 1024 * 1024),
    )(plane, near, *chunks)


def project_kernel(planes, spans, here_ref, slots, w_hbm, *refs):
    came, refs = refs[:planes], refs[planes:]
    home, outs, (parts, w, sem, w_sem) = refs[0], refs[1 : planes + 1], refs[planes + 1 :]
    plane, block = here_ref[0], here_ref[1]
    copies = [pltpu.make_async_copy(w_hbm, w, w_sem)]
    for k in range(planes):
        copies.append(pltpu.make_async_copy(came[k], parts.at[plane ^ block ^ k], sem.at[k]))
    for copy in copies:
        copy.start()
    for copy in copies:
        copy.wait()
    rows = parts.shape[1]
    row = 0
    for start, length in spans:
        part = length // planes
        for p in range(planes):
            at = start + p * part
            home[at : at + part, :] = parts[p, row : row + part, :]
        row += part
    n = home.shape[0]
    place = lax.broadcasted_iota(jnp.int32, (n, n), 0)
    place = ((place // rows) ^ plane) * rows + place % rows
    pick = (place == slots[...]).astype(jnp.float32).astype(jnp.bfloat16)
    ordered = jnp.dot(pick, home[...], preferred_element_type=jnp.float32).astype(jnp.bfloat16)
    made = jnp.dot(ordered, w[...], preferred_element_type=jnp.float32).astype(jnp.bfloat16)
    for d in range(planes):
        outs[d][...] = made[d * rows : (d + 1) * rows]


def project(here, slots, w_proj, came, spans):
    planes = len(came)
    rows, columns = came[0].shape
    vmem = pl.BlockSpec(memory_space=pltpu.VMEM)
    made = jax.ShapeDtypeStruct((rows, w_proj.shape[1]), jnp.bfloat16)
    return pl.pallas_call(
        functools.partial(project_kernel, planes, spans),
        out_shape=(jax.ShapeDtypeStruct((planes * rows, columns), jnp.bfloat16), *[made] * planes),
        in_specs=[pl.BlockSpec(memory_space=pltpu.SMEM), vmem]
        + [pl.BlockSpec(memory_space=pl.ANY)] * (1 + planes),
        out_specs=(vmem,) * (1 + planes),
        scratch_shapes=[
            pltpu.VMEM((planes, rows, columns), jnp.bfloat16),
            pltpu.VMEM(w_proj.shape, w_proj.dtype),
            pltpu.SemaphoreType.DMA((planes,)),
            pltpu.SemaphoreType.DMA,
        ],
        cost_estimate=SHORT,
        compiler_params=pltpu.CompilerParams(vmem_limit_bytes=16 * 1024 * 1024),
    )(here, slots, in_hbm(w_proj), *came)


def page_copies(len_ref, kv_hbm, kv_ref, sem, r):
    page = kv_ref.shape[1] // PAGES
    out = []
    for p in range(PAGES):
        at = pl.ds(p * page, page)
        copy = pltpu.make_async_copy(kv_hbm.at[r, at], kv_ref.at[r, at], sem.at[r, p])
        out.append((copy, len_ref[r] > p * page))
    return out


def talker_kernel(here_ref, len_ref, gain, *refs):
    w_hbm, terms, refs = refs[:6], refs[6:-10], refs[-10:]
    kv_hbm, new_kv, out_ref, kv_ref, sem, w_ref, w_sem, qkv, spreads, gathereds = refs
    block, turn = here_ref[1], here_ref[2]
    blocks = qkv.shape[0]
    rows, cached, kv_width = kv_ref.shape
    width = kv_width // 2
    page = cached // PAGES
    heads = out_ref.shape[1] // HEAD_DIM
    group = heads // blocks
    slot = LANES // ROW_STEP
    sets = spreads.shape[0]
    key, value = group * HEAD_DIM, (group + 1) * HEAD_DIM
    inv = 1.0 / HEAD_DIM**0.5

    half = w_ref.shape[1] // 2
    w_parts = [(w_ref.at[0],), (w_ref.at[1],)]
    for e in (2, 3):
        w_parts.append(
            [
                w_ref.at[e, pl.ds(pl.multiple_of(which * half, half), half)]
                for which in (turn, 1 - turn)
            ]
        )
    w_copies, at = [], 0
    for parts in w_parts:
        w_copies.append([])
        for part in parts:
            w_copies[-1].append(pltpu.make_async_copy(w_hbm[at], part, w_sem.at[at]))
            w_copies[-1][-1].start()
            at += 1

    @pl.loop(0, rows)
    def _(r):
        for p, (copy, needed) in enumerate(page_copies(len_ref, kv_hbm, kv_ref, sem, r)):
            if p == 0:
                copy.start()
            else:
                pl.when(needed)(copy.start)

    total = terms[0][...].astype(jnp.float32)
    for term in terms[1:]:
        total = total + term[...].astype(jnp.float32)
    scale = lax.rsqrt(jnp.mean(total * total, axis=1, keepdims=True) + 1e-06)
    normed = (total * scale * gain[...]).astype(jnp.bfloat16)
    for e in range(blocks):
        for copy in w_copies[e]:
            copy.wait()
        made = jnp.dot(normed, w_ref[e], preferred_element_type=jnp.float32)
        qkv[e ^ block] = made.astype(jnp.bfloat16).astype(jnp.float32)
    for g in range(blocks):
        for place, start in ((g, key), (blocks + g, value)):
            new_kv[:, place * HEAD_DIM : (place + 1) * HEAD_DIM] = qkv[
                g, :, start : start + HEAD_DIM
            ].astype(jnp.bfloat16)

    spreads[...] = jnp.zeros_like(spreads)
    lane = lax.broadcasted_iota(jnp.int32, (HEAD_DIM, LANES), 1)
    lane_row, lane_block = lane // slot, lane % slot // group
    row_block = lax.broadcasted_iota(jnp.int32, (slot, HEAD_DIM), 0) // group
    own_row = lax.broadcasted_iota(jnp.int32, (ROW_STEP, LANES), 0)

    def scores_of(at, spread):
        here = pl.ds(at, ROW_STEP)
        for h in range(heads):
            g, j = h // group, h % group
            spread[pl.ds(h, ROW_STEP, stride=slot), :] = qkv[
                g, here, j * HEAD_DIM : (j + 1) * HEAD_DIM
            ]
        query = spread[...].T
        by_block = [
            jnp.where(lane_block == g, query, 0.0).astype(jnp.bfloat16) for g in range(blocks)
        ]
        scores = jnp.zeros((cached, LANES), jnp.float32)
        for r in range(ROW_STEP):
            mine = lane_row == r
            right = jnp.concatenate(
                [jnp.where(mine, q, jnp.zeros_like(q)) for q in by_block], axis=0
            )
            scores = scores + jnp.dot(
                kv_ref[at + r, :, :width], right, preferred_element_type=jnp.float32
            )
        own = jnp.zeros((ROW_STEP, LANES), jnp.float32)
        for g in range(blocks):
            new_key = qkv[g, here, key:value].astype(jnp.bfloat16)
            own = own + jnp.dot(new_key, by_block[g], preferred_element_type=jnp.float32)
        own = jnp.where(own_row == lane_row[:ROW_STEP], own, 0.0)
        return scores * inv, jnp.sum(own, axis=0, keepdims=True) * inv

    def softmax(at, scores, own):
        lens = jnp.zeros((1, LANES), jnp.int32)
        for r in range(ROW_STEP):
            lens = jnp.where(lane_row[:1] == r, len_ref[at + r], lens)
        valid = lax.broadcasted_iota(jnp.int32, scores.shape, 0) < lens
        scores = jnp.where(valid, scores, -jnp.inf)
        top = jnp.maximum(jnp.max(scores, axis=0, keepdims=True), own)
        expo = jnp.where(valid, jnp.exp(scores - top), 0.0)
        own_expo = jnp.exp(own - top)
        total = jnp.sum(expo, axis=0, keepdims=True) + own_expo
        probs = (expo / total).T.astype(jnp.bfloat16)
        own_prob = (own_expo / total).astype(jnp.bfloat16).astype(jnp.float32)
        return probs, jnp.broadcast_to(own_prob, (LANES, LANES)).T

    def context(at, probs, own_prob, gathered):
        here = pl.ds(at, ROW_STEP)
        value_rows = qkv.at[:, here, value:]
        for r in range(ROW_STEP):
            lanes = slice(r * slot, (r + 1) * slot)
            made = jnp.dot(
                probs[lanes], kv_ref[at + r, :, width:], preferred_element_type=jnp.float32
            )
            ctx = jnp.zeros((slot, HEAD_DIM), jnp.float32)
            new = jnp.zeros((slot, HEAD_DIM), jnp.float32)
            for g in range(blocks):
                block = made[:, g * HEAD_DIM : (g + 1) * HEAD_DIM]
                ctx = jnp.where(row_block == g, block, ctx)
                new = jnp.where(row_block == g, value_rows[g, r : r + 1, :], new)
            gathered[lanes, :] = ctx + own_prob[lanes] * new
        for h in range(heads):
            out_ref[here, h * HEAD_DIM : (h + 1) * HEAD_DIM] = gathered[
                pl.ds(h, ROW_STEP, stride=slot), :
            ]

    @pl.loop(0, rows // (sets * ROW_STEP))
    def _(i):
        first = pl.multiple_of(i * sets * ROW_STEP, sets * ROW_STEP)
        for k in range(sets * ROW_STEP):
            r = first + k
            for p, (copy, needed) in enumerate(page_copies(len_ref, kv_hbm, kv_ref, sem, r)):
                if p == 0:
                    copy.wait()
                    continue
                pl.when(needed)(copy.wait)

                @pl.when(jnp.logical_not(needed))
                def _(p=p, r=r):
                    kv_ref[r, p * page : (p + 1) * page, :] = jnp.zeros(
                        (page, kv_width), kv_ref.dtype
                    )

        ats = [pl.multiple_of(first + k * ROW_STEP, ROW_STEP) for k in range(sets)]
        scored = [scores_of(at, spreads.at[k]) for k, at in enumerate(ats)]
        weighed = [softmax(at, *s) for at, s in zip(ats, scored)]
        for k, at in enumerate(ats):
            context(at, *weighed[k], gathereds.at[k])


def talker(here, terms, talker_gain, weights, kv_len, kv_cache):
    rows, cached, kv_width = kv_cache.shape
    wide, columns = weights[0].shape
    blocks = 4
    q_width = blocks * columns - kv_width
    sets = 2
    vmem = pl.BlockSpec(memory_space=pltpu.VMEM)
    smem = pl.BlockSpec(memory_space=pltpu.SMEM)
    return pl.pallas_call(
        talker_kernel,
        out_shape=(
            jax.ShapeDtypeStruct((rows, kv_width), jnp.bfloat16),
            jax.ShapeDtypeStruct((rows, q_width), jnp.float32),
        ),
        in_specs=[smem, smem, vmem]
        + [pl.BlockSpec(memory_space=pl.ANY)] * len(weights)
        + [vmem] * len(terms)
        + [pl.BlockSpec(memory_space=pl.ANY)],
        out_specs=(vmem, vmem),
        scratch_shapes=[
            pltpu.VMEM((rows, cached, kv_width), jnp.bfloat16),
            pltpu.SemaphoreType.DMA((rows, PAGES)),
            pltpu.VMEM((blocks, wide, columns), jnp.bfloat16),
            pltpu.SemaphoreType.DMA((len(weights),)),
            pltpu.VMEM((blocks, rows, columns), jnp.float32),
            pltpu.VMEM((sets, LANES, HEAD_DIM), jnp.float32),
            pltpu.VMEM((sets, LANES, HEAD_DIM), jnp.float32),
        ],
        cost_estimate=SHORT,
        compiler_params=pltpu.CompilerParams(vmem_limit_bytes=40 * 1024 * 1024),
    )(here, kv_len, talker_gain.reshape(1, wide), *weights, *terms, in_hbm(kv_cache))


def rms_norm(talker_in, talker_gain):
    scale = lax.rsqrt(jnp.mean(talker_in * talker_in, axis=1, keepdims=True) + 1e-06)
    return (talker_in * scale * talker_gain).astype(jnp.bfloat16)


def talker_step(talker_in, talker_gain, w_query, w_key, w_value, kv_len, kv_cache):
    owned = talker_in.shape[0]
    cached = kv_cache.shape[1]
    kv_width = w_key.shape[1]
    head_dim = HEAD_DIM
    kv_heads = kv_width // head_dim
    group = w_query.shape[1] // kv_width
    normed = rms_norm(talker_in, talker_gain)
    query = jnp.dot(normed, w_query, preferred_element_type=jnp.float32).astype(jnp.bfloat16)
    new_key = jnp.dot(normed, w_key, preferred_element_type=jnp.float32).astype(jnp.bfloat16)
    new_value = jnp.dot(normed, w_value, preferred_element_type=jnp.float32).astype(jnp.bfloat16)
    talker_kv = jnp.concatenate([new_key, new_value], axis=1)
    qb = query.reshape(owned, kv_heads, group, head_dim)
    keys = kv_cache[:, :, :kv_width].reshape(owned, cached, kv_heads, head_dim)
    values = kv_cache[:, :, kv_width:].reshape(owned, cached, kv_heads, head_dim)
    nk = new_key.reshape(owned, kv_heads, head_dim)
    nv = new_value.reshape(owned, kv_heads, head_dim)
    inv = 1.0 / head_dim**0.5
    scores = jnp.einsum("rgjd,rpgd->rgjp", qb, keys, preferred_element_type=jnp.float32) * inv
    own = jnp.einsum("rgjd,rgd->rgj", qb, nk, preferred_element_type=jnp.float32) * inv
    valid = (jnp.arange(cached, dtype=jnp.int32)[None, :] < kv_len[:, None])[:, None, None, :]
    scores = jnp.where(valid, scores, -jnp.inf)
    top = jnp.maximum(jnp.max(scores, axis=3), own)
    expo = jnp.where(valid, jnp.exp(scores - top[..., None]), 0.0)
    own_expo = jnp.exp(own - top)
    total = jnp.sum(expo, axis=3) + own_expo
    probs = (expo / total[..., None]).astype(jnp.bfloat16)
    own_prob = (own_expo / total).astype(jnp.bfloat16)
    ctx = jnp.einsum("rgjp,rpgd->rgjd", probs, values, preferred_element_type=jnp.float32)
    ctx = ctx + own_prob.astype(jnp.float32)[..., None] * nv.astype(jnp.float32)[:, :, None, :]
    return (talker_kv, ctx.reshape(owned, w_query.shape[1]))


def any_mesh(
    thinker_act,
    w_think,
    w_proj,
    talker_gain,
    w_query,
    w_key,
    w_value,
    talker_slot,
    kv_len,
    kv_cache,
):
    partial_sums = jnp.dot(
        thinker_act,
        lax.all_gather(w_think, ("section", "rows"), axis=1, tiled=True),
        preferred_element_type=jnp.float32,
    )
    full_query, full_key, full_value = (
        lax.all_gather(w_query, ("section", "rows"), axis=1, tiled=True),
        lax.all_gather(w_key, ("section", "rows"), axis=1, tiled=True),
        lax.all_gather(w_value, ("section", "rows"), axis=1, tiled=True),
    )
    mine = lax.psum_scatter(partial_sums, "mp", scatter_dimension=1, tiled=True)
    thinker_out = mine.astype(jnp.bfloat16)
    order = jnp.argsort(talker_slot[0], stable=True)
    sorted_out = thinker_out[order]
    talker_in = lax.psum_scatter(
        jnp.dot(sorted_out, w_proj, preferred_element_type=jnp.float32),
        "mp",
        scatter_dimension=0,
        tiled=True,
    )
    talker_kv, talker_ctx = talker_step(
        talker_in, talker_gain, full_query, full_key, full_value, kv_len, kv_cache
    )
    return (thinker_out, talker_kv, talker_ctx)


PLANE = ("section", "rows")
GROUP = ("mp", "section", "rows")


def over_core(x):
    return lax.ppermute(x, "rows", [(0, 1), (1, 0)])


def over_section(x):
    return lax.ppermute(x, "section", [(0, 1), (1, 0)])


def over_plane(x, e):
    return lax.ppermute(x, PLANE, [(b, b ^ e) for b in range(4)])


def over_groups(x):
    return lax.ppermute(x, "groups", [(0, 1), (1, 0)])


def after(x, *others):
    return lax.optimization_barrier((x, *others))[0]


def four_planes(
    thinker_act,
    w_think,
    w_proj,
    talker_gain,
    w_query,
    w_key,
    w_value,
    talker_slot,
    kv_len,
    kv_cache,
):
    planes = 4
    g, m, c = lax.axis_index("groups"), lax.axis_index("mp"), lax.axis_index(PLANE)
    here, plane = jnp.stack([m, c, g]), m.reshape(1)

    rows = thinker_act.shape[0]
    spans = [(0, rows // 3), (rows // 3, rows - rows // 3)]
    across = [over_section(thinker_act[start : start + n]) for start, n in spans]
    near = down([in_hbm(thinker_act), over_core(thinker_act)], w_think, planes, spans)
    near_terms = lax.all_to_all(near, "mp", 0, 0)
    mine = jnp.concatenate([w_query, w_key, w_value], axis=1)
    half = mine.shape[0] // 2
    my_half = lax.dynamic_slice_in_dim(mine, g * half, half, axis=0)

    ready, far_terms = (near,), []
    for x, (_, n) in zip(across, spans):
        x = after(x, *ready)
        far = down([x, over_core(x)], w_think, planes, [(0, n)])
        far_terms.append(lax.all_to_all(far, "mp", 0, 0))
        ready = (near_terms, far_terms[0], mine, my_half)

    my_half = over_section(after(my_half, far))
    near_sums = add(after(near_terms, far))

    came = [
        lax.ppermute(x, GROUP, [(p * 4 + b, b * 4 + (b ^ p ^ k)) for p in range(4) for b in range(4)])
        for k, x in enumerate(add_and_deal(plane, near_sums, far_terms))
    ]
    my_half = after(my_half, near_sums)
    came[0], other_half = lax.optimization_barrier((came[0], over_groups(my_half)))
    thinker_out, *projected = project(here, talker_slot, w_proj, came, spans)
    terms = projected[:1]
    for d in range(1, planes):
        terms.append(lax.ppermute(projected[d], "mp", [(p, p ^ d) for p in range(planes)]))
    other_half = after(other_half, projected[0])
    halves = [my_half, other_half, over_core(my_half), over_core(other_half)]
    weights = [mine, over_core(mine), *halves]
    new_kv, ctx = talker(here, terms, talker_gain, weights, kv_len, kv_cache)
    return (thinker_out, new_kv, ctx)


def solution(mesh):
    in_specs = (
        P(("groups", "section", "rows"), "mp"),
        P("mp", ("section", "rows")),
        P("mp", None),
        P(),
        P(None, ("section", "rows")),
        P(None, ("section", "rows")),
        P(None, ("section", "rows")),
        P(("groups", "section", "rows"), None),
        P(("groups", "mp", "section", "rows")),
        P(("groups", "mp", "section", "rows"), None, None),
    )
    out_specs = (
        P(("groups", "section", "rows"), "mp"),
        P(("groups", "mp", "section", "rows"), None),
        P(("groups", "mp", "section", "rows"), None),
    )
    sizes = tuple(mesh.shape[a] for a in ("groups", "section", "rows", "mp"))
    shards = four_planes if sizes == (2, 2, 2, 4) else any_mesh
    return jax.shard_map(shards, mesh=mesh, in_specs=in_specs, out_specs=out_specs, check_vma=False)
```

```python
import functools

import jax
import jax.numpy as jnp
from jax import lax
from jax.experimental import pallas as pl
from jax.experimental.pallas import tpu as pltpu
from jax.sharding import PartitionSpec as P

HEAD_DIM = 128
ROW_STEP = 8
LANES = 128
PAGES = 2
SHORT = pl.CostEstimate(flops=1, bytes_accessed=1, transcendentals=0)


def in_hbm(x):
    return pltpu.with_memory_space_constraint(x, pltpu.HBM)


def down_kernel(planes, cuts, groups, *refs):
    xs, (w, out, x_all, w_all, acc, x_sem, w_sem) = refs[:groups], refs[groups:]
    n = xs[0].shape[0]
    loads = []
    for s, (lo, hi) in enumerate(cuts):
        deep = pl.ds(lo, hi - lo)
        copies = [pltpu.make_async_copy(w.at[deep], w_all.at[deep], w_sem.at[s])]
        for i in range(groups):
            copies.append(
                pltpu.make_async_copy(
                    xs[i].at[:, deep], x_all.at[pl.ds(i * n, n), deep], x_sem.at[s, i]
                )
            )
        for copy in copies:
            copy.start()
        loads.append(copies)
    for s, (lo, hi) in enumerate(cuts):
        for copy in loads[s]:
            copy.wait()
        part = jnp.dot(x_all[:, lo:hi], w_all[lo:hi, :], preferred_element_type=jnp.float32)
        acc[...] = part if s == 0 else acc[...] + part
    part = n // planes
    for i in range(groups):
        for p in range(planes):
            at = i * n + p * part
            out[p, i * part : (i + 1) * part, :] = acc[at : at + part, :].astype(out.dtype)


def down(xs, w, planes):
    depth, columns = w.shape
    groups, n = len(xs), xs[0].shape[0]
    tiles, parts = depth // LANES, 6
    ends = [LANES * (tiles * i // parts) for i in range(parts)] + [depth]
    return pl.pallas_call(
        functools.partial(down_kernel, planes, list(zip(ends[:-1], ends[1:])), groups),
        out_shape=jax.ShapeDtypeStruct((planes, groups * n // planes, columns), jnp.bfloat16),
        in_specs=[pl.BlockSpec(memory_space=pl.ANY)] * (groups + 1),
        out_specs=pl.BlockSpec(memory_space=pltpu.VMEM),
        scratch_shapes=[
            pltpu.VMEM((groups * n, depth), jnp.bfloat16),
            pltpu.VMEM((depth, columns), jnp.bfloat16),
            pltpu.VMEM((groups * n, columns), jnp.float32),
            pltpu.SemaphoreType.DMA((parts, groups)),
            pltpu.SemaphoreType.DMA((parts,)),
        ],
        cost_estimate=SHORT,
        compiler_params=pltpu.CompilerParams(vmem_limit_bytes=24 * 1024 * 1024),
    )(*xs, in_hbm(w))


def add_kernel(terms, out):
    total = terms[0].astype(jnp.float32)
    for k in range(1, terms.shape[0]):
        total = total + terms[k].astype(jnp.float32)
    out[...] = total.astype(jnp.bfloat16)


def add(terms):
    vmem = pl.BlockSpec(memory_space=pltpu.VMEM)
    return pl.pallas_call(
        add_kernel,
        out_shape=jax.ShapeDtypeStruct(terms.shape[1:], jnp.bfloat16),
        in_specs=[vmem],
        out_specs=vmem,
        cost_estimate=SHORT,
        compiler_params=pltpu.CompilerParams(vmem_limit_bytes=16 * 1024 * 1024),
    )(terms)


def add_and_deal_kernel(plane_ref, near, terms, *refs):
    outs, sums = refs[:-1], refs[-1]
    total = terms[0].astype(jnp.float32)
    for k in range(1, terms.shape[0]):
        total = total + terms[k].astype(jnp.float32)
    rows = sums.shape[1]
    half = len(outs) // 2
    for e in range(half):
        sums[e] = near[e * rows : (e + 1) * rows, :]
        sums[half + e] = total[e * rows : (e + 1) * rows].astype(jnp.bfloat16)
    for k, out in enumerate(outs):
        out[...] = sums[plane_ref[0] ^ k]


def add_and_deal(plane, near, terms):
    rows, columns = near.shape
    blocks = 4
    part = jax.ShapeDtypeStruct((2 * rows // blocks, columns), jnp.bfloat16)
    vmem = pl.BlockSpec(memory_space=pltpu.VMEM)
    return pl.pallas_call(
        add_and_deal_kernel,
        out_shape=(part,) * blocks,
        in_specs=[pl.BlockSpec(memory_space=pltpu.SMEM), vmem, vmem],
        out_specs=(vmem,) * blocks,
        scratch_shapes=[pltpu.VMEM((blocks, *part.shape), jnp.bfloat16)],
        cost_estimate=SHORT,
        compiler_params=pltpu.CompilerParams(vmem_limit_bytes=16 * 1024 * 1024),
    )(plane, near, terms)


def project_kernel(planes, here_ref, slots, w_hbm, *refs):
    came, refs = refs[:planes], refs[planes:]
    home, outs, (parts, w, sem, w_sem) = refs[0], refs[1 : planes + 1], refs[planes + 1 :]
    plane, block = here_ref[0], here_ref[1]
    copies = [pltpu.make_async_copy(w_hbm, w, w_sem)]
    for k in range(planes):
        copies.append(pltpu.make_async_copy(came[k], parts.at[plane ^ block ^ k], sem.at[k]))
    for copy in copies:
        copy.start()
    for copy in copies:
        copy.wait()
    rows = parts.shape[1]
    for p in range(planes):
        home[p * rows : (p + 1) * rows, :] = parts[p]
    n = home.shape[0]
    place = lax.broadcasted_iota(jnp.int32, (n, n), 0)
    place = ((place // rows) ^ plane) * rows + place % rows
    pick = (place == slots[...]).astype(jnp.float32).astype(jnp.bfloat16)
    ordered = jnp.dot(pick, home[...], preferred_element_type=jnp.float32).astype(jnp.bfloat16)
    made = jnp.dot(ordered, w[...], preferred_element_type=jnp.float32).astype(jnp.bfloat16)
    for d in range(planes):
        outs[d][...] = made[d * rows : (d + 1) * rows]


def project(here, slots, w_proj, came):
    planes = len(came)
    rows, columns = came[0].shape
    vmem = pl.BlockSpec(memory_space=pltpu.VMEM)
    made = jax.ShapeDtypeStruct((rows, w_proj.shape[1]), jnp.bfloat16)
    return pl.pallas_call(
        functools.partial(project_kernel, planes),
        out_shape=(jax.ShapeDtypeStruct((planes * rows, columns), jnp.bfloat16), *[made] * planes),
        in_specs=[pl.BlockSpec(memory_space=pltpu.SMEM), vmem]
        + [pl.BlockSpec(memory_space=pl.ANY)] * (1 + planes),
        out_specs=(vmem,) * (1 + planes),
        scratch_shapes=[
            pltpu.VMEM((planes, rows, columns), jnp.bfloat16),
            pltpu.VMEM(w_proj.shape, w_proj.dtype),
            pltpu.SemaphoreType.DMA((planes,)),
            pltpu.SemaphoreType.DMA,
        ],
        cost_estimate=SHORT,
        compiler_params=pltpu.CompilerParams(vmem_limit_bytes=16 * 1024 * 1024),
    )(here, slots, in_hbm(w_proj), *came)


def page_copies(len_ref, kv_hbm, kv_ref, first_sem, sem, at):
    page = kv_ref.shape[1] // PAGES
    rows, first = pl.ds(at, ROW_STEP), pl.ds(0, page)
    out = [
        (
            pltpu.make_async_copy(
                kv_hbm.at[rows, first], kv_ref.at[rows, first], first_sem.at[at // ROW_STEP]
            ),
            None,
            None,
        )
    ]
    for r in range(ROW_STEP):
        for p in range(1, PAGES):
            here = pl.ds(p * page, page)
            copy = pltpu.make_async_copy(
                kv_hbm.at[at + r, here], kv_ref.at[at + r, here], sem.at[at + r, p]
            )
            out.append((copy, len_ref[at + r] > p * page, (at + r, here)))
    return out


def talker_kernel(here_ref, len_ref, gain, *refs):
    w_hbm, terms, refs = refs[:6], refs[6:-11], refs[-11:]
    kv_hbm, new_kv, out_ref, kv_ref, first_sem, sem, w_ref, w_sem, qkv, spreads, gathereds = refs
    block, turn = here_ref[1], here_ref[2]
    blocks = qkv.shape[0]
    rows, cached, kv_width = kv_ref.shape
    width = kv_width // 2
    page = cached // PAGES
    heads = out_ref.shape[1] // HEAD_DIM
    group = heads // blocks
    slot = LANES // ROW_STEP
    sets = spreads.shape[0]
    key, value = group * HEAD_DIM, (group + 1) * HEAD_DIM
    inv = 1.0 / HEAD_DIM**0.5

    half = w_ref.shape[1] // 2
    w_parts = [(w_ref.at[0],), (w_ref.at[1],)]
    for e in (2, 3):
        w_parts.append(
            [
                w_ref.at[e, pl.ds(pl.multiple_of(which * half, half), half)]
                for which in (turn, 1 - turn)
            ]
        )
    w_copies, at = [], 0
    for parts in w_parts:
        w_copies.append([])
        for part in parts:
            w_copies[-1].append(pltpu.make_async_copy(w_hbm[at], part, w_sem.at[at]))
            w_copies[-1][-1].start()
            at += 1

    @pl.loop(0, rows // ROW_STEP)
    def _(i):
        at = pl.multiple_of(i * ROW_STEP, ROW_STEP)
        for copy, needed, _ in page_copies(len_ref, kv_hbm, kv_ref, first_sem, sem, at):
            if needed is None:
                copy.start()
            else:
                pl.when(needed)(copy.start)

    total = terms[0][...].astype(jnp.float32)
    for term in terms[1:]:
        total = total + term[...].astype(jnp.float32)
    scale = lax.rsqrt(jnp.mean(total * total, axis=1, keepdims=True) + 1e-06)
    normed = (total * scale * gain[...]).astype(jnp.bfloat16)
    for e in range(blocks):
        for copy in w_copies[e]:
            copy.wait()
        made = jnp.dot(normed, w_ref[e], preferred_element_type=jnp.float32)
        qkv[e ^ block] = made.astype(jnp.bfloat16).astype(jnp.float32)
    for g in range(blocks):
        for place, start in ((g, key), (blocks + g, value)):
            new_kv[:, place * HEAD_DIM : (place + 1) * HEAD_DIM] = qkv[
                g, :, start : start + HEAD_DIM
            ].astype(jnp.bfloat16)

    spreads[...] = jnp.zeros_like(spreads)
    lane = lax.broadcasted_iota(jnp.int32, (HEAD_DIM, LANES), 1)
    lane_row, lane_block = lane // slot, lane % slot // group
    row_block = lax.broadcasted_iota(jnp.int32, (slot, HEAD_DIM), 0) // group
    own_row = lax.broadcasted_iota(jnp.int32, (ROW_STEP, LANES), 0)

    def scores_of(at, spread):
        here = pl.ds(at, ROW_STEP)
        for h in range(heads):
            g, j = h // group, h % group
            spread[pl.ds(h, ROW_STEP, stride=slot), :] = qkv[
                g, here, j * HEAD_DIM : (j + 1) * HEAD_DIM
            ]
        query = spread[...].T
        by_block = [
            jnp.where(lane_block == g, query, 0.0).astype(jnp.bfloat16) for g in range(blocks)
        ]
        scores = jnp.zeros((cached, LANES), jnp.float32)
        for r in range(ROW_STEP):
            mine = lane_row == r
            right = jnp.concatenate(
                [jnp.where(mine, q, jnp.zeros_like(q)) for q in by_block], axis=0
            )
            scores = scores + jnp.dot(
                kv_ref[at + r, :, :width], right, preferred_element_type=jnp.float32
            )
        own = jnp.zeros((ROW_STEP, LANES), jnp.float32)
        for g in range(blocks):
            new_key = qkv[g, here, key:value].astype(jnp.bfloat16)
            own = own + jnp.dot(new_key, by_block[g], preferred_element_type=jnp.float32)
        own = jnp.where(own_row == lane_row[:ROW_STEP], own, 0.0)
        return scores * inv, jnp.sum(own, axis=0, keepdims=True) * inv

    def softmax(at, scores, own):
        lens = jnp.zeros((1, LANES), jnp.int32)
        for r in range(ROW_STEP):
            lens = jnp.where(lane_row[:1] == r, len_ref[at + r], lens)
        valid = lax.broadcasted_iota(jnp.int32, scores.shape, 0) < lens
        scores = jnp.where(valid, scores, -jnp.inf)
        top = jnp.maximum(jnp.max(scores, axis=0, keepdims=True), own)
        expo = jnp.where(valid, jnp.exp(scores - top), 0.0)
        own_expo = jnp.exp(own - top)
        total = jnp.sum(expo, axis=0, keepdims=True) + own_expo
        probs = (expo / total).T.astype(jnp.bfloat16)
        own_prob = (own_expo / total).astype(jnp.bfloat16).astype(jnp.float32)
        return probs, jnp.broadcast_to(own_prob, (LANES, LANES)).T

    def context(at, probs, own_prob, gathered):
        here = pl.ds(at, ROW_STEP)
        value_rows = qkv.at[:, here, value:]
        for r in range(ROW_STEP):
            lanes = slice(r * slot, (r + 1) * slot)
            made = jnp.dot(
                probs[lanes], kv_ref[at + r, :, width:], preferred_element_type=jnp.float32
            )
            ctx = jnp.zeros((slot, HEAD_DIM), jnp.float32)
            new = jnp.zeros((slot, HEAD_DIM), jnp.float32)
            for g in range(blocks):
                block = made[:, g * HEAD_DIM : (g + 1) * HEAD_DIM]
                ctx = jnp.where(row_block == g, block, ctx)
                new = jnp.where(row_block == g, value_rows[g, r : r + 1, :], new)
            gathered[lanes, :] = ctx + own_prob[lanes] * new
        for h in range(heads):
            out_ref[here, h * HEAD_DIM : (h + 1) * HEAD_DIM] = gathered[
                pl.ds(h, ROW_STEP, stride=slot), :
            ]

    @pl.loop(0, rows // (sets * ROW_STEP))
    def _(i):
        first = pl.multiple_of(i * sets * ROW_STEP, sets * ROW_STEP)
        ats = [pl.multiple_of(first + k * ROW_STEP, ROW_STEP) for k in range(sets)]
        for at in ats:
            for copy, needed, place in page_copies(
                len_ref, kv_hbm, kv_ref, first_sem, sem, at
            ):
                if needed is None:
                    copy.wait()
                    continue
                pl.when(needed)(copy.wait)

                @pl.when(jnp.logical_not(needed))
                def _(place=place):
                    kv_ref[place[0], place[1], :] = jnp.zeros((page, kv_width), kv_ref.dtype)

        scored = [scores_of(at, spreads.at[k]) for k, at in enumerate(ats)]
        weighed = [softmax(at, *s) for at, s in zip(ats, scored)]
        for k, at in enumerate(ats):
            context(at, *weighed[k], gathereds.at[k])


def talker(here, terms, talker_gain, weights, kv_len, kv_cache):
    rows, cached, kv_width = kv_cache.shape
    wide, columns = weights[0].shape
    blocks = 4
    q_width = blocks * columns - kv_width
    sets = 3
    vmem = pl.BlockSpec(memory_space=pltpu.VMEM)
    smem = pl.BlockSpec(memory_space=pltpu.SMEM)
    return pl.pallas_call(
        talker_kernel,
        out_shape=(
            jax.ShapeDtypeStruct((rows, kv_width), jnp.bfloat16),
            jax.ShapeDtypeStruct((rows, q_width), jnp.float32),
        ),
        in_specs=[smem, smem, vmem]
        + [pl.BlockSpec(memory_space=pl.ANY)] * len(weights)
        + [vmem] * len(terms)
        + [pl.BlockSpec(memory_space=pl.ANY)],
        out_specs=(vmem, vmem),
        scratch_shapes=[
            pltpu.VMEM((rows, cached, kv_width), jnp.bfloat16),
            pltpu.SemaphoreType.DMA((rows // ROW_STEP,)),
            pltpu.SemaphoreType.DMA((rows, PAGES)),
            pltpu.VMEM((blocks, wide, columns), jnp.bfloat16),
            pltpu.SemaphoreType.DMA((len(weights),)),
            pltpu.VMEM((blocks, rows, columns), jnp.float32),
            pltpu.VMEM((sets, LANES, HEAD_DIM), jnp.float32),
            pltpu.VMEM((sets, LANES, HEAD_DIM), jnp.float32),
        ],
        cost_estimate=SHORT,
        compiler_params=pltpu.CompilerParams(vmem_limit_bytes=40 * 1024 * 1024),
    )(here, kv_len, talker_gain.reshape(1, wide), *weights, *terms, in_hbm(kv_cache))


def rms_norm(talker_in, talker_gain):
    scale = lax.rsqrt(jnp.mean(talker_in * talker_in, axis=1, keepdims=True) + 1e-06)
    return (talker_in * scale * talker_gain).astype(jnp.bfloat16)


def talker_step(talker_in, talker_gain, w_query, w_key, w_value, kv_len, kv_cache):
    owned = talker_in.shape[0]
    cached = kv_cache.shape[1]
    kv_width = w_key.shape[1]
    head_dim = HEAD_DIM
    kv_heads = kv_width // head_dim
    group = w_query.shape[1] // kv_width
    normed = rms_norm(talker_in, talker_gain)
    query = jnp.dot(normed, w_query, preferred_element_type=jnp.float32).astype(jnp.bfloat16)
    new_key = jnp.dot(normed, w_key, preferred_element_type=jnp.float32).astype(jnp.bfloat16)
    new_value = jnp.dot(normed, w_value, preferred_element_type=jnp.float32).astype(jnp.bfloat16)
    talker_kv = jnp.concatenate([new_key, new_value], axis=1)
    qb = query.reshape(owned, kv_heads, group, head_dim)
    keys = kv_cache[:, :, :kv_width].reshape(owned, cached, kv_heads, head_dim)
    values = kv_cache[:, :, kv_width:].reshape(owned, cached, kv_heads, head_dim)
    nk = new_key.reshape(owned, kv_heads, head_dim)
    nv = new_value.reshape(owned, kv_heads, head_dim)
    inv = 1.0 / head_dim**0.5
    scores = jnp.einsum("rgjd,rpgd->rgjp", qb, keys, preferred_element_type=jnp.float32) * inv
    own = jnp.einsum("rgjd,rgd->rgj", qb, nk, preferred_element_type=jnp.float32) * inv
    valid = (jnp.arange(cached, dtype=jnp.int32)[None, :] < kv_len[:, None])[:, None, None, :]
    scores = jnp.where(valid, scores, -jnp.inf)
    top = jnp.maximum(jnp.max(scores, axis=3), own)
    expo = jnp.where(valid, jnp.exp(scores - top[..., None]), 0.0)
    own_expo = jnp.exp(own - top)
    total = jnp.sum(expo, axis=3) + own_expo
    probs = (expo / total[..., None]).astype(jnp.bfloat16)
    own_prob = (own_expo / total).astype(jnp.bfloat16)
    ctx = jnp.einsum("rgjp,rpgd->rgjd", probs, values, preferred_element_type=jnp.float32)
    ctx = ctx + own_prob.astype(jnp.float32)[..., None] * nv.astype(jnp.float32)[:, :, None, :]
    return (talker_kv, ctx.reshape(owned, w_query.shape[1]))


def any_mesh(
    thinker_act,
    w_think,
    w_proj,
    talker_gain,
    w_query,
    w_key,
    w_value,
    talker_slot,
    kv_len,
    kv_cache,
):
    partial_sums = jnp.dot(
        thinker_act,
        lax.all_gather(w_think, ("section", "rows"), axis=1, tiled=True),
        preferred_element_type=jnp.float32,
    )
    full_query, full_key, full_value = (
        lax.all_gather(w_query, ("section", "rows"), axis=1, tiled=True),
        lax.all_gather(w_key, ("section", "rows"), axis=1, tiled=True),
        lax.all_gather(w_value, ("section", "rows"), axis=1, tiled=True),
    )
    mine = lax.psum_scatter(partial_sums, "mp", scatter_dimension=1, tiled=True)
    thinker_out = mine.astype(jnp.bfloat16)
    order = jnp.argsort(talker_slot[0], stable=True)
    sorted_out = thinker_out[order]
    talker_in = lax.psum_scatter(
        jnp.dot(sorted_out, w_proj, preferred_element_type=jnp.float32),
        "mp",
        scatter_dimension=0,
        tiled=True,
    )
    talker_kv, talker_ctx = talker_step(
        talker_in, talker_gain, full_query, full_key, full_value, kv_len, kv_cache
    )
    return (thinker_out, talker_kv, talker_ctx)


PLANE = ("section", "rows")
GROUP = ("mp", "section", "rows")


def over_core(x):
    return lax.ppermute(x, "rows", [(0, 1), (1, 0)])


def over_section(x):
    return lax.ppermute(x, "section", [(0, 1), (1, 0)])


def over_plane(x, e):
    return lax.ppermute(x, PLANE, [(b, b ^ e) for b in range(4)])


def over_groups(x):
    return lax.ppermute(x, "groups", [(0, 1), (1, 0)])


def after(x, *others):
    return lax.optimization_barrier((x, *others))[0]


def four_planes(
    thinker_act,
    w_think,
    w_proj,
    talker_gain,
    w_query,
    w_key,
    w_value,
    talker_slot,
    kv_len,
    kv_cache,
):
    planes = 4
    g, m, c = lax.axis_index("groups"), lax.axis_index("mp"), lax.axis_index(PLANE)
    here, plane = jnp.stack([m, c, g]), m.reshape(1)

    across, peer = over_section(thinker_act), over_core(thinker_act)
    near = down([in_hbm(thinker_act), peer], w_think, planes)
    near_terms = lax.all_to_all(near, "mp", 0, 0)
    mine = jnp.concatenate([w_query, w_key, w_value], axis=1)
    half = mine.shape[0] // 2
    my_half = lax.dynamic_slice_in_dim(mine, g * half, half, axis=0)

    across, near_terms, mine, my_half = lax.optimization_barrier(
        (across, near_terms, mine, my_half)
    )
    far = down([across, over_core(across)], w_think, planes)
    far_terms = lax.all_to_all(far, "mp", 0, 0)

    my_half = over_section(after(my_half, far))
    near_sums = add(after(near_terms, far))

    came = [
        lax.ppermute(x, GROUP, [(p * 4 + b, b * 4 + (b ^ p ^ k)) for p in range(4) for b in range(4)])
        for k, x in enumerate(add_and_deal(plane, near_sums, far_terms))
    ]
    my_half = after(my_half, near_sums)
    came[0], other_half = lax.optimization_barrier((came[0], over_groups(my_half)))
    thinker_out, *projected = project(here, talker_slot, w_proj, came)
    terms = projected[:1]
    for d in range(1, planes):
        terms.append(lax.ppermute(projected[d], "mp", [(p, p ^ d) for p in range(planes)]))
    other_half = after(other_half, projected[0])
    halves = [my_half, other_half, over_core(my_half), over_core(other_half)]
    weights = [mine, over_core(mine), *halves]
    new_kv, ctx = talker(here, terms, talker_gain, weights, kv_len, kv_cache)
    return (thinker_out, new_kv, ctx)


def solution(mesh):
    in_specs = (
        P(("groups", "section", "rows"), "mp"),
        P("mp", ("section", "rows")),
        P("mp", None),
        P(),
        P(None, ("section", "rows")),
        P(None, ("section", "rows")),
        P(None, ("section", "rows")),
        P(("groups", "section", "rows"), None),
        P(("groups", "mp", "section", "rows")),
        P(("groups", "mp", "section", "rows"), None, None),
    )
    out_specs = (
        P(("groups", "section", "rows"), "mp"),
        P(("groups", "mp", "section", "rows"), None),
        P(("groups", "mp", "section", "rows"), None),
    )
    sizes = tuple(mesh.shape[a] for a in ("groups", "section", "rows", "mp"))
    shards = four_planes if sizes == (2, 2, 2, 4) else any_mesh
    return jax.shard_map(shards, mesh=mesh, in_specs=in_specs, out_specs=out_specs, check_vma=False)
```

```python
import functools

import jax
import jax.numpy as jnp
from jax import lax
from jax.experimental import pallas as pl
from jax.experimental.pallas import tpu as pltpu
from jax.sharding import PartitionSpec as P

HEAD_DIM = 128
ROW_STEP = 8
LANES = 128
PAGES = 2
SHORT = pl.CostEstimate(flops=1, bytes_accessed=1, transcendentals=0)


def in_hbm(x):
    return pltpu.with_memory_space_constraint(x, pltpu.HBM)


def down_kernel(planes, cuts, groups, *refs):
    xs, (w, out, x_all, w_all, acc, x_sem, w_sem) = refs[:groups], refs[groups:]
    n = xs[0].shape[0]
    loads = []
    for s, (lo, hi) in enumerate(cuts):
        deep = pl.ds(lo, hi - lo)
        copies = [pltpu.make_async_copy(w.at[deep], w_all.at[deep], w_sem.at[s])]
        for i in range(groups):
            copies.append(
                pltpu.make_async_copy(
                    xs[i].at[:, deep], x_all.at[pl.ds(i * n, n), deep], x_sem.at[s, i]
                )
            )
        for copy in copies:
            copy.start()
        loads.append(copies)
    for s, (lo, hi) in enumerate(cuts):
        for copy in loads[s]:
            copy.wait()
        part = jnp.dot(x_all[:, lo:hi], w_all[lo:hi, :], preferred_element_type=jnp.float32)
        acc[...] = part if s == 0 else acc[...] + part
    part = n // planes
    for i in range(groups):
        for p in range(planes):
            at = i * n + p * part
            out[p, i * part : (i + 1) * part, :] = acc[at : at + part, :].astype(out.dtype)


def down(xs, w, planes):
    depth, columns = w.shape
    groups, n = len(xs), xs[0].shape[0]
    tiles, parts = depth // LANES, 6
    ends = [LANES * (tiles * i // parts) for i in range(parts)] + [depth]
    return pl.pallas_call(
        functools.partial(down_kernel, planes, list(zip(ends[:-1], ends[1:])), groups),
        out_shape=jax.ShapeDtypeStruct((planes, groups * n // planes, columns), jnp.bfloat16),
        in_specs=[pl.BlockSpec(memory_space=pl.ANY)] * (groups + 1),
        out_specs=pl.BlockSpec(memory_space=pltpu.VMEM),
        scratch_shapes=[
            pltpu.VMEM((groups * n, depth), jnp.bfloat16),
            pltpu.VMEM((depth, columns), jnp.bfloat16),
            pltpu.VMEM((groups * n, columns), jnp.float32),
            pltpu.SemaphoreType.DMA((parts, groups)),
            pltpu.SemaphoreType.DMA((parts,)),
        ],
        cost_estimate=SHORT,
        compiler_params=pltpu.CompilerParams(vmem_limit_bytes=24 * 1024 * 1024),
    )(*xs, in_hbm(w))


def add_kernel(terms, out):
    total = terms[0].astype(jnp.float32)
    for k in range(1, terms.shape[0]):
        total = total + terms[k].astype(jnp.float32)
    out[...] = total.astype(jnp.bfloat16)


def add(terms):
    vmem = pl.BlockSpec(memory_space=pltpu.VMEM)
    return pl.pallas_call(
        add_kernel,
        out_shape=jax.ShapeDtypeStruct(terms.shape[1:], jnp.bfloat16),
        in_specs=[vmem],
        out_specs=vmem,
        cost_estimate=SHORT,
        compiler_params=pltpu.CompilerParams(vmem_limit_bytes=16 * 1024 * 1024),
    )(terms)


def add_and_deal_kernel(plane_ref, near, terms, *refs):
    outs, sums = refs[:-1], refs[-1]
    total = terms[0].astype(jnp.float32)
    for k in range(1, terms.shape[0]):
        total = total + terms[k].astype(jnp.float32)
    rows = sums.shape[1]
    half = sums.shape[0] // 2
    for e in range(half):
        sums[e] = near[e * rows : (e + 1) * rows, :]
        sums[half + e] = total[e * rows : (e + 1) * rows].astype(jnp.bfloat16)
    low = plane_ref[0] & 1
    for k, out in enumerate(outs):
        section = (plane_ref[0] // 2) ^ k
        out[0] = sums[2 * section + low]
        out[1] = sums[2 * section + 1 - low]


def add_and_deal(plane, near, terms):
    rows, columns = near.shape
    blocks = 4
    pair = jax.ShapeDtypeStruct((2, 2 * rows // blocks, columns), jnp.bfloat16)
    vmem = pl.BlockSpec(memory_space=pltpu.VMEM)
    return pl.pallas_call(
        add_and_deal_kernel,
        out_shape=(pair,) * 2,
        in_specs=[pl.BlockSpec(memory_space=pltpu.SMEM), vmem, vmem],
        out_specs=(vmem,) * 2,
        scratch_shapes=[pltpu.VMEM((blocks, *pair.shape[1:]), jnp.bfloat16)],
        cost_estimate=SHORT,
        compiler_params=pltpu.CompilerParams(vmem_limit_bytes=16 * 1024 * 1024),
    )(plane, near, terms)


def project_kernel(planes, here_ref, slots, w_hbm, *refs):
    came, refs = refs[:planes], refs[planes:]
    home, outs, (parts, w, sem, w_sem) = refs[0], refs[1 : planes + 1], refs[planes + 1 :]
    plane, block = here_ref[0], here_ref[1]
    copies = [pltpu.make_async_copy(w_hbm, w, w_sem)]
    for k in range(planes):
        mine = came[k].at[k % 2]
        copies.append(pltpu.make_async_copy(mine, parts.at[plane ^ block ^ k], sem.at[k]))
    for copy in copies:
        copy.start()
    for copy in copies:
        copy.wait()
    rows = parts.shape[1]
    for p in range(planes):
        home[p * rows : (p + 1) * rows, :] = parts[p]
    n = home.shape[0]
    place = lax.broadcasted_iota(jnp.int32, (n, n), 0)
    place = ((place // rows) ^ plane) * rows + place % rows
    pick = (place == slots[...]).astype(jnp.float32).astype(jnp.bfloat16)
    ordered = jnp.dot(pick, home[...], preferred_element_type=jnp.float32).astype(jnp.bfloat16)
    made = jnp.dot(ordered, w[...], preferred_element_type=jnp.float32).astype(jnp.bfloat16)
    for d in range(planes):
        outs[d][...] = made[d * rows : (d + 1) * rows]


def project(here, slots, w_proj, came):
    planes = len(came)
    _, rows, columns = came[0].shape
    vmem = pl.BlockSpec(memory_space=pltpu.VMEM)
    made = jax.ShapeDtypeStruct((rows, w_proj.shape[1]), jnp.bfloat16)
    return pl.pallas_call(
        functools.partial(project_kernel, planes),
        out_shape=(jax.ShapeDtypeStruct((planes * rows, columns), jnp.bfloat16), *[made] * planes),
        in_specs=[pl.BlockSpec(memory_space=pltpu.SMEM), vmem]
        + [pl.BlockSpec(memory_space=pl.ANY)] * (1 + planes),
        out_specs=(vmem,) * (1 + planes),
        scratch_shapes=[
            pltpu.VMEM((planes, rows, columns), jnp.bfloat16),
            pltpu.VMEM(w_proj.shape, w_proj.dtype),
            pltpu.SemaphoreType.DMA((planes,)),
            pltpu.SemaphoreType.DMA,
        ],
        cost_estimate=SHORT,
        compiler_params=pltpu.CompilerParams(vmem_limit_bytes=16 * 1024 * 1024),
    )(here, slots, in_hbm(w_proj), *came)


def page_copies(len_ref, kv_hbm, kv_ref, sem, r):
    page = kv_ref.shape[1] // PAGES
    out = []
    for p in range(PAGES):
        at = pl.ds(p * page, page)
        copy = pltpu.make_async_copy(kv_hbm.at[r, at], kv_ref.at[r, at], sem.at[r, p])
        out.append((copy, len_ref[r] > p * page))
    return out


def talker_kernel(here_ref, len_ref, gain, *refs):
    w_hbm, terms, refs = refs[:6], refs[6:-10], refs[-10:]
    kv_hbm, new_kv, out_ref, kv_ref, sem, w_ref, w_sem, qkv, spreads, gathereds = refs
    block, turn = here_ref[1], here_ref[2]
    blocks = qkv.shape[0]
    rows, cached, kv_width = kv_ref.shape
    width = kv_width // 2
    page = cached // PAGES
    heads = out_ref.shape[1] // HEAD_DIM
    group = heads // blocks
    slot = LANES // ROW_STEP
    sets = spreads.shape[0]
    key, value = group * HEAD_DIM, (group + 1) * HEAD_DIM
    inv = 1.0 / HEAD_DIM**0.5

    half = w_ref.shape[1] // 2
    w_parts = [(w_ref.at[0],), (w_ref.at[1],)]
    for e in (2, 3):
        w_parts.append(
            [
                w_ref.at[e, pl.ds(pl.multiple_of(which * half, half), half)]
                for which in (turn, 1 - turn)
            ]
        )
    w_copies, at = [], 0
    for parts in w_parts:
        w_copies.append([])
        for part in parts:
            w_copies[-1].append(pltpu.make_async_copy(w_hbm[at], part, w_sem.at[at]))
            w_copies[-1][-1].start()
            at += 1

    @pl.loop(0, rows)
    def _(r):
        for p, (copy, needed) in enumerate(page_copies(len_ref, kv_hbm, kv_ref, sem, r)):
            if p == 0:
                copy.start()
            else:
                pl.when(needed)(copy.start)

    total = terms[0][...].astype(jnp.float32)
    for term in terms[1:]:
        total = total + term[...].astype(jnp.float32)
    scale = lax.rsqrt(jnp.mean(total * total, axis=1, keepdims=True) + 1e-06)
    normed = (total * scale * gain[...]).astype(jnp.bfloat16)
    for e in range(blocks):
        for copy in w_copies[e]:
            copy.wait()
        made = jnp.dot(normed, w_ref[e], preferred_element_type=jnp.float32)
        qkv[e ^ block] = made.astype(jnp.bfloat16).astype(jnp.float32)
    for g in range(blocks):
        for place, start in ((g, key), (blocks + g, value)):
            new_kv[:, place * HEAD_DIM : (place + 1) * HEAD_DIM] = qkv[
                g, :, start : start + HEAD_DIM
            ].astype(jnp.bfloat16)

    spreads[...] = jnp.zeros_like(spreads)
    lane = lax.broadcasted_iota(jnp.int32, (HEAD_DIM, LANES), 1)
    lane_row, lane_block = lane // slot, lane % slot // group
    row_block = lax.broadcasted_iota(jnp.int32, (slot, HEAD_DIM), 0) // group
    own_row = lax.broadcasted_iota(jnp.int32, (ROW_STEP, LANES), 0)

    def scores_of(at, spread):
        here = pl.ds(at, ROW_STEP)
        for h in range(heads):
            g, j = h // group, h % group
            spread[pl.ds(h, ROW_STEP, stride=slot), :] = qkv[
                g, here, j * HEAD_DIM : (j + 1) * HEAD_DIM
            ]
        query = spread[...].T
        by_block = [
            jnp.where(lane_block == g, query, 0.0).astype(jnp.bfloat16) for g in range(blocks)
        ]
        scores = jnp.zeros((cached, LANES), jnp.float32)
        for r in range(ROW_STEP):
            mine = lane_row == r
            right = jnp.concatenate(
                [jnp.where(mine, q, jnp.zeros_like(q)) for q in by_block], axis=0
            )
            scores = scores + jnp.dot(
                kv_ref[at + r, :, :width], right, preferred_element_type=jnp.float32
            )
        own = jnp.zeros((ROW_STEP, LANES), jnp.float32)
        for g in range(blocks):
            new_key = qkv[g, here, key:value].astype(jnp.bfloat16)
            own = own + jnp.dot(new_key, by_block[g], preferred_element_type=jnp.float32)
        own = jnp.where(own_row == lane_row[:ROW_STEP], own, 0.0)
        return scores * inv, jnp.sum(own, axis=0, keepdims=True) * inv

    def softmax(at, scores, own):
        lens = jnp.zeros((1, LANES), jnp.int32)
        for r in range(ROW_STEP):
            lens = jnp.where(lane_row[:1] == r, len_ref[at + r], lens)
        valid = lax.broadcasted_iota(jnp.int32, scores.shape, 0) < lens
        scores = jnp.where(valid, scores, -jnp.inf)
        top = jnp.maximum(jnp.max(scores, axis=0, keepdims=True), own)
        expo = jnp.where(valid, jnp.exp(scores - top), 0.0)
        own_expo = jnp.exp(own - top)
        total = jnp.sum(expo, axis=0, keepdims=True) + own_expo
        probs = (expo / total).T.astype(jnp.bfloat16)
        own_prob = (own_expo / total).astype(jnp.bfloat16).astype(jnp.float32)
        return probs, jnp.broadcast_to(own_prob, (LANES, LANES)).T

    def context(at, probs, own_prob, gathered):
        here = pl.ds(at, ROW_STEP)
        value_rows = qkv.at[:, here, value:]
        for r in range(ROW_STEP):
            lanes = slice(r * slot, (r + 1) * slot)
            made = jnp.dot(
                probs[lanes], kv_ref[at + r, :, width:], preferred_element_type=jnp.float32
            )
            ctx = jnp.zeros((slot, HEAD_DIM), jnp.float32)
            new = jnp.zeros((slot, HEAD_DIM), jnp.float32)
            for g in range(blocks):
                block = made[:, g * HEAD_DIM : (g + 1) * HEAD_DIM]
                ctx = jnp.where(row_block == g, block, ctx)
                new = jnp.where(row_block == g, value_rows[g, r : r + 1, :], new)
            gathered[lanes, :] = ctx + own_prob[lanes] * new
        for h in range(heads):
            out_ref[here, h * HEAD_DIM : (h + 1) * HEAD_DIM] = gathered[
                pl.ds(h, ROW_STEP, stride=slot), :
            ]

    @pl.loop(0, rows // (sets * ROW_STEP))
    def _(i):
        first = pl.multiple_of(i * sets * ROW_STEP, sets * ROW_STEP)
        for k in range(sets * ROW_STEP):
            r = first + k
            for p, (copy, needed) in enumerate(page_copies(len_ref, kv_hbm, kv_ref, sem, r)):
                if p == 0:
                    copy.wait()
                    continue
                pl.when(needed)(copy.wait)

                @pl.when(jnp.logical_not(needed))
                def _(p=p, r=r):
                    kv_ref[r, p * page : (p + 1) * page, :] = jnp.zeros(
                        (page, kv_width), kv_ref.dtype
                    )

        ats = [pl.multiple_of(first + k * ROW_STEP, ROW_STEP) for k in range(sets)]
        scored = [scores_of(at, spreads.at[k]) for k, at in enumerate(ats)]
        weighed = [softmax(at, *s) for at, s in zip(ats, scored)]
        for k, at in enumerate(ats):
            context(at, *weighed[k], gathereds.at[k])


def talker(here, terms, talker_gain, weights, kv_len, kv_cache):
    rows, cached, kv_width = kv_cache.shape
    wide, columns = weights[0].shape
    blocks = 4
    q_width = blocks * columns - kv_width
    sets = 2
    vmem = pl.BlockSpec(memory_space=pltpu.VMEM)
    smem = pl.BlockSpec(memory_space=pltpu.SMEM)
    return pl.pallas_call(
        talker_kernel,
        out_shape=(
            jax.ShapeDtypeStruct((rows, kv_width), jnp.bfloat16),
            jax.ShapeDtypeStruct((rows, q_width), jnp.float32),
        ),
        in_specs=[smem, smem, vmem]
        + [pl.BlockSpec(memory_space=pl.ANY)] * len(weights)
        + [vmem] * len(terms)
        + [pl.BlockSpec(memory_space=pl.ANY)],
        out_specs=(vmem, vmem),
        scratch_shapes=[
            pltpu.VMEM((rows, cached, kv_width), jnp.bfloat16),
            pltpu.SemaphoreType.DMA((rows, PAGES)),
            pltpu.VMEM((blocks, wide, columns), jnp.bfloat16),
            pltpu.SemaphoreType.DMA((len(weights),)),
            pltpu.VMEM((blocks, rows, columns), jnp.float32),
            pltpu.VMEM((sets, LANES, HEAD_DIM), jnp.float32),
            pltpu.VMEM((sets, LANES, HEAD_DIM), jnp.float32),
        ],
        cost_estimate=SHORT,
        compiler_params=pltpu.CompilerParams(vmem_limit_bytes=40 * 1024 * 1024),
    )(here, kv_len, talker_gain.reshape(1, wide), *weights, *terms, in_hbm(kv_cache))


def rms_norm(talker_in, talker_gain):
    scale = lax.rsqrt(jnp.mean(talker_in * talker_in, axis=1, keepdims=True) + 1e-06)
    return (talker_in * scale * talker_gain).astype(jnp.bfloat16)


def talker_step(talker_in, talker_gain, w_query, w_key, w_value, kv_len, kv_cache):
    owned = talker_in.shape[0]
    cached = kv_cache.shape[1]
    kv_width = w_key.shape[1]
    head_dim = HEAD_DIM
    kv_heads = kv_width // head_dim
    group = w_query.shape[1] // kv_width
    normed = rms_norm(talker_in, talker_gain)
    query = jnp.dot(normed, w_query, preferred_element_type=jnp.float32).astype(jnp.bfloat16)
    new_key = jnp.dot(normed, w_key, preferred_element_type=jnp.float32).astype(jnp.bfloat16)
    new_value = jnp.dot(normed, w_value, preferred_element_type=jnp.float32).astype(jnp.bfloat16)
    talker_kv = jnp.concatenate([new_key, new_value], axis=1)
    qb = query.reshape(owned, kv_heads, group, head_dim)
    keys = kv_cache[:, :, :kv_width].reshape(owned, cached, kv_heads, head_dim)
    values = kv_cache[:, :, kv_width:].reshape(owned, cached, kv_heads, head_dim)
    nk = new_key.reshape(owned, kv_heads, head_dim)
    nv = new_value.reshape(owned, kv_heads, head_dim)
    inv = 1.0 / head_dim**0.5
    scores = jnp.einsum("rgjd,rpgd->rgjp", qb, keys, preferred_element_type=jnp.float32) * inv
    own = jnp.einsum("rgjd,rgd->rgj", qb, nk, preferred_element_type=jnp.float32) * inv
    valid = (jnp.arange(cached, dtype=jnp.int32)[None, :] < kv_len[:, None])[:, None, None, :]
    scores = jnp.where(valid, scores, -jnp.inf)
    top = jnp.maximum(jnp.max(scores, axis=3), own)
    expo = jnp.where(valid, jnp.exp(scores - top[..., None]), 0.0)
    own_expo = jnp.exp(own - top)
    total = jnp.sum(expo, axis=3) + own_expo
    probs = (expo / total[..., None]).astype(jnp.bfloat16)
    own_prob = (own_expo / total).astype(jnp.bfloat16)
    ctx = jnp.einsum("rgjp,rpgd->rgjd", probs, values, preferred_element_type=jnp.float32)
    ctx = ctx + own_prob.astype(jnp.float32)[..., None] * nv.astype(jnp.float32)[:, :, None, :]
    return (talker_kv, ctx.reshape(owned, w_query.shape[1]))


def any_mesh(
    thinker_act,
    w_think,
    w_proj,
    talker_gain,
    w_query,
    w_key,
    w_value,
    talker_slot,
    kv_len,
    kv_cache,
):
    partial_sums = jnp.dot(
        thinker_act,
        lax.all_gather(w_think, ("section", "rows"), axis=1, tiled=True),
        preferred_element_type=jnp.float32,
    )
    full_query, full_key, full_value = (
        lax.all_gather(w_query, ("section", "rows"), axis=1, tiled=True),
        lax.all_gather(w_key, ("section", "rows"), axis=1, tiled=True),
        lax.all_gather(w_value, ("section", "rows"), axis=1, tiled=True),
    )
    mine = lax.psum_scatter(partial_sums, "mp", scatter_dimension=1, tiled=True)
    thinker_out = mine.astype(jnp.bfloat16)
    order = jnp.argsort(talker_slot[0], stable=True)
    sorted_out = thinker_out[order]
    talker_in = lax.psum_scatter(
        jnp.dot(sorted_out, w_proj, preferred_element_type=jnp.float32),
        "mp",
        scatter_dimension=0,
        tiled=True,
    )
    talker_kv, talker_ctx = talker_step(
        talker_in, talker_gain, full_query, full_key, full_value, kv_len, kv_cache
    )
    return (thinker_out, talker_kv, talker_ctx)


PLANE = ("section", "rows")
GROUP = ("mp", "section", "rows")


def over_core(x):
    return lax.ppermute(x, "rows", [(0, 1), (1, 0)])


def over_section(x):
    return lax.ppermute(x, "section", [(0, 1), (1, 0)])


def over_plane(x, e):
    return lax.ppermute(x, PLANE, [(b, b ^ e) for b in range(4)])


def over_groups(x):
    return lax.ppermute(x, "groups", [(0, 1), (1, 0)])


def after(x, *others):
    return lax.optimization_barrier((x, *others))[0]


def four_planes(
    thinker_act,
    w_think,
    w_proj,
    talker_gain,
    w_query,
    w_key,
    w_value,
    talker_slot,
    kv_len,
    kv_cache,
):
    planes = 4
    g, m, c = lax.axis_index("groups"), lax.axis_index("mp"), lax.axis_index(PLANE)
    here, plane = jnp.stack([m, c, g]), m.reshape(1)

    across, peer = over_section(thinker_act), over_core(thinker_act)
    near = down([in_hbm(thinker_act), peer], w_think, planes)
    near_terms = lax.all_to_all(near, "mp", 0, 0)
    mine = jnp.concatenate([w_query, w_key, w_value], axis=1)
    half = mine.shape[0] // 2
    my_half = lax.dynamic_slice_in_dim(mine, g * half, half, axis=0)

    across, near_terms, mine, my_half = lax.optimization_barrier(
        (across, near_terms, mine, my_half)
    )
    far = down([across, over_core(across)], w_think, planes)
    far_terms = lax.all_to_all(far, "mp", 0, 0)

    my_half = over_section(after(my_half, far))
    near_sums = add(after(near_terms, far))

    came = []
    for k, pair in enumerate(add_and_deal(plane, near_sums, far_terms)):
        route = [(p * 4 + b, b * 4 + (b ^ p ^ (2 * k))) for p in range(4) for b in range(4)]
        pair = lax.ppermute(pair, GROUP, route)
        came += [pair, over_core(pair)]
    my_half = after(my_half, near_sums)
    came[0], other_half = lax.optimization_barrier((came[0], over_groups(my_half)))
    thinker_out, *projected = project(here, talker_slot, w_proj, came)
    terms = projected[:1]
    for d in range(1, planes):
        terms.append(lax.ppermute(projected[d], "mp", [(p, p ^ d) for p in range(planes)]))
    other_half = after(other_half, projected[0])
    halves = [my_half, other_half, over_core(my_half), over_core(other_half)]
    weights = [mine, over_core(mine), *halves]
    new_kv, ctx = talker(here, terms, talker_gain, weights, kv_len, kv_cache)
    return (thinker_out, new_kv, ctx)


def solution(mesh):
    in_specs = (
        P(("groups", "section", "rows"), "mp"),
        P("mp", ("section", "rows")),
        P("mp", None),
        P(),
        P(None, ("section", "rows")),
        P(None, ("section", "rows")),
        P(None, ("section", "rows")),
        P(("groups", "section", "rows"), None),
        P(("groups", "mp", "section", "rows")),
        P(("groups", "mp", "section", "rows"), None, None),
    )
    out_specs = (
        P(("groups", "section", "rows"), "mp"),
        P(("groups", "mp", "section", "rows"), None),
        P(("groups", "mp", "section", "rows"), None),
    )
    sizes = tuple(mesh.shape[a] for a in ("groups", "section", "rows", "mp"))
    shards = four_planes if sizes == (2, 2, 2, 4) else any_mesh
    return jax.shard_map(shards, mesh=mesh, in_specs=in_specs, out_specs=out_specs, check_vma=False)
```

```python
import functools

import jax
import jax.numpy as jnp
from jax import lax
from jax.experimental import pallas as pl
from jax.experimental.pallas import tpu as pltpu
from jax.sharding import PartitionSpec as P

HEAD_DIM = 128
ROW_STEP = 8
LANES = 128
PAGES = 2
SHORT = pl.CostEstimate(flops=1, bytes_accessed=1, transcendentals=0)


def in_hbm(x):
    return pltpu.with_memory_space_constraint(x, pltpu.HBM)


def down_kernel(planes, cuts, groups, *refs):
    xs, (w, out, x_all, w_all, acc, x_sem, w_sem) = refs[:groups], refs[groups:]
    n = xs[0].shape[0]
    loads = []
    for s, (lo, hi) in enumerate(cuts):
        deep = pl.ds(lo, hi - lo)
        copies = [pltpu.make_async_copy(w.at[deep], w_all.at[deep], w_sem.at[s])]
        for i in range(groups):
            copies.append(
                pltpu.make_async_copy(
                    xs[i].at[:, deep], x_all.at[pl.ds(i * n, n), deep], x_sem.at[s, i]
                )
            )
        for copy in copies:
            copy.start()
        loads.append(copies)
    for s, (lo, hi) in enumerate(cuts):
        for copy in loads[s]:
            copy.wait()
        part = jnp.dot(x_all[:, lo:hi], w_all[lo:hi, :], preferred_element_type=jnp.float32)
        acc[...] = part if s == 0 else acc[...] + part
    part = n // planes
    for i in range(groups):
        for p in range(planes):
            at = i * n + p * part
            out[p, i * part : (i + 1) * part, :] = acc[at : at + part, :].astype(out.dtype)


def down(xs, w, planes):
    depth, columns = w.shape
    groups, n = len(xs), xs[0].shape[0]
    tiles, parts = depth // LANES, 6
    ends = [LANES * (tiles * i // parts) for i in range(parts)] + [depth]
    return pl.pallas_call(
        functools.partial(down_kernel, planes, list(zip(ends[:-1], ends[1:])), groups),
        out_shape=jax.ShapeDtypeStruct((planes, groups * n // planes, columns), jnp.bfloat16),
        in_specs=[pl.BlockSpec(memory_space=pl.ANY)] * (groups + 1),
        out_specs=pl.BlockSpec(memory_space=pltpu.VMEM),
        scratch_shapes=[
            pltpu.VMEM((groups * n, depth), jnp.bfloat16),
            pltpu.VMEM((depth, columns), jnp.bfloat16),
            pltpu.VMEM((groups * n, columns), jnp.float32),
            pltpu.SemaphoreType.DMA((parts, groups)),
            pltpu.SemaphoreType.DMA((parts,)),
        ],
        cost_estimate=SHORT,
        compiler_params=pltpu.CompilerParams(vmem_limit_bytes=24 * 1024 * 1024),
    )(*xs, in_hbm(w))


def add_kernel(terms, out):
    total = terms[0].astype(jnp.float32)
    for k in range(1, terms.shape[0]):
        total = total + terms[k].astype(jnp.float32)
    out[...] = total.astype(jnp.bfloat16)


def add(terms):
    vmem = pl.BlockSpec(memory_space=pltpu.VMEM)
    return pl.pallas_call(
        add_kernel,
        out_shape=jax.ShapeDtypeStruct(terms.shape[1:], jnp.bfloat16),
        in_specs=[vmem],
        out_specs=vmem,
        cost_estimate=SHORT,
        compiler_params=pltpu.CompilerParams(vmem_limit_bytes=16 * 1024 * 1024),
    )(terms)


def add_and_deal_kernel(plane_ref, near, terms, *refs):
    outs, sums = refs[:-1], refs[-1]
    total = terms[0].astype(jnp.float32)
    for k in range(1, terms.shape[0]):
        total = total + terms[k].astype(jnp.float32)
    rows = sums.shape[1]
    half = len(outs) // 2
    for e in range(half):
        sums[e] = near[e * rows : (e + 1) * rows, :]
        sums[half + e] = total[e * rows : (e + 1) * rows].astype(jnp.bfloat16)
    for k, out in enumerate(outs):
        out[...] = sums[plane_ref[0] ^ k]


def add_and_deal(plane, near, terms):
    rows, columns = near.shape
    blocks = 4
    part = jax.ShapeDtypeStruct((2 * rows // blocks, columns), jnp.bfloat16)
    vmem = pl.BlockSpec(memory_space=pltpu.VMEM)
    return pl.pallas_call(
        add_and_deal_kernel,
        out_shape=(part,) * blocks,
        in_specs=[pl.BlockSpec(memory_space=pltpu.SMEM), vmem, vmem],
        out_specs=(vmem,) * blocks,
        scratch_shapes=[pltpu.VMEM((blocks, *part.shape), jnp.bfloat16)],
        cost_estimate=SHORT,
        compiler_params=pltpu.CompilerParams(vmem_limit_bytes=16 * 1024 * 1024),
    )(plane, near, terms)


def project_kernel(planes, here_ref, slots, w_hbm, *refs):
    came, refs = refs[:planes], refs[planes:]
    home, outs, (parts, w, sem, w_sem) = refs[0], refs[1 : planes + 1], refs[planes + 1 :]
    plane, block = here_ref[0], here_ref[1]
    copies = [pltpu.make_async_copy(w_hbm, w, w_sem)]
    for k in range(planes):
        copies.append(pltpu.make_async_copy(came[k], parts.at[plane ^ block ^ k], sem.at[k]))
    for copy in copies:
        copy.start()
    for copy in copies:
        copy.wait()
    rows = parts.shape[1]
    for p in range(planes):
        home[p * rows : (p + 1) * rows, :] = parts[p]
    n = home.shape[0]
    place = lax.broadcasted_iota(jnp.int32, (n, n), 0)
    place = ((place // rows) ^ plane) * rows + place % rows
    pick = (place == slots[...]).astype(jnp.float32).astype(jnp.bfloat16)
    ordered = jnp.dot(pick, home[...], preferred_element_type=jnp.float32).astype(jnp.bfloat16)
    made = jnp.dot(ordered, w[...], preferred_element_type=jnp.float32).astype(jnp.bfloat16)
    for d in range(planes):
        outs[d][...] = made[d * rows : (d + 1) * rows]


def project(here, slots, w_proj, came):
    planes = len(came)
    rows, columns = came[0].shape
    vmem = pl.BlockSpec(memory_space=pltpu.VMEM)
    made = jax.ShapeDtypeStruct((rows, w_proj.shape[1]), jnp.bfloat16)
    return pl.pallas_call(
        functools.partial(project_kernel, planes),
        out_shape=(jax.ShapeDtypeStruct((planes * rows, columns), jnp.bfloat16), *[made] * planes),
        in_specs=[pl.BlockSpec(memory_space=pltpu.SMEM), vmem]
        + [pl.BlockSpec(memory_space=pl.ANY)] * (1 + planes),
        out_specs=(vmem,) * (1 + planes),
        scratch_shapes=[
            pltpu.VMEM((planes, rows, columns), jnp.bfloat16),
            pltpu.VMEM(w_proj.shape, w_proj.dtype),
            pltpu.SemaphoreType.DMA((planes,)),
            pltpu.SemaphoreType.DMA,
        ],
        cost_estimate=SHORT,
        compiler_params=pltpu.CompilerParams(vmem_limit_bytes=16 * 1024 * 1024),
    )(here, slots, in_hbm(w_proj), *came)


def page_copies(len_ref, kv_hbm, kv_ref, sem, r):
    page = kv_ref.shape[1] // PAGES
    out = []
    for p in range(PAGES):
        at = pl.ds(p * page, page)
        copy = pltpu.make_async_copy(kv_hbm.at[r, at], kv_ref.at[r, at], sem.at[r, p])
        out.append((copy, len_ref[r] > p * page))
    return out


def stage_kernel(len_ref, kv_hbm, kv_ref, sem):
    rows, cached, kv_width = kv_ref.shape
    page = cached // PAGES

    @pl.loop(0, rows)
    def _(r):
        for p, (copy, needed) in enumerate(page_copies(len_ref, kv_hbm, kv_ref, sem, r)):
            if p == 0:
                copy.start()
            else:
                pl.when(needed)(copy.start)

                @pl.when(jnp.logical_not(needed))
                def _(p=p, r=r):
                    kv_ref[r, p * page : (p + 1) * page, :] = jnp.zeros(
                        (page, kv_width), kv_ref.dtype
                    )

    @pl.loop(0, rows)
    def _(r):
        for p, (copy, needed) in enumerate(page_copies(len_ref, kv_hbm, kv_ref, sem, r)):
            if p == 0:
                copy.wait()
            else:
                pl.when(needed)(copy.wait)


def stage(kv_len, kv_cache):
    return pl.pallas_call(
        stage_kernel,
        out_shape=pltpu.VMEM(kv_cache.shape, kv_cache.dtype),
        in_specs=[pl.BlockSpec(memory_space=pltpu.SMEM), pl.BlockSpec(memory_space=pl.ANY)],
        out_specs=pl.BlockSpec(memory_space=pltpu.VMEM),
        scratch_shapes=[pltpu.SemaphoreType.DMA((kv_cache.shape[0], PAGES))],
        cost_estimate=SHORT,
        compiler_params=pltpu.CompilerParams(vmem_limit_bytes=8 * 1024 * 1024),
    )(kv_len, in_hbm(kv_cache))


def talker_kernel(here_ref, len_ref, gain, *refs):
    w_hbm, terms, refs = refs[:6], refs[6:-8], refs[-8:]
    kv_ref, new_kv, out_ref, w_ref, w_sem, qkv, spreads, gathereds = refs
    block, turn = here_ref[1], here_ref[2]
    blocks = qkv.shape[0]
    rows, cached, kv_width = kv_ref.shape
    width = kv_width // 2
    heads = out_ref.shape[1] // HEAD_DIM
    group = heads // blocks
    slot = LANES // ROW_STEP
    sets = spreads.shape[0]
    key, value = group * HEAD_DIM, (group + 1) * HEAD_DIM
    inv = 1.0 / HEAD_DIM**0.5

    half = w_ref.shape[1] // 2
    w_parts = [(w_ref.at[0],), (w_ref.at[1],)]
    for e in (2, 3):
        w_parts.append(
            [
                w_ref.at[e, pl.ds(pl.multiple_of(which * half, half), half)]
                for which in (turn, 1 - turn)
            ]
        )
    w_copies, at = [], 0
    for parts in w_parts:
        w_copies.append([])
        for part in parts:
            w_copies[-1].append(pltpu.make_async_copy(w_hbm[at], part, w_sem.at[at]))
            w_copies[-1][-1].start()
            at += 1

    total = terms[0][...].astype(jnp.float32)
    for term in terms[1:]:
        total = total + term[...].astype(jnp.float32)
    scale = lax.rsqrt(jnp.mean(total * total, axis=1, keepdims=True) + 1e-06)
    normed = (total * scale * gain[...]).astype(jnp.bfloat16)
    for e in range(blocks):
        for copy in w_copies[e]:
            copy.wait()
        made = jnp.dot(normed, w_ref[e], preferred_element_type=jnp.float32)
        qkv[e ^ block] = made.astype(jnp.bfloat16).astype(jnp.float32)
    for g in range(blocks):
        for place, start in ((g, key), (blocks + g, value)):
            new_kv[:, place * HEAD_DIM : (place + 1) * HEAD_DIM] = qkv[
                g, :, start : start + HEAD_DIM
            ].astype(jnp.bfloat16)

    spreads[...] = jnp.zeros_like(spreads)
    lane = lax.broadcasted_iota(jnp.int32, (HEAD_DIM, LANES), 1)
    lane_row, lane_block = lane // slot, lane % slot // group
    row_block = lax.broadcasted_iota(jnp.int32, (slot, HEAD_DIM), 0) // group
    own_row = lax.broadcasted_iota(jnp.int32, (ROW_STEP, LANES), 0)

    def scores_of(at, spread):
        here = pl.ds(at, ROW_STEP)
        for h in range(heads):
            g, j = h // group, h % group
            spread[pl.ds(h, ROW_STEP, stride=slot), :] = qkv[
                g, here, j * HEAD_DIM : (j + 1) * HEAD_DIM
            ]
        query = spread[...].T
        by_block = [
            jnp.where(lane_block == g, query, 0.0).astype(jnp.bfloat16) for g in range(blocks)
        ]
        scores = jnp.zeros((cached, LANES), jnp.float32)
        for r in range(ROW_STEP):
            mine = lane_row == r
            right = jnp.concatenate(
                [jnp.where(mine, q, jnp.zeros_like(q)) for q in by_block], axis=0
            )
            scores = scores + jnp.dot(
                kv_ref[at + r, :, :width], right, preferred_element_type=jnp.float32
            )
        own = jnp.zeros((ROW_STEP, LANES), jnp.float32)
        for g in range(blocks):
            new_key = qkv[g, here, key:value].astype(jnp.bfloat16)
            own = own + jnp.dot(new_key, by_block[g], preferred_element_type=jnp.float32)
        own = jnp.where(own_row == lane_row[:ROW_STEP], own, 0.0)
        return scores * inv, jnp.sum(own, axis=0, keepdims=True) * inv

    def softmax(at, scores, own):
        lens = jnp.zeros((1, LANES), jnp.int32)
        for r in range(ROW_STEP):
            lens = jnp.where(lane_row[:1] == r, len_ref[at + r], lens)
        valid = lax.broadcasted_iota(jnp.int32, scores.shape, 0) < lens
        scores = jnp.where(valid, scores, -jnp.inf)
        top = jnp.maximum(jnp.max(scores, axis=0, keepdims=True), own)
        expo = jnp.where(valid, jnp.exp(scores - top), 0.0)
        own_expo = jnp.exp(own - top)
        total = jnp.sum(expo, axis=0, keepdims=True) + own_expo
        probs = (expo / total).T.astype(jnp.bfloat16)
        own_prob = (own_expo / total).astype(jnp.bfloat16).astype(jnp.float32)
        return probs, jnp.broadcast_to(own_prob, (LANES, LANES)).T

    def context(at, probs, own_prob, gathered):
        here = pl.ds(at, ROW_STEP)
        value_rows = qkv.at[:, here, value:]
        for r in range(ROW_STEP):
            lanes = slice(r * slot, (r + 1) * slot)
            made = jnp.dot(
                probs[lanes], kv_ref[at + r, :, width:], preferred_element_type=jnp.float32
            )
            ctx = jnp.zeros((slot, HEAD_DIM), jnp.float32)
            new = jnp.zeros((slot, HEAD_DIM), jnp.float32)
            for g in range(blocks):
                block = made[:, g * HEAD_DIM : (g + 1) * HEAD_DIM]
                ctx = jnp.where(row_block == g, block, ctx)
                new = jnp.where(row_block == g, value_rows[g, r : r + 1, :], new)
            gathered[lanes, :] = ctx + own_prob[lanes] * new
        for h in range(heads):
            out_ref[here, h * HEAD_DIM : (h + 1) * HEAD_DIM] = gathered[
                pl.ds(h, ROW_STEP, stride=slot), :
            ]

    @pl.loop(0, rows // (sets * ROW_STEP))
    def _(i):
        first = pl.multiple_of(i * sets * ROW_STEP, sets * ROW_STEP)
        ats = [pl.multiple_of(first + k * ROW_STEP, ROW_STEP) for k in range(sets)]
        scored = [scores_of(at, spreads.at[k]) for k, at in enumerate(ats)]
        weighed = [softmax(at, *s) for at, s in zip(ats, scored)]
        for k, at in enumerate(ats):
            context(at, *weighed[k], gathereds.at[k])


def talker(here, terms, talker_gain, weights, kv_len, kv_cache):
    rows, cached, kv_width = kv_cache.shape
    wide, columns = weights[0].shape
    blocks = 4
    q_width = blocks * columns - kv_width
    sets = 2
    vmem = pl.BlockSpec(memory_space=pltpu.VMEM)
    smem = pl.BlockSpec(memory_space=pltpu.SMEM)
    return pl.pallas_call(
        talker_kernel,
        out_shape=(
            jax.ShapeDtypeStruct((rows, kv_width), jnp.bfloat16),
            jax.ShapeDtypeStruct((rows, q_width), jnp.float32),
        ),
        in_specs=[smem, smem, vmem]
        + [pl.BlockSpec(memory_space=pl.ANY)] * len(weights)
        + [vmem] * len(terms)
        + [vmem],
        out_specs=(vmem, vmem),
        scratch_shapes=[
            pltpu.VMEM((blocks, wide, columns), jnp.bfloat16),
            pltpu.SemaphoreType.DMA((len(weights),)),
            pltpu.VMEM((blocks, rows, columns), jnp.float32),
            pltpu.VMEM((sets, LANES, HEAD_DIM), jnp.float32),
            pltpu.VMEM((sets, LANES, HEAD_DIM), jnp.float32),
        ],
        cost_estimate=SHORT,
        compiler_params=pltpu.CompilerParams(vmem_limit_bytes=16 * 1024 * 1024),
    )(here, kv_len, talker_gain.reshape(1, wide), *weights, *terms, kv_cache)


def rms_norm(talker_in, talker_gain):
    scale = lax.rsqrt(jnp.mean(talker_in * talker_in, axis=1, keepdims=True) + 1e-06)
    return (talker_in * scale * talker_gain).astype(jnp.bfloat16)


def talker_step(talker_in, talker_gain, w_query, w_key, w_value, kv_len, kv_cache):
    owned = talker_in.shape[0]
    cached = kv_cache.shape[1]
    kv_width = w_key.shape[1]
    head_dim = HEAD_DIM
    kv_heads = kv_width // head_dim
    group = w_query.shape[1] // kv_width
    normed = rms_norm(talker_in, talker_gain)
    query = jnp.dot(normed, w_query, preferred_element_type=jnp.float32).astype(jnp.bfloat16)
    new_key = jnp.dot(normed, w_key, preferred_element_type=jnp.float32).astype(jnp.bfloat16)
    new_value = jnp.dot(normed, w_value, preferred_element_type=jnp.float32).astype(jnp.bfloat16)
    talker_kv = jnp.concatenate([new_key, new_value], axis=1)
    qb = query.reshape(owned, kv_heads, group, head_dim)
    keys = kv_cache[:, :, :kv_width].reshape(owned, cached, kv_heads, head_dim)
    values = kv_cache[:, :, kv_width:].reshape(owned, cached, kv_heads, head_dim)
    nk = new_key.reshape(owned, kv_heads, head_dim)
    nv = new_value.reshape(owned, kv_heads, head_dim)
    inv = 1.0 / head_dim**0.5
    scores = jnp.einsum("rgjd,rpgd->rgjp", qb, keys, preferred_element_type=jnp.float32) * inv
    own = jnp.einsum("rgjd,rgd->rgj", qb, nk, preferred_element_type=jnp.float32) * inv
    valid = (jnp.arange(cached, dtype=jnp.int32)[None, :] < kv_len[:, None])[:, None, None, :]
    scores = jnp.where(valid, scores, -jnp.inf)
    top = jnp.maximum(jnp.max(scores, axis=3), own)
    expo = jnp.where(valid, jnp.exp(scores - top[..., None]), 0.0)
    own_expo = jnp.exp(own - top)
    total = jnp.sum(expo, axis=3) + own_expo
    probs = (expo / total[..., None]).astype(jnp.bfloat16)
    own_prob = (own_expo / total).astype(jnp.bfloat16)
    ctx = jnp.einsum("rgjp,rpgd->rgjd", probs, values, preferred_element_type=jnp.float32)
    ctx = ctx + own_prob.astype(jnp.float32)[..., None] * nv.astype(jnp.float32)[:, :, None, :]
    return (talker_kv, ctx.reshape(owned, w_query.shape[1]))


def any_mesh(
    thinker_act,
    w_think,
    w_proj,
    talker_gain,
    w_query,
    w_key,
    w_value,
    talker_slot,
    kv_len,
    kv_cache,
):
    partial_sums = jnp.dot(
        thinker_act,
        lax.all_gather(w_think, ("section", "rows"), axis=1, tiled=True),
        preferred_element_type=jnp.float32,
    )
    full_query, full_key, full_value = (
        lax.all_gather(w_query, ("section", "rows"), axis=1, tiled=True),
        lax.all_gather(w_key, ("section", "rows"), axis=1, tiled=True),
        lax.all_gather(w_value, ("section", "rows"), axis=1, tiled=True),
    )
    mine = lax.psum_scatter(partial_sums, "mp", scatter_dimension=1, tiled=True)
    thinker_out = mine.astype(jnp.bfloat16)
    order = jnp.argsort(talker_slot[0], stable=True)
    sorted_out = thinker_out[order]
    talker_in = lax.psum_scatter(
        jnp.dot(sorted_out, w_proj, preferred_element_type=jnp.float32),
        "mp",
        scatter_dimension=0,
        tiled=True,
    )
    talker_kv, talker_ctx = talker_step(
        talker_in, talker_gain, full_query, full_key, full_value, kv_len, kv_cache
    )
    return (thinker_out, talker_kv, talker_ctx)


PLANE = ("section", "rows")
GROUP = ("mp", "section", "rows")


def over_core(x):
    return lax.ppermute(x, "rows", [(0, 1), (1, 0)])


def over_section(x):
    return lax.ppermute(x, "section", [(0, 1), (1, 0)])


def over_plane(x, e):
    return lax.ppermute(x, PLANE, [(b, b ^ e) for b in range(4)])


def over_groups(x):
    return lax.ppermute(x, "groups", [(0, 1), (1, 0)])


def after(x, *others):
    return lax.optimization_barrier((x, *others))[0]


def four_planes(
    thinker_act,
    w_think,
    w_proj,
    talker_gain,
    w_query,
    w_key,
    w_value,
    talker_slot,
    kv_len,
    kv_cache,
):
    planes = 4
    g, m, c = lax.axis_index("groups"), lax.axis_index("mp"), lax.axis_index(PLANE)
    here, plane = jnp.stack([m, c, g]), m.reshape(1)

    across, peer = over_section(thinker_act), over_core(thinker_act)
    near = down([in_hbm(thinker_act), peer], w_think, planes)
    near_terms = lax.all_to_all(near, "mp", 0, 0)
    mine = jnp.concatenate([w_query, w_key, w_value], axis=1)
    half = mine.shape[0] // 2
    my_half = lax.dynamic_slice_in_dim(mine, g * half, half, axis=0)

    across, near_terms, mine, my_half = lax.optimization_barrier(
        (across, near_terms, mine, my_half)
    )
    far = down([across, over_core(across)], w_think, planes)
    far_terms = lax.all_to_all(far, "mp", 0, 0)

    my_half = over_section(after(my_half, far))
    near_sums = add(after(near_terms, far))

    came = [
        lax.ppermute(x, GROUP, [(p * 4 + b, b * 4 + (b ^ p ^ k)) for p in range(4) for b in range(4)])
        for k, x in enumerate(add_and_deal(plane, near_sums, far_terms))
    ]
    my_half = after(my_half, near_sums)
    came[0], other_half = lax.optimization_barrier((came[0], over_groups(my_half)))
    thinker_out, *projected = project(here, talker_slot, w_proj, came)
    terms = projected[:1]
    for d in range(1, planes):
        terms.append(lax.ppermute(projected[d], "mp", [(p, p ^ d) for p in range(planes)]))
    other_half = after(other_half, projected[0])
    halves = [my_half, other_half, over_core(my_half), over_core(other_half)]
    weights = [mine, over_core(mine), *halves]
    staged = stage(after(kv_len, projected[0]), kv_cache)
    new_kv, ctx = talker(here, terms, talker_gain, weights, kv_len, staged)
    return (thinker_out, new_kv, ctx)


def solution(mesh):
    in_specs = (
        P(("groups", "section", "rows"), "mp"),
        P("mp", ("section", "rows")),
        P("mp", None),
        P(),
        P(None, ("section", "rows")),
        P(None, ("section", "rows")),
        P(None, ("section", "rows")),
        P(("groups", "section", "rows"), None),
        P(("groups", "mp", "section", "rows")),
        P(("groups", "mp", "section", "rows"), None, None),
    )
    out_specs = (
        P(("groups", "section", "rows"), "mp"),
        P(("groups", "mp", "section", "rows"), None),
        P(("groups", "mp", "section", "rows"), None),
    )
    sizes = tuple(mesh.shape[a] for a in ("groups", "section", "rows", "mp"))
    shards = four_planes if sizes == (2, 2, 2, 4) else any_mesh
    return jax.shard_map(shards, mesh=mesh, in_specs=in_specs, out_specs=out_specs, check_vma=False)
```

```python
import functools

import jax
import jax.numpy as jnp
from jax import lax
from jax.experimental import pallas as pl
from jax.experimental.pallas import tpu as pltpu
from jax.sharding import PartitionSpec as P

HEAD_DIM = 128
ROW_STEP = 8
LANES = 128
PAGES = 2
SHORT = pl.CostEstimate(flops=1, bytes_accessed=1, transcendentals=0)


def in_hbm(x):
    return pltpu.with_memory_space_constraint(x, pltpu.HBM)


def down_kernel(planes, cuts, groups, *refs):
    xs, (w, out, x_all, w_all, acc, x_sem, w_sem) = refs[:groups], refs[groups:]
    n = xs[0].shape[0]
    loads = []
    for s, (lo, hi) in enumerate(cuts):
        deep = pl.ds(lo, hi - lo)
        copies = [pltpu.make_async_copy(w.at[deep], w_all.at[deep], w_sem.at[s])]
        for i in range(groups):
            copies.append(
                pltpu.make_async_copy(
                    xs[i].at[:, deep], x_all.at[pl.ds(i * n, n), deep], x_sem.at[s, i]
                )
            )
        for copy in copies:
            copy.start()
        loads.append(copies)
    for s, (lo, hi) in enumerate(cuts):
        for copy in loads[s]:
            copy.wait()
        part = jnp.dot(x_all[:, lo:hi], w_all[lo:hi, :], preferred_element_type=jnp.float32)
        acc[...] = part if s == 0 else acc[...] + part
    part = n // planes
    for i in range(groups):
        for p in range(planes):
            at = i * n + p * part
            out[p, i * part : (i + 1) * part, :] = acc[at : at + part, :].astype(out.dtype)


def down(xs, w, planes):
    depth, columns = w.shape
    groups, n = len(xs), xs[0].shape[0]
    tiles, parts = depth // LANES, 6
    ends = [LANES * (tiles * i // parts) for i in range(parts)] + [depth]
    return pl.pallas_call(
        functools.partial(down_kernel, planes, list(zip(ends[:-1], ends[1:])), groups),
        out_shape=jax.ShapeDtypeStruct((planes, groups * n // planes, columns), jnp.bfloat16),
        in_specs=[pl.BlockSpec(memory_space=pl.ANY)] * (groups + 1),
        out_specs=pl.BlockSpec(memory_space=pltpu.VMEM),
        scratch_shapes=[
            pltpu.VMEM((groups * n, depth), jnp.bfloat16),
            pltpu.VMEM((depth, columns), jnp.bfloat16),
            pltpu.VMEM((groups * n, columns), jnp.float32),
            pltpu.SemaphoreType.DMA((parts, groups)),
            pltpu.SemaphoreType.DMA((parts,)),
        ],
        cost_estimate=SHORT,
        compiler_params=pltpu.CompilerParams(vmem_limit_bytes=24 * 1024 * 1024),
    )(*xs, in_hbm(w))


def add_kernel(terms, out):
    total = terms[0].astype(jnp.float32)
    for k in range(1, terms.shape[0]):
        total = total + terms[k].astype(jnp.float32)
    out[...] = total.astype(jnp.bfloat16)


def add(terms):
    vmem = pl.BlockSpec(memory_space=pltpu.VMEM)
    return pl.pallas_call(
        add_kernel,
        out_shape=jax.ShapeDtypeStruct(terms.shape[1:], jnp.bfloat16),
        in_specs=[vmem],
        out_specs=vmem,
        cost_estimate=SHORT,
        compiler_params=pltpu.CompilerParams(vmem_limit_bytes=10 * 1024 * 1024),
    )(terms)


def add_and_deal_kernel(plane_ref, near, terms, *refs):
    outs, sums = refs[:-1], refs[-1]
    total = terms[0].astype(jnp.float32)
    for k in range(1, terms.shape[0]):
        total = total + terms[k].astype(jnp.float32)
    rows = sums.shape[1]
    half = len(outs) // 2
    for e in range(half):
        sums[e] = near[e * rows : (e + 1) * rows, :]
        sums[half + e] = total[e * rows : (e + 1) * rows].astype(jnp.bfloat16)
    for k, out in enumerate(outs):
        out[...] = sums[plane_ref[0] ^ k]


def add_and_deal(plane, near, terms):
    rows, columns = near.shape
    blocks = 4
    part = jax.ShapeDtypeStruct((2 * rows // blocks, columns), jnp.bfloat16)
    vmem = pl.BlockSpec(memory_space=pltpu.VMEM)
    return pl.pallas_call(
        add_and_deal_kernel,
        out_shape=(part,) * blocks,
        in_specs=[pl.BlockSpec(memory_space=pltpu.SMEM), vmem, vmem],
        out_specs=(vmem,) * blocks,
        scratch_shapes=[pltpu.VMEM((blocks, *part.shape), jnp.bfloat16)],
        cost_estimate=SHORT,
        compiler_params=pltpu.CompilerParams(vmem_limit_bytes=10 * 1024 * 1024),
    )(plane, near, terms)


def project_kernel(planes, here_ref, slots, w_hbm, *refs):
    came, refs = refs[:planes], refs[planes:]
    home, outs, (parts, w, sem, w_sem) = refs[0], refs[1 : planes + 1], refs[planes + 1 :]
    plane, block = here_ref[0], here_ref[1]
    copies = [pltpu.make_async_copy(w_hbm, w, w_sem)]
    for k in range(planes):
        copies.append(pltpu.make_async_copy(came[k], parts.at[plane ^ block ^ k], sem.at[k]))
    for copy in copies:
        copy.start()
    for copy in copies:
        copy.wait()
    rows = parts.shape[1]
    for p in range(planes):
        home[p * rows : (p + 1) * rows, :] = parts[p]
    n = home.shape[0]
    place = lax.broadcasted_iota(jnp.int32, (n, n), 0)
    place = ((place // rows) ^ plane) * rows + place % rows
    pick = (place == slots[...]).astype(jnp.float32).astype(jnp.bfloat16)
    ordered = jnp.dot(pick, home[...], preferred_element_type=jnp.float32).astype(jnp.bfloat16)
    made = jnp.dot(ordered, w[...], preferred_element_type=jnp.float32).astype(jnp.bfloat16)
    for d in range(planes):
        outs[d][...] = made[d * rows : (d + 1) * rows]


def project(here, slots, w_proj, came):
    planes = len(came)
    rows, columns = came[0].shape
    vmem = pl.BlockSpec(memory_space=pltpu.VMEM)
    made = jax.ShapeDtypeStruct((rows, w_proj.shape[1]), jnp.bfloat16)
    return pl.pallas_call(
        functools.partial(project_kernel, planes),
        out_shape=(jax.ShapeDtypeStruct((planes * rows, columns), jnp.bfloat16), *[made] * planes),
        in_specs=[pl.BlockSpec(memory_space=pltpu.SMEM), vmem]
        + [pl.BlockSpec(memory_space=pl.ANY)] * (1 + planes),
        out_specs=(vmem,) * (1 + planes),
        scratch_shapes=[
            pltpu.VMEM((planes, rows, columns), jnp.bfloat16),
            pltpu.VMEM(w_proj.shape, w_proj.dtype),
            pltpu.SemaphoreType.DMA((planes,)),
            pltpu.SemaphoreType.DMA,
        ],
        cost_estimate=SHORT,
        compiler_params=pltpu.CompilerParams(vmem_limit_bytes=10 * 1024 * 1024),
    )(here, slots, in_hbm(w_proj), *came)


def page_copies(len_ref, kv_hbm, kv_ref, sem, r):
    page = kv_ref.shape[1] // PAGES
    out = []
    for p in range(PAGES):
        at = pl.ds(p * page, page)
        copy = pltpu.make_async_copy(kv_hbm.at[r, at], kv_ref.at[r, at], sem.at[r, p])
        out.append((copy, len_ref[r] > p * page))
    return out


def stage_kernel(len_ref, kv_hbm, kv_ref, sem):
    rows, cached, kv_width = kv_ref.shape
    page = cached // PAGES

    @pl.loop(0, rows)
    def _(r):
        for p, (copy, needed) in enumerate(page_copies(len_ref, kv_hbm, kv_ref, sem, r)):
            if p == 0:
                copy.start()
            else:
                pl.when(needed)(copy.start)

                @pl.when(jnp.logical_not(needed))
                def _(p=p, r=r):
                    kv_ref[r, p * page : (p + 1) * page, :] = jnp.zeros(
                        (page, kv_width), kv_ref.dtype
                    )

    @pl.loop(0, rows)
    def _(r):
        for p, (copy, needed) in enumerate(page_copies(len_ref, kv_hbm, kv_ref, sem, r)):
            if p == 0:
                copy.wait()
            else:
                pl.when(needed)(copy.wait)


def stage(kv_len, kv_cache):
    return pl.pallas_call(
        stage_kernel,
        out_shape=pltpu.VMEM(kv_cache.shape, kv_cache.dtype),
        in_specs=[pl.BlockSpec(memory_space=pltpu.SMEM), pl.BlockSpec(memory_space=pl.ANY)],
        out_specs=pl.BlockSpec(memory_space=pltpu.VMEM),
        scratch_shapes=[pltpu.SemaphoreType.DMA((kv_cache.shape[0], PAGES))],
        cost_estimate=SHORT,
        compiler_params=pltpu.CompilerParams(vmem_limit_bytes=8 * 1024 * 1024),
    )(kv_len, in_hbm(kv_cache))


def talker_kernel(here_ref, len_ref, gain, *refs):
    w_hbm, terms, refs = refs[:6], refs[6:-8], refs[-8:]
    kv_ref, new_kv, out_ref, w_ref, w_sem, qkv, spreads, gathereds = refs
    block, turn = here_ref[1], here_ref[2]
    blocks = qkv.shape[0]
    rows, cached, kv_width = kv_ref.shape
    width = kv_width // 2
    heads = out_ref.shape[1] // HEAD_DIM
    group = heads // blocks
    slot = LANES // ROW_STEP
    sets = spreads.shape[0]
    key, value = group * HEAD_DIM, (group + 1) * HEAD_DIM
    inv = 1.0 / HEAD_DIM**0.5

    half = w_ref.shape[1] // 2
    w_parts = [(w_ref.at[0],), (w_ref.at[1],)]
    for e in (2, 3):
        w_parts.append(
            [
                w_ref.at[e, pl.ds(pl.multiple_of(which * half, half), half)]
                for which in (turn, 1 - turn)
            ]
        )
    w_copies, at = [], 0
    for parts in w_parts:
        w_copies.append([])
        for part in parts:
            w_copies[-1].append(pltpu.make_async_copy(w_hbm[at], part, w_sem.at[at]))
            w_copies[-1][-1].start()
            at += 1

    total = terms[0][...].astype(jnp.float32)
    for term in terms[1:]:
        total = total + term[...].astype(jnp.float32)
    scale = lax.rsqrt(jnp.mean(total * total, axis=1, keepdims=True) + 1e-06)
    normed = (total * scale * gain[...]).astype(jnp.bfloat16)
    for e in range(blocks):
        for copy in w_copies[e]:
            copy.wait()
        made = jnp.dot(normed, w_ref[e], preferred_element_type=jnp.float32)
        qkv[e ^ block] = made.astype(jnp.bfloat16).astype(jnp.float32)
    for g in range(blocks):
        for place, start in ((g, key), (blocks + g, value)):
            new_kv[:, place * HEAD_DIM : (place + 1) * HEAD_DIM] = qkv[
                g, :, start : start + HEAD_DIM
            ].astype(jnp.bfloat16)

    spreads[...] = jnp.zeros_like(spreads)
    lane = lax.broadcasted_iota(jnp.int32, (HEAD_DIM, LANES), 1)
    lane_row, lane_block = lane // slot, lane % slot // group
    row_block = lax.broadcasted_iota(jnp.int32, (slot, HEAD_DIM), 0) // group
    own_row = lax.broadcasted_iota(jnp.int32, (ROW_STEP, LANES), 0)

    def scores_of(at, spread):
        here = pl.ds(at, ROW_STEP)
        for h in range(heads):
            g, j = h // group, h % group
            spread[pl.ds(h, ROW_STEP, stride=slot), :] = qkv[
                g, here, j * HEAD_DIM : (j + 1) * HEAD_DIM
            ]
        query = spread[...].T
        by_block = [
            jnp.where(lane_block == g, query, 0.0).astype(jnp.bfloat16) for g in range(blocks)
        ]
        scores = jnp.zeros((cached, LANES), jnp.float32)
        for r in range(ROW_STEP):
            mine = lane_row == r
            right = jnp.concatenate(
                [jnp.where(mine, q, jnp.zeros_like(q)) for q in by_block], axis=0
            )
            scores = scores + jnp.dot(
                kv_ref[at + r, :, :width], right, preferred_element_type=jnp.float32
            )
        own = jnp.zeros((ROW_STEP, LANES), jnp.float32)
        for g in range(blocks):
            new_key = qkv[g, here, key:value].astype(jnp.bfloat16)
            own = own + jnp.dot(new_key, by_block[g], preferred_element_type=jnp.float32)
        own = jnp.where(own_row == lane_row[:ROW_STEP], own, 0.0)
        return scores * inv, jnp.sum(own, axis=0, keepdims=True) * inv

    def softmax(at, scores, own):
        lens = jnp.zeros((1, LANES), jnp.int32)
        for r in range(ROW_STEP):
            lens = jnp.where(lane_row[:1] == r, len_ref[at + r], lens)
        valid = lax.broadcasted_iota(jnp.int32, scores.shape, 0) < lens
        scores = jnp.where(valid, scores, -jnp.inf)
        top = jnp.maximum(jnp.max(scores, axis=0, keepdims=True), own)
        expo = jnp.where(valid, jnp.exp(scores - top), 0.0)
        own_expo = jnp.exp(own - top)
        total = jnp.sum(expo, axis=0, keepdims=True) + own_expo
        probs = (expo / total).T.astype(jnp.bfloat16)
        own_prob = (own_expo / total).astype(jnp.bfloat16).astype(jnp.float32)
        return probs, jnp.broadcast_to(own_prob, (LANES, LANES)).T

    def context(at, probs, own_prob, gathered):
        here = pl.ds(at, ROW_STEP)
        value_rows = qkv.at[:, here, value:]
        for r in range(ROW_STEP):
            lanes = slice(r * slot, (r + 1) * slot)
            made = jnp.dot(
                probs[lanes], kv_ref[at + r, :, width:], preferred_element_type=jnp.float32
            )
            ctx = jnp.zeros((slot, HEAD_DIM), jnp.float32)
            new = jnp.zeros((slot, HEAD_DIM), jnp.float32)
            for g in range(blocks):
                block = made[:, g * HEAD_DIM : (g + 1) * HEAD_DIM]
                ctx = jnp.where(row_block == g, block, ctx)
                new = jnp.where(row_block == g, value_rows[g, r : r + 1, :], new)
            gathered[lanes, :] = ctx + own_prob[lanes] * new
        for h in range(heads):
            out_ref[here, h * HEAD_DIM : (h + 1) * HEAD_DIM] = gathered[
                pl.ds(h, ROW_STEP, stride=slot), :
            ]

    @pl.loop(0, rows // (sets * ROW_STEP))
    def _(i):
        first = pl.multiple_of(i * sets * ROW_STEP, sets * ROW_STEP)
        ats = [pl.multiple_of(first + k * ROW_STEP, ROW_STEP) for k in range(sets)]
        scored = [scores_of(at, spreads.at[k]) for k, at in enumerate(ats)]
        weighed = [softmax(at, *s) for at, s in zip(ats, scored)]
        for k, at in enumerate(ats):
            context(at, *weighed[k], gathereds.at[k])


def talker(here, terms, talker_gain, weights, kv_len, kv_cache):
    rows, cached, kv_width = kv_cache.shape
    wide, columns = weights[0].shape
    blocks = 4
    q_width = blocks * columns - kv_width
    sets = 2
    vmem = pl.BlockSpec(memory_space=pltpu.VMEM)
    smem = pl.BlockSpec(memory_space=pltpu.SMEM)
    return pl.pallas_call(
        talker_kernel,
        out_shape=(
            jax.ShapeDtypeStruct((rows, kv_width), jnp.bfloat16),
            jax.ShapeDtypeStruct((rows, q_width), jnp.float32),
        ),
        in_specs=[smem, smem, vmem]
        + [pl.BlockSpec(memory_space=pl.ANY)] * len(weights)
        + [vmem] * len(terms)
        + [vmem],
        out_specs=(vmem, vmem),
        scratch_shapes=[
            pltpu.VMEM((blocks, wide, columns), jnp.bfloat16),
            pltpu.SemaphoreType.DMA((len(weights),)),
            pltpu.VMEM((blocks, rows, columns), jnp.float32),
            pltpu.VMEM((sets, LANES, HEAD_DIM), jnp.float32),
            pltpu.VMEM((sets, LANES, HEAD_DIM), jnp.float32),
        ],
        cost_estimate=SHORT,
        compiler_params=pltpu.CompilerParams(vmem_limit_bytes=10 * 1024 * 1024),
    )(here, kv_len, talker_gain.reshape(1, wide), *weights, *terms, kv_cache)


def rms_norm(talker_in, talker_gain):
    scale = lax.rsqrt(jnp.mean(talker_in * talker_in, axis=1, keepdims=True) + 1e-06)
    return (talker_in * scale * talker_gain).astype(jnp.bfloat16)


def talker_step(talker_in, talker_gain, w_query, w_key, w_value, kv_len, kv_cache):
    owned = talker_in.shape[0]
    cached = kv_cache.shape[1]
    kv_width = w_key.shape[1]
    head_dim = HEAD_DIM
    kv_heads = kv_width // head_dim
    group = w_query.shape[1] // kv_width
    normed = rms_norm(talker_in, talker_gain)
    query = jnp.dot(normed, w_query, preferred_element_type=jnp.float32).astype(jnp.bfloat16)
    new_key = jnp.dot(normed, w_key, preferred_element_type=jnp.float32).astype(jnp.bfloat16)
    new_value = jnp.dot(normed, w_value, preferred_element_type=jnp.float32).astype(jnp.bfloat16)
    talker_kv = jnp.concatenate([new_key, new_value], axis=1)
    qb = query.reshape(owned, kv_heads, group, head_dim)
    keys = kv_cache[:, :, :kv_width].reshape(owned, cached, kv_heads, head_dim)
    values = kv_cache[:, :, kv_width:].reshape(owned, cached, kv_heads, head_dim)
    nk = new_key.reshape(owned, kv_heads, head_dim)
    nv = new_value.reshape(owned, kv_heads, head_dim)
    inv = 1.0 / head_dim**0.5
    scores = jnp.einsum("rgjd,rpgd->rgjp", qb, keys, preferred_element_type=jnp.float32) * inv
    own = jnp.einsum("rgjd,rgd->rgj", qb, nk, preferred_element_type=jnp.float32) * inv
    valid = (jnp.arange(cached, dtype=jnp.int32)[None, :] < kv_len[:, None])[:, None, None, :]
    scores = jnp.where(valid, scores, -jnp.inf)
    top = jnp.maximum(jnp.max(scores, axis=3), own)
    expo = jnp.where(valid, jnp.exp(scores - top[..., None]), 0.0)
    own_expo = jnp.exp(own - top)
    total = jnp.sum(expo, axis=3) + own_expo
    probs = (expo / total[..., None]).astype(jnp.bfloat16)
    own_prob = (own_expo / total).astype(jnp.bfloat16)
    ctx = jnp.einsum("rgjp,rpgd->rgjd", probs, values, preferred_element_type=jnp.float32)
    ctx = ctx + own_prob.astype(jnp.float32)[..., None] * nv.astype(jnp.float32)[:, :, None, :]
    return (talker_kv, ctx.reshape(owned, w_query.shape[1]))


def any_mesh(
    thinker_act,
    w_think,
    w_proj,
    talker_gain,
    w_query,
    w_key,
    w_value,
    talker_slot,
    kv_len,
    kv_cache,
):
    partial_sums = jnp.dot(
        thinker_act,
        lax.all_gather(w_think, ("section", "rows"), axis=1, tiled=True),
        preferred_element_type=jnp.float32,
    )
    full_query, full_key, full_value = (
        lax.all_gather(w_query, ("section", "rows"), axis=1, tiled=True),
        lax.all_gather(w_key, ("section", "rows"), axis=1, tiled=True),
        lax.all_gather(w_value, ("section", "rows"), axis=1, tiled=True),
    )
    mine = lax.psum_scatter(partial_sums, "mp", scatter_dimension=1, tiled=True)
    thinker_out = mine.astype(jnp.bfloat16)
    order = jnp.argsort(talker_slot[0], stable=True)
    sorted_out = thinker_out[order]
    talker_in = lax.psum_scatter(
        jnp.dot(sorted_out, w_proj, preferred_element_type=jnp.float32),
        "mp",
        scatter_dimension=0,
        tiled=True,
    )
    talker_kv, talker_ctx = talker_step(
        talker_in, talker_gain, full_query, full_key, full_value, kv_len, kv_cache
    )
    return (thinker_out, talker_kv, talker_ctx)


PLANE = ("section", "rows")
GROUP = ("mp", "section", "rows")


def over_core(x):
    return lax.ppermute(x, "rows", [(0, 1), (1, 0)])


def over_section(x):
    return lax.ppermute(x, "section", [(0, 1), (1, 0)])


def over_plane(x, e):
    return lax.ppermute(x, PLANE, [(b, b ^ e) for b in range(4)])


def over_groups(x):
    return lax.ppermute(x, "groups", [(0, 1), (1, 0)])


def after(x, *others):
    return lax.optimization_barrier((x, *others))[0]


def four_planes(
    thinker_act,
    w_think,
    w_proj,
    talker_gain,
    w_query,
    w_key,
    w_value,
    talker_slot,
    kv_len,
    kv_cache,
):
    planes = 4
    g, m, c = lax.axis_index("groups"), lax.axis_index("mp"), lax.axis_index(PLANE)
    here, plane = jnp.stack([m, c, g]), m.reshape(1)

    across, peer = over_section(thinker_act), over_core(thinker_act)
    near = down([in_hbm(thinker_act), peer], w_think, planes)
    near_terms = lax.all_to_all(near, "mp", 0, 0)
    mine = jnp.concatenate([w_query, w_key, w_value], axis=1)
    half = mine.shape[0] // 2
    my_half = lax.dynamic_slice_in_dim(mine, g * half, half, axis=0)

    across, near_terms, mine, my_half = lax.optimization_barrier(
        (across, near_terms, mine, my_half)
    )
    far = down([across, over_core(across)], w_think, planes)
    far_terms = lax.all_to_all(far, "mp", 0, 0)

    my_half = over_section(after(my_half, far))
    near_sums = add(after(near_terms, far))
    staged = stage(after(kv_len, far), kv_cache)
    far_terms, staged = lax.optimization_barrier((far_terms, staged))

    came = [
        lax.ppermute(x, GROUP, [(p * 4 + b, b * 4 + (b ^ p ^ k)) for p in range(4) for b in range(4)])
        for k, x in enumerate(add_and_deal(plane, near_sums, far_terms))
    ]
    my_half = after(my_half, near_sums)
    came[0], other_half = lax.optimization_barrier((came[0], over_groups(my_half)))
    thinker_out, *projected = project(here, talker_slot, w_proj, came)
    terms = projected[:1]
    for d in range(1, planes):
        terms.append(lax.ppermute(projected[d], "mp", [(p, p ^ d) for p in range(planes)]))
    other_half = after(other_half, projected[0])
    halves = [my_half, other_half, over_core(my_half), over_core(other_half)]
    weights = [mine, over_core(mine), *halves]
    new_kv, ctx = talker(here, terms, talker_gain, weights, kv_len, staged)
    return (thinker_out, new_kv, ctx)


def solution(mesh):
    in_specs = (
        P(("groups", "section", "rows"), "mp"),
        P("mp", ("section", "rows")),
        P("mp", None),
        P(),
        P(None, ("section", "rows")),
        P(None, ("section", "rows")),
        P(None, ("section", "rows")),
        P(("groups", "section", "rows"), None),
        P(("groups", "mp", "section", "rows")),
        P(("groups", "mp", "section", "rows"), None, None),
    )
    out_specs = (
        P(("groups", "section", "rows"), "mp"),
        P(("groups", "mp", "section", "rows"), None),
        P(("groups", "mp", "section", "rows"), None),
    )
    sizes = tuple(mesh.shape[a] for a in ("groups", "section", "rows", "mp"))
    shards = four_planes if sizes == (2, 2, 2, 4) else any_mesh
    return jax.shard_map(shards, mesh=mesh, in_specs=in_specs, out_specs=out_specs, check_vma=False)
```
